32 devices in a mesh: blk: 16 (over z, x, core), tensor: 2 (over y).
Axes of the slice: x: 2, y: 2, z: 4, core: 2. Of those that a mesh axis runs over, the one named last changes fastest.
Arguments:
- tokens: bfloat16 [2048, 1024], P('blk'), may hold values from -6 to 6
- query_vecs: bfloat16 [4096, 128], replicated, may hold values from -6 to 6
- out_cotangent: bfloat16 [2048, 1024], P('blk'), may hold values from -6 to 6
- doc_lengths: int32 [4], replicated, may hold values from 1 to 2045, as said below
- live_mask: int32 [2048], P('blk'), may hold values from 0 to 1, as said below
- positives: int32 [128], replicated, may hold values from 0 to 3
- triple_weight: float32 [1024, 3, 1024], P('blk', None, 'tensor'), may hold values from -0.1875 to 0.1875
- triple_bias: float32 [3, 1024], P(None, 'tensor'), may hold values from -1.75 to 1.75
- output_weight: float32 [1024, 1024], P('tensor', 'blk'), may hold values from -2 to 2
- output_bias: float32 [1024], replicated, may hold values from -1.75 to 1.75
- first_gain: float32 [1024], replicated, may hold values from 0.5 to 1.5
- first_shift: float32 [1024], replicated, may hold values from -1.75 to 1.75
- expand_weight: float32 [1024, 4096], P('blk', 'tensor'), may hold values from -0.1875 to 0.1875
- expand_bias: float32 [4096], P('tensor'), may hold values from -1.75 to 1.75
- contract_weight: float32 [4096, 1024], P('tensor', 'blk'), may hold values from -0.09375 to 0.09375
- contract_bias: float32 [1024], replicated, may hold values from -1.75 to 1.75
- second_gain: float32 [1024], replicated, may hold values from 0.5 to 1.5
- second_shift: float32 [1024], replicated, may hold values from -1.75 to 1.75
- head_weight: float32 [1024, 128], replicated, may hold values from -0.1875 to 0.1875
Outputs:
- mixed: bfloat16 [2048, 1024], P('blk')
- loss: float32 [], replicated
- tokens_grad: float32 [2048, 1024], P('blk')
- queries_grad: float32 [4096, 128], replicated
- triple_grad: float32 [1024, 3, 1024], P('blk', None, 'tensor')
- triplebias_grad: float32 [3, 1024], P(None, 'tensor')
- output_grad: float32 [1024, 1024], P('tensor', 'blk')
- outputbias_grad: float32 [1024], replicated
- firstgain_grad: float32 [1024], replicated
- firstshift_grad: float32 [1024], replicated
- expand_grad: float32 [1024, 4096], P('blk', 'tensor')
- expandbias_grad: float32 [4096], P('tensor')
- contract_grad: float32 [4096, 1024], P('tensor', 'blk')
- contractbias_grad: float32 [1024], replicated
- secondgain_grad: float32 [1024], replicated
- secondshift_grad: float32 [1024], replicated
- head_grad: float32 [1024, 128], replicated
The draws below stay inside these ranges and needn't reach their ends.
Inputs may be any that keep to these rules, and one draw needn't show every extreme that they name: `doc_lengths`: every aligned run of 2048 packed positions holds whole documents, 4 of them; in each run the longest is exactly 2045 tokens. `live_mask`: the first token of every document is live.
All inputs are finite; a program needn't handle non-finite values.
Results may differ from the reference program's by a relative error of at most 0.014.
The reference program's roundings to bfloat16 on the way count: a program that leaves them out, or rounds other values in their place, can miss the bound.
Values may be sent and summed in bfloat16 or wider, within the bound.
No kernel may reach another device: no remote copies, remote signals or barrier semaphores. Data moves between devices by JAX's collectives and lax.ppermute only.
A program may use at most 192 MiB of HBM per device.

```python
import math
import jax
import jax.numpy as jnp
from jax import lax

D = 1024
HEADS = 16
HEAD_DIM = 64
FF = 4096
PROJ = 128
DOC_MEAN = 512
QUERIES = 128
QUERY_LEN = 32
TOK_DEV = 128
TOKENS = 2048
PACK = 2048
DOCS = 4
DOC_MOST = 2045
QTOKENS = 4096
N_BLK = 16


def packing(key):
    pick_key, weight_key = jax.random.split(key, 2)
    row_count = TOKENS // PACK
    per_row = DOCS // row_count
    others_count = per_row - 1
    longest = jax.random.randint(pick_key, (row_count,), 0, per_row)
    weights = jax.random.randint(weight_key, (row_count, per_row), 2, 6)
    order = jnp.arange(per_row)[None, :]
    others = order != longest[:, None]
    weight_sum = jnp.maximum(jnp.sum(jnp.where(others, weights, 0), axis=1, keepdims=True), 1)
    rest = PACK - DOC_MOST
    base = jnp.where(others, 1 + (rest - others_count) * weights // weight_sum, 0)
    remainder = rest - jnp.sum(base, axis=1, keepdims=True)
    recipient = (longest[:, None] + 1) % per_row
    lengths = base + jnp.where(order == recipient, remainder, 0)
    lengths = lengths + jnp.where(order == longest[:, None], DOC_MOST, 0)
    return lengths.reshape(DOCS).astype(jnp.int32)


def draw_doc_lengths(key, part):
    return packing(key)


def draw_live_mask(key, part):
    lengths = packing(key)
    key = jax.random.fold_in(key, 7)
    coins = jax.random.randint(key, (TOKENS,), 0, 8)
    starts = jnp.cumsum(lengths) - lengths
    array_rows = starts % N_BLK * TOK_DEV + starts // N_BLK
    firsts = jnp.zeros((TOKENS,), jnp.int32).at[array_rows].set(1)
    return jnp.maximum((coins > 0).astype(jnp.int32), firsts)


def plant(drawn, rng, least, largest):
    extent = drawn.shape
    spot = [jax.random.randint(jax.random.fold_in(rng, axis), (), 0, extent[axis]) for axis in range(len(extent))]
    drawn = drawn.at[tuple(spot)].set(least)
    longest = extent.index(max(extent))
    spot[longest] = (spot[longest] + 1) % extent[longest]
    return drawn.at[tuple(spot)].set(largest)


def block_levels(stream_key, extent, cuts, low, high):
    def one(axis_at, blocks):
        draws = jax.random.uniform(jax.random.fold_in(jax.random.fold_in(stream_key, 6), axis_at), (blocks,), jnp.float32, low / len(cuts), high / len(cuts))
        return jnp.repeat(jnp.exp(draws), extent[axis_at] // blocks).reshape((-1,) + (1,) * (len(extent) - axis_at - 1))

    factor_of = one(*cuts[0])
    for cut in cuts[1:]:
        factor_of = factor_of * one(*cut)
    return factor_of


def scatter_about(stream_key, extent, scale, most, pieces=(), held_as=jnp.bfloat16):
    level = block_levels(stream_key, extent, pieces, -0.22, 0.18) if pieces else 1.0
    values = jax.random.normal(stream_key, extent, jnp.float32) * scale * level
    return jnp.minimum(jnp.maximum(values, -most), most).astype(held_as)


def setup_inputs(seed: int = 0) -> dict:
    key_of = jax.random.split(jax.random.key(seed), 20)
    tokens = scatter_about(key_of[0], (TOKENS, D), 1.0, 6.0, ((0, 16),))
    query_vecs = scatter_about(key_of[1], (QTOKENS, PROJ), 1.0, 6.0)
    out_cotangent = scatter_about(key_of[2], (TOKENS, D), 1.0, 6.0, ((0, 16),))
    doc_lengths = draw_doc_lengths(jax.random.fold_in(key_of[19], 71), 0)
    live_mask = draw_live_mask(jax.random.fold_in(key_of[19], 71), 0)
    positives = plant(jax.random.randint(key_of[5], (QUERIES,), 0, DOCS), jax.random.fold_in(key_of[5], 1), 0, DOCS - 1).astype(jnp.int32)
    triple_weight = scatter_about(key_of[6], (D, 3, D), D ** -0.5, 0.1875, ((0, 16), (2, 2)), jnp.float32)
    triple_bias = scatter_about(key_of[7], (3, D), 0.3, 1.75, ((1, 2),), jnp.float32)
    output_weight = scatter_about(key_of[8], (D, D), (0.5 * DOC_MEAN ** 0.5 * D ** (0 - 0.5)), 2.0, ((0, 2), (1, 16)), jnp.float32)
    output_bias = scatter_about(key_of[9], (D,), 0.3, 1.75, (), jnp.float32)
    first_gain = jnp.clip(1.0 + 0.1 * jax.random.normal(key_of[10], (D,), jnp.float32), 0.5, 1.5)
    first_shift = scatter_about(key_of[11], (D,), 0.3, 1.75, (), jnp.float32)
    expand_weight = scatter_about(key_of[12], (D, FF), D ** -0.5, 0.1875, ((0, 16), (1, 2)), jnp.float32)
    expand_bias = scatter_about(key_of[13], (FF,), 0.3, 1.75, ((0, 2),), jnp.float32)
    contract_weight = scatter_about(key_of[14], (FF, D), FF ** -0.5, 0.09375, ((0, 2), (1, 16)), jnp.float32)
    contract_bias = scatter_about(key_of[15], (D,), 0.3, 1.75, (), jnp.float32)
    second_gain = jnp.clip(1.0 + 0.1 * jax.random.normal(key_of[16], (D,), jnp.float32), 0.5, 1.5)
    second_shift = scatter_about(key_of[17], (D,), 0.3, 1.75, (), jnp.float32)
    head_weight = scatter_about(key_of[18], (D, PROJ), D ** -0.5, 0.1875, (), jnp.float32)
    return dict(tokens=tokens, query_vecs=query_vecs, out_cotangent=out_cotangent, doc_lengths=doc_lengths, live_mask=live_mask, positives=positives, triple_weight=triple_weight, triple_bias=triple_bias, output_weight=output_weight, output_bias=output_bias, first_gain=first_gain, first_shift=first_shift, expand_weight=expand_weight, expand_bias=expand_bias, contract_weight=contract_weight, contract_bias=contract_bias, second_gain=second_gain, second_shift=second_shift, head_weight=head_weight)


@jax.custom_vjp
def low(v):
    return lax.optimization_barrier(v.astype(jnp.bfloat16)).astype(jnp.float32)

@jax.custom_vjp
def low_back(v):
    return v

def low_keep(v):
    return (low(v), None)

def low_pass(kept, grad):
    return (grad,)

def back_keep(v):
    return (v, None)

def back_low(kept, grad):
    return (low(grad),)
low.defvjp(low_keep, low_pass)
low_back.defvjp(back_keep, back_low)
SOFTMAX_TEMPER = 0.05
FLOOR_SCORE = -1e+30
NORM_EPSILON = 1e-05
UNIT_EPSILON = 1e-06
PRECISE = lax.Precision.HIGHEST

def layer_norm(value, gain, shift):
    center = value - lax.optimization_barrier(jnp.mean(value, axis=-1, keepdims=True))
    spread = lax.optimization_barrier(jnp.mean(center * center, axis=-1, keepdims=True))
    return center * lax.rsqrt(spread + NORM_EPSILON) * gain + shift

def unit_rows(value):
    return value * lax.rsqrt(lax.optimization_barrier(jnp.sum(value * value, axis=-1, keepdims=True)) + UNIT_EPSILON)

def rotate(value, angles):
    half = value.shape[-1] // 2
    cosine = jnp.cos(angles)[:, None, :]
    sine = jnp.sin(angles)[:, None, :]
    former = value[..., :half]
    latter = value[..., half:]
    return jnp.concatenate([former * cosine - latter * sine, latter * cosine + former * sine], axis=-1)

def doc_layout(doc_lengths, places):
    ends = jnp.cumsum(doc_lengths).astype(jnp.int32)
    starts = (ends - doc_lengths).astype(jnp.int32)
    passed = starts[None, :] <= places[:, None]
    doc_index = (lax.optimization_barrier(jnp.sum(passed.astype(jnp.int32), axis=1)) - 1).astype(jnp.int32)
    begin = lax.optimization_barrier(jnp.max(jnp.where(passed, starts[None, :], 0), axis=1)).astype(jnp.int32)
    return (doc_index, (places - begin).astype(jnp.int32))

def angles_of(position, head_dim):
    exponent = jnp.arange(0, head_dim, 2).astype(jnp.float32) / head_dim
    inverse = jnp.exp(-math.log(10000.0) * exponent)
    return position.astype(jnp.float32)[:, None] * inverse[None, :]

def reference(tokens, query_vecs, out_cotangent, doc_lengths, live_mask, positives, triple_weight, triple_bias, output_weight, output_bias, first_gain, first_shift, expand_weight, expand_bias, contract_weight, contract_bias, second_gain, second_shift, head_weight):
    rows_all = jnp.arange(TOKENS, dtype=jnp.int32)
    places = (rows_all % TOK_DEV * N_BLK + rows_all // TOK_DEV).astype(jnp.int32)
    doc_index, position = doc_layout(doc_lengths, places)
    angles = angles_of(position, HEAD_DIM)
    live_tokens = live_mask.astype(jnp.float32)
    labels = jnp.arange(DOCS, dtype=jnp.int32)
    onehot = (doc_index[:, None] == labels[None, :]).astype(jnp.float32)
    chosen = (positives[:, None] == labels[None, :]).astype(jnp.float32)
    cotangent = out_cotangent.astype(jnp.float32)
    block = math.gcd(512, TOKENS)
    scale = HEAD_DIM ** (-0.5)

    def objective(inputs, queries, params):
        triple_w, triple_b, output_w, output_b, gain_one, shift_one, expand_w, expand_b, contract_w, contract_b, gain_two, shift_two, head_w = params
        triple = low_back(jnp.einsum('td,dce->tce', inputs, low(triple_w), precision=PRECISE) + triple_b[None])
        shaped = triple.reshape(TOKENS, 3, HEADS, HEAD_DIM)
        query_rot = low(rotate(shaped[:, 0], angles))
        key_rot = low(rotate(shaped[:, 1], angles))
        value_low = low(shaped[:, 2])

        def attend(item):
            query_block, doc_block = item
            raw = low_back(jnp.einsum('qhe,khe->qhk', query_block, key_rot, precision=PRECISE))
            allowed = ((doc_block[:, None] == doc_index[None, :]) & (live_tokens[None, :] > 0.0))[:, None, :]
            score = jnp.where(allowed, raw * scale, FLOOR_SCORE)
            peak = lax.optimization_barrier(jnp.max(score, axis=-1, keepdims=True))
            weight = jnp.where(allowed, jnp.exp(score - peak), 0.0)
            prob = weight / lax.optimization_barrier(jnp.sum(weight, axis=-1, keepdims=True))
            return jnp.einsum('qhk,khe->qhe', prob, value_low, precision=PRECISE)
        attended = lax.map(jax.checkpoint(attend), (query_rot.reshape(TOKENS // block, block, HEADS, HEAD_DIM), doc_index.reshape(TOKENS // block, block)))
        attended_low = low(low_back(attended.reshape(TOKENS, D)))
        branch = low_back(jnp.dot(attended_low, low(output_w), precision=PRECISE) + output_b)
        first = layer_norm(inputs + branch, gain_one, shift_one)
        hidden_in = low_back(jnp.dot(low(first), low(expand_w), precision=PRECISE) + expand_b)
        hidden = low(jax.nn.gelu(hidden_in, approximate=False))
        expanded = low_back(jnp.dot(hidden, low(contract_w), precision=PRECISE) + contract_b)
        second = layer_norm(first + expanded, gain_two, shift_two)
        embed = low_back(jnp.dot(low(second), low(head_w), precision=PRECISE))
        unit = low(unit_rows(embed))
        query_unit = low(unit_rows(queries))
        similarity_scores = low_back(jnp.dot(unit, query_unit.T, precision=PRECISE))
        exponent_values = jnp.exp(similarity_scores / SOFTMAX_TEMPER) * live_tokens[:, None]
        score_totals = jnp.dot(exponent_values.T, onehot, precision=PRECISE)
        token_counts = lax.optimization_barrier(jnp.sum(onehot * live_tokens[:, None], axis=0))
        token_scores = SOFTMAX_TEMPER * (jnp.log(score_totals) - jnp.log(token_counts)[None, :])
        doc_score = lax.optimization_barrier(jnp.sum(token_scores.reshape(QUERIES, QUERY_LEN, DOCS), axis=1))
        best = lax.optimization_barrier(jnp.max(doc_score, axis=1, keepdims=True))
        spread = best[:, 0] + jnp.log(lax.optimization_barrier(jnp.sum(jnp.exp(doc_score - best), axis=1)))
        loss = jnp.mean(spread - lax.optimization_barrier(jnp.sum(doc_score * chosen, axis=1)))
        return (loss + jnp.sum(second * cotangent), (second, loss))
    params = (triple_weight, triple_bias, output_weight, output_bias, first_gain, first_shift, expand_weight, expand_bias, contract_weight, contract_bias, second_gain, second_shift, head_weight)
    value, pull, extra = jax.vjp(objective, tokens.astype(jnp.float32), query_vecs.astype(jnp.float32), params, has_aux=True)
    tokens_grad, queries_grad, grads = pull(jnp.ones_like(value))
    second, loss = extra
    return (second.astype(jnp.bfloat16), loss, tokens_grad, queries_grad, grads[0], grads[1], grads[2], grads[3], grads[4], grads[5], grads[6], grads[7], grads[8], grads[9], grads[10], grads[11], grads[12])
```

```python
from functools import partial
import math

import jax
import jax.numpy as jnp
import numpy as np
from jax import lax
from jax.experimental import pallas as pl
from jax.experimental.pallas import tpu as pltpu
from jax.sharding import Mesh, PartitionSpec as P

HEAD_DIM = 64
PAIR = 2 * HEAD_DIM

SOFTMAX_TEMPER = 0.05
FLOOR_SCORE = -1e30
NORM_EPSILON = 1e-05
UNIT_EPSILON = 1e-06
PRECISE = lax.Precision.HIGHEST
LOW = jnp.bfloat16
WIDE = jnp.float32

BLK = ("o", "z", "x", "c")
NZ = 4
FOUR = [0, 1, 2, 3]


def xor_z(value, mask):
    return lax.ppermute(value, "z", [(i, i ^ mask) for i in FOUR])


def xor_w(value, mask):
    return lax.ppermute(value, ("x", "y"), [(i, i ^ mask) for i in FOUR])


def flip(value, axis):
    return lax.ppermute(value, axis, [(0, 1), (1, 0)])


def pick(value, index, axis=0):
    return lax.dynamic_index_in_dim(value, index, axis, keepdims=False)


def place(pieces):
    first = pieces[0][1]
    whole = jnp.zeros((len(pieces),) + first.shape, first.dtype)
    for index, piece in pieces:
        whole = lax.dynamic_update_slice_in_dim(whole, piece[None], index, 0)
    return whole


def both(mine, other, where):
    return place([(where, mine), (1 - where, other)])


def gather_w(value, me):
    return place([(me, value)] + [(me ^ m, xor_w(value, m)) for m in (1, 2, 3)])


def scatter_w(parts, me):
    total = pick(parts, me).astype(WIDE)
    for m in (1, 2, 3):
        total = total + xor_w(pick(parts, me ^ m), m).astype(WIDE)
    return total


def scatter_z(parts, me):
    total = pick(parts, me).astype(WIDE)
    for m in (1, 2, 3):
        total = total + xor_z(pick(parts, me ^ m), m).astype(WIDE)
    return total


def layer_norm(value, gain, shift):
    center = value - jnp.mean(value, axis=-1, keepdims=True)
    spread = jnp.mean(center * center, axis=-1, keepdims=True)
    return center * lax.rsqrt(spread + NORM_EPSILON) * gain + shift


def unit_rows(value):
    return value * lax.rsqrt(jnp.sum(value * value, axis=-1, keepdims=True) + UNIT_EPSILON)


def doc_layout(doc_lengths, places):
    ends = jnp.cumsum(doc_lengths)
    starts = ends - doc_lengths
    passed = starts[None, :] <= places[:, None]
    doc_index = jnp.sum(passed.astype(jnp.int32), axis=1) - 1
    begin = jnp.max(jnp.where(passed, starts[None, :], 0), axis=1)
    return (doc_index, places - begin)


def angles_of(position, head_dim):
    exponent = jnp.arange(0, head_dim, 2).astype(jnp.float32) / head_dim
    inverse = jnp.exp(-math.log(10000.0) * exponent)
    return position.astype(jnp.float32)[:, None] * inverse[None, :]


def turn(value, cosine, sine):
    half = value.shape[-1] // 2
    former, latter = value[:, :half], value[:, half:]
    return jnp.concatenate(
        [former * cosine - latter * sine, latter * cosine + former * sine], axis=-1
    )


def dot_nn(a, b):
    return lax.dot_general(a, b, (((1,), (0,)), ((), ())), preferred_element_type=WIDE)


def dot_nt(a, b):
    return lax.dot_general(a, b, (((1,), (1,)), ((), ())), preferred_element_type=WIDE)


def dot_tn(a, b):
    return lax.dot_general(a, b, (((0,), (0,)), ((), ())), preferred_element_type=WIDE)


def attend_kernel(q_ref, kv0_ref, kv1_ref, qdoc_ref, kdoc0_ref, kdoc1_ref, out_ref, log_ref):
    scale = HEAD_DIM ** (-0.5)
    queries = q_ref[...]
    kv = (kv0_ref[...], kv1_ref[...])
    doc = qdoc_ref[...]
    allowed = [doc == ref[...] for ref in (kdoc0_ref, kdoc1_ref)]
    scores = [
        jnp.where(ok, dot_nt(queries, keys) * scale, FLOOR_SCORE) for ok, keys in zip(allowed, kv)
    ]
    peak = jnp.maximum(*[jnp.max(s, axis=-1, keepdims=True) for s in scores])
    weights = [jnp.where(ok, jnp.exp(s - peak), 0.0) for ok, s in zip(allowed, scores)]
    total = sum(jnp.sum(w, axis=-1, keepdims=True) for w in weights)
    mixed = sum(dot_nn(w.astype(LOW), keys) for w, keys in zip(weights, kv))
    out_ref[...] = mixed / total
    log_ref[...] = peak + jnp.log(total)


def attend(queries, kv0, kv1, qdoc, kdoc0, kdoc1):
    rows, keys = queries.shape[0], kv0.shape[0]
    size = max(64, min(256, 256 * 1024 // keys))
    full = lambda n, m: pl.BlockSpec((n, m), lambda i: (0, 0))
    part = lambda m: pl.BlockSpec((size, m), lambda i: (i, 0))
    return pl.pallas_call(
        attend_kernel,
        grid=(rows // size,),
        in_specs=[part(PAIR), full(keys, PAIR), full(keys, PAIR), part(1), full(1, keys), full(1, keys)],
        out_specs=[part(PAIR), part(1)],
        out_shape=[
            jax.ShapeDtypeStruct((rows, PAIR), WIDE),
            jax.ShapeDtypeStruct((rows, 1), WIDE),
        ],
        compiler_params=pltpu.CompilerParams(vmem_limit_bytes=48 * 1024 * 1024),
        name="attend",
    )(queries, kv0, kv1, qdoc, kdoc0, kdoc1)


def attend_back_kernel(
    q_ref, g_ref, o_ref, log_ref, kv0_ref, kv1_ref, qdoc_ref, kdoc0_ref, kdoc1_ref,
    dq_ref, dkv0_ref, dkv1_ref,
):
    scale = HEAD_DIM ** (-0.5)

    @pl.when(pl.program_id(0) == 0)
    def _():
        dkv0_ref[...] = jnp.zeros_like(dkv0_ref)
        dkv1_ref[...] = jnp.zeros_like(dkv1_ref)

    queries, grads = q_ref[...], g_ref[...]
    delta = jnp.sum(grads.astype(WIDE) * o_ref[...], axis=-1, keepdims=True)
    doc, log_total = qdoc_ref[...], log_ref[...]
    total = jnp.zeros(dq_ref.shape, WIDE)
    for kv_ref, kdoc_ref, dkv_ref in (
        (kv0_ref, kdoc0_ref, dkv0_ref),
        (kv1_ref, kdoc1_ref, dkv1_ref),
    ):
        keys = kv_ref[...]
        raw = dot_nt(queries, keys)
        probs = jnp.where(doc == kdoc_ref[...], jnp.exp(raw * scale - log_total), 0.0)
        dprobs = dot_nt(grads, keys)
        dscores = (probs * (dprobs - delta) * scale).astype(LOW)
        total = total + dot_nn(dscores, keys)
        dkv_ref[...] += dot_tn(dscores, queries) + dot_tn(probs.astype(LOW), grads)
    dq_ref[...] = total


def attend_back(queries, grads, out, log_total, kv0, kv1, qdoc, kdoc0, kdoc1):
    rows, keys = queries.shape[0], kv0.shape[0]
    size = max(64, min(256, 256 * 1024 // keys))
    full = lambda n, m: pl.BlockSpec((n, m), lambda i: (0, 0))
    part = lambda m: pl.BlockSpec((size, m), lambda i: (i, 0))
    return pl.pallas_call(
        attend_back_kernel,
        grid=(rows // size,),
        in_specs=[
            part(PAIR), part(PAIR), part(PAIR), part(1),
            full(keys, PAIR), full(keys, PAIR), part(1), full(1, keys), full(1, keys),
        ],
        out_specs=[part(PAIR), full(keys, PAIR), full(keys, PAIR)],
        out_shape=[
            jax.ShapeDtypeStruct((rows, PAIR), WIDE),
            jax.ShapeDtypeStruct((keys, PAIR), WIDE),
            jax.ShapeDtypeStruct((keys, PAIR), WIDE),
        ],
        compiler_params=pltpu.CompilerParams(vmem_limit_bytes=56 * 1024 * 1024),
        name="attend_back",
    )(queries, grads, out, log_total, kv0, kv1, qdoc, kdoc0, kdoc1)


def shards(
    tokens,
    query_vecs,
    out_cotangent,
    doc_lengths,
    live_mask,
    positives,
    triple_weight,
    triple_bias,
    output_weight,
    output_bias,
    first_gain,
    first_shift,
    expand_weight,
    expand_bias,
    contract_weight,
    contract_bias,
    second_gain,
    second_shift,
    head_weight,
):
    outer = lax.axis_size("o")
    mo, mz, mx, mc, my = [lax.axis_index(a) for a in ("o", "z", "x", "c", "y")]
    mw = mx * 2 + my
    rows, width = tokens.shape
    own = rows // 2
    slab = triple_weight.shape[0]
    docs = doc_lengths.shape[0]
    queries_count = positives.shape[0]
    blocks = outer * NZ * 4

    def widen(value):
        return lax.all_gather(value, "o") if outer > 1 else value[None]

    def narrow(value):
        return lax.psum_scatter(value, "o") if outer > 1 else value[0]

    def sum_outer(value):
        return lax.psum(value, "o") if outer > 1 else value

    triple_low = triple_weight.astype(LOW)
    by_head = triple_low.reshape(slab, 3, 2, NZ, HEAD_DIM)
    to_heads = by_head.transpose(3, 2, 0, 1, 4).reshape(NZ * 2, slab, 3 * HEAD_DIM)
    extra = jnp.zeros((16, 3 * HEAD_DIM), LOW).at[0, :rows].set(live_mask.astype(LOW))
    extra = jnp.broadcast_to(extra[None], (NZ * 2,) + extra.shape)
    head_pack = lax.all_to_all(
        jnp.concatenate([to_heads, extra], axis=1), ("z", "x"), 0, 0
    ).reshape(NZ, 2, slab + 16, 3 * HEAD_DIM)
    head_pack = widen(both(head_pack, flip(head_pack, "c"), mc))
    head_pack = head_pack.transpose(0, 2, 3, 1, 4, 5)
    head_triple = head_pack[..., :slab, :].reshape(width, 3 * HEAD_DIM)
    live_all = head_pack[..., slab, :rows]

    pieces = [(mz, tokens)] + [(mz ^ m, xor_z(tokens, m)) for m in (1, 2, 3)]
    sheets = []
    for index, piece in pieces:
        sheets.append((index * 2 + mx, piece))
        sheets.append((index * 2 + 1 - mx, flip(piece, "x")))
    head_tokens = place(sheets).reshape(NZ * 2 * rows, width)

    def quarter(weight):
        return weight.transpose(1, 0, 2)

    triple_cols = triple_low.reshape(slab, 3, 2, NZ, HEAD_DIM).transpose(2, 0, 3, 1, 4)
    triple_cols = triple_cols.reshape(2, slab, NZ * 3 * HEAD_DIM)
    output_cols = quarter(output_weight.T.astype(LOW).reshape(slab, 2, -1))
    expand_cols = quarter(expand_weight.astype(LOW).reshape(slab, 2, -1))
    contract_cols = quarter(contract_weight.T.astype(LOW).reshape(slab, 2, -1))

    def gather_slabs(cols):
        piece = both(pick(cols, mx), flip(pick(cols, 1 - mx), "x"), mx)
        line = place([(mz, piece)] + [(mz ^ m, xor_z(piece, m)) for m in (1, 2, 3)])
        pair = widen(both(line, flip(line, "c"), mc))
        return pair.transpose(0, 2, 3, 1, 4, 5).reshape(width, -1)

    near = gather_slabs(jnp.concatenate([output_cols, expand_cols], axis=-1))
    out_n = output_cols.shape[-1]
    output_q, expand_q = near[:, :out_n], near[:, out_n:]
    contract_q = gather_slabs(contract_cols)
    triple_q = gather_slabs(triple_cols)

    where = jnp.arange(rows, dtype=jnp.int32) * blocks

    def block_places(o, c):
        block = (o * NZ * 2 + jnp.arange(NZ * 2, dtype=jnp.int32)) * 2 + c
        return (block[:, None] + where[None, :]).reshape(-1)

    own_places = block_places(mo, mc)
    own_doc, own_position = doc_layout(doc_lengths, own_places)

    def key_doc(c):
        places = jnp.concatenate([block_places(o, c) for o in range(outer)])
        doc = doc_layout(doc_lengths, places)[0]
        alive = pick(live_all, c, 3).reshape(-1) > 0
        return jnp.where(alive, doc, -1)

    kdoc0, kdoc1 = key_doc(mc), key_doc(1 - mc)
    labels = jnp.arange(docs, dtype=jnp.int32)
    token_counts = sum(
        jnp.sum((kd[:, None] == labels[None, :]).astype(WIDE), axis=0) for kd in (kdoc0, kdoc1)
    )
    angles = angles_of(own_position, HEAD_DIM)
    cosine, sine = jnp.cos(angles), jnp.sin(angles)

    head_bias = triple_bias.reshape(3, 2, NZ, HEAD_DIM)
    head_bias = pick(pick(head_bias, mx, 1), mz, 1).reshape(1, 3 * HEAD_DIM)
    triple = dot_nn(head_tokens, head_triple) + head_bias
    query_rot = turn(triple[:, :HEAD_DIM], cosine, sine).astype(LOW)
    key_rot = turn(triple[:, HEAD_DIM:PAIR], cosine, sine).astype(LOW)
    kv = jnp.concatenate([key_rot, triple[:, PAIR:].astype(LOW)], axis=1)
    nothing = jnp.zeros_like(query_rot)
    queries = jnp.concatenate([query_rot, nothing], axis=1)
    kv_other = flip(kv, "c")
    kv0, kv1 = [widen(v).reshape(-1, PAIR) for v in (kv, kv_other)]
    meta = (own_doc[:, None], kdoc0[None, :], kdoc1[None, :])
    out, log_total = attend(queries, kv0, kv1, *meta)

    def heads_to_group(value):
        parts = value.reshape(NZ, 2 * rows, -1)
        got = lax.all_to_all(parts, "z", 0, 0)
        return got.transpose(1, 0, 2).reshape(2 * rows, -1)

    def group_to_heads(value):
        parts = value.reshape(2 * rows, NZ, -1).transpose(1, 0, 2)
        return lax.all_to_all(parts, "z", 0, 0).reshape(NZ * 2 * rows, -1)

    attended_low = heads_to_group(out[:, HEAD_DIM:].astype(LOW))
    branch_part = dot_nt(attended_low, output_q).astype(LOW).reshape(4, own, width)
    branch = scatter_w(branch_part, mw) + output_bias
    mine = lax.dynamic_slice_in_dim(tokens, my * own, own, 0)
    first_in = mine.astype(WIDE) + branch
    first = layer_norm(first_in, first_gain, first_shift)
    first_low = gather_w(first.astype(LOW), mw).reshape(4 * own, width)
    half = expand_bias.shape[0] // 2
    hidden_in = dot_nn(first_low, expand_q) + lax.dynamic_slice_in_dim(expand_bias, mx * half, half, 0)
    gelu = partial(jax.nn.gelu, approximate=False)
    hidden = gelu(hidden_in).astype(LOW)
    expanded_part = dot_nt(hidden, contract_q).astype(LOW).reshape(4, own, width)
    expanded = scatter_w(expanded_part, mw) + contract_bias
    second_in = first + expanded
    second = layer_norm(second_in, second_gain, second_shift)
    second_low = second.astype(LOW)
    head_low = head_weight.astype(LOW)
    embed = dot_nn(second_low, head_low)
    unit_low = unit_rows(embed).astype(LOW)

    units = gather_w(unit_low, mw).reshape(4 * own, -1)
    shares = query_vecs.shape[0] // 32
    query_view = query_vecs.reshape(NZ, 2, 2, 2, shares, -1)
    my_queries = pick(pick(query_view, mx, 1), my, 2).reshape(NZ * 2 * shares, -1).astype(WIDE)
    query_unit = unit_rows(my_queries).astype(LOW)
    group_places = ((mo * NZ + mz) * 2 + jnp.arange(2, dtype=jnp.int32)) * 2 + mc
    group_places = (group_places[:, None] + where[None, :]).reshape(-1)
    group_doc = doc_layout(doc_lengths, group_places)[0]
    group_live = pick(pick(pick(live_all, mo, 0), mz, 0), mc, 1).reshape(-1).astype(WIDE)
    onehot = (group_doc[:, None] == labels[None, :]).astype(WIDE)
    similar = dot_nt(units, query_unit)
    expo = jnp.exp(similar / SOFTMAX_TEMPER) * group_live[:, None]
    totals = lax.dot_general(
        onehot, expo, (((0,), (0,)), ((), ())), precision=PRECISE, preferred_element_type=WIDE
    )
    totals = totals + flip(totals, "c")
    totals = sum_outer(totals + xor_z(totals, 1) + xor_z(totals, 2) + xor_z(totals, 3))
    my_count = queries_count // 4
    query_len = totals.shape[1] // my_count
    token_scores = SOFTMAX_TEMPER * (jnp.log(totals) - jnp.log(token_counts)[:, None])
    doc_score = jnp.sum(token_scores.reshape(docs, my_count, query_len), axis=2)
    best = jnp.max(doc_score, axis=0, keepdims=True)
    shifted = jnp.exp(doc_score - best)
    shifted_sum = jnp.sum(shifted, axis=0, keepdims=True)
    positive_view = positives.reshape(NZ, 2, 2, 2, -1)
    my_positives = pick(pick(positive_view, mx, 1), my, 2).reshape(-1)
    chosen = (my_positives[None, :] == labels[:, None]).astype(WIDE)
    loss_part = (
        jnp.sum(best[0] + jnp.log(shifted_sum[0]) - jnp.sum(doc_score * chosen, axis=0))
        / queries_count
    )
    grad_doc = (shifted / shifted_sum - chosen) / queries_count
    coefficient = (grad_doc[:, :, None] / totals.reshape(docs, my_count, query_len)).reshape(docs, -1)
    grad_similar = (
        lax.dot_general(
            onehot, coefficient, (((1,), (0,)), ((), ())), precision=PRECISE,
            preferred_element_type=WIDE,
        )
        * expo
    ).astype(LOW)
    grad_unit = scatter_w(dot_nn(grad_similar, query_unit).reshape(4, own, -1), mw)
    grad_query_unit = dot_tn(grad_similar, units).reshape(NZ, 2, shares, -1)
    grad_query_unit = pick(grad_query_unit, mc, 1) + flip(pick(grad_query_unit, 1 - mc, 1), "c")
    grad_query_unit = sum_outer(scatter_z(grad_query_unit, mz))
    own_queries = pick(pick(my_queries.reshape(NZ, 2, shares, -1), mz, 0), mc, 0)
    unused, query_back = jax.vjp(unit_rows, own_queries)
    queries_grad = lax.all_gather(
        query_back(grad_query_unit)[0], ("z", "x", "c", "y"), axis=0, tiled=True
    )

    unused, unit_back = jax.vjp(unit_rows, embed)
    grad_embed = unit_back(grad_unit)[0].astype(LOW)
    head_part = dot_tn(second_low, grad_embed)
    cotangent = lax.dynamic_slice_in_dim(out_cotangent, my * own, own, 0).astype(WIDE)
    grad_second = dot_nt(grad_embed, head_low) + cotangent
    unused, second_back = jax.vjp(layer_norm, second_in, second_gain, second_shift)
    grad_second_in, gain_two_part, shift_two_part = second_back(grad_second)
    grad_expanded_own = grad_second_in.astype(LOW)
    contract_bias_part = jnp.sum(grad_expanded_own, axis=0, dtype=WIDE)
    grad_expanded = gather_w(grad_expanded_own, mw).reshape(4 * own, width)
    grad_hidden = dot_nn(grad_expanded, contract_q)
    unused, gelu_back = jax.vjp(gelu, hidden_in)
    grad_hidden_in = gelu_back(grad_hidden)[0].astype(LOW)
    expand_bias_part = jnp.sum(grad_hidden_in, axis=0, dtype=WIDE)
    grad_first_part = dot_nt(grad_hidden_in, expand_q).astype(LOW).reshape(4, own, width)
    grad_first = grad_second_in + scatter_w(grad_first_part, mw)

    def scatter_slabs(part):
        parts = part.astype(LOW).reshape(outer, NZ, 2, 2, slab, -1)
        parts = narrow(parts)
        kept = pick(parts, mc, 2).astype(WIDE) + flip(pick(parts, 1 - mc, 2), "c").astype(WIDE)
        line = scatter_z(kept.astype(LOW), mz)
        mine_x, other_x = pick(line, mx), flip(pick(line, 1 - mx).astype(LOW), "x")
        return both(mine_x, other_x.astype(WIDE), mx).transpose(1, 0, 2)

    contract_grad = scatter_slabs(dot_tn(grad_expanded, hidden)).reshape(slab, -1).T
    expand_grad = scatter_slabs(dot_tn(first_low, grad_hidden_in)).reshape(slab, -1)

    unused, first_back = jax.vjp(layer_norm, first_in, first_gain, first_shift)
    grad_first_in, gain_one_part, shift_one_part = first_back(grad_first)
    grad_branch_own = grad_first_in.astype(LOW)
    output_bias_part = jnp.sum(grad_branch_own, axis=0, dtype=WIDE)
    grad_branch = gather_w(grad_branch_own, mw).reshape(4 * own, width)
    grad_attended = dot_nn(grad_branch, output_q).astype(LOW)
    output_grad = scatter_slabs(dot_tn(grad_branch, attended_low)).reshape(slab, -1).T
    grad_out = group_to_heads(grad_attended)
    grad_out = jnp.concatenate([nothing, grad_out], axis=1)
    grad_query, dkv0, dkv1 = attend_back(queries, grad_out, out, log_total, kv0, kv1, *meta)
    dkv0, dkv1 = [narrow(v.reshape(outer, -1, PAIR)) for v in (dkv0, dkv1)]
    dkv = dkv0 + flip(dkv1, "c")
    grad_triple = jnp.concatenate(
        [
            turn(grad_query[:, :HEAD_DIM], cosine, -sine),
            turn(dkv[:, :HEAD_DIM], cosine, -sine),
            dkv[:, HEAD_DIM:],
        ],
        axis=1,
    ).astype(LOW)

    triple_part = dot_tn(head_tokens, grad_triple).reshape(outer, NZ, 2, 2, slab, -1)
    triple_part = narrow(triple_part)
    bias_part = jnp.sum(grad_triple, axis=0, dtype=WIDE)
    bias_rows = jnp.zeros((NZ, 2, 2, 16, 3 * HEAD_DIM), WIDE).at[..., 0, :].set(sum_outer(bias_part))
    packed = jnp.concatenate([triple_part, bias_rows], axis=3).astype(LOW)
    packed = pick(packed, mc, 2).astype(WIDE) + flip(pick(packed, 1 - mc, 2), "c").astype(WIDE)
    packed = packed.astype(LOW).reshape(NZ * 2, slab + 16, 3 * HEAD_DIM)
    packed = lax.all_to_all(packed, ("z", "x"), 0, 0).astype(WIDE)
    packed = packed.reshape(NZ, 2, slab + 16, 3, HEAD_DIM).transpose(2, 3, 1, 0, 4)
    packed = packed.reshape(slab + 16, 3, 2 * NZ * HEAD_DIM)
    triple_grad, triple_bias_grad = packed[:slab], packed[slab]

    group_triple = heads_to_group(grad_triple)
    tokens_part = dot_nt(group_triple, triple_q).astype(LOW).reshape(4, own, width)
    tokens_own = grad_first_in + scatter_w(tokens_part, mw)
    tokens_grad = both(tokens_own, flip(tokens_own, "y"), my).reshape(rows, width)
    mixed_own = second.astype(LOW)
    mixed = both(mixed_own, flip(mixed_own, "y"), my).reshape(rows, width)

    quarters = jnp.zeros((2, 2, half), WIDE)
    quarters = lax.dynamic_update_slice(quarters, expand_bias_part[None, None], (my, mx, 0))
    vectors = jnp.concatenate(
        [
            output_bias_part, gain_one_part, shift_one_part,
            contract_bias_part, gain_two_part, shift_two_part,
            quarters.reshape(-1),
        ]
    ).reshape(-1, 128)
    loss_row = jnp.zeros((1, 128), WIDE).at[0, 0].set(loss_part / (outer * NZ * 2))
    small = jnp.concatenate([head_part, vectors, loss_row])
    used = small.shape[0]
    chunk = -(-used // 128) * 8
    small = jnp.pad(small, ((0, chunk * 16 - used), (0, 0))).reshape(4, 4, chunk, 128)
    small = scatter_w(small, mw)
    small = scatter_z(small, mz)
    small = sum_outer(small + flip(small, "c"))
    small = place([(mz, small)] + [(mz ^ m, xor_z(small, m)) for m in (1, 2, 3)])
    small = gather_w(small, mw).reshape(-1, 128)
    head_grad = small[:width]
    tail = small[width : used - 1].reshape(-1)
    vector = lambda i: tail[i * width : (i + 1) * width]
    expand_bias_total = pick(tail[6 * width :].reshape(2, -1), my)
    loss = small[used - 1, 0]

    return (
        mixed,
        loss,
        tokens_grad,
        queries_grad,
        triple_grad,
        triple_bias_grad,
        output_grad,
        vector(0),
        vector(1),
        vector(2),
        expand_grad,
        expand_bias_total,
        contract_grad,
        vector(3),
        vector(4),
        vector(5),
        head_grad,
    )


def solution(mesh):
    outer = mesh.shape["blk"] // 16
    five = Mesh(mesh.devices.reshape(outer, NZ, 2, 2, mesh.shape["tensor"]), BLK + ("y",))
    blk, tensor = BLK, "y"
    return jax.shard_map(
        shards,
        mesh=five,
        in_specs=(
            P(blk, None),
            P(),
            P(blk, None),
            P(),
            P(blk),
            P(),
            P(blk, None, tensor),
            P(None, tensor),
            P(tensor, blk),
            P(),
            P(),
            P(),
            P(blk, tensor),
            P(tensor),
            P(tensor, blk),
            P(),
            P(),
            P(),
            P(),
        ),
        out_specs=(
            P(blk, None),
            P(),
            P(blk, None),
            P(),
            P(blk, None, tensor),
            P(None, tensor),
            P(tensor, blk),
            P(),
            P(),
            P(),
            P(blk, tensor),
            P(tensor),
            P(tensor, blk),
            P(),
            P(),
            P(),
            P(),
        ),
        check_vma=False,
    )
```

```python
from functools import partial
import math

import jax
import jax.numpy as jnp
import numpy as np
from jax import lax
from jax.experimental import pallas as pl
from jax.experimental.pallas import tpu as pltpu
from jax.sharding import Mesh, PartitionSpec as P

HEAD_DIM = 64
PAIR = 2 * HEAD_DIM

SOFTMAX_TEMPER = 0.05
FLOOR_SCORE = -1e30
NORM_EPSILON = 1e-05
UNIT_EPSILON = 1e-06
PRECISE = lax.Precision.HIGHEST
LOW = jnp.bfloat16
WIDE = jnp.float32

BLK = ("o", "z", "x", "c")
NZ = 4
FOUR = [0, 1, 2, 3]

VMEM_BYTES = 56 * 1024 * 1024
LANES = (0, 64, 192)
QUAD = 4 * HEAD_DIM


def xor_z(value, mask):
    return lax.ppermute(value, "z", [(i, i ^ mask) for i in FOUR])


def xor_s(value, mask):
    return lax.ppermute(value, ("x", "c"), [(i, i ^ mask) for i in FOUR])


def flip(value, axis):
    return lax.ppermute(value, axis, [(0, 1), (1, 0)])


def pick(value, index, axis=0):
    return lax.dynamic_index_in_dim(value, index, axis, keepdims=False)


def after(value, *others):
    return lax.optimization_barrier((value,) + others)[0]


def place(pieces):
    first = pieces[0][1]
    whole = jnp.zeros((len(pieces),) + first.shape, first.dtype)
    for index, piece in pieces:
        whole = lax.dynamic_update_slice_in_dim(whole, piece[None], index, 0)
    return whole


def both(mine, other, where):
    return place([(where, mine), (1 - where, other)])


def doc_layout(doc_lengths, places):
    ends = jnp.cumsum(doc_lengths)
    starts = ends - doc_lengths
    passed = starts <= places[..., None]
    doc_index = jnp.sum(passed.astype(jnp.int32), axis=-1) - 1
    begin = jnp.max(jnp.where(passed, starts, 0), axis=-1)
    return (doc_index, places - begin)


def dot_nn(a, b, precision=None):
    return lax.dot_general(
        a, b, (((1,), (0,)), ((), ())), precision=precision, preferred_element_type=WIDE
    )


def dot_nt(a, b, precision=None):
    return lax.dot_general(
        a, b, (((1,), (1,)), ((), ())), precision=precision, preferred_element_type=WIDE
    )


def dot_tn(a, b, precision=None):
    return lax.dot_general(
        a, b, (((0,), (0,)), ((), ())), precision=precision, preferred_element_type=WIDE
    )


def shape(dims, dtype):
    return jax.ShapeDtypeStruct(dims, dtype)


PARAMS = pltpu.CompilerParams(vmem_limit_bytes=VMEM_BYTES)

TAKES = dict(
    prep=2.5, heads=2.0, project=3.8, attend=7.5, branch=3.5, forward=7.7, second=3.6, middle=12.0, first_back=3.8, attend_back=9.8, triple=2.9, triple_weight=3.8, tokens=3.9,
    tokens_sum=2.1, weights=5.2, output=2.3, core_sum=3.9, line_sum=2.7, columns=2.2, pair_sum=1.8,
    triple_out=1.9, query_units=2.8, query_sum=1.9, query_c=2.5, query_back=1.6, spread=3.5,
)


SCALE = 1.0


def cost(name):
    took = TAKES[name] * SCALE
    return pl.CostEstimate(
        flops=int(took * 1.15e9), bytes_accessed=int(took * 3.7e6), transcendentals=0
    )


def whole(kernel, name, index, inputs, outputs, scratch=(), slabs=()):
    return pl.pallas_call(
        kernel,
        in_specs=[pl.BlockSpec(memory_space=pltpu.SMEM)]
        + [pl.BlockSpec(memory_space=pltpu.VMEM)] * len(inputs)
        + [pl.BlockSpec(memory_space=pl.ANY)] * len(slabs),
        out_specs=[pl.BlockSpec(memory_space=pltpu.VMEM)] * len(outputs),
        out_shape=list(outputs),
        scratch_shapes=list(scratch),
        compiler_params=PARAMS,
        cost_estimate=cost(name),
        name=name,
    )(index, *inputs, *slabs)


def slab_copy(slabs, at, weight, sems):
    there = slabs.at[:, pl.ds(at, weight.shape[1])]
    return pltpu.make_async_copy(there, weight, sems.at[0])


def slab_scratch(rows, cols):
    return [pltpu.VMEM((rows, cols), LOW), pltpu.SemaphoreType.DMA((1,))]


def finish(copy, weight):
    copy.wait()
    return weight[...]


def prep_kernel(idx, tw, ow, ew, cw, live, heads, low, tri):
    slab, span = ew.shape
    alive = jnp.broadcast_to(live[...], (16, live.shape[1])).astype(WIDE).astype(LOW)
    for spot in range(NZ * 2):
        at = spot * HEAD_DIM
        for part, lane in enumerate(LANES):
            heads[spot, :slab, lane : lane + HEAD_DIM] = tw[part, :, at : at + HEAD_DIM].astype(LOW)
        heads[spot, :slab, PAIR : PAIR + HEAD_DIM] = jnp.zeros((slab, HEAD_DIM), LOW)
        heads[spot, slab:, : live.shape[1]] = alive
        heads[spot, slab:, PAIR:] = jnp.zeros((16, PAIR), LOW)
    low[:, :span] = ew[...].astype(LOW)
    low[:, span : 2 * span] = cw[...].astype(LOW)
    low[:, 2 * span :] = ow[...].astype(LOW)
    for part in range(3):
        tri[:, part * 2 * QUAD : (part + 1) * 2 * QUAD] = tw[part].astype(LOW)


def heads_kernel(idx, own, other, weight, live0, live1):
    slab, mc = own.shape[1] - 16, idx[3]
    for spot in range(NZ * 2):
        for source, c, live in ((own, mc, live0), (other, 1 - mc, live1)):
            rows = pl.ds(pl.multiple_of((spot * 2 + c) * slab, slab), slab)
            weight[rows, :] = source[spot, :slab, :]
            live[spot : spot + 1, :] = source[spot, slab : slab + 16, :PAIR].astype(WIDE)[:1]


def swap_halves(value):
    lane = lax.broadcasted_iota(jnp.int32, value.shape, 1)
    half = HEAD_DIM // 2
    return jnp.where(
        (lane & half) == 0,
        pltpu.roll(value, PAIR - half, 1),
        pltpu.roll(value, half, 1),
    )


def turn(value, cosine, sine):
    return value * cosine + swap_halves(value) * sine


def project_kernel(idx, *refs):
    sheets, (weight, cosine, sine, bias, query, kv) = refs[:8], refs[8:]
    rows = sheets[0].shape[0]
    mz, mx = idx[1], idx[2]
    mine = mz * 2 + mx
    parts = []
    for part in range(3):
        total = jnp.zeros((1, HEAD_DIM), WIDE)
        for h in range(NZ * 2):
            here = bias[part : part + 1, h * HEAD_DIM : (h + 1) * HEAD_DIM]
            total = jnp.where(mine == h, here, total)
        parts.append(total)
    empty = jnp.zeros((1, HEAD_DIM), WIDE)
    offset = jnp.concatenate([parts[0], parts[1], empty, parts[2]], axis=1)
    weights = weight[...]
    low_lanes = lax.broadcasted_iota(jnp.int32, (rows, PAIR), 1) < HEAD_DIM
    for z in range(NZ):
        for x in range(2):
            spot = (mz ^ z) * 2 + (mx ^ x)
            at = pl.ds(pl.multiple_of(spot * rows, rows), rows)
            triple = dot_nn(sheets[z * 2 + x][...], weights) + offset
            turned = turn(triple[:, :PAIR], cosine[at, :], sine[at, :])
            query[at, :] = jnp.where(low_lanes, turned, 0.0).astype(LOW)
            kv[at, :] = jnp.where(
                low_lanes, pltpu.roll(turned, HEAD_DIM, 1), triple[:, PAIR:]
            ).astype(LOW)


def key_row(ref):
    rows = ref[...]
    return jnp.concatenate([rows[i : i + 1] for i in range(rows.shape[0])], axis=1)


def attend_kernel(q_ref, kv0_ref, kv1_ref, qdoc_ref, kdoc0_ref, kdoc1_ref, out_ref, log_ref, pack_ref):
    scale = HEAD_DIM ** (-0.5)
    rows = q_ref.shape[3]
    queries = q_ref[0].reshape(4 * rows, PAIR)
    kv = (kv0_ref[...], kv1_ref[...])
    doc = qdoc_ref[0].reshape(4 * rows, 1)
    allowed = [doc == key_row(ref) for ref in (kdoc0_ref, kdoc1_ref)]
    scores = [
        jnp.where(ok, dot_nt(queries, keys) * scale, FLOOR_SCORE) for ok, keys in zip(allowed, kv)
    ]
    peak = jnp.maximum(*[jnp.max(s, axis=-1, keepdims=True) for s in scores])
    weights = [jnp.where(ok, jnp.exp(s - peak), 0.0) for ok, s in zip(allowed, scores)]
    total = sum(jnp.sum(w, axis=-1, keepdims=True) for w in weights)
    mixed = sum(dot_nn(w.astype(LOW), keys) for w, keys in zip(weights, kv)) / total
    out_ref[0] = mixed.reshape(2, 2, rows, PAIR)
    log_ref[0] = (peak + jnp.log(total)).reshape(2, 2, rows, 1)
    low_lanes = lax.broadcasted_iota(jnp.int32, (rows, PAIR), 1) < HEAD_DIM
    for x in range(2):
        upper = mixed[2 * x * rows : (2 * x + 1) * rows]
        lower = mixed[(2 * x + 1) * rows : (2 * x + 2) * rows]
        pack_ref[0, x] = jnp.where(low_lanes, pltpu.roll(upper, HEAD_DIM, 1), lower).astype(LOW)


def attend_specs(rows, keys, key_rows):
    half = rows // 2
    size = max(16, min(half, half * 2048 // (2 * keys)))
    full = lambda n, m: pl.BlockSpec((n, m), lambda i, j: (0, 0))
    part = lambda m: pl.BlockSpec((1, 2, 2, size, m), lambda i, j: (i, 0, 0, j, 0))
    pack = pl.BlockSpec((1, 2, size, PAIR), lambda i, j: (i, 0, j, 0))
    kv, docs = full(keys, PAIR), full(key_rows, rows)
    return (NZ, half // size), part, pack, kv, docs


def attend(queries, kv0, kv1, qdoc, kdoc0, kdoc1):
    rows = kdoc0.shape[1]
    half = rows // 2
    grid, part, pack, kv, docs = attend_specs(rows, kv0.shape[0], kdoc0.shape[0])
    return pl.pallas_call(
        attend_kernel,
        grid=grid,
        in_specs=[part(PAIR), kv, kv, part(1), docs, docs],
        out_specs=[part(PAIR), part(1), pack],
        out_shape=[
            shape((NZ, 2, 2, half, PAIR), WIDE),
            shape((NZ, 2, 2, half, 1), WIDE),
            shape((NZ, 2, half, PAIR), LOW),
        ],
        compiler_params=PARAMS,
        cost_estimate=cost("attend"),
        name="attend",
    )(queries.reshape(NZ, 2, 2, half, PAIR), kv0, kv1, qdoc, kdoc0, kdoc1)


def attend_back_kernel(
    q_ref, g_ref, o_ref, log_ref, kv0_ref, kv1_ref, qdoc_ref, kdoc0_ref, kdoc1_ref,
    dq_ref, dkv0_ref, dkv1_ref,
):
    scale = HEAD_DIM ** (-0.5)
    rows = q_ref.shape[3]

    @pl.when((pl.program_id(0) == 0) & (pl.program_id(1) == 0))
    def _():
        dkv0_ref[...] = jnp.zeros_like(dkv0_ref)
        dkv1_ref[...] = jnp.zeros_like(dkv1_ref)

    queries = q_ref[0].reshape(4 * rows, PAIR)
    high_lanes = lax.broadcasted_iota(jnp.int32, (rows, PAIR), 1) >= HEAD_DIM
    parts = []
    for x in range(2):
        packed = g_ref[0, x].astype(WIDE)
        parts.append(jnp.where(high_lanes, pltpu.roll(packed, HEAD_DIM, 1), 0.0))
        parts.append(jnp.where(high_lanes, packed, 0.0))
    wide = jnp.concatenate(parts, axis=0)
    grads = wide.astype(LOW)
    delta = jnp.sum(wide * o_ref[0].reshape(4 * rows, PAIR), axis=-1, keepdims=True)
    doc, log_total = qdoc_ref[0].reshape(4 * rows, 1), log_ref[0].reshape(4 * rows, 1)
    total = jnp.zeros((4 * rows, PAIR), WIDE)
    for kv_ref, kdoc_ref, dkv_ref in (
        (kv0_ref, kdoc0_ref, dkv0_ref),
        (kv1_ref, kdoc1_ref, dkv1_ref),
    ):
        keys = kv_ref[...]
        raw = dot_nt(queries, keys)
        probs = jnp.where(doc == key_row(kdoc_ref), jnp.exp(raw * scale - log_total), 0.0)
        dprobs = dot_nt(grads, keys)
        dscores = (probs * (dprobs - delta) * scale).astype(LOW)
        total = total + dot_nn(dscores, keys)
        dkv_ref[...] += dot_tn(dscores, queries) + dot_tn(probs.astype(LOW), grads)
    dq_ref[0] = total.reshape(2, 2, rows, PAIR)


def attend_back(queries, grads, out, log_total, kv0, kv1, qdoc, kdoc0, kdoc1):
    rows, keys = kdoc0.shape[1], kv0.shape[0]
    half = rows // 2
    grid, part, pack, kv, docs = attend_specs(rows, keys, kdoc0.shape[0])
    return pl.pallas_call(
        attend_back_kernel,
        grid=grid,
        in_specs=[part(PAIR), pack, part(PAIR), part(1), kv, kv, part(1), docs, docs],
        out_specs=[part(PAIR), kv, kv],
        out_shape=[
            shape((NZ, 2, 2, half, PAIR), WIDE),
            shape((keys, PAIR), WIDE),
            shape((keys, PAIR), WIDE),
        ],
        compiler_params=PARAMS,
        cost_estimate=cost("attend_back"),
        name="attend_back",
    )(queries.reshape(NZ, 2, 2, half, PAIR), grads, out, log_total, kv0, kv1, qdoc, kdoc0, kdoc1)


def branch_kernel(idx, got, slabs, low, part, held, sems):
    copy = slab_copy(slabs, slabs.shape[1] - held.shape[1], held, sems)
    copy.start()
    half = got.shape[1]
    for h in range(NZ * 2):
        lanes = slice(h * HEAD_DIM, (h + 1) * HEAD_DIM)
        low[:half, lanes] = got[h, :, :HEAD_DIM]
        low[half:, lanes] = got[h, :, HEAD_DIM:]
    part[...] = dot_nt(low[...], finish(copy, held)).astype(LOW)


def normalize(value):
    center = value - jnp.mean(value, axis=-1, keepdims=True)
    spread = jnp.mean(center * center, axis=-1, keepdims=True)
    inverse = lax.rsqrt(spread + NORM_EPSILON)
    return center * inverse, inverse


def pair(own, other):
    return own[...].astype(WIDE) + other[...].astype(WIDE)


def forward_kernel(
    idx, own, other, tokens, bias, gain, shift, hidden_bias, attended, slabs,
    first, unitary, inverse, hidden_in, keep, send, part,
    low, hidden, expand, sems1, contract, sems2,
):
    copy1 = slab_copy(slabs, 0, expand, sems1)
    copy2 = slab_copy(slabs, expand.shape[1], contract, sems2)
    copy1.start()
    copy2.start()
    value = tokens[...].astype(WIDE) + (pair(own, other) + bias[...])
    unitary[...], inverse[...] = normalize(value)
    first[...] = unitary[...] * gain[...] + shift[...]
    low[...] = first[...].astype(LOW)
    value = dot_nn(low[...], finish(copy1, expand)) + hidden_bias[...]
    hidden_in[...] = value
    hidden[...] = (0.5 * value * (1.0 + lax.erf(value * (0.5**0.5)))).astype(LOW)
    part[...] = dot_nt(hidden[...], finish(copy2, contract)).astype(LOW)
    rows, width = low.shape
    few = rows * QUAD // width
    for out, x in ((keep, idx[2]), (send, 1 - idx[2])):
        out[:rows, :] = low[...]
        out[rows : 2 * rows, :] = columns_of(hidden, x, width)
        for i in range(width // QUAD):
            out[2 * rows :, i * QUAD : (i + 1) * QUAD] = attended[
                i * few : (i + 1) * few, pl.ds(pl.multiple_of(x * QUAD, QUAD), QUAD)
            ]


def columns_of(ref, x, span):
    return ref[:, pl.ds(pl.multiple_of(x * span, 128), span)]


def unit_scale(value):
    return lax.rsqrt(jnp.sum(value * value, axis=-1, keepdims=True) + UNIT_EPSILON)


def second_kernel(
    idx, own, other, first, bias, gain, shift, head, query, kdoc,
    low, unitary, inverse, embed, unit, expo, totals,
):
    value = first[...] + (pair(own, other) + bias[...])
    unitary[...], inverse[...] = normalize(value)
    low[...] = (unitary[...] * gain[...] + shift[...]).astype(LOW)
    embed[...] = dot_nn(low[...], head[...].astype(LOW))
    unit[...] = (embed[...] * unit_scale(embed[...])).astype(LOW)
    expo[...] = jnp.exp(dot_nt(unit[...], query[...]) / SOFTMAX_TEMPER)
    totals[...] = dot_nn(member(idx, kdoc, totals.shape[0]), expo[...], PRECISE)


def query_kernel(idx, vecs, out):
    value = vecs[...].astype(WIDE)
    out[...] = (value * unit_scale(value)).astype(LOW)


def member(idx, kdoc, docs):
    row = kdoc[pl.ds((idx[0] * NZ + idx[1]) * 2 + idx[2], 1), :]
    label = lax.broadcasted_iota(jnp.int32, (docs, row.shape[1]), 0)
    return jnp.where(row == label, 1.0, 0.0)


def group_sum(value, length):
    column = lax.broadcasted_iota(jnp.int32, value.shape, 1)
    span = value.shape[1]
    step = 1
    while step < length:
        ahead, behind = pltpu.roll(value, span - step, 1), pltpu.roll(value, step, 1)
        value = value + jnp.where((column & step) == 0, ahead, behind)
        step *= 2
    return value


def loss_of(count, totals, kdocs, positive):
    docs, columns = totals.shape
    length = columns // count
    label = lax.broadcasted_iota(jnp.int32, (docs, 1), 0)
    tokens = jnp.zeros((docs, 1), WIDE)
    for ref in kdocs:
        tokens = tokens + jnp.sum(jnp.where(key_row(ref) == label, 1.0, 0.0), axis=1, keepdims=True)
    doc_score = group_sum(SOFTMAX_TEMPER * (jnp.log(totals) - jnp.log(tokens)), length)
    best = jnp.max(doc_score, axis=0, keepdims=True)
    shifted = jnp.exp(doc_score - best)
    shifted_sum = jnp.sum(shifted, axis=0, keepdims=True)
    chosen = jnp.where(label == positive, 1.0, 0.0)
    each = best + jnp.log(shifted_sum) - jnp.sum(doc_score * chosen, axis=0, keepdims=True)
    loss = jnp.sum(each, axis=1, keepdims=True) / columns
    return loss, (shifted / shifted_sum - chosen) / (totals * count)


def core_sum_kernel(idx, keep, got, own, send):
    own[...] = keep[0] + got[0].astype(WIDE)
    send[...] = (keep[1] + got[1].astype(WIDE)).astype(LOW)


def query_sum_kernel(idx, own, other, *outs):
    for z, out in enumerate(outs):
        out[...] = (own[z] + other[z].astype(WIDE)).astype(out.dtype)


def unit_back(value, grad):
    scale = unit_scale(value)
    along = jnp.sum(grad * value, axis=-1, keepdims=True)
    return scale * grad - value * (along * scale * scale * scale)


def query_back_kernel(idx, own, r1, r2, r3, value, out):
    total = own[...] + r1[...].astype(WIDE) + (r2[...].astype(WIDE) + r3[...].astype(WIDE))
    shares = value.shape[0]
    out[:shares, :] = unit_back(value[...].astype(WIDE), total[:shares]).astype(LOW)
    out[shares:, :] = total[shares:].astype(LOW)


def spread_kernel(idx, got, queries, head, *vectors):
    rows = got.shape[1]
    chunk = head.shape[0] // (NZ * 4)
    shares = rows - chunk - 16
    pieces = []
    for i in range(NZ * 4):
        queries[i * shares : (i + 1) * shares, :] = got[i, :shares, :].astype(WIDE)
        head[i * chunk : (i + 1) * chunk, :] = got[i, shares : shares + chunk, :].astype(WIDE)
        pieces.append(got[i, shares + chunk :, :].astype(WIDE))
    row = 0
    for out in vectors:
        for i in range(0, out.shape[0], 8):
            out[i : i + 8, :] = pieces[row // 16][row % 16 : row % 16 + 8]
            row += 8


def norm_back(grad, gain, unitary, inverse):
    scaled = grad * gain
    along = jnp.mean(scaled * unitary, axis=-1, keepdims=True)
    return inverse * (scaled - jnp.mean(scaled, axis=-1, keepdims=True) - unitary * along)


def column_sum(value):
    return jnp.sum(value, axis=0, keepdims=True)


def middle_kernel(
    count, idx, t0, t1, t2, t3, kdoc0, kdoc1, positive, expo, query, unit,
    embed, low, head, cotangent, unitary, inverse, gain, hidden_in, slabs,
    grad_in, keep, send, part, loss, q0, q1,
    similar, grad_low, grad_hidden_in, head_part, rows_part, expand, sems1, contract, sems2,
):
    copy1 = slab_copy(slabs, 0, expand, sems1)
    copy2 = slab_copy(slabs, expand.shape[1], contract, sems2)
    copy2.start()
    copy1.start()
    totals = (t0[...] + t1[...]) + (t2[...] + t3[...])
    value, coefficient = loss_of(count, totals, (kdoc0, kdoc1), positive[...])
    loss[...] = jnp.broadcast_to(value, loss.shape)
    here = member(idx, kdoc0, totals.shape[0])
    similar[...] = (dot_tn(here, coefficient, PRECISE) * expo[...]).astype(LOW)
    grad_embed = unit_back(embed[...], dot_nn(similar[...], query[...])).astype(LOW)
    rows, width = embed.shape[0], low.shape[1]
    head_part[...] = dot_tn(low[...], grad_embed)
    grad_second = dot_nt(grad_embed, head[...].astype(LOW)) + cotangent[...].astype(WIDE)
    grad_in[...] = norm_back(grad_second, gain[...], unitary[...], inverse[...])
    grad_low[...] = grad_in[...].astype(LOW)
    sums = [
        column_sum(grad_low[...].astype(WIDE)),
        column_sum(grad_second * unitary[...]),
        column_sum(grad_second),
    ]
    value = hidden_in[...]
    grad = dot_nn(grad_low[...], finish(copy2, contract))
    bell = jnp.exp(-0.5 * value * value) * (1.0 / math.sqrt(2.0 * math.pi))
    slope = 0.5 * (1.0 + lax.erf(value * (0.5**0.5))) + value * bell
    grad_hidden_in[...] = (slope * grad).astype(LOW)
    sums.append(column_sum(grad_hidden_in[...].astype(WIDE)))
    part[...] = dot_nt(grad_hidden_in[...], finish(copy1, expand)).astype(LOW)
    for out, x in ((keep, idx[2]), (send, 1 - idx[2])):
        out[:rows, :] = grad_low[...]
        out[rows:, :] = columns_of(grad_hidden_in, x, width)
    rows_part[...] = jnp.zeros_like(rows_part)
    at = 0
    for value in sums:
        for i in range(value.shape[1] // PAIR):
            rows_part[at : at + 1, :] = value[:, i * PAIR : (i + 1) * PAIR]
            at += 1
    chunk = width // (NZ * 4)
    shares = q0.shape[2] - chunk - 16
    for mask in range(4):
        there = (idx[2] * 2 + idx[3]) ^ mask
        for z in range(NZ):
            out = (q0, q1)[mask % 2].at[mask // 2]
            at = (idx[1] ^ z) * 4 + there
            columns_here = pl.ds(pl.multiple_of(at * shares, shares), shares)
            out[z, :shares, :] = dot_tn(similar[:, columns_here], unit[...]).astype(out.dtype)
            out[z, shares : shares + chunk, :] = head_part[
                pl.ds(pl.multiple_of(at * chunk, chunk), chunk), :
            ].astype(out.dtype)
            out[z, shares + chunk :, :] = rows_part[
                pl.ds(pl.multiple_of(at * 16, 16), 16), :
            ].astype(out.dtype)


def slab_products(idx, left, right, outs, at):
    slab = outs[0].shape[-2]
    for z, out in enumerate(outs):
        mine = []
        for x in range(2):
            spot = (idx[1] ^ z) * 2 + (idx[2] ^ x)
            lanes = left[:, pl.ds(pl.multiple_of(spot * 2 * slab, 2 * slab), 2 * slab)]
            mine.append(jnp.where(idx[3] == 0, lanes[:, :slab], lanes[:, slab:]))
        both_rows = dot_tn(jnp.concatenate(mine, axis=1), right)
        for x in range(2):
            out[at + (x,)] = both_rows[x * slab : (x + 1) * slab].astype(out.dtype)


def weights_kernel(idx, f0, f1, f2, f3, g0, g1, g2, g3, own, s1, s2, s3, left, right):
    rows = g0.shape[0] // 2
    firsts, grads = (f0, f1, f2, f3), (g0, g1, g2, g3)
    for at, lefts, rights in ((0, grads, firsts), (1, firsts, grads)):
        for i in range(4):
            left[i * rows : (i + 1) * rows, :] = lefts[i][:rows, :]
            right[i * rows : (i + 1) * rows, :] = rights[i][rows : 2 * rows, :]
        slab_products(idx, left, right[...], (own, s1, s2, s3), (at,))


def output_kernel(idx, f0, f1, f2, f3, g0, g1, g2, g3, own, s1, s2, s3, left, right):
    rows, width = g0.shape
    few = rows * QUAD // width
    for i, (f, g) in enumerate(zip((f0, f1, f2, f3), (g0, g1, g2, g3))):
        left[i * rows : (i + 1) * rows, :] = g[...]
        for j in range(width // QUAD):
            right[i * rows + j * few : i * rows + (j + 1) * few, :] = f[
                2 * rows :, j * QUAD : (j + 1) * QUAD
            ]
    slab_products(idx, left, right[...], (own, s1, s2, s3), ())


def line_sum_kernel(idx, a0, a1, a2, a3, b0, b1, b2, b3, keep, keep_out, send):
    span = keep.shape[-1]
    total = a0[...] + a1[...].astype(WIDE) + (a2[...].astype(WIDE) + a3[...].astype(WIDE))
    keep[...] = total[:, 0]
    send[:, :span] = total[0, 1].astype(LOW)
    send[:, span : 2 * span] = total[1, 1].astype(LOW)
    total = b0[...] + b1[...].astype(WIDE) + (b2[...].astype(WIDE) + b3[...].astype(WIDE))
    keep_out[...] = total[0]
    send[:, 2 * span :] = total[1].astype(LOW)


def columns_kernel(idx, keep, keep_out, got, contract, expand, output):
    span = keep.shape[-1]
    for at, mine, out in ((0, keep[0], contract), (span, keep[1], expand), (2 * span, keep_out[...], output)):
        cols = mine.shape[1]
        out[:, pl.ds(pl.multiple_of(idx[2] * cols, 128), cols)] = mine
        out[:, pl.ds(pl.multiple_of((1 - idx[2]) * cols, 128), cols)] = got[
            :, at : at + cols
        ].astype(WIDE)


def first_back_kernel(
    idx, own, other, grad_second_in, unitary, inverse, gain, slabs,
    grad_in, grad_low, vectors, pack, held, sems,
):
    copy = slab_copy(slabs, slabs.shape[1] - held.shape[1], held, sems)
    copy.start()
    grad_first = grad_second_in[...] + pair(own, other)
    grad_in[...] = norm_back(grad_first, gain[...], unitary[...], inverse[...])
    grad_low[...] = grad_in[...].astype(LOW)
    vectors[...] = jnp.zeros_like(vectors)
    vectors[0:1, :] = column_sum(grad_low[...].astype(WIDE))
    vectors[1:2, :] = column_sum(grad_first * unitary[...])
    vectors[2:3, :] = column_sum(grad_first)
    grad = dot_nn(grad_low[...], finish(copy, held)).astype(LOW)
    half = pack.shape[1]
    for h in range(NZ * 2):
        lanes = slice(h * HEAD_DIM, (h + 1) * HEAD_DIM)
        pack[h, :, :HEAD_DIM] = grad[:half, lanes]
        pack[h, :, HEAD_DIM:] = grad[half:, lanes]


def triple_kernel(idx, dq, dkv, got, cosine, sine, out):
    rows = dq.shape[0]
    low_lanes = lax.broadcasted_iota(jnp.int32, (rows, PAIR), 1) < HEAD_DIM
    grads = dkv[...] + got[...]
    both_parts = jnp.where(low_lanes, dq[...], pltpu.roll(grads, HEAD_DIM, 1))
    turned = turn(both_parts, cosine[...], -sine[...])
    out[:, :PAIR] = turned.astype(LOW)
    out[:, PAIR:] = jnp.where(low_lanes, 0.0, grads).astype(LOW)


def extra_rows(bias, vectors):
    cols = bias.shape[1]
    rows = [bias]
    for i in range(3):
        for j in range(vectors.shape[1] // cols):
            rows.append(vectors[i : i + 1, j * cols : (j + 1) * cols])
    return jnp.concatenate(rows + [jnp.zeros((16 - len(rows), cols), WIDE)], axis=0)


def triple_weight_kernel(idx, *refs):
    sheets, (grad, vectors, keep, send, total) = refs[:8], refs[8:]
    mz, mx, mc = idx[1], idx[2], idx[3]
    rows = sheets[0].shape[0]
    slab = keep.shape[1] - 16
    for z in range(NZ):
        for x in range(2):
            spot = (mz ^ z) * 2 + (mx ^ x)
            at = pl.ds(pl.multiple_of(spot * rows, rows), rows)
            part = dot_tn(sheets[z * 2 + x][...], grad[at, :])
            if z + x == 0:
                total[...] = part
            else:
                total[...] += part
    extra = extra_rows(column_sum(grad[...].astype(WIDE)), vectors).astype(LOW)
    for spot in range(NZ * 2):
        for out, c in ((keep, mc), (send, 1 - mc)):
            at = pl.ds(pl.multiple_of((spot * 2 + c) * slab, slab), slab)
            out[spot, :slab, :] = total[at, :].astype(LOW)
            out[spot, slab:, :] = extra


def pair_sum_kernel(idx, one, two, out):
    out[...] = (one[...].astype(WIDE) + two[...].astype(WIDE)).astype(out.dtype)


def triple_out_kernel(idx, got, weight, bias, *vectors):
    slab = weight.shape[1]
    total = 0.0
    for spot in range(NZ * 2):
        at = spot * HEAD_DIM
        here = got[spot].astype(WIDE)
        for part, lane in enumerate(LANES):
            weight[part, :, at : at + HEAD_DIM] = here[:slab, lane : lane + HEAD_DIM]
            bias[part : part + 1, at : at + HEAD_DIM] = here[slab : slab + 1, lane : lane + HEAD_DIM]
        total = total + here[slab:]
    row = 1
    for out in vectors:
        for i in range(0, out.shape[0], 2):
            out[i : i + 1, :] = total[row : row + 1, :PAIR]
            out[i + 1 : i + 2, :] = total[row : row + 1, PAIR:]
            row += 1


def tokens_kernel(idx, got, weight, part, group):
    for h in range(NZ * 2):
        for p, lane in enumerate(LANES):
            at = (p * NZ * 2 + h) * HEAD_DIM
            group[:, at : at + HEAD_DIM] = got[h, :, lane : lane + HEAD_DIM]
    part[...] = dot_nt(group[...], weight[...]).astype(LOW)


def tokens_sum_kernel(idx, own, other, grad, out):
    out[...] = grad[...] + pair(own, other)


def shards(
    tokens,
    query_vecs,
    out_cotangent,
    doc_lengths,
    live_mask,
    positives,
    triple_weight,
    triple_bias,
    output_weight,
    output_bias,
    first_gain,
    first_shift,
    expand_weight,
    expand_bias,
    contract_weight,
    contract_bias,
    second_gain,
    second_shift,
    head_weight,
):
    outer = lax.axis_size("o")
    mo, mz, mx, mc, my = [lax.axis_index(a) for a in ("o", "z", "x", "c", "y")]
    index = jnp.stack([mo, mz, mx, mc, my]).astype(jnp.int32)
    rows, width = tokens.shape
    half = rows // 2
    slab = triple_weight.shape[0]
    docs = doc_lengths.shape[0]
    queries_count = positives.shape[0]
    blocks = outer * NZ * 4
    span = expand_weight.shape[1]
    quarter = span // 2
    proj = head_weight.shape[1]
    line = lambda vector: vector.reshape(1, -1)

    def widen(value):
        return lax.all_gather(value, "o") if outer > 1 else value[None]

    def narrow(value):
        return lax.psum_scatter(value, "o") if outer > 1 else value[0]

    def sum_outer(value):
        return lax.psum(value, "o") if outer > 1 else value

    by_z = [tokens] + [xor_z(tokens, m) for m in (1, 2, 3)]
    sheets = [tokens, flip(tokens, "x"), by_z[1], flip(by_z[1], "x")]

    heads, low_slab, triple_slab = whole(
        prep_kernel,
        "prep",
        index,
        (
            triple_weight.transpose(1, 0, 2),
            output_weight.T,
            expand_weight,
            contract_weight.T,
            line(live_mask),
        ),
        [shape((NZ * 2, slab + 16, QUAD), LOW)]
        + [shape((slab, n), LOW) for n in (2 * span + 2 * QUAD, 6 * QUAD)],
    )
    heads = lax.all_to_all(heads, ("z", "x"), 0, 0)
    for piece in by_z[2:]:
        sheets += [piece, flip(after(piece, heads), "x")]
    heads_other = flip(after(heads, sheets[1], sheets[3]), "c")
    if outer > 1:
        pack = widen(both(heads, heads_other, mc)).transpose(0, 2, 1, 3, 4)
        head_triple = pack[..., :slab, :].reshape(width, QUAD)
        live0, live1 = [
            pick(pack, c, 2)[..., slab, :rows].astype(WIDE).reshape(-1, rows) for c in (mc, 1 - mc)
        ]
    else:
        head_triple, live0, live1 = whole(
            heads_kernel,
            "heads",
            index,
            (heads, heads_other),
            [shape((width, QUAD), LOW)] + [shape((NZ * 2, rows), WIDE)] * 2,
        )

    where = jnp.arange(rows, dtype=jnp.int32) * blocks
    rank = jnp.arange(NZ * 2, dtype=jnp.int32) * 2

    def key_doc(live, c):
        block = jnp.arange(outer * NZ * 2, dtype=jnp.int32) * 2 + c
        doc = doc_layout(doc_lengths, block[:, None] + where[None, :])[0]
        return jnp.where(live > 0, doc, -1)

    kdoc0, kdoc1 = key_doc(live0, mc), key_doc(live1, 1 - mc)
    own_places = (mo * NZ * 4 + rank + mc)[:, None] + where[None, :]
    own_doc, own_position = doc_layout(doc_lengths, own_places.reshape(-1))
    lane = jnp.arange(PAIR) % (HEAD_DIM // 2)
    exponent = (2 * lane).astype(WIDE) / HEAD_DIM
    angles = own_position.astype(WIDE)[:, None] * jnp.exp(-math.log(10000.0) * exponent)[None, :]
    sign = jnp.where(jnp.arange(PAIR) % HEAD_DIM < HEAD_DIM // 2, -1.0, 1.0).astype(WIDE)
    cosine, sine = jnp.cos(angles), jnp.sin(angles) * sign[None, :]
    qdoc = own_doc.reshape(NZ, 2, 2, half, 1)
    query_unit = whole(
        query_kernel, "query_units", index, (query_vecs,), [shape(query_vecs.shape, LOW)]
    )[0]
    shares = query_vecs.shape[0] // (NZ * 4)
    positive = line(jnp.repeat(positives, query_vecs.shape[0] // queries_count))

    gathered = lax.all_gather(after(low_slab, *by_z[1:]), BLK, axis=0, tiled=True)
    triple_low = lax.all_gather(after(triple_slab, gathered), BLK, axis=0, tiled=True)

    count = NZ * 2 * rows
    queries, kv = whole(
        project_kernel,
        "project",
        index,
        (*sheets, head_triple, cosine, sine, triple_bias),
        [shape((count, PAIR), LOW)] * 2,
    )
    kv0, kv1 = [widen(v).reshape(-1, PAIR) for v in (kv, flip(kv, "c"))]
    meta = (qdoc, kdoc0, kdoc1)
    out, log_total, pack = attend(queries, kv0, kv1, *meta)
    wide_rows, low_rows, thin_rows = [shape((rows, n), t) for n, t in ((width, WIDE), (width, LOW), (1, WIDE))]

    def to_blocks(value):
        return lax.all_to_all(value.reshape((NZ * 2,) + value.shape[-2:]), ("z", "x"), 0, 0)

    pack = to_blocks(pack)
    attended_low, part = whole(
        branch_kernel,
        "branch",
        index,
        (pack,),
        [shape((rows, 2 * QUAD), LOW), low_rows],
        slab_scratch(width, 2 * QUAD),
        (gathered,),
    )
    both_slabs = slab_scratch(width, span) * 2
    few = rows * QUAD // width
    first, unitary1, inverse1, hidden_in, keep, send, part = whole(
        forward_kernel,
        "forward",
        index,
        (
            part, flip(part, "y"), tokens, line(output_bias), line(first_gain), line(first_shift),
            line(expand_bias), attended_low,
        ),
        [wide_rows, wide_rows, thin_rows, shape((rows, span), WIDE)]
        + [shape((2 * rows + few, width), LOW)] * 2
        + [low_rows],
        [pltpu.VMEM((rows, width), LOW), pltpu.VMEM((rows, span), LOW)] + both_slabs,
        (gathered,),
    )

    def over_z(parts):
        return [parts[0]] + [xor_z(parts[m], m) for m in (1, 2, 3)]

    def four_cores(keep, send):
        two = [keep, flip(send, "x")]
        return two + [flip(value, "c") for value in two]

    firsts = four_cores(keep, send)
    my_tokens = query_unit.shape[0]
    part_other = flip(part, "y")
    second_low, unitary2, inverse2, embed, unit_low, expo, totals = whole(
        second_kernel,
        "second",
        index,
        (
            part, part_other, first, line(contract_bias), line(second_gain), line(second_shift),
            head_weight, query_unit, kdoc0,
        ),
        [low_rows, wide_rows, thin_rows, shape((rows, proj), WIDE), shape((rows, proj), LOW)]
        + [shape((rows, my_tokens), WIDE), shape((docs, my_tokens), WIDE)],
    )

    def tree(own, one, two, three):
        return (own + one) + (two + three)

    totals = sum_outer(tree(totals, *[xor_s(totals, m) for m in (1, 2, 3)]))
    chunk = width // (NZ * 4)
    message = (NZ, shares + chunk + 16, proj)
    grad_second_in, keep, send, part, loss, *query_parts = whole(
        partial(middle_kernel, queries_count),
        "middle",
        index,
        (
            totals, *[xor_z(totals, m) for m in (1, 2, 3)], kdoc0, kdoc1, positive, expo, query_unit,
            unit_low, embed, second_low, head_weight, out_cotangent, unitary2, inverse2,
            line(second_gain), hidden_in,
        ),
        [wide_rows]
        + [shape((2 * rows, width), LOW)] * 2
        + [low_rows, shape((8, proj), WIDE), shape((2,) + message, WIDE), shape((2,) + message, LOW)],
        [
            pltpu.VMEM((rows, my_tokens), LOW),
            pltpu.VMEM((rows, width), LOW),
            pltpu.VMEM((rows, span), LOW),
            pltpu.VMEM((width, proj), WIDE),
            pltpu.VMEM((NZ * 4 * 16, proj), WIDE),
        ]
        + both_slabs,
        (gathered,),
    )
    grads = four_cores(keep, send)
    part_other = flip(part, "y")
    grad_first_in, grad_branch, vectors1, pack = whole(
        first_back_kernel,
        "first_back",
        index,
        (part, part_other, grad_second_in, unitary1, inverse1, line(first_gain)),
        [wide_rows, low_rows, shape((8, width), WIDE), shape((NZ * 2, half, PAIR), LOW)],
        slab_scratch(width, 2 * QUAD),
        (gathered,),
    )
    grad_out = to_blocks(pack)

    branches = four_cores(grad_branch, grad_branch)
    dims, dims_out = (2, 2, slab, quarter), (2, slab, QUAD)
    left_right = [pltpu.VMEM((4 * rows, width), LOW)]
    if outer == 1:
        weight_parts = whole(
            weights_kernel,
            "weights",
            index,
            (*firsts, *grads),
            [shape(dims, WIDE)] + [shape(dims, LOW)] * 3,
            left_right * 2,
        )
        output_parts = whole(
            output_kernel,
            "output",
            index,
            (*firsts, *branches),
            [shape(dims_out, WIDE)] + [shape(dims_out, LOW)] * 3,
            left_right + [pltpu.VMEM((4 * rows, QUAD), LOW)],
        )
    else:

        def parts_of(left, right):
            part = dot_tn(jnp.concatenate(left), jnp.concatenate(right))
            part = pick(narrow(part.reshape(outer, NZ, 2, 2, slab, -1)), mc, 2)
            for axis, spot in ((0, mz), (1, mx)):
                part = jnp.take(part, jnp.arange(part.shape[axis]) ^ spot, axis=axis)
            return part

        top, mid = slice(0, rows), slice(rows, 2 * rows)
        wide = [f[2 * rows :].reshape(few, 4, QUAD).transpose(1, 0, 2).reshape(rows, QUAD) for f in firsts]
        weight_parts = jnp.stack(
            [
                parts_of([g[top] for g in grads], [f[mid] for f in firsts]),
                parts_of([f[top] for f in firsts], [g[mid] for g in grads]),
            ],
            axis=1,
        )
        output_parts = parts_of(branches, wide)
        weight_parts = [weight_parts[0]] + [weight_parts[m].astype(LOW) for m in (1, 2, 3)]
        output_parts = [output_parts[0]] + [output_parts[m].astype(LOW) for m in (1, 2, 3)]

    two = [shape(message, WIDE), shape(message, LOW)]
    parts = whole(core_sum_kernel, "query_c", index, (query_parts[0], flip(query_parts[1], "c")), two)
    parts = whole(
        query_sum_kernel,
        "query_sum",
        index,
        (parts[0], flip(parts[1], "x")),
        [shape(message[1:], WIDE)] + [shape(message[1:], LOW)] * 3,
    )
    parts = [sum_outer(p) for p in parts]
    block = (mz * 2 + mx) * 2 + mc
    own_queries = lax.dynamic_slice_in_dim(query_vecs, block * shares, shares, 0)
    mine = whole(
        query_back_kernel, "query_back", index, (*over_z(parts), own_queries), [shape(message[1:], LOW)]
    )[0]
    grad_query, dkv0, dkv1 = attend_back(
        after(queries, weight_parts[0]), grad_out.reshape(NZ, 2, half, PAIR), out, log_total, kv0, kv1, *meta
    )

    weight_in, output_in = over_z(weight_parts), over_z(output_parts)
    dkv0, dkv1 = [narrow(v.reshape(outer, -1, PAIR)) for v in (dkv0, dkv1)]
    grad_triple = whole(
        triple_kernel,
        "triple",
        index,
        (after(grad_query.reshape(count, PAIR), mine, weight_in[1]), dkv0, flip(dkv1, "c"), cosine, sine),
        [shape((count, QUAD), LOW)],
    )[0]

    block_triple = to_blocks(grad_triple.reshape(NZ * 2, rows, QUAD))
    dims = (NZ * 2, slab + 16, QUAD)
    if outer == 1:
        keep, send = whole(
            triple_weight_kernel,
            "triple_weight",
            index,
            (*sheets, grad_triple, vectors1),
            [shape(dims, LOW)] * 2,
            [pltpu.VMEM((width, QUAD), WIDE)],
        )
    else:
        ordered = place(
            [((mz ^ (i // 2)) * 2 + (mx ^ (i % 2)), sheet) for i, sheet in enumerate(sheets)]
        ).reshape(count, width)
        part = narrow(dot_tn(ordered, grad_triple).reshape(outer, NZ * 2, 2, slab, QUAD))
        bias = sum_outer(jnp.sum(grad_triple, axis=0, dtype=WIDE))
        bias = extra_rows(line(bias), sum_outer(vectors1))
        bias = jnp.broadcast_to(bias, (NZ * 2, 2, 16, QUAD))
        part = jnp.concatenate([part, bias], axis=2).astype(LOW)
        keep, send = pick(part, mc, 1), pick(part, 1 - mc, 1)
    packed = whole(
        pair_sum_kernel, "pair_sum", index, (keep, flip(send, "c")), [shape(dims, LOW)]
    )[0]
    vector = shape((width // PAIR, PAIR), WIDE)
    triple_grad, triple_bias_grad, output_bias_grad, gain_one, shift_one = whole(
        triple_out_kernel,
        "triple_out",
        index,
        (lax.all_to_all(after(packed, block_triple), ("z", "x"), 0, 0),),
        [shape((3, slab, 2 * QUAD), WIDE), shape((3, 2 * QUAD), WIDE)] + [vector] * 3,
    )
    part = whole(
        tokens_kernel,
        "tokens",
        index,
        (after(block_triple, keep, output_parts[0], weight_in[2]), triple_low),
        [low_rows],
        [pltpu.VMEM((rows, 6 * QUAD), LOW)],
    )[0]
    keep, keep_out, send = whole(
        line_sum_kernel,
        "line_sum",
        index,
        (after(weight_in[0], part), *weight_in[1:], *output_in),
        [shape((2, slab, quarter), WIDE), shape((slab, QUAD), WIDE), shape((slab, 2 * quarter + QUAD), LOW)],
    )
    contract_grad, expand_grad, output_grad = whole(
        columns_kernel,
        "columns",
        index,
        (keep, keep_out, flip(send, "x")),
        [shape((slab, n), WIDE) for n in (span, span, 2 * QUAD)],
    )
    tokens_grad = whole(
        tokens_sum_kernel, "tokens_sum", index, (part, flip(part, "y"), grad_first_in), [wide_rows]
    )[0]

    queries_grad, head_grad, contract_bias_grad, gain_two, shift_two, expand_bias_grad = whole(
        spread_kernel,
        "spread",
        index,
        (lax.all_gather(mine, ("z", "x", "c")).reshape(NZ * 4, *message[1:]),),
        [shape((query_vecs.shape[0], proj), WIDE), shape((width, proj), WIDE)]
        + [vector] * 3
        + [shape((span // PAIR, PAIR), WIDE)],
    )

    return (
        second_low,
        loss[0, 0],
        tokens_grad,
        queries_grad,
        triple_grad.transpose(1, 0, 2),
        triple_bias_grad,
        output_grad.T,
        output_bias_grad.reshape(-1),
        gain_one.reshape(-1),
        shift_one.reshape(-1),
        expand_grad,
        expand_bias_grad.reshape(-1),
        contract_grad.T,
        contract_bias_grad.reshape(-1),
        gain_two.reshape(-1),
        shift_two.reshape(-1),
        head_grad,
    )


def solution(mesh):
    outer = mesh.shape["blk"] // 16
    five = Mesh(mesh.devices.reshape(outer, NZ, 2, 2, mesh.shape["tensor"]), BLK + ("y",))
    blk, tensor = BLK, "y"
    return jax.shard_map(
        shards,
        mesh=five,
        in_specs=(
            P(blk, None),
            P(),
            P(blk, None),
            P(),
            P(blk),
            P(),
            P(blk, None, tensor),
            P(None, tensor),
            P(tensor, blk),
            P(),
            P(),
            P(),
            P(blk, tensor),
            P(tensor),
            P(tensor, blk),
            P(),
            P(),
            P(),
            P(),
        ),
        out_specs=(
            P(blk, None),
            P(),
            P(blk, None),
            P(),
            P(blk, None, tensor),
            P(None, tensor),
            P(tensor, blk),
            P(),
            P(),
            P(),
            P(blk, tensor),
            P(tensor),
            P(tensor, blk),
            P(),
            P(),
            P(),
            P(),
        ),
        check_vma=False,
    )
```

```python
from functools import partial
import math

import jax
import jax.numpy as jnp
import numpy as np
from jax import lax
from jax.experimental import pallas as pl
from jax.experimental.pallas import tpu as pltpu
from jax.sharding import Mesh, PartitionSpec as P

HEAD_DIM = 64
PAIR = 2 * HEAD_DIM

SOFTMAX_TEMPER = 0.05
FLOOR_SCORE = -1e30
NORM_EPSILON = 1e-05
UNIT_EPSILON = 1e-06
PRECISE = lax.Precision.HIGHEST
LOW = jnp.bfloat16
WIDE = jnp.float32

BLK = ("o", "z", "x", "c")
NZ = 4
FOUR = [0, 1, 2, 3]

VMEM_BYTES = 56 * 1024 * 1024
LANES = (0, 64, 192)
QUAD = 4 * HEAD_DIM


def xor_z(value, mask):
    return lax.ppermute(value, "z", [(i, i ^ mask) for i in FOUR])


def xor_s(value, mask):
    return lax.ppermute(value, ("x", "c"), [(i, i ^ mask) for i in FOUR])


def flip(value, axis):
    return lax.ppermute(value, axis, [(0, 1), (1, 0)])


def pick(value, index, axis=0):
    return lax.dynamic_index_in_dim(value, index, axis, keepdims=False)


def after(value, *others):
    return lax.optimization_barrier((value,) + others)[0]


def place(pieces):
    first = pieces[0][1]
    whole = jnp.zeros((len(pieces),) + first.shape, first.dtype)
    for index, piece in pieces:
        whole = lax.dynamic_update_slice_in_dim(whole, piece[None], index, 0)
    return whole


def both(mine, other, where):
    return place([(where, mine), (1 - where, other)])


def doc_layout(doc_lengths, places):
    ends = jnp.cumsum(doc_lengths)
    starts = ends - doc_lengths
    passed = starts <= places[..., None]
    doc_index = jnp.sum(passed.astype(jnp.int32), axis=-1) - 1
    begin = jnp.max(jnp.where(passed, starts, 0), axis=-1)
    return (doc_index, places - begin)


def dot_nn(a, b, precision=None):
    return lax.dot_general(
        a, b, (((1,), (0,)), ((), ())), precision=precision, preferred_element_type=WIDE
    )


def dot_nt(a, b, precision=None):
    return lax.dot_general(
        a, b, (((1,), (1,)), ((), ())), precision=precision, preferred_element_type=WIDE
    )


def dot_tn(a, b, precision=None):
    return lax.dot_general(
        a, b, (((0,), (0,)), ((), ())), precision=precision, preferred_element_type=WIDE
    )


def shape(dims, dtype):
    return jax.ShapeDtypeStruct(dims, dtype)


PARAMS = pltpu.CompilerParams(vmem_limit_bytes=VMEM_BYTES)

TAKES = dict(
    prep=2.5, heads=2.0, project=3.8, attend=7.5, branch=3.5, forward=7.7, second=3.6, middle=12.0, first_back=3.8, attend_back=9.8, triple=2.9, triple_weight=3.8, tokens=3.9,
    tokens_sum=2.1, weights=5.2, output=2.3, core_sum=3.9, line_sum=2.7, columns=2.2, pair_sum=1.8,
    triple_out=1.9, query_units=2.8, query_sum=1.9, query_c=2.5, query_back=1.6, spread=3.5,
)


SCALE = 1.0


def cost(name):
    took = TAKES[name] * SCALE
    return pl.CostEstimate(
        flops=int(took * 1.15e9), bytes_accessed=int(took * 3.7e6), transcendentals=0
    )


def whole(kernel, name, index, inputs, outputs, scratch=(), slabs=()):
    return pl.pallas_call(
        kernel,
        in_specs=[pl.BlockSpec(memory_space=pltpu.SMEM)]
        + [pl.BlockSpec(memory_space=pltpu.VMEM)] * len(inputs)
        + [pl.BlockSpec(memory_space=pl.ANY)] * len(slabs),
        out_specs=[pl.BlockSpec(memory_space=pltpu.VMEM)] * len(outputs),
        out_shape=list(outputs),
        scratch_shapes=list(scratch),
        compiler_params=PARAMS,
        cost_estimate=cost(name),
        name=name,
    )(index, *inputs, *slabs)


def slab_copy(slabs, at, weight, sems):
    there = slabs.at[:, pl.ds(at, weight.shape[1])]
    return pltpu.make_async_copy(there, weight, sems.at[0])


def piece_copies(idx, pieces, weight, sems):
    if len(pieces) == 1:
        return [pltpu.make_async_copy(pieces[0], weight, sems.at[0])]
    count, rows, cols = pieces[0].shape
    slab = (rows - 16) // 3
    copies = []
    for c, piece in enumerate(pieces):
        for spot in range(count):
            row = (spot * 2 + (idx[3] ^ c)) * slab
            for i in range(2):
                here = piece.at[spot, pl.ds((i + 1) * slab + 16, slab), :]
                there = weight.at[pl.ds(pl.multiple_of(row, slab), slab), pl.ds(i * cols, cols)]
                copies.append(pltpu.make_async_copy(here, there, sems.at[len(copies)]))
    return copies


def piece_scratch(rows, cols):
    return [pltpu.VMEM((rows, cols), LOW), pltpu.SemaphoreType.DMA((NZ * 8,))]


def slab_scratch(rows, cols):
    return [pltpu.VMEM((rows, cols), LOW), pltpu.SemaphoreType.DMA((1,))]


def start(copies):
    for copy in copies:
        copy.start()


def finish(copies, weight):
    for copy in copies:
        copy.wait()
    return weight[...]


def prep_kernel(idx, tw, ow, ew, cw, live, heads, low, tri):
    slab, span = ew.shape
    alive = jnp.broadcast_to(live[...], (16, live.shape[1])).astype(WIDE).astype(LOW)
    for spot in range(NZ * 2):
        at = spot * HEAD_DIM
        for part, lane in enumerate(LANES):
            heads[spot, :slab, lane : lane + HEAD_DIM] = tw[part, :, at : at + HEAD_DIM].astype(LOW)
        heads[spot, :slab, PAIR : PAIR + HEAD_DIM] = jnp.zeros((slab, HEAD_DIM), LOW)
        heads[spot, slab : slab + 16, : live.shape[1]] = alive
        heads[spot, slab : slab + 16, PAIR:] = jnp.zeros((16, PAIR), LOW)
        heads[spot, slab + 16 : 2 * slab + 16, :] = ow[:, :QUAD].astype(LOW)
        heads[spot, 2 * slab + 16 :, :] = ow[:, QUAD:].astype(LOW)
    low[:, :span] = ew[...].astype(LOW)
    low[:, span:] = cw[...].astype(LOW)
    for part in range(3):
        tri[:, part * 2 * QUAD : (part + 1) * 2 * QUAD] = tw[part].astype(LOW)


def heads_kernel(idx, own, other, weight, live0, live1):
    slab, mc = (own.shape[1] - 16) // 3, idx[3]
    for spot in range(NZ * 2):
        for source, c, live in ((own, mc, live0), (other, 1 - mc, live1)):
            rows = pl.ds(pl.multiple_of((spot * 2 + c) * slab, slab), slab)
            weight[rows, :] = source[spot, :slab, :]
            live[spot : spot + 1, :] = source[spot, slab : slab + 16, :PAIR].astype(WIDE)[:1]


def swap_halves(value):
    lane = lax.broadcasted_iota(jnp.int32, value.shape, 1)
    half = HEAD_DIM // 2
    return jnp.where(
        (lane & half) == 0,
        pltpu.roll(value, PAIR - half, 1),
        pltpu.roll(value, half, 1),
    )


def turn(value, cosine, sine):
    return value * cosine + swap_halves(value) * sine


def sheet_rows(idx, sheets):
    rows = sheets[0].shape[0]
    half = rows // 2
    parts = []
    for x in range(2):
        spot = idx[1] * 2 + (idx[2] ^ x)
        parts.append((sheets[x][...], pl.ds(pl.multiple_of(spot * rows, rows), rows)))
    for at, sheet in enumerate(sheets[2:]):
        z, y = at // 2 + 1, at % 2
        for x in range(2):
            spot = (idx[1] ^ z) * 2 + (idx[2] ^ x)
            row = spot * rows + (idx[4] ^ y) * half
            parts.append((sheet[x], pl.ds(pl.multiple_of(row, half), half)))
    return parts


def project_kernel(idx, *refs):
    sheets, (weight, cosine, sine, bias, query, kv) = refs[:8], refs[8:]
    parts = sheet_rows(idx, sheets)
    mz, mx = idx[1], idx[2]
    mine = mz * 2 + mx
    biases = []
    for part in range(3):
        total = jnp.zeros((1, HEAD_DIM), WIDE)
        for h in range(NZ * 2):
            here = bias[part : part + 1, h * HEAD_DIM : (h + 1) * HEAD_DIM]
            total = jnp.where(mine == h, here, total)
        biases.append(total)
    empty = jnp.zeros((1, HEAD_DIM), WIDE)
    offset = jnp.concatenate([biases[0], biases[1], empty, biases[2]], axis=1)
    weights = weight[...]
    for value, at in parts:
        low_lanes = lax.broadcasted_iota(jnp.int32, (value.shape[0], PAIR), 1) < HEAD_DIM
        triple = dot_nn(value, weights) + offset
        turned = turn(triple[:, :PAIR], cosine[at, :], sine[at, :])
        query[at, :] = jnp.where(low_lanes, turned, 0.0).astype(LOW)
        kv[at, :] = jnp.where(
            low_lanes, pltpu.roll(turned, HEAD_DIM, 1), triple[:, PAIR:]
        ).astype(LOW)


def key_row(ref):
    rows = ref[...]
    return jnp.concatenate([rows[i : i + 1] for i in range(rows.shape[0])], axis=1)


def attend_kernel(q_ref, kv0_ref, kv1_ref, qdoc_ref, kdoc0_ref, kdoc1_ref, out_ref, log_ref, pack_ref):
    scale = HEAD_DIM ** (-0.5)
    rows = q_ref.shape[3]
    queries = q_ref[0].reshape(4 * rows, PAIR)
    kv = (kv0_ref[...], kv1_ref[...])
    doc = qdoc_ref[0].reshape(4 * rows, 1)
    allowed = [doc == key_row(ref) for ref in (kdoc0_ref, kdoc1_ref)]
    scores = [
        jnp.where(ok, dot_nt(queries, keys) * scale, FLOOR_SCORE) for ok, keys in zip(allowed, kv)
    ]
    peak = jnp.maximum(*[jnp.max(s, axis=-1, keepdims=True) for s in scores])
    weights = [jnp.where(ok, jnp.exp(s - peak), 0.0) for ok, s in zip(allowed, scores)]
    total = sum(jnp.sum(w, axis=-1, keepdims=True) for w in weights)
    mixed = sum(dot_nn(w.astype(LOW), keys) for w, keys in zip(weights, kv)) / total
    out_ref[0] = mixed.reshape(2, 2, rows, PAIR)
    log_ref[0] = (peak + jnp.log(total)).reshape(2, 2, rows, 1)
    low_lanes = lax.broadcasted_iota(jnp.int32, (rows, PAIR), 1) < HEAD_DIM
    for x in range(2):
        upper = mixed[2 * x * rows : (2 * x + 1) * rows]
        lower = mixed[(2 * x + 1) * rows : (2 * x + 2) * rows]
        pack_ref[0, x] = jnp.where(low_lanes, pltpu.roll(upper, HEAD_DIM, 1), lower).astype(LOW)


def attend_specs(rows, keys, key_rows):
    half = rows // 2
    size = max(16, min(half, half * 2048 // (2 * keys)))
    full = lambda n, m: pl.BlockSpec((n, m), lambda i, j: (0, 0))
    part = lambda m: pl.BlockSpec((1, 2, 2, size, m), lambda i, j: (i, 0, 0, j, 0))
    pack = pl.BlockSpec((1, 2, size, PAIR), lambda i, j: (i, 0, j, 0))
    kv, docs = full(keys, PAIR), full(key_rows, rows)
    return (NZ, half // size), part, pack, kv, docs


def attend(queries, kv0, kv1, qdoc, kdoc0, kdoc1):
    rows = kdoc0.shape[1]
    half = rows // 2
    grid, part, pack, kv, docs = attend_specs(rows, kv0.shape[0], kdoc0.shape[0])
    return pl.pallas_call(
        attend_kernel,
        grid=grid,
        in_specs=[part(PAIR), kv, kv, part(1), docs, docs],
        out_specs=[part(PAIR), part(1), pack],
        out_shape=[
            shape((NZ, 2, 2, half, PAIR), WIDE),
            shape((NZ, 2, 2, half, 1), WIDE),
            shape((NZ, 2, half, PAIR), LOW),
        ],
        compiler_params=PARAMS,
        cost_estimate=cost("attend"),
        name="attend",
    )(queries.reshape(NZ, 2, 2, half, PAIR), kv0, kv1, qdoc, kdoc0, kdoc1)


def attend_back_kernel(
    q_ref, g_ref, o_ref, log_ref, kv0_ref, kv1_ref, qdoc_ref, kdoc0_ref, kdoc1_ref,
    dq_ref, dkv0_ref, dkv1_ref,
):
    scale = HEAD_DIM ** (-0.5)
    rows = q_ref.shape[3]

    @pl.when((pl.program_id(0) == 0) & (pl.program_id(1) == 0))
    def _():
        dkv0_ref[...] = jnp.zeros_like(dkv0_ref)
        dkv1_ref[...] = jnp.zeros_like(dkv1_ref)

    queries = q_ref[0].reshape(4 * rows, PAIR)
    high_lanes = lax.broadcasted_iota(jnp.int32, (rows, PAIR), 1) >= HEAD_DIM
    parts = []
    for x in range(2):
        packed = g_ref[0, x].astype(WIDE)
        parts.append(jnp.where(high_lanes, pltpu.roll(packed, HEAD_DIM, 1), 0.0))
        parts.append(jnp.where(high_lanes, packed, 0.0))
    wide = jnp.concatenate(parts, axis=0)
    grads = wide.astype(LOW)
    delta = jnp.sum(wide * o_ref[0].reshape(4 * rows, PAIR), axis=-1, keepdims=True)
    doc, log_total = qdoc_ref[0].reshape(4 * rows, 1), log_ref[0].reshape(4 * rows, 1)
    total = jnp.zeros((4 * rows, PAIR), WIDE)
    for kv_ref, kdoc_ref, dkv_ref in (
        (kv0_ref, kdoc0_ref, dkv0_ref),
        (kv1_ref, kdoc1_ref, dkv1_ref),
    ):
        keys = kv_ref[...]
        raw = dot_nt(queries, keys)
        probs = jnp.where(doc == key_row(kdoc_ref), jnp.exp(raw * scale - log_total), 0.0)
        dprobs = dot_nt(grads, keys)
        dscores = (probs * (dprobs - delta) * scale).astype(LOW)
        total = total + dot_nn(dscores, keys)
        dkv_ref[...] += dot_tn(dscores, queries) + dot_tn(probs.astype(LOW), grads)
    dq_ref[0] = total.reshape(2, 2, rows, PAIR)


def attend_back(queries, grads, out, log_total, kv0, kv1, qdoc, kdoc0, kdoc1):
    rows, keys = kdoc0.shape[1], kv0.shape[0]
    half = rows // 2
    grid, part, pack, kv, docs = attend_specs(rows, keys, kdoc0.shape[0])
    return pl.pallas_call(
        attend_back_kernel,
        grid=grid,
        in_specs=[part(PAIR), pack, part(PAIR), part(1), kv, kv, part(1), docs, docs],
        out_specs=[part(PAIR), kv, kv],
        out_shape=[
            shape((NZ, 2, 2, half, PAIR), WIDE),
            shape((keys, PAIR), WIDE),
            shape((keys, PAIR), WIDE),
        ],
        compiler_params=PARAMS,
        cost_estimate=cost("attend_back"),
        name="attend_back",
    )(queries.reshape(NZ, 2, 2, half, PAIR), grads, out, log_total, kv0, kv1, qdoc, kdoc0, kdoc1)


def branch_kernel(pieces, idx, got, *refs):
    slabs, (low, part, held, sems) = refs[:pieces], refs[pieces:]
    copy = piece_copies(idx, slabs, held, sems)
    start(copy)
    half = got.shape[1]
    for h in range(NZ * 2):
        lanes = slice(h * HEAD_DIM, (h + 1) * HEAD_DIM)
        low[:half, lanes] = got[h, :, :HEAD_DIM]
        low[half:, lanes] = got[h, :, HEAD_DIM:]
    part[...] = dot_nt(low[...], finish(copy, held)).astype(LOW)


def normalize(value):
    center = value - jnp.mean(value, axis=-1, keepdims=True)
    spread = jnp.mean(center * center, axis=-1, keepdims=True)
    inverse = lax.rsqrt(spread + NORM_EPSILON)
    return center * inverse, inverse


def pair(own, other):
    return own[...].astype(WIDE) + other[...].astype(WIDE)


def forward_kernel(
    idx, own, other, tokens, bias, gain, shift, hidden_bias, attended, slabs,
    first, unitary, inverse, hidden_in, keep, send, part,
    low, hidden, expand, sems1, contract, sems2,
):
    copy1 = [slab_copy(slabs, 0, expand, sems1)]
    copy2 = [slab_copy(slabs, expand.shape[1], contract, sems2)]
    start(copy1 + copy2)
    value = tokens[...].astype(WIDE) + (pair(own, other) + bias[...])
    unitary[...], inverse[...] = normalize(value)
    first[...] = unitary[...] * gain[...] + shift[...]
    low[...] = first[...].astype(LOW)
    value = dot_nn(low[...], finish(copy1, expand)) + hidden_bias[...]
    hidden_in[...] = value
    hidden[...] = (0.5 * value * (1.0 + lax.erf(value * (0.5**0.5)))).astype(LOW)
    part[...] = dot_nt(hidden[...], finish(copy2, contract)).astype(LOW)
    rows, width = low.shape
    few = rows * QUAD // width
    for out, x in ((keep, idx[2]), (send, 1 - idx[2])):
        out[:rows, :] = low[...]
        out[rows : 2 * rows, :] = columns_of(hidden, x, width)
        for i in range(width // QUAD):
            out[2 * rows :, i * QUAD : (i + 1) * QUAD] = attended[
                i * few : (i + 1) * few, pl.ds(pl.multiple_of(x * QUAD, QUAD), QUAD)
            ]


def columns_of(ref, x, span):
    return ref[:, pl.ds(pl.multiple_of(x * span, 128), span)]


def unit_scale(value):
    return lax.rsqrt(jnp.sum(value * value, axis=-1, keepdims=True) + UNIT_EPSILON)


def second_kernel(
    idx, own, other, first, bias, gain, shift, head, query, kdoc,
    low, unitary, inverse, embed, unit, expo, totals,
):
    value = first[...] + (pair(own, other) + bias[...])
    unitary[...], inverse[...] = normalize(value)
    low[...] = (unitary[...] * gain[...] + shift[...]).astype(LOW)
    embed[...] = dot_nn(low[...], head[...].astype(LOW))
    unit[...] = (embed[...] * unit_scale(embed[...])).astype(LOW)
    expo[...] = jnp.exp(dot_nt(unit[...], query[...]) / SOFTMAX_TEMPER)
    totals[...] = dot_nn(member(idx, kdoc, totals.shape[0]), expo[...], PRECISE)


def query_kernel(idx, vecs, out, own):
    block, shares = (idx[1] * 2 + idx[2]) * 2 + idx[3], own.shape[0]
    own[...] = vecs[pl.ds(pl.multiple_of(block * shares, shares), shares), :]
    value = vecs[...].astype(WIDE)
    out[...] = (value * unit_scale(value)).astype(LOW)


def member(idx, kdoc, docs):
    row = kdoc[pl.ds((idx[0] * NZ + idx[1]) * 2 + idx[2], 1), :]
    label = lax.broadcasted_iota(jnp.int32, (docs, row.shape[1]), 0)
    return jnp.where(row == label, 1.0, 0.0)


def group_sum(value, length):
    column = lax.broadcasted_iota(jnp.int32, value.shape, 1)
    span = value.shape[1]
    step = 1
    while step < length:
        ahead, behind = pltpu.roll(value, span - step, 1), pltpu.roll(value, step, 1)
        value = value + jnp.where((column & step) == 0, ahead, behind)
        step *= 2
    return value


def loss_of(count, totals, kdocs, positive):
    docs, columns = totals.shape
    length = columns // count
    label = lax.broadcasted_iota(jnp.int32, (docs, 1), 0)
    tokens = jnp.zeros((docs, 1), WIDE)
    for ref in kdocs:
        tokens = tokens + jnp.sum(jnp.where(key_row(ref) == label, 1.0, 0.0), axis=1, keepdims=True)
    doc_score = group_sum(SOFTMAX_TEMPER * (jnp.log(totals) - jnp.log(tokens)), length)
    best = jnp.max(doc_score, axis=0, keepdims=True)
    shifted = jnp.exp(doc_score - best)
    shifted_sum = jnp.sum(shifted, axis=0, keepdims=True)
    chosen = jnp.where(label == positive, 1.0, 0.0)
    each = best + jnp.log(shifted_sum) - jnp.sum(doc_score * chosen, axis=0, keepdims=True)
    loss = jnp.sum(each, axis=1, keepdims=True) / columns
    return loss, (shifted / shifted_sum - chosen) / (totals * count)


def core_sum_kernel(idx, pack, keep, got, out):
    half = pack.shape[1]
    for spot in range(pack.shape[0]):
        out[spot, :half, :] = pack[spot]
        out[spot, half:, :] = (keep[spot] + got[spot].astype(WIDE)).astype(LOW)


def unit_back(value, grad):
    scale = unit_scale(value)
    along = jnp.sum(grad * value, axis=-1, keepdims=True)
    return scale * grad - value * (along * scale * scale * scale)


def query_back_kernel(half, idx, got, value, out):
    total = [got[spot, half:, :].astype(WIDE) for spot in range(NZ * 2)]
    while len(total) > 1:
        total = [a + b for a, b in zip(total[::2], total[1::2])]
    total, shares = total[0], value.shape[0]
    out[:shares, :] = unit_back(value[...].astype(WIDE), total[:shares]).astype(LOW)
    out[shares:, :] = total[shares:].astype(LOW)


def spread_kernel(idx, got, queries, head, *vectors):
    rows = got.shape[1]
    chunk = head.shape[0] // (NZ * 4)
    shares = rows - 2 * chunk
    pieces = []
    for i in range(NZ * 4):
        queries[i * shares : (i + 1) * shares, :] = got[i, :shares, :].astype(WIDE)
        head[i * chunk : (i + 1) * chunk, :] = got[i, shares : shares + chunk, :].astype(WIDE)
        pieces.append(got[i, shares + chunk : shares + chunk + 16, :].astype(WIDE))
    row = 0
    for out in vectors:
        for i in range(0, out.shape[0], 8):
            out[i : i + 8, :] = pieces[row // 16][row % 16 : row % 16 + 8]
            row += 8


def norm_back(grad, gain, unitary, inverse):
    scaled = grad * gain
    along = jnp.mean(scaled * unitary, axis=-1, keepdims=True)
    return inverse * (scaled - jnp.mean(scaled, axis=-1, keepdims=True) - unitary * along)


def column_sum(value):
    return jnp.sum(value, axis=0, keepdims=True)


def middle_kernel(
    count, idx, t0, t1, t2, t3, kdoc0, kdoc1, positive, expo, query, unit,
    embed, low, head, cotangent, unitary, inverse, gain, hidden_in, slabs,
    grad_in, keep, send, part, loss, q0, q1,
    similar, grad_low, grad_hidden_in, head_part, rows_part, expand, sems1, contract, sems2,
):
    copy1 = [slab_copy(slabs, 0, expand, sems1)]
    copy2 = [slab_copy(slabs, expand.shape[1], contract, sems2)]
    start(copy2 + copy1)
    totals = (t0[...] + t1[...]) + (t2[...] + t3[...])
    value, coefficient = loss_of(count, totals, (kdoc0, kdoc1), positive[...])
    loss[...] = jnp.broadcast_to(value, loss.shape)
    here = member(idx, kdoc0, totals.shape[0])
    similar[...] = (dot_tn(here, coefficient, PRECISE) * expo[...]).astype(LOW)
    grad_embed = unit_back(embed[...], dot_nn(similar[...], query[...])).astype(LOW)
    rows, width = embed.shape[0], low.shape[1]
    head_part[...] = dot_tn(low[...], grad_embed)
    grad_second = dot_nt(grad_embed, head[...].astype(LOW)) + cotangent[...].astype(WIDE)
    grad_in[...] = norm_back(grad_second, gain[...], unitary[...], inverse[...])
    grad_low[...] = grad_in[...].astype(LOW)
    sums = [
        column_sum(grad_low[...].astype(WIDE)),
        column_sum(grad_second * unitary[...]),
        column_sum(grad_second),
    ]
    value = hidden_in[...]
    grad = dot_nn(grad_low[...], finish(copy2, contract))
    bell = jnp.exp(-0.5 * value * value) * (1.0 / math.sqrt(2.0 * math.pi))
    slope = 0.5 * (1.0 + lax.erf(value * (0.5**0.5))) + value * bell
    grad_hidden_in[...] = (slope * grad).astype(LOW)
    sums.append(column_sum(grad_hidden_in[...].astype(WIDE)))
    part[...] = dot_nt(grad_hidden_in[...], finish(copy1, expand)).astype(LOW)
    for out, x in ((keep, idx[2]), (send, 1 - idx[2])):
        out[:rows, :] = grad_low[...]
        out[rows:, :] = columns_of(grad_hidden_in, x, width)
    rows_part[...] = jnp.zeros_like(rows_part)
    at = 0
    for value in sums:
        for i in range(value.shape[1] // PAIR):
            rows_part[at : at + 1, :] = value[:, i * PAIR : (i + 1) * PAIR]
            at += 1
    chunk = width // (NZ * 4)
    shares = q0.shape[1] - 2 * chunk
    for z in range(NZ * 2):
        for c, out in enumerate((q0, q1)):
            at = z * 2 + (idx[3] ^ c)
            columns_here = pl.ds(pl.multiple_of(at * shares, shares), shares)
            out[z, :shares, :] = dot_tn(similar[:, columns_here], unit[...]).astype(out.dtype)
            out[z, shares : shares + chunk, :] = head_part[
                pl.ds(pl.multiple_of(at * chunk, chunk), chunk), :
            ].astype(out.dtype)
            out[z, shares + chunk : shares + chunk + 16, :] = rows_part[
                pl.ds(pl.multiple_of(at * 16, 16), 16), :
            ].astype(out.dtype)
            out[z, shares + chunk + 16 :, :] = jnp.zeros((chunk - 16, PAIR), out.dtype)


def slab_products(idx, left, right, outs):
    slab = outs[0].shape[-2]
    for z, out in enumerate(outs):
        mine = []
        for x in range(2):
            spot = (idx[1] ^ z) * 2 + (idx[2] ^ x)
            lanes = left[:, pl.ds(pl.multiple_of(spot * 2 * slab, 2 * slab), 2 * slab)]
            mine.append(jnp.where(idx[3] == 0, lanes[:, :slab], lanes[:, slab:]))
        both_rows = dot_tn(jnp.concatenate(mine, axis=1), right)
        for x in range(2):
            out[x] = both_rows[x * slab : (x + 1) * slab].astype(out.dtype)


def weights_kernel(idx, f0, f1, f2, f3, g0, g1, g2, g3, *refs):
    (*outs, left, right) = refs
    rows = g0.shape[0] // 2
    firsts, grads = (f0, f1, f2, f3), (g0, g1, g2, g3)
    for lefts, rights, group in ((grads, firsts, outs[:4]), (firsts, grads, outs[4:])):
        for i in range(4):
            left[i * rows : (i + 1) * rows, :] = lefts[i][:rows, :]
            right[i * rows : (i + 1) * rows, :] = rights[i][rows : 2 * rows, :]
        slab_products(idx, left, right[...], group)


def output_kernel(idx, f0, f1, f2, f3, g0, g1, g2, g3, e1, e2, e3, own, s1, s2, s3, left, right):
    rows, width = g0.shape
    few = rows * QUAD // width
    for i, (f, g) in enumerate(zip((f0, f1, f2, f3), (g0, g1, g2, g3))):
        left[i * rows : (i + 1) * rows, :] = g[...]
        for j in range(width // QUAD):
            right[i * rows + j * few : i * rows + (j + 1) * few, :] = f[
                2 * rows :, j * QUAD : (j + 1) * QUAD
            ]
    span = e1.shape[-1]
    for out, expand in ((s1, e1), (s2, e2), (s3, e3)):
        out[:, :, :span] = expand[...]
    slab_products(
        idx, left, right[...], [own] + [out.at[:, :, span:] for out in (s1, s2, s3)]
    )


def line_sum_kernel(idx, c0, c1, c2, c3, e0, o0, b1, b2, b3, keep, keep_out, send):
    span = c0.shape[2]
    for x in range(2):
        wide = c0[x] + c1[x].astype(WIDE) + (c2[x].astype(WIDE) + c3[x].astype(WIDE))
        both = b1[x].astype(WIDE) + (b2[x].astype(WIDE) + b3[x].astype(WIDE))
        expand, thin = e0[x] + both[:, :span], o0[x] + both[:, span:]
        if x == 0:
            keep[0], keep[1], keep_out[...] = wide, expand, thin
        else:
            send[:, :span] = wide.astype(LOW)
            send[:, span : 2 * span] = expand.astype(LOW)
            send[:, 2 * span :] = thin.astype(LOW)


def columns_kernel(idx, keep, keep_out, got, contract, expand, output):
    span = keep.shape[-1]
    for at, mine, out in ((0, keep[0], contract), (span, keep[1], expand), (2 * span, keep_out[...], output)):
        cols = mine.shape[1]
        out[:, pl.ds(pl.multiple_of(idx[2] * cols, 128), cols)] = mine
        out[:, pl.ds(pl.multiple_of((1 - idx[2]) * cols, 128), cols)] = got[
            :, at : at + cols
        ].astype(WIDE)


def first_back_kernel(
    pieces, idx, own, other, grad_second_in, unitary, inverse, gain, *refs
):
    slabs, (grad_in, grad_low, vectors, pack, held, sems) = refs[:pieces], refs[pieces:]
    copy = piece_copies(idx, slabs, held, sems)
    start(copy)
    grad_first = grad_second_in[...] + pair(own, other)
    grad_in[...] = norm_back(grad_first, gain[...], unitary[...], inverse[...])
    grad_low[...] = grad_in[...].astype(LOW)
    vectors[...] = jnp.zeros_like(vectors)
    vectors[0:1, :] = column_sum(grad_low[...].astype(WIDE))
    vectors[1:2, :] = column_sum(grad_first * unitary[...])
    vectors[2:3, :] = column_sum(grad_first)
    grad = dot_nn(grad_low[...], finish(copy, held)).astype(LOW)
    half = pack.shape[1]
    for h in range(NZ * 2):
        lanes = slice(h * HEAD_DIM, (h + 1) * HEAD_DIM)
        pack[h, :, :HEAD_DIM] = grad[:half, lanes]
        pack[h, :, HEAD_DIM:] = grad[half:, lanes]


def triple_kernel(idx, dq, dkv, got, cosine, sine, out):
    rows = dq.shape[0]
    low_lanes = lax.broadcasted_iota(jnp.int32, (rows, PAIR), 1) < HEAD_DIM
    grads = dkv[...] + got[...]
    both_parts = jnp.where(low_lanes, dq[...], pltpu.roll(grads, HEAD_DIM, 1))
    turned = turn(both_parts, cosine[...], -sine[...])
    out[:, :PAIR] = turned.astype(LOW)
    out[:, PAIR:] = jnp.where(low_lanes, 0.0, grads).astype(LOW)


def extra_rows(bias, vectors):
    cols = bias.shape[1]
    rows = [bias]
    for i in range(3):
        for j in range(vectors.shape[1] // cols):
            rows.append(vectors[i : i + 1, j * cols : (j + 1) * cols])
    return jnp.concatenate(rows + [jnp.zeros((16 - len(rows), cols), WIDE)], axis=0)


def triple_weight_kernel(idx, *refs):
    sheets, (grad, vectors, keep, send, total) = refs[:8], refs[8:]
    mc = idx[3]
    slab = keep.shape[1] - 16
    for i, (value, at) in enumerate(sheet_rows(idx, sheets)):
        part = dot_tn(value, grad[at, :])
        if i == 0:
            total[...] = part
        else:
            total[...] += part
    extra = extra_rows(column_sum(grad[...].astype(WIDE)), vectors).astype(LOW)
    for spot in range(NZ * 2):
        for out, c in ((keep, mc), (send, 1 - mc)):
            at = pl.ds(pl.multiple_of((spot * 2 + c) * slab, slab), slab)
            out[spot, :slab, :] = total[at, :].astype(LOW)
            out[spot, slab:, :] = extra


def pair_sum_kernel(idx, one, two, out):
    out[...] = (one[...].astype(WIDE) + two[...].astype(WIDE)).astype(out.dtype)


def triple_out_kernel(idx, got, weight, bias, *vectors):
    slab = weight.shape[1]
    total = 0.0
    for spot in range(NZ * 2):
        at = spot * HEAD_DIM
        here = got[spot].astype(WIDE)
        for part, lane in enumerate(LANES):
            weight[part, :, at : at + HEAD_DIM] = here[:slab, lane : lane + HEAD_DIM]
            bias[part : part + 1, at : at + HEAD_DIM] = here[slab : slab + 1, lane : lane + HEAD_DIM]
        total = total + here[slab:]
    row = 1
    for out in vectors:
        for i in range(0, out.shape[0], 2):
            out[i : i + 1, :] = total[row : row + 1, :PAIR]
            out[i + 1 : i + 2, :] = total[row : row + 1, PAIR:]
            row += 1


def tokens_kernel(idx, got, weight, part, group):
    for h in range(NZ * 2):
        for p, lane in enumerate(LANES):
            at = (p * NZ * 2 + h) * HEAD_DIM
            group[:, at : at + HEAD_DIM] = got[h, :, lane : lane + HEAD_DIM]
    part[...] = dot_nt(group[...], weight[...]).astype(LOW)


def tokens_sum_kernel(idx, own, other, grad, out):
    out[...] = grad[...] + pair(own, other)


def shards(
    tokens,
    query_vecs,
    out_cotangent,
    doc_lengths,
    live_mask,
    positives,
    triple_weight,
    triple_bias,
    output_weight,
    output_bias,
    first_gain,
    first_shift,
    expand_weight,
    expand_bias,
    contract_weight,
    contract_bias,
    second_gain,
    second_shift,
    head_weight,
):
    outer = lax.axis_size("o")
    mo, mz, mx, mc, my = [lax.axis_index(a) for a in ("o", "z", "x", "c", "y")]
    index = jnp.stack([mo, mz, mx, mc, my]).astype(jnp.int32)
    rows, width = tokens.shape
    half = rows // 2
    slab = triple_weight.shape[0]
    docs = doc_lengths.shape[0]
    queries_count = positives.shape[0]
    blocks = outer * NZ * 4
    span = expand_weight.shape[1]
    quarter = span // 2
    proj = head_weight.shape[1]
    line = lambda vector: vector.reshape(1, -1)

    def widen(value):
        return lax.all_gather(value, "o") if outer > 1 else value[None]

    def narrow(value):
        return lax.psum_scatter(value, "o") if outer > 1 else value[0]

    def sum_outer(value):
        return lax.psum(value, "o") if outer > 1 else value

    def stage(work):
        like = jax.eval_shape(work)
        idle = lambda: jax.tree.map(lambda leaf: jnp.zeros(leaf.shape, leaf.dtype), like)
        return lax.cond(doc_lengths[0] >= 0, work, idle)

    def key_doc(live, c):
        block = jnp.arange(outer * NZ * 2, dtype=jnp.int32) * 2 + c
        doc = doc_layout(doc_lengths, block[:, None] + where[None, :])[0]
        return jnp.where(live > 0, doc, -1)

    def head_weights(heads, heads_other):
        if outer > 1:
            pack = widen(both(heads, heads_other, mc)).transpose(0, 2, 1, 3, 4)
            head_triple = pack[..., :slab, :].reshape(width, QUAD)
            outs = pack[..., slab + 16 :, :].reshape(-1, 2, slab, QUAD).transpose(0, 2, 1, 3)
            outs = (outs.reshape(width, 2 * QUAD),)
            live0, live1 = [
                pick(pack, c, 2)[..., slab, :rows].astype(WIDE).reshape(-1, rows)
                for c in (mc, 1 - mc)
            ]
        else:
            outs = (heads, heads_other)
            head_triple, live0, live1 = whole(
                heads_kernel,
                "heads",
                index,
                (heads, heads_other),
                [shape((width, QUAD), LOW)] + [shape((NZ * 2, rows), WIDE)] * 2,
            )
        return head_triple, key_doc(live0, mc), key_doc(live1, 1 - mc), outs

    half_tokens = lax.dynamic_slice_in_dim(tokens, my * half, half, 0)
    by_z = [half_tokens] + [xor_z(half_tokens, m) for m in (1, 2, 3)]
    own_other = flip(tokens, "x")

    heads, low_slab, triple_slab = whole(
        prep_kernel,
        "prep",
        index,
        (
            triple_weight.transpose(1, 0, 2),
            output_weight.T,
            expand_weight,
            contract_weight.T,
            line(live_mask),
        ),
        [shape((NZ * 2, 3 * slab + 16, QUAD), LOW)]
        + [shape((slab, n), LOW) for n in (2 * span, 6 * QUAD)],
    )

    where = jnp.arange(rows, dtype=jnp.int32) * blocks
    rank = jnp.arange(NZ * 2, dtype=jnp.int32) * 2
    shares = query_vecs.shape[0] // (NZ * 4)
    by_z = list(lax.optimization_barrier((*by_z, heads, own_other))[:NZ])
    by_x = [flip(piece, "x") for piece in by_z[1:]]
    gathered = lax.all_gather(after(low_slab, *by_z[1:]), BLK, axis=0, tiled=True)

    def tables_stage():
        own_places = (mo * NZ * 4 + rank + mc)[:, None] + where[None, :]
        own_doc, own_position = doc_layout(doc_lengths, own_places.reshape(-1))
        lane = jnp.arange(PAIR) % (HEAD_DIM // 2)
        exponent = (2 * lane).astype(WIDE) / HEAD_DIM
        angles = own_position.astype(WIDE)[:, None] * jnp.exp(-math.log(10000.0) * exponent)[None, :]
        sign = jnp.where(jnp.arange(PAIR) % HEAD_DIM < HEAD_DIM // 2, -1.0, 1.0).astype(WIDE)
        tables = jnp.cos(angles), jnp.sin(angles) * sign[None, :]
        units = whole(
            query_kernel,
            "query_units",
            index,
            (after(query_vecs, by_z[1]),),
            [shape(query_vecs.shape, LOW), shape((shares, proj), LOW)],
        )
        positive = line(jnp.repeat(positives, query_vecs.shape[0] // queries_count))
        return tables, list(units), positive, own_doc.reshape(NZ, 2, 2, half, 1)

    (cosine, sine), (query_unit, own_queries), positive, qdoc = stage(tables_stage)
    positive, qdoc = lax.optimization_barrier((positive, qdoc))
    by_x = list(lax.optimization_barrier((*by_x, cosine))[:3])

    sheets = [tokens, own_other]
    for piece, turned in zip(by_z[1:], by_x):
        two = jnp.stack([piece, turned])
        sheets += [two, flip(two, "y")]

    def head_stage():
        got = lax.all_to_all(after(heads, sheets[2], sheets[4], sheets[6]), ("z", "x"), 0, 0)
        return head_weights(got, flip(got, "c"))

    head_triple, kdoc0, kdoc1, outs = stage(head_stage)
    pieces = len(outs)
    sheets = list(lax.optimization_barrier((*sheets, head_triple))[: len(sheets)])

    count = NZ * 2 * rows

    def project_stage():
        queries, kv = whole(
            project_kernel,
            "project",
            index,
            (*sheets, head_triple, cosine, sine, triple_bias),
            [shape((count, PAIR), LOW)] * 2,
        )
        return queries, kv, flip(kv, "c")

    queries, kv, kv_other = stage(project_stage)
    kv0, kv1 = [widen(v).reshape(-1, PAIR) for v in (kv, kv_other)]
    meta = (qdoc, kdoc0, kdoc1)

    def to_blocks(value):
        return lax.all_to_all(value.reshape((NZ * 2,) + value.shape[-2:]), ("z", "x"), 0, 0)

    def attention_stage():
        out, log_total, pack = attend(queries, kv0, kv1, *meta)
        return out, log_total, to_blocks(pack)

    out, log_total, pack = stage(attention_stage)
    wide_rows, low_rows, thin_rows = [shape((rows, n), t) for n, t in ((width, WIDE), (width, LOW), (1, WIDE))]
    def branch_stage():
        low, part = whole(
            partial(branch_kernel, pieces),
            "branch",
            index,
            (pack,),
            [shape((rows, 2 * QUAD), LOW), low_rows],
            piece_scratch(width, 2 * QUAD),
            outs,
        )
        return low, part, flip(part, "y")

    attended_low, part, part_other = stage(branch_stage)
    gathered = after(gathered, part)
    both_slabs = slab_scratch(width, span) * 2
    triple_low = lax.all_gather(after(triple_slab, part), BLK, axis=0, tiled=True)
    few = rows * QUAD // width
    first, unitary1, inverse1, hidden_in, keep, send, part = whole(
        forward_kernel,
        "forward",
        index,
        (
            part, part_other, tokens, line(output_bias), line(first_gain), line(first_shift),
            line(expand_bias), attended_low,
        ),
        [wide_rows, wide_rows, thin_rows, shape((rows, span), WIDE)]
        + [shape((2 * rows + few, width), LOW)] * 2
        + [low_rows],
        [pltpu.VMEM((rows, width), LOW), pltpu.VMEM((rows, span), LOW)] + both_slabs,
        (gathered,),
    )

    def over_z(parts):
        return [parts[0]] + [xor_z(parts[m], m) for m in (1, 2, 3)]

    def four_cores(keep, send):
        two = [keep, flip(send, "x")]
        return two + [flip(value, "c") for value in two]

    first_keep, first_other, first_across = keep, flip(send, "x"), flip(keep, "c")
    my_tokens = query_unit.shape[0]

    def second_stage():
        return whole(
            second_kernel,
            "second",
            index,
            (
                part, flip(part, "y"), first, line(contract_bias), line(second_gain),
                line(second_shift), head_weight, query_unit, kdoc0,
            ),
            [low_rows, wide_rows, thin_rows, shape((rows, proj), WIDE), shape((rows, proj), LOW)]
            + [shape((rows, my_tokens), WIDE), shape((docs, my_tokens), WIDE)],
        )

    second_low, unitary2, inverse2, embed, unit_low, expo, totals = stage(second_stage)
    firsts = [first_keep, first_other, first_across, flip(first_other, "c")]
    totals = after(totals, first_other, first_across)

    def tree(own, one, two, three):
        return (own + one) + (two + three)

    chunk = width // (NZ * 4)
    message = (NZ * 2, shares + 2 * chunk, proj)
    def middle_stage():
        sums = sum_outer(tree(totals, *[xor_s(totals, m) for m in (1, 2, 3)]))
        return whole(
            partial(middle_kernel, queries_count),
            "middle",
            index,
            (
                sums, *[xor_z(sums, m) for m in (1, 2, 3)], kdoc0, kdoc1, positive, expo, query_unit,
                unit_low, embed, second_low, head_weight, out_cotangent, unitary2, inverse2,
                line(second_gain), hidden_in,
            ),
            [wide_rows]
            + [shape((2 * rows, width), LOW)] * 2
            + [low_rows, shape((8, proj), WIDE), shape(message, WIDE), shape(message, LOW)],
            [
                pltpu.VMEM((rows, my_tokens), LOW),
                pltpu.VMEM((rows, width), LOW),
                pltpu.VMEM((rows, span), LOW),
                pltpu.VMEM((width, proj), WIDE),
                pltpu.VMEM((NZ * 4 * 16, proj), WIDE),
            ]
            + both_slabs,
            (gathered,),
        )

    grad_second_in, keep, send, part, loss, *query_parts = stage(middle_stage)

    keep_other, keep_across = flip(send, "x"), flip(keep, "c")
    message_other = flip(query_parts[1], "c")

    def first_stage():
        return whole(
            partial(first_back_kernel, pieces),
            "first_back",
            index,
            (part, flip(part, "y"), grad_second_in, unitary1, inverse1, line(first_gain)),
            [wide_rows, low_rows, shape((8, width), WIDE), shape((NZ * 2, half, PAIR), LOW)],
            piece_scratch(width, 2 * QUAD),
            outs,
        )

    grad_first_in, grad_branch, vectors1, pack = stage(first_stage)
    keep_other, message_other = lax.optimization_barrier((keep_other, message_other, grad_branch))[:2]
    grads = [keep, keep_other, keep_across, flip(keep_other, "c")]
    pack = whole(
        core_sum_kernel,
        "query_c",
        index,
        (pack, query_parts[0], message_other),
        [shape((NZ * 2, half + message[1], proj), LOW)],
    )[0]

    dims, dims_out = (2, slab, quarter), (2, slab, QUAD)
    dims_both = (2, slab, quarter + QUAD)
    left_right = [pltpu.VMEM((4 * rows, width), LOW)]

    def parts_of(left, right):
        part = dot_tn(jnp.concatenate(left), jnp.concatenate(right))
        part = pick(narrow(part.reshape(outer, NZ, 2, 2, slab, -1)), mc, 2)
        for axis, spot in ((0, mz), (1, mx)):
            part = jnp.take(part, jnp.arange(part.shape[axis]) ^ spot, axis=axis)
        return part

    def low_parts(parts):
        return [parts[0]] + [parts[m].astype(LOW) for m in (1, 2, 3)]

    def weights_stage():
        got = to_blocks(pack)
        got = got, flip(grad_branch, "x"), flip(grad_branch, "c")
        if outer == 1:
            parts = whole(
                weights_kernel,
                "weights",
                index,
                (*firsts, *grads),
                ([shape(dims, WIDE)] + [shape(dims, LOW)] * 3) * 2,
                left_right * 2,
            )
            return got, list(parts)
        top, mid = slice(0, rows), slice(rows, 2 * rows)
        contract = parts_of([g[top] for g in grads], [f[mid] for f in firsts])
        expand = parts_of([f[top] for f in firsts], [g[mid] for g in grads])
        return got, low_parts(contract) + low_parts(expand)

    (grad_out, branch_other, branch_across), weight_parts = stage(weights_stage)
    contract_parts, expand_parts = weight_parts[:4], weight_parts[4:]
    mine = whole(
        partial(query_back_kernel, half),
        "query_back",
        index,
        (sum_outer(grad_out), own_queries),
        [shape(message[1:], LOW)],
    )[0]
    spread = lax.all_gather(mine, ("z", "x", "c"))
    contract_in = over_z([mine, *lax.optimization_barrier((*contract_parts[1:], mine))[:3]])[1:]

    def attend_stage():
        grad_query, dkv0, dkv1 = attend_back(
            queries, grad_out.reshape(NZ, 2, -1, PAIR), out, log_total, kv0, kv1, *meta
        )
        dkv0, dkv1 = [narrow(v.reshape(outer, -1, PAIR)) for v in (dkv0, dkv1)]
        triple = whole(
            triple_kernel,
            "triple",
            index,
            (grad_query.reshape(count, PAIR), dkv0, flip(dkv1, "c"), cosine, sine),
            [shape((count, QUAD), LOW)],
        )[0]
        return triple, flip(branch_other, "c")

    grad_triple, branch_last = stage(attend_stage)
    branches = [grad_branch, branch_other, branch_across, branch_last]
    grad_triple, *contract_in = lax.optimization_barrier((grad_triple, *contract_in))

    dims_triple = (NZ * 2, slab + 16, QUAD)
    vector = shape((width // PAIR, PAIR), WIDE)

    def triple_parts():
        if outer == 1:
            return whole(
                triple_weight_kernel,
                "triple_weight",
                index,
                (*sheets, grad_triple, vectors1),
                [shape(dims_triple, LOW)] * 2,
                [pltpu.VMEM((width, QUAD), WIDE)],
            )
        ordered = [(mz * 2 + (mx ^ x), sheets[x]) for x in range(2)]
        for m in (1, 2, 3):
            two = both(*sheets[2 * m : 2 * m + 2], my)
            for x in range(2):
                ordered.append(((mz ^ m) * 2 + (mx ^ x), two[:, x].reshape(rows, width)))
        ordered = place(ordered).reshape(count, width)
        part = narrow(dot_tn(ordered, grad_triple).reshape(outer, NZ * 2, 2, slab, QUAD))
        bias = sum_outer(jnp.sum(grad_triple, axis=0, dtype=WIDE))
        bias = extra_rows(line(bias), sum_outer(vectors1))
        bias = jnp.broadcast_to(bias, (NZ * 2, 2, 16, QUAD))
        part = jnp.concatenate([part, bias], axis=2).astype(LOW)
        return pick(part, mc, 1), pick(part, 1 - mc, 1)

    def output_parts_of():
        if outer == 1:
            return whole(
                output_kernel,
                "output",
                index,
                (*firsts, *branches, *expand_parts[1:]),
                [shape(dims_out, WIDE)] + [shape(dims_both, LOW)] * 3,
                left_right + [pltpu.VMEM((4 * rows, QUAD), LOW)],
            )
        wide = [f[2 * rows :].reshape(few, 4, QUAD).transpose(1, 0, 2).reshape(rows, QUAD) for f in firsts]
        parts = low_parts(parts_of(branches, wide))
        return parts[:1] + [jnp.concatenate(both, axis=-1) for both in zip(expand_parts[1:], parts[1:])]

    def triple_stage():
        block_triple = to_blocks(grad_triple.reshape(NZ * 2, rows, QUAD))
        keep, send = triple_parts()
        output_parts = output_parts_of()
        packed = whole(
            pair_sum_kernel, "pair_sum", index, (keep, flip(send, "c")), [shape(dims_triple, LOW)]
        )[0]
        return block_triple, packed, list(output_parts)

    block_triple, packed, output_parts = stage(triple_stage)
    both_in = over_z([expand_parts[0]] + list(output_parts[1:]))[1:]

    def tokens_stage():
        part = whole(
            tokens_kernel,
            "tokens",
            index,
            (block_triple, triple_low),
            [low_rows],
            [pltpu.VMEM((rows, 6 * QUAD), LOW)],
        )[0]
        return whole(
            tokens_sum_kernel, "tokens_sum", index, (part, flip(part, "y"), grad_first_in), [wide_rows]
        )[0]

    tokens_grad = stage(tokens_stage)
    triple_grad, triple_bias_grad, output_bias_grad, gain_one, shift_one = whole(
        triple_out_kernel,
        "triple_out",
        index,
        (lax.all_to_all(after(packed, tokens_grad), ("z", "x"), 0, 0),),
        [shape((3, slab, 2 * QUAD), WIDE), shape((3, 2 * QUAD), WIDE)] + [vector] * 3,
    )
    contract_own, spread = after(contract_parts[0], tokens_grad), after(spread, tokens_grad)
    keep, keep_out, send = whole(
        line_sum_kernel,
        "line_sum",
        index,
        (contract_own, *contract_in, expand_parts[0], output_parts[0], *both_in),
        [shape((2, slab, quarter), WIDE), shape((slab, QUAD), WIDE), shape((slab, 2 * quarter + QUAD), LOW)],
    )
    contract_grad, expand_grad, output_grad = whole(
        columns_kernel,
        "columns",
        index,
        (keep, keep_out, flip(send, "x")),
        [shape((slab, n), WIDE) for n in (span, span, 2 * QUAD)],
    )
    queries_grad, head_grad, contract_bias_grad, gain_two, shift_two, expand_bias_grad = whole(
        spread_kernel,
        "spread",
        index,
        (spread.reshape(NZ * 4, *message[1:]),),
        [shape((query_vecs.shape[0], proj), WIDE), shape((width, proj), WIDE)]
        + [vector] * 3
        + [shape((span // PAIR, PAIR), WIDE)],
    )

    return (
        second_low,
        after(loss, tokens_grad)[0, 0],
        tokens_grad,
        queries_grad,
        triple_grad.transpose(1, 0, 2),
        triple_bias_grad,
        output_grad.T,
        output_bias_grad.reshape(-1),
        gain_one.reshape(-1),
        shift_one.reshape(-1),
        expand_grad,
        expand_bias_grad.reshape(-1),
        contract_grad.T,
        contract_bias_grad.reshape(-1),
        gain_two.reshape(-1),
        shift_two.reshape(-1),
        head_grad,
    )


def solution(mesh):
    outer = mesh.shape["blk"] // 16
    five = Mesh(mesh.devices.reshape(outer, NZ, 2, 2, mesh.shape["tensor"]), BLK + ("y",))
    blk, tensor = BLK, "y"
    return jax.shard_map(
        shards,
        mesh=five,
        in_specs=(
            P(blk, None),
            P(),
            P(blk, None),
            P(),
            P(blk),
            P(),
            P(blk, None, tensor),
            P(None, tensor),
            P(tensor, blk),
            P(),
            P(),
            P(),
            P(blk, tensor),
            P(tensor),
            P(tensor, blk),
            P(),
            P(),
            P(),
            P(),
        ),
        out_specs=(
            P(blk, None),
            P(),
            P(blk, None),
            P(),
            P(blk, None, tensor),
            P(None, tensor),
            P(tensor, blk),
            P(),
            P(),
            P(),
            P(blk, tensor),
            P(tensor),
            P(tensor, blk),
            P(),
            P(),
            P(),
            P(),
        ),
        check_vma=False,
    )
```

```python
from functools import partial
import math

import jax
import jax.numpy as jnp
import numpy as np
from jax import lax
from jax.experimental import pallas as pl
from jax.experimental.pallas import tpu as pltpu
from jax.sharding import Mesh, PartitionSpec as P

HEAD_DIM = 64
PAIR = 2 * HEAD_DIM

SOFTMAX_TEMPER = 0.05
FLOOR_SCORE = -1e30
NORM_EPSILON = 1e-05
UNIT_EPSILON = 1e-06
PRECISE = lax.Precision.HIGHEST
LOW = jnp.bfloat16
WIDE = jnp.float32

BLK = ("o", "z", "x", "c")
NZ = 4
FOUR = [0, 1, 2, 3]

VMEM_BYTES = 56 * 1024 * 1024
LANES = (0, 64, 192)
QUAD = 4 * HEAD_DIM


def xor_z(value, mask):
    return lax.ppermute(value, "z", [(i, i ^ mask) for i in FOUR])


def xor_s(value, mask):
    return lax.ppermute(value, ("x", "c"), [(i, i ^ mask) for i in FOUR])


def flip(value, axis):
    return lax.ppermute(value, axis, [(0, 1), (1, 0)])


def pick(value, index, axis=0):
    return lax.dynamic_index_in_dim(value, index, axis, keepdims=False)


def after(value, *others):
    return lax.optimization_barrier((value,) + others)[0]


def place(pieces):
    first = pieces[0][1]
    whole = jnp.zeros((len(pieces),) + first.shape, first.dtype)
    for index, piece in pieces:
        whole = lax.dynamic_update_slice_in_dim(whole, piece[None], index, 0)
    return whole


def both(mine, other, where):
    return place([(where, mine), (1 - where, other)])


def doc_layout(doc_lengths, places):
    ends = jnp.cumsum(doc_lengths)
    starts = ends - doc_lengths
    passed = starts <= places[..., None]
    doc_index = jnp.sum(passed.astype(jnp.int32), axis=-1) - 1
    begin = jnp.max(jnp.where(passed, starts, 0), axis=-1)
    return (doc_index, places - begin)


def dot_nn(a, b, precision=None):
    return lax.dot_general(
        a, b, (((1,), (0,)), ((), ())), precision=precision, preferred_element_type=WIDE
    )


def dot_nt(a, b, precision=None):
    return lax.dot_general(
        a, b, (((1,), (1,)), ((), ())), precision=precision, preferred_element_type=WIDE
    )


def dot_tn(a, b, precision=None):
    return lax.dot_general(
        a, b, (((0,), (0,)), ((), ())), precision=precision, preferred_element_type=WIDE
    )


def shape(dims, dtype):
    return jax.ShapeDtypeStruct(dims, dtype)


PARAMS = pltpu.CompilerParams(vmem_limit_bytes=VMEM_BYTES)

TAKES = dict(
    prep=2.5, heads=2.0, project=3.8, attend=7.5, branch=3.5, forward=7.7, second=3.6, middle=12.0, first_back=3.8, attend_back=9.8, triple=2.9, triple_weight=3.8, tokens=3.9,
    tokens_sum=2.1, weights=5.2, output=2.3, core_sum=3.9, line_sum=2.7, pair=2.0, columns=2.2, pair_sum=1.8,
    triple_out=1.9, query_units=2.8, query_back=3.5, spread=3.5,
)


SCALE = 1.0


def cost(name):
    took = TAKES[name] * SCALE
    return pl.CostEstimate(
        flops=int(took * 1.15e9), bytes_accessed=int(took * 3.7e6), transcendentals=0
    )


def whole(kernel, name, index, inputs, outputs, scratch=(), slabs=()):
    return pl.pallas_call(
        kernel,
        in_specs=[pl.BlockSpec(memory_space=pltpu.SMEM)]
        + [pl.BlockSpec(memory_space=pltpu.VMEM)] * len(inputs)
        + [pl.BlockSpec(memory_space=pl.ANY)] * len(slabs),
        out_specs=[pl.BlockSpec(memory_space=pltpu.VMEM)] * len(outputs),
        out_shape=list(outputs),
        scratch_shapes=list(scratch),
        compiler_params=PARAMS,
        cost_estimate=cost(name),
        name=name,
    )(index, *inputs, *slabs)


def slab_copy(slabs, at, weight, sems):
    there = slabs.at[:, pl.ds(at, weight.shape[1])]
    return pltpu.make_async_copy(there, weight, sems.at[0])


def piece_copies(idx, pieces, weight, sems):
    if len(pieces) == 1:
        return [pltpu.make_async_copy(pieces[0], weight, sems.at[0])]
    count, rows, cols = pieces[0].shape
    slab = (rows - 16) // 3
    copies = []
    for c, piece in enumerate(pieces):
        for spot in range(count):
            row = (spot * 2 + (idx[3] ^ c)) * slab
            for i in range(2):
                here = piece.at[spot, pl.ds((i + 1) * slab + 16, slab), :]
                there = weight.at[pl.ds(pl.multiple_of(row, slab), slab), pl.ds(i * cols, cols)]
                copies.append(pltpu.make_async_copy(here, there, sems.at[len(copies)]))
    return copies


def piece_scratch(rows, cols):
    return [pltpu.VMEM((rows, cols), LOW), pltpu.SemaphoreType.DMA((NZ * 8,))]


def slab_scratch(rows, cols):
    return [pltpu.VMEM((rows, cols), LOW), pltpu.SemaphoreType.DMA((1,))]


def start(copies):
    for copy in copies:
        copy.start()


def finish(copies, weight):
    for copy in copies:
        copy.wait()
    return weight[...]


def prep_kernel(idx, tw, ow, ew, cw, live, heads, low, tri):
    slab, span = ew.shape
    alive = jnp.broadcast_to(live[...], (16, live.shape[1])).astype(WIDE).astype(LOW)
    for spot in range(NZ * 2):
        at = spot * HEAD_DIM
        for part, lane in enumerate(LANES):
            heads[spot, :slab, lane : lane + HEAD_DIM] = tw[part, :, at : at + HEAD_DIM].astype(LOW)
        heads[spot, :slab, PAIR : PAIR + HEAD_DIM] = jnp.zeros((slab, HEAD_DIM), LOW)
        heads[spot, slab : slab + 16, : live.shape[1]] = alive
        heads[spot, slab : slab + 16, PAIR:] = jnp.zeros((16, PAIR), LOW)
        heads[spot, slab + 16 : 2 * slab + 16, :] = ow[:, :QUAD].astype(LOW)
        heads[spot, 2 * slab + 16 :, :] = ow[:, QUAD:].astype(LOW)
    low[:, :span] = ew[...].astype(LOW)
    low[:, span:] = cw[...].astype(LOW)
    for part in range(3):
        tri[:, part * 2 * QUAD : (part + 1) * 2 * QUAD] = tw[part].astype(LOW)


def heads_kernel(idx, own, other, weight, live0, live1):
    slab, mc = (own.shape[1] - 16) // 3, idx[3]
    for spot in range(NZ * 2):
        for source, c, live in ((own, mc, live0), (other, 1 - mc, live1)):
            rows = pl.ds(pl.multiple_of((spot * 2 + c) * slab, slab), slab)
            weight[rows, :] = source[spot, :slab, :]
            live[spot : spot + 1, :] = source[spot, slab : slab + 16, :PAIR].astype(WIDE)[:1]


def swap_halves(value):
    lane = lax.broadcasted_iota(jnp.int32, value.shape, 1)
    half = HEAD_DIM // 2
    return jnp.where(
        (lane & half) == 0,
        pltpu.roll(value, PAIR - half, 1),
        pltpu.roll(value, half, 1),
    )


def turn(value, cosine, sine):
    return value * cosine + swap_halves(value) * sine


def sheet_rows(idx, sheets):
    rows = sheets[0].shape[0]
    half = rows // 2
    parts = []
    for x in range(2):
        spot = idx[1] * 2 + (idx[2] ^ x)
        parts.append((sheets[x][...], pl.ds(pl.multiple_of(spot * rows, rows), rows)))
    for at, sheet in enumerate(sheets[2:]):
        z, y = at // 2 + 1, at % 2
        for x in range(2):
            spot = (idx[1] ^ z) * 2 + (idx[2] ^ x)
            row = spot * rows + (idx[4] ^ y) * half
            parts.append((sheet[x], pl.ds(pl.multiple_of(row, half), half)))
    return parts


def project_kernel(idx, *refs):
    sheets, (weight, cosine, sine, bias, query, kv) = refs[:8], refs[8:]
    parts = sheet_rows(idx, sheets)
    mz, mx = idx[1], idx[2]
    mine = mz * 2 + mx
    biases = []
    for part in range(3):
        total = jnp.zeros((1, HEAD_DIM), WIDE)
        for h in range(NZ * 2):
            here = bias[part : part + 1, h * HEAD_DIM : (h + 1) * HEAD_DIM]
            total = jnp.where(mine == h, here, total)
        biases.append(total)
    empty = jnp.zeros((1, HEAD_DIM), WIDE)
    offset = jnp.concatenate([biases[0], biases[1], empty, biases[2]], axis=1)
    weights = weight[...]
    for value, at in parts:
        low_lanes = lax.broadcasted_iota(jnp.int32, (value.shape[0], PAIR), 1) < HEAD_DIM
        triple = dot_nn(value, weights) + offset
        turned = turn(triple[:, :PAIR], cosine[at, :], sine[at, :])
        query[at, :] = jnp.where(low_lanes, turned, 0.0).astype(LOW)
        kv[at, :] = jnp.where(
            low_lanes, pltpu.roll(turned, HEAD_DIM, 1), triple[:, PAIR:]
        ).astype(LOW)


def key_row(ref):
    rows = ref[...]
    return jnp.concatenate([rows[i : i + 1] for i in range(rows.shape[0])], axis=1)


def attend_kernel(q_ref, kv0_ref, kv1_ref, qdoc_ref, kdoc0_ref, kdoc1_ref, out_ref, log_ref, pack_ref):
    scale = HEAD_DIM ** (-0.5)
    rows = q_ref.shape[3]
    queries = q_ref[0].reshape(4 * rows, PAIR)
    kv = (kv0_ref[...], kv1_ref[...])
    doc = qdoc_ref[0].reshape(4 * rows, 1)
    allowed = [doc == key_row(ref) for ref in (kdoc0_ref, kdoc1_ref)]
    scores = [
        jnp.where(ok, dot_nt(queries, keys) * scale, FLOOR_SCORE) for ok, keys in zip(allowed, kv)
    ]
    peak = jnp.maximum(*[jnp.max(s, axis=-1, keepdims=True) for s in scores])
    weights = [jnp.where(ok, jnp.exp(s - peak), 0.0) for ok, s in zip(allowed, scores)]
    total = sum(jnp.sum(w, axis=-1, keepdims=True) for w in weights)
    mixed = sum(dot_nn(w.astype(LOW), keys) for w, keys in zip(weights, kv)) / total
    out_ref[0] = mixed.reshape(2, 2, rows, PAIR)
    log_ref[0] = (peak + jnp.log(total)).reshape(2, 2, rows, 1)
    low_lanes = lax.broadcasted_iota(jnp.int32, (rows, PAIR), 1) < HEAD_DIM
    for x in range(2):
        upper = mixed[2 * x * rows : (2 * x + 1) * rows]
        lower = mixed[(2 * x + 1) * rows : (2 * x + 2) * rows]
        pack_ref[0, x] = jnp.where(low_lanes, pltpu.roll(upper, HEAD_DIM, 1), lower).astype(LOW)


def attend_specs(rows, keys, key_rows):
    half = rows // 2
    size = max(16, min(half, half * 2048 // (2 * keys)))
    full = lambda n, m: pl.BlockSpec((n, m), lambda i, j: (0, 0))
    part = lambda m: pl.BlockSpec((1, 2, 2, size, m), lambda i, j: (i, 0, 0, j, 0))
    pack = pl.BlockSpec((1, 2, size, PAIR), lambda i, j: (i, 0, j, 0))
    kv, docs = full(keys, PAIR), full(key_rows, rows)
    return (NZ, half // size), part, pack, kv, docs


def attend(queries, kv0, kv1, qdoc, kdoc0, kdoc1):
    rows = kdoc0.shape[1]
    half = rows // 2
    grid, part, pack, kv, docs = attend_specs(rows, kv0.shape[0], kdoc0.shape[0])
    return pl.pallas_call(
        attend_kernel,
        grid=grid,
        in_specs=[part(PAIR), kv, kv, part(1), docs, docs],
        out_specs=[part(PAIR), part(1), pack],
        out_shape=[
            shape((NZ, 2, 2, half, PAIR), WIDE),
            shape((NZ, 2, 2, half, 1), WIDE),
            shape((NZ, 2, half, PAIR), LOW),
        ],
        compiler_params=PARAMS,
        cost_estimate=cost("attend"),
        name="attend",
    )(queries.reshape(NZ, 2, 2, half, PAIR), kv0, kv1, qdoc, kdoc0, kdoc1)


def attend_back_kernel(
    q_ref, g_ref, o_ref, log_ref, kv0_ref, kv1_ref, qdoc_ref, kdoc0_ref, kdoc1_ref,
    dq_ref, dkv0_ref, dkv1_ref,
):
    scale = HEAD_DIM ** (-0.5)
    rows = q_ref.shape[3]

    @pl.when((pl.program_id(0) == 0) & (pl.program_id(1) == 0))
    def _():
        dkv0_ref[...] = jnp.zeros_like(dkv0_ref)
        dkv1_ref[...] = jnp.zeros_like(dkv1_ref)

    queries = q_ref[0].reshape(4 * rows, PAIR)
    high_lanes = lax.broadcasted_iota(jnp.int32, (rows, PAIR), 1) >= HEAD_DIM
    parts = []
    for x in range(2):
        packed = g_ref[0, x].astype(WIDE)
        parts.append(jnp.where(high_lanes, pltpu.roll(packed, HEAD_DIM, 1), 0.0))
        parts.append(jnp.where(high_lanes, packed, 0.0))
    wide = jnp.concatenate(parts, axis=0)
    grads = wide.astype(LOW)
    delta = jnp.sum(wide * o_ref[0].reshape(4 * rows, PAIR), axis=-1, keepdims=True)
    doc, log_total = qdoc_ref[0].reshape(4 * rows, 1), log_ref[0].reshape(4 * rows, 1)
    total = jnp.zeros((4 * rows, PAIR), WIDE)
    for kv_ref, kdoc_ref, dkv_ref in (
        (kv0_ref, kdoc0_ref, dkv0_ref),
        (kv1_ref, kdoc1_ref, dkv1_ref),
    ):
        keys = kv_ref[...]
        raw = dot_nt(queries, keys)
        probs = jnp.where(doc == key_row(kdoc_ref), jnp.exp(raw * scale - log_total), 0.0)
        dprobs = dot_nt(grads, keys)
        dscores = (probs * (dprobs - delta) * scale).astype(LOW)
        total = total + dot_nn(dscores, keys)
        dkv_ref[...] += dot_tn(dscores, queries) + dot_tn(probs.astype(LOW), grads)
    dq_ref[0] = total.reshape(2, 2, rows, PAIR)


def attend_back(queries, grads, out, log_total, kv0, kv1, qdoc, kdoc0, kdoc1):
    rows, keys = kdoc0.shape[1], kv0.shape[0]
    half = rows // 2
    grid, part, pack, kv, docs = attend_specs(rows, keys, kdoc0.shape[0])
    return pl.pallas_call(
        attend_back_kernel,
        grid=grid,
        in_specs=[part(PAIR), pack, part(PAIR), part(1), kv, kv, part(1), docs, docs],
        out_specs=[part(PAIR), kv, kv],
        out_shape=[
            shape((NZ, 2, 2, half, PAIR), WIDE),
            shape((keys, PAIR), WIDE),
            shape((keys, PAIR), WIDE),
        ],
        compiler_params=PARAMS,
        cost_estimate=cost("attend_back"),
        name="attend_back",
    )(queries.reshape(NZ, 2, 2, half, PAIR), grads, out, log_total, kv0, kv1, qdoc, kdoc0, kdoc1)


def branch_kernel(pieces, idx, got, *refs):
    slabs, (low, part, held, sems) = refs[:pieces], refs[pieces:]
    copy = piece_copies(idx, slabs, held, sems)
    start(copy)
    half = got.shape[1]
    for h in range(NZ * 2):
        lanes = slice(h * HEAD_DIM, (h + 1) * HEAD_DIM)
        low[:half, lanes] = got[h, :, :HEAD_DIM]
        low[half:, lanes] = got[h, :, HEAD_DIM:]
    part[...] = dot_nt(low[...], finish(copy, held)).astype(LOW)


def normalize(value):
    center = value - jnp.mean(value, axis=-1, keepdims=True)
    spread = jnp.mean(center * center, axis=-1, keepdims=True)
    inverse = lax.rsqrt(spread + NORM_EPSILON)
    return center * inverse, inverse


def pair(own, other):
    return own[...].astype(WIDE) + other[...].astype(WIDE)


def forward_kernel(
    idx, own, other, tokens, bias, gain, shift, hidden_bias, attended, slabs,
    first, unitary, inverse, hidden_in, keep, send, part,
    low, hidden, expand, sems1, contract, sems2,
):
    copy1 = [slab_copy(slabs, 0, expand, sems1)]
    copy2 = [slab_copy(slabs, expand.shape[1], contract, sems2)]
    start(copy1 + copy2)
    value = tokens[...].astype(WIDE) + (pair(own, other) + bias[...])
    unitary[...], inverse[...] = normalize(value)
    first[...] = unitary[...] * gain[...] + shift[...]
    low[...] = first[...].astype(LOW)
    value = dot_nn(low[...], finish(copy1, expand)) + hidden_bias[...]
    hidden_in[...] = value
    hidden[...] = (0.5 * value * (1.0 + lax.erf(value * (0.5**0.5)))).astype(LOW)
    part[...] = dot_nt(hidden[...], finish(copy2, contract)).astype(LOW)
    rows, width = low.shape
    few = rows * QUAD // width
    for out, x in ((keep, idx[2]), (send, 1 - idx[2])):
        out[:rows, :] = low[...]
        out[rows : 2 * rows, :] = columns_of(hidden, x, width)
        for i in range(width // QUAD):
            out[2 * rows :, i * QUAD : (i + 1) * QUAD] = attended[
                i * few : (i + 1) * few, pl.ds(pl.multiple_of(x * QUAD, QUAD), QUAD)
            ]


def columns_of(ref, x, span):
    return ref[:, pl.ds(pl.multiple_of(x * span, 128), span)]


def unit_scale(value):
    return lax.rsqrt(jnp.sum(value * value, axis=-1, keepdims=True) + UNIT_EPSILON)


def second_kernel(
    idx, own, other, first, bias, gain, shift, head, query, kdoc,
    low, unitary, inverse, embed, unit, expo, totals, message,
):
    value = first[...] + (pair(own, other) + bias[...])
    unitary[...], inverse[...] = normalize(value)
    low[...] = (unitary[...] * gain[...] + shift[...]).astype(LOW)
    embed[...] = dot_nn(low[...], head[...].astype(LOW))
    unit[...] = (embed[...] * unit_scale(embed[...])).astype(LOW)
    message[...] = unit[...].astype(WIDE)
    expo[...] = jnp.exp(dot_nt(unit[...], query[...]) / SOFTMAX_TEMPER)
    totals[...] = dot_nn(member(idx, kdoc, totals.shape[0]), expo[...], PRECISE)


def query_kernel(idx, vecs, out, own):
    block, shares = (idx[1] * 2 + idx[2]) * 2 + idx[3], own.shape[0]
    own[...] = vecs[pl.ds(pl.multiple_of(block * shares, shares), shares), :]
    value = vecs[...].astype(WIDE)
    out[...] = (value * unit_scale(value)).astype(LOW)


def member(idx, kdoc, docs):
    row = kdoc[pl.ds((idx[0] * NZ + idx[1]) * 2 + idx[2], 1), :]
    label = lax.broadcasted_iota(jnp.int32, (docs, row.shape[1]), 0)
    return jnp.where(row == label, 1.0, 0.0)


def group_sum(value, length):
    column = lax.broadcasted_iota(jnp.int32, value.shape, 1)
    span = value.shape[1]
    step = 1
    while step < length:
        ahead, behind = pltpu.roll(value, span - step, 1), pltpu.roll(value, step, 1)
        value = value + jnp.where((column & step) == 0, ahead, behind)
        step *= 2
    return value


def loss_of(count, totals, kdocs, positive):
    docs, columns = totals.shape
    length = columns // count
    label = lax.broadcasted_iota(jnp.int32, (docs, 1), 0)
    tokens = jnp.zeros((docs, 1), WIDE)
    for ref in kdocs:
        tokens = tokens + jnp.sum(jnp.where(key_row(ref) == label, 1.0, 0.0), axis=1, keepdims=True)
    doc_score = group_sum(SOFTMAX_TEMPER * (jnp.log(totals) - jnp.log(tokens)), length)
    best = jnp.max(doc_score, axis=0, keepdims=True)
    shifted = jnp.exp(doc_score - best)
    shifted_sum = jnp.sum(shifted, axis=0, keepdims=True)
    chosen = jnp.where(label == positive, 1.0, 0.0)
    each = best + jnp.log(shifted_sum) - jnp.sum(doc_score * chosen, axis=0, keepdims=True)
    loss = jnp.sum(each, axis=1, keepdims=True) / columns
    return loss, (shifted / shifted_sum - chosen) / (totals * count)


def unit_back(value, grad):
    scale = unit_scale(value)
    along = jnp.sum(grad * value, axis=-1, keepdims=True)
    return scale * grad - value * (along * scale * scale * scale)


def query_back_kernel(half, idx, kdoc0, kdoc1, coefficients, value, units, got, out):
    shares = value.shape[0]
    block = (idx[1] * 2 + idx[2]) * 2 + idx[3]
    columns_here = pl.ds(pl.multiple_of(block * shares, shares), shares)
    coefficient = coefficients[:, columns_here]
    docs = coefficient.shape[0]
    pads = jnp.zeros((-docs % 8, shares), WIDE)
    coefficient = jnp.transpose(jnp.concatenate([coefficient, pads]) if docs % 8 else coefficient)
    queries = value[...].astype(WIDE)
    query = (queries * unit_scale(queries)).astype(LOW)
    rows, group = kdoc0.shape[1], 4
    count = units.shape[0] // rows

    def add(at, total):
        labels = []
        for step in range(group):
            block = at * group + step
            spot = block // 2
            labels.append(
                jnp.where(block % 2 == idx[3], kdoc0[pl.ds(spot, 1), :], kdoc1[pl.ds(spot, 1), :])
            )
        row = jnp.concatenate(labels, axis=1)
        unit = units[pl.ds(at * group * rows, group * rows), :].astype(LOW)
        if docs <= 8:
            chosen = jnp.zeros((shares, group * rows), WIDE)
            for doc in range(docs):
                chosen = jnp.where(row == doc, coefficient[:, doc : doc + 1], chosen)
        else:
            label = lax.broadcasted_iota(jnp.int32, (coefficient.shape[1], group * rows), 0)
            chosen = dot_nn(coefficient, jnp.where(row == label, 1.0, 0.0), PRECISE)
        expo = jnp.exp(dot_nt(query, unit) / SOFTMAX_TEMPER)
        return total + dot_nn((chosen * expo).astype(LOW), unit)

    steps, total = count // group, jnp.zeros(queries.shape, WIDE)
    if steps <= 4:
        for at in range(steps):
            total = add(at, total)
    else:
        total = lax.fori_loop(0, steps, add, total)
    out[:shares, :] = unit_back(queries, total).astype(LOW)
    sums = [got[spot, half:, :].astype(WIDE) for spot in range(NZ * 2)]
    while len(sums) > 1:
        sums = [a + b for a, b in zip(sums[::2], sums[1::2])]
    out[shares:, :] = sums[0].astype(LOW)


def spread_kernel(idx, got, queries, head, *vectors):
    rows = got.shape[1]
    chunk = head.shape[0] // (NZ * 4)
    shares = rows - chunk - 16
    pieces = []
    for i in range(NZ * 4):
        queries[i * shares : (i + 1) * shares, :] = got[i, :shares, :].astype(WIDE)
        head[i * chunk : (i + 1) * chunk, :] = got[i, shares : shares + chunk, :].astype(WIDE)
        pieces.append(got[i, shares + chunk : shares + chunk + 16, :].astype(WIDE))
    row = 0
    for out in vectors:
        for i in range(0, out.shape[0], 8):
            out[i : i + 8, :] = pieces[row // 16][row % 16 : row % 16 + 8]
            row += 8


def norm_back(grad, gain, unitary, inverse):
    scaled = grad * gain
    along = jnp.mean(scaled * unitary, axis=-1, keepdims=True)
    return inverse * (scaled - jnp.mean(scaled, axis=-1, keepdims=True) - unitary * along)


def column_sum(value):
    return jnp.sum(value, axis=0, keepdims=True)


def middle_kernel(
    count, idx, t0, t1, t2, t3, kdoc0, kdoc1, positive, expo, query, unit,
    embed, low, head, cotangent, unitary, inverse, gain, hidden_in, slabs,
    grad_in, keep, send, part, loss, coefficients, sums0, sums1,
    similar, grad_low, grad_hidden_in, head_part, rows_part, expand, sems1, contract, sems2,
):
    copy1 = [slab_copy(slabs, 0, expand, sems1)]
    copy2 = [slab_copy(slabs, expand.shape[1], contract, sems2)]
    start(copy2 + copy1)
    totals = (t0[...] + t1[...]) + (t2[...] + t3[...])
    value, coefficient = loss_of(count, totals, (kdoc0, kdoc1), positive[...])
    loss[...] = jnp.broadcast_to(value, loss.shape)
    coefficients[...] = coefficient
    here = member(idx, kdoc0, totals.shape[0])
    similar[...] = (dot_tn(here, coefficient, PRECISE) * expo[...]).astype(LOW)
    grad_embed = unit_back(embed[...], dot_nn(similar[...], query[...])).astype(LOW)
    rows, width = embed.shape[0], low.shape[1]
    head_part[...] = dot_tn(low[...], grad_embed)
    grad_second = dot_nt(grad_embed, head[...].astype(LOW)) + cotangent[...].astype(WIDE)
    grad_in[...] = norm_back(grad_second, gain[...], unitary[...], inverse[...])
    grad_low[...] = grad_in[...].astype(LOW)
    sums = [
        column_sum(grad_low[...].astype(WIDE)),
        column_sum(grad_second * unitary[...]),
        column_sum(grad_second),
    ]
    value = hidden_in[...]
    grad = dot_nn(grad_low[...], finish(copy2, contract))
    bell = jnp.exp(-0.5 * value * value) * (1.0 / math.sqrt(2.0 * math.pi))
    slope = 0.5 * (1.0 + lax.erf(value * (0.5**0.5))) + value * bell
    grad_hidden_in[...] = (slope * grad).astype(LOW)
    sums.append(column_sum(grad_hidden_in[...].astype(WIDE)))
    part[...] = dot_nt(grad_hidden_in[...], finish(copy1, expand)).astype(LOW)
    for out, x in ((keep, idx[2]), (send, 1 - idx[2])):
        out[:rows, :] = grad_low[...]
        out[rows:, :] = columns_of(grad_hidden_in, x, width)
    rows_part[...] = jnp.zeros_like(rows_part)
    at = 0
    for value in sums:
        for i in range(value.shape[1] // PAIR):
            rows_part[at : at + 1, :] = value[:, i * PAIR : (i + 1) * PAIR]
            at += 1
    chunk = width // (NZ * 4)
    for spot in range(NZ * 2):
        for out, c in ((sums0, idx[3]), (sums1, 1 - idx[3])):
            at = spot * 2 + c
            out[spot, :chunk, :] = head_part[
                pl.ds(pl.multiple_of(at * chunk, chunk), chunk), :
            ].astype(out.dtype)
            out[spot, chunk:, :] = rows_part[pl.ds(pl.multiple_of(at * 16, 16), 16), :].astype(
                out.dtype
            )


def slab_products(idx, left, right, outs):
    slab = outs[0].shape[-2]
    for z, out in enumerate(outs):
        mine = []
        for x in range(2):
            spot = (idx[1] ^ z) * 2 + (idx[2] ^ x)
            lanes = left[:, pl.ds(pl.multiple_of(spot * 2 * slab, 2 * slab), 2 * slab)]
            mine.append(jnp.where(idx[3] == 0, lanes[:, :slab], lanes[:, slab:]))
        both_rows = dot_tn(jnp.concatenate(mine, axis=1), right)
        for x in range(2):
            out[x] = both_rows[x * slab : (x + 1) * slab].astype(out.dtype)


def weights_kernel(idx, f0, f1, f2, f3, g0, g1, g2, g3, *refs):
    keep0, send0, keep1, send1, left, right = refs
    rows = g0.shape[0] // 2
    firsts, grads = (f0, f1, f2, f3), (g0, g1, g2, g3)
    for keep, send, lefts, rights in ((keep0, send0, grads, firsts), (keep1, send1, firsts, grads)):
        for i in range(4):
            left[i * rows : (i + 1) * rows, :] = lefts[i][:rows, :]
            right[i * rows : (i + 1) * rows, :] = rights[i][rows : 2 * rows, :]
        slab_products(idx, left, right[...], [keep.at[0], send.at[0], keep.at[1], send.at[1]])


def pair_kernel(idx, *refs):
    count = (len(refs) - 1) // 3
    gots, owns, send, at = refs[: 2 * count], refs[2 * count : -1], refs[-1], 0
    for i, own in enumerate(owns):
        keep, got, span = gots[2 * i], gots[2 * i + 1], own.shape[-1]
        own[...] = keep[0] + got[0].astype(WIDE)
        send[:, :, at : at + span] = (keep[1] + got[1].astype(WIDE)).astype(LOW)
        at += span


def output_kernel(idx, f0, f1, f2, f3, g0, g1, g2, g3, keep, send, left, right):
    rows, width = g0.shape
    few = rows * QUAD // width
    for i, (f, g) in enumerate(zip((f0, f1, f2, f3), (g0, g1, g2, g3))):
        left[i * rows : (i + 1) * rows, :] = g[...]
        for j in range(width // QUAD):
            right[i * rows + j * few : i * rows + (j + 1) * few, :] = f[
                2 * rows :, j * QUAD : (j + 1) * QUAD
            ]
    slab_products(idx, left, right[...], [keep.at[0], send.at[0], keep.at[1], send.at[1]])


def line_sum_kernel(idx, own0, got0, own1, own2, got, keep, keep_out, send):
    at = 0
    for own, other, out in (
        (own0, got0[...], keep.at[0]),
        (own1, got[:, :, : own1.shape[-1]], keep.at[1]),
        (own2, got[:, :, own1.shape[-1] :], keep_out),
    ):
        span = own.shape[-1]
        out[...] = own[0] + other[0].astype(WIDE)
        send[:, at : at + span] = (own[1] + other[1].astype(WIDE)).astype(LOW)
        at += span


def columns_kernel(idx, keep, keep_out, got, contract, expand, output):
    span = keep.shape[-1]
    for at, mine, out in ((0, keep[0], contract), (span, keep[1], expand), (2 * span, keep_out[...], output)):
        cols = mine.shape[1]
        out[:, pl.ds(pl.multiple_of(idx[2] * cols, 128), cols)] = mine
        out[:, pl.ds(pl.multiple_of((1 - idx[2]) * cols, 128), cols)] = got[
            :, at : at + cols
        ].astype(WIDE)


def first_back_kernel(
    pieces, idx, own, other, grad_second_in, unitary, inverse, gain, sums0, sums1, *refs
):
    slabs, (grad_in, grad_low, vectors, pack, held, sems) = refs[:pieces], refs[pieces:]
    copy = piece_copies(idx, slabs, held, sems)
    start(copy)
    grad_first = grad_second_in[...] + pair(own, other)
    grad_in[...] = norm_back(grad_first, gain[...], unitary[...], inverse[...])
    grad_low[...] = grad_in[...].astype(LOW)
    vectors[...] = jnp.zeros_like(vectors)
    vectors[0:1, :] = column_sum(grad_low[...].astype(WIDE))
    vectors[1:2, :] = column_sum(grad_first * unitary[...])
    vectors[2:3, :] = column_sum(grad_first)
    grad = dot_nn(grad_low[...], finish(copy, held)).astype(LOW)
    half = grad.shape[0] // 2
    for h in range(NZ * 2):
        lanes = slice(h * HEAD_DIM, (h + 1) * HEAD_DIM)
        pack[h, :half, :HEAD_DIM] = grad[:half, lanes]
        pack[h, :half, HEAD_DIM:] = grad[half:, lanes]
        pack[h, half:, :] = (sums0[h] + sums1[h].astype(WIDE)).astype(LOW)


def triple_kernel(idx, dq, dkv, got, cosine, sine, out):
    rows = dq.shape[0]
    low_lanes = lax.broadcasted_iota(jnp.int32, (rows, PAIR), 1) < HEAD_DIM
    grads = dkv[...] + got[...]
    both_parts = jnp.where(low_lanes, dq[...], pltpu.roll(grads, HEAD_DIM, 1))
    turned = turn(both_parts, cosine[...], -sine[...])
    out[:, :PAIR] = turned.astype(LOW)
    out[:, PAIR:] = jnp.where(low_lanes, 0.0, grads).astype(LOW)


def extra_rows(bias, vectors):
    cols = bias.shape[1]
    rows = [bias]
    for i in range(3):
        for j in range(vectors.shape[1] // cols):
            rows.append(vectors[i : i + 1, j * cols : (j + 1) * cols])
    return jnp.concatenate(rows + [jnp.zeros((16 - len(rows), cols), WIDE)], axis=0)


def triple_weight_kernel(idx, *refs):
    sheets, (grad, vectors, keep, send, total) = refs[:8], refs[8:]
    mc = idx[3]
    slab = keep.shape[1] - 16
    for i, (value, at) in enumerate(sheet_rows(idx, sheets)):
        part = dot_tn(value, grad[at, :])
        if i == 0:
            total[...] = part
        else:
            total[...] += part
    extra = extra_rows(column_sum(grad[...].astype(WIDE)), vectors).astype(LOW)
    for spot in range(NZ * 2):
        for out, c in ((keep, mc), (send, 1 - mc)):
            at = pl.ds(pl.multiple_of((spot * 2 + c) * slab, slab), slab)
            out[spot, :slab, :] = total[at, :].astype(LOW)
            out[spot, slab:, :] = extra


def pair_sum_kernel(idx, one, two, out):
    out[...] = (one[...].astype(WIDE) + two[...].astype(WIDE)).astype(out.dtype)


def triple_out_kernel(idx, got, weight, bias, *vectors):
    slab = weight.shape[1]
    total = 0.0
    for spot in range(NZ * 2):
        at = spot * HEAD_DIM
        here = got[spot].astype(WIDE)
        for part, lane in enumerate(LANES):
            weight[part, :, at : at + HEAD_DIM] = here[:slab, lane : lane + HEAD_DIM]
            bias[part : part + 1, at : at + HEAD_DIM] = here[slab : slab + 1, lane : lane + HEAD_DIM]
        total = total + here[slab:]
    row = 1
    for out in vectors:
        for i in range(0, out.shape[0], 2):
            out[i : i + 1, :] = total[row : row + 1, :PAIR]
            out[i + 1 : i + 2, :] = total[row : row + 1, PAIR:]
            row += 1


def tokens_kernel(idx, got, message, part, group, held, sems):
    copy = slab_copy(message, 0, held, sems)
    copy.start()
    for h in range(NZ * 2):
        for p, lane in enumerate(LANES):
            at = (p * NZ * 2 + h) * HEAD_DIM
            group[:, at : at + HEAD_DIM] = got[h, :, lane : lane + HEAD_DIM]
    copy.wait()
    part[...] = dot_nt(group[...], held[...]).astype(LOW)


def tokens_sum_kernel(idx, own, other, grad, out):
    out[...] = grad[...] + pair(own, other)


def shards(
    tokens,
    query_vecs,
    out_cotangent,
    doc_lengths,
    live_mask,
    positives,
    triple_weight,
    triple_bias,
    output_weight,
    output_bias,
    first_gain,
    first_shift,
    expand_weight,
    expand_bias,
    contract_weight,
    contract_bias,
    second_gain,
    second_shift,
    head_weight,
):
    outer = lax.axis_size("o")
    mo, mz, mx, mc, my = [lax.axis_index(a) for a in ("o", "z", "x", "c", "y")]
    index = jnp.stack([mo, mz, mx, mc, my]).astype(jnp.int32)
    rows, width = tokens.shape
    half = rows // 2
    slab = triple_weight.shape[0]
    docs = doc_lengths.shape[0]
    queries_count = positives.shape[0]
    blocks = outer * NZ * 4
    span = expand_weight.shape[1]
    quarter = span // 2
    proj = head_weight.shape[1]
    line = lambda vector: vector.reshape(1, -1)

    def widen(value):
        return lax.all_gather(value, "o") if outer > 1 else value[None]

    def narrow(value):
        return lax.psum_scatter(value, "o") if outer > 1 else value[0]

    def sum_outer(value):
        return lax.psum(value, "o") if outer > 1 else value

    def stage(work):
        like = jax.eval_shape(work)
        idle = lambda: jax.tree.map(lambda leaf: jnp.zeros(leaf.shape, leaf.dtype), like)
        return lax.cond(doc_lengths[0] >= 0, work, idle)

    def key_doc(live, c):
        block = jnp.arange(outer * NZ * 2, dtype=jnp.int32) * 2 + c
        doc = doc_layout(doc_lengths, block[:, None] + where[None, :])[0]
        return jnp.where(live > 0, doc, -1)

    def head_weights(heads, heads_other):
        if outer > 1:
            pack = widen(both(heads, heads_other, mc)).transpose(0, 2, 1, 3, 4)
            head_triple = pack[..., :slab, :].reshape(width, QUAD)
            outs = pack[..., slab + 16 :, :].reshape(-1, 2, slab, QUAD).transpose(0, 2, 1, 3)
            outs = (outs.reshape(width, 2 * QUAD),)
            live0, live1 = [
                pick(pack, c, 2)[..., slab, :rows].astype(WIDE).reshape(-1, rows)
                for c in (mc, 1 - mc)
            ]
        else:
            outs = (heads, heads_other)
            head_triple, live0, live1 = whole(
                heads_kernel,
                "heads",
                index,
                (heads, heads_other),
                [shape((width, QUAD), LOW)] + [shape((NZ * 2, rows), WIDE)] * 2,
            )
        return head_triple, key_doc(live0, mc), key_doc(live1, 1 - mc), outs

    half_tokens = lax.dynamic_slice_in_dim(tokens, my * half, half, 0)
    by_z = [half_tokens] + [xor_z(half_tokens, m) for m in (1, 2, 3)]
    own_other = flip(tokens, "x")

    heads, low_slab, triple_slab = whole(
        prep_kernel,
        "prep",
        index,
        (
            triple_weight.transpose(1, 0, 2),
            output_weight.T,
            expand_weight,
            contract_weight.T,
            line(live_mask),
        ),
        [shape((NZ * 2, 3 * slab + 16, QUAD), LOW)]
        + [shape((slab, n), LOW) for n in (2 * span, 6 * QUAD)],
    )

    where = jnp.arange(rows, dtype=jnp.int32) * blocks
    rank = jnp.arange(NZ * 2, dtype=jnp.int32) * 2
    shares = query_vecs.shape[0] // (NZ * 4)
    by_z = list(lax.optimization_barrier((*by_z, heads, own_other))[:NZ])
    gathered = lax.all_gather(after(low_slab, *by_z[1:]), BLK, axis=0, tiled=True)

    def heads_stage():
        got = lax.all_to_all(heads, ("z", "x"), 0, 0)
        sheets = [tokens, own_other]
        for piece in by_z[1:]:
            two = jnp.stack([piece, flip(piece, "x")])
            sheets += [two, flip(two, "y")]
        own_places = (mo * NZ * 4 + rank + mc)[:, None] + where[None, :]
        own_doc, own_position = doc_layout(doc_lengths, own_places.reshape(-1))
        lane = jnp.arange(PAIR) % (HEAD_DIM // 2)
        exponent = (2 * lane).astype(WIDE) / HEAD_DIM
        angles = own_position.astype(WIDE)[:, None] * jnp.exp(-math.log(10000.0) * exponent)[None, :]
        sign = jnp.where(jnp.arange(PAIR) % HEAD_DIM < HEAD_DIM // 2, -1.0, 1.0).astype(WIDE)
        tables = jnp.cos(angles), jnp.sin(angles) * sign[None, :]
        units = whole(
            query_kernel,
            "query_units",
            index,
            (query_vecs,),
            [shape(query_vecs.shape, LOW), shape((shares, proj), LOW)],
        )
        positive = line(jnp.repeat(positives, query_vecs.shape[0] // queries_count))
        got = after(got, sheets[3], sheets[5], sheets[7], tables[0], units[0])
        head = head_weights(got, flip(got, "c"))
        return head, sheets[2:], tables, list(units), positive, own_doc.reshape(NZ, 2, 2, half, 1)

    head, sheets, (cosine, sine), (query_unit, own_queries), positive, qdoc = stage(heads_stage)
    head_triple, kdoc0, kdoc1, outs = head
    pieces = len(outs)
    sheets = [tokens, own_other] + sheets
    positive, qdoc = lax.optimization_barrier((positive, qdoc))
    count = NZ * 2 * rows

    def project_stage():
        queries, kv = whole(
            project_kernel,
            "project",
            index,
            (*sheets, head_triple, cosine, sine, triple_bias),
            [shape((count, PAIR), LOW)] * 2,
        )
        return queries, kv, flip(kv, "c")

    queries, kv, kv_other = stage(project_stage)
    kv0, kv1 = [widen(v).reshape(-1, PAIR) for v in (kv, kv_other)]
    meta = (qdoc, kdoc0, kdoc1)

    def to_blocks(value):
        return lax.all_to_all(value.reshape((NZ * 2,) + value.shape[-2:]), ("z", "x"), 0, 0)

    def attention_stage():
        out, log_total, pack = attend(queries, kv0, kv1, *meta)
        return out, log_total, to_blocks(pack)

    out, log_total, pack = stage(attention_stage)
    wide_rows, low_rows, thin_rows = [shape((rows, n), t) for n, t in ((width, WIDE), (width, LOW), (1, WIDE))]
    def branch_stage():
        low, part = whole(
            partial(branch_kernel, pieces),
            "branch",
            index,
            (pack,),
            [shape((rows, 2 * QUAD), LOW), low_rows],
            piece_scratch(width, 2 * QUAD),
            outs,
        )
        return low, part, flip(part, "y")

    attended_low, part, part_other = stage(branch_stage)
    gathered = after(gathered, part)
    both_slabs = slab_scratch(width, span) * 2
    triple_low = lax.all_gather(after(triple_slab, part), BLK, axis=0, tiled=True)
    few = rows * QUAD // width
    first, unitary1, inverse1, hidden_in, keep, send, part = whole(
        forward_kernel,
        "forward",
        index,
        (
            part, part_other, tokens, line(output_bias), line(first_gain), line(first_shift),
            line(expand_bias), attended_low,
        ),
        [wide_rows, wide_rows, thin_rows, shape((rows, span), WIDE)]
        + [shape((2 * rows + few, width), LOW)] * 2
        + [low_rows],
        [pltpu.VMEM((rows, width), LOW), pltpu.VMEM((rows, span), LOW)] + both_slabs,
        (gathered,),
    )

    def over_z(parts):
        return [parts[0]] + [xor_z(parts[m], m) for m in (1, 2, 3)]

    def four_cores(keep, send):
        two = [keep, flip(send, "x")]
        return two + [flip(value, "c") for value in two]

    first_keep, first_other, first_across = keep, flip(send, "x"), flip(keep, "c")
    my_tokens = query_unit.shape[0]

    def second_stage():
        return whole(
            second_kernel,
            "second",
            index,
            (
                part, flip(part, "y"), first, line(contract_bias), line(second_gain),
                line(second_shift), head_weight, query_unit, kdoc0,
            ),
            [low_rows, wide_rows, thin_rows] + [shape((rows, proj), t) for t in (WIDE, LOW)]
            + [shape((rows, my_tokens), WIDE), shape((docs, my_tokens), WIDE)]
            + [shape((rows, proj), WIDE)],
        )

    second_low, unitary2, inverse2, embed, unit_low, expo, totals, message = stage(second_stage)
    firsts = [first_keep, first_other, first_across, flip(first_other, "c")]
    totals = after(totals, first_other, first_across)

    def tree(own, one, two, three):
        return (own + one) + (two + three)

    chunk = width // (NZ * 4)
    sums_dims = (NZ * 2, chunk + 16, proj)
    def middle_stage():
        sums = sum_outer(tree(totals, *[xor_s(totals, m) for m in (1, 2, 3)]))
        return whole(
            partial(middle_kernel, queries_count),
            "middle",
            index,
            (
                sums, *[xor_z(sums, m) for m in (1, 2, 3)], kdoc0, kdoc1, positive, expo, query_unit,
                unit_low, embed, second_low, head_weight, out_cotangent, unitary2, inverse2,
                line(second_gain), hidden_in,
            ),
            [wide_rows]
            + [shape((2 * rows, width), LOW)] * 2
            + [low_rows, shape((8, proj), WIDE), shape((docs, my_tokens), WIDE)]
            + [shape(sums_dims, WIDE), shape(sums_dims, LOW)],
            [
                pltpu.VMEM((rows, my_tokens), LOW),
                pltpu.VMEM((rows, width), LOW),
                pltpu.VMEM((rows, span), LOW),
                pltpu.VMEM((width, proj), WIDE),
                pltpu.VMEM((NZ * 4 * 16, proj), WIDE),
            ]
            + both_slabs,
            (gathered,),
        )

    grad_second_in, keep, send, part, loss, coefficients, sums_own, sums_send = stage(middle_stage)

    triple_low, part = lax.optimization_barrier((triple_low, part))
    units = lax.all_gather(after(message, part), BLK, axis=0, tiled=True)
    keep_other, keep_across = flip(send, "x"), flip(keep, "c")

    def first_stage():
        return whole(
            partial(first_back_kernel, pieces),
            "first_back",
            index,
            (
                part, flip(part, "y"), grad_second_in, unitary1, inverse1, line(first_gain),
                sums_own, flip(sums_send, "c"),
            ),
            [wide_rows, low_rows, shape((8, width), WIDE)]
            + [shape((NZ * 2, half + chunk + 16, PAIR), LOW)],
            piece_scratch(width, 2 * QUAD),
            outs,
        )

    grad_first_in, grad_branch, vectors1, pack = stage(first_stage)
    keep_other = after(keep_other, grad_branch)
    grads = [keep, keep_other, keep_across, flip(keep_other, "c")]
    dims, dims_out = (2, slab, quarter), (2, slab, QUAD)
    dims_both = (2, slab, quarter + QUAD)
    left_right = [pltpu.VMEM((4 * rows, width), LOW)]

    def parts_of(left, right):
        part = dot_tn(jnp.concatenate(left), jnp.concatenate(right))
        part = pick(narrow(part.reshape(outer, NZ, 2, 2, slab, -1)), mc, 2)
        for axis, spot in ((0, mz), (1, mx)):
            part = jnp.take(part, jnp.arange(part.shape[axis]) ^ spot, axis=axis)
        return part

    def low_parts(parts):
        return [parts[0]] + [parts[m].astype(LOW) for m in (1, 2, 3)]

    def weights_stage():
        got = to_blocks(pack)
        other = flip(grad_branch, "x")
        got = got, [grad_branch, other, flip(grad_branch, "c"), flip(other, "c")]
        if outer == 1:
            parts = whole(
                weights_kernel,
                "weights",
                index,
                (*firsts, *grads),
                [shape((2,) + dims, WIDE), shape((2,) + dims, LOW)] * 2,
                left_right * 2,
            )
            return got, list(parts)
        top, mid = slice(0, rows), slice(rows, 2 * rows)
        contract = parts_of([g[top] for g in grads], [f[mid] for f in firsts])
        expand = parts_of([f[top] for f in firsts], [g[mid] for g in grads])
        return got, [part for p in (contract, expand) for part in (p[::2], p[1::2].astype(LOW))]

    (grad_out, branches), weight_parts = stage(weights_stage)
    contract_keep, contract_send, expand_keep, expand_send = weight_parts
    contract_got, expand_got = xor_z(contract_send, 1), xor_z(expand_send, 1)

    def attend_stage():
        grad_query, dkv0, dkv1 = attend_back(
            queries, grad_out.reshape(NZ, 2, -1, PAIR), out, log_total, kv0, kv1, *meta
        )
        dkv0, dkv1 = [narrow(v.reshape(outer, -1, PAIR)) for v in (dkv0, dkv1)]
        triple = whole(
            triple_kernel,
            "triple",
            index,
            (grad_query.reshape(count, PAIR), dkv0, flip(dkv1, "c"), cosine, sine),
            [shape((count, QUAD), LOW)],
        )[0]
        mine = whole(
            partial(query_back_kernel, half),
            "query_back",
            index,
            (kdoc0, kdoc1, coefficients, own_queries, units, sum_outer(grad_out)),
            [shape((shares + chunk + 16, proj), LOW)],
        )[0]
        return triple, mine

    grad_triple, mine = stage(attend_stage)
    grad_triple, contract_got = lax.optimization_barrier((grad_triple, contract_got))
    contract_own, contract_send = whole(
        pair_kernel, "pair", index, (contract_keep, contract_got), [shape(dims, t) for t in (WIDE, LOW)]
    )
    contract_got = xor_z(contract_send, 2)
    grad_triple = after(grad_triple, contract_own)
    dims_triple = (NZ * 2, slab + 16, QUAD)
    vector = shape((width // PAIR, PAIR), WIDE)

    def triple_parts():
        if outer == 1:
            return whole(
                triple_weight_kernel,
                "triple_weight",
                index,
                (*sheets, grad_triple, vectors1),
                [shape(dims_triple, LOW)] * 2,
                [pltpu.VMEM((width, QUAD), WIDE)],
            )
        ordered = [(mz * 2 + (mx ^ x), sheets[x]) for x in range(2)]
        for m in (1, 2, 3):
            two = both(*sheets[2 * m : 2 * m + 2], my)
            for x in range(2):
                ordered.append(((mz ^ m) * 2 + (mx ^ x), two[:, x].reshape(rows, width)))
        ordered = place(ordered).reshape(count, width)
        part = narrow(dot_tn(ordered, grad_triple).reshape(outer, NZ * 2, 2, slab, QUAD))
        bias = sum_outer(jnp.sum(grad_triple, axis=0, dtype=WIDE))
        bias = extra_rows(line(bias), sum_outer(vectors1))
        bias = jnp.broadcast_to(bias, (NZ * 2, 2, 16, QUAD))
        part = jnp.concatenate([part, bias], axis=2).astype(LOW)
        return pick(part, mc, 1), pick(part, 1 - mc, 1)

    def output_parts_of():
        if outer == 1:
            return whole(
                output_kernel,
                "output",
                index,
                (*firsts, *branches),
                [shape((2,) + dims_out, t) for t in (WIDE, LOW)],
                left_right + [pltpu.VMEM((4 * rows, QUAD), LOW)],
            )
        wide = [f[2 * rows :].reshape(few, 4, QUAD).transpose(1, 0, 2).reshape(rows, QUAD) for f in firsts]
        parts = parts_of(branches, wide)
        return parts[::2], parts[1::2].astype(LOW)

    def triple_stage():
        block_triple = to_blocks(grad_triple.reshape(NZ * 2, rows, QUAD))
        keep, send = triple_parts()
        output_parts = output_parts_of()
        packed = whole(
            pair_sum_kernel, "pair_sum", index, (keep, flip(send, "c")), [shape(dims_triple, LOW)]
        )[0]
        return block_triple, packed, output_parts[0], xor_z(output_parts[1], 1)

    block_triple, packed, output_keep, output_got = stage(triple_stage)
    block_triple, contract_got, expand_got = lax.optimization_barrier(
        (block_triple, contract_got, expand_got)
    )
    expand_own, output_own, both_send = whole(
        pair_kernel,
        "pair",
        index,
        (expand_keep, expand_got, output_keep, output_got),
        [shape(dims, WIDE), shape(dims_out, WIDE), shape(dims_both, LOW)],
    )
    both_got = xor_z(both_send, 2)
    block_triple = after(block_triple, expand_own)
    spread = lax.all_gather(after(mine, expand_own), ("z", "x", "c"))

    def tokens_stage():
        part = whole(
            tokens_kernel,
            "tokens",
            index,
            (block_triple,),
            [low_rows],
            [pltpu.VMEM((rows, 6 * QUAD), LOW)] + slab_scratch(width, 6 * QUAD),
            (triple_low,),
        )[0]
        tokens_grad = whole(
            tokens_sum_kernel, "tokens_sum", index, (part, flip(part, "y"), grad_first_in), [wide_rows]
        )[0]
        return tokens_grad, lax.all_to_all(after(packed, part), ("z", "x"), 0, 0)

    tokens_grad, packed = stage(tokens_stage)
    contract_own, spread = after(contract_own, tokens_grad), after(spread, tokens_grad)
    keep, keep_out, send = whole(
        line_sum_kernel,
        "line_sum",
        index,
        (contract_own, contract_got, expand_own, output_own, both_got),
        [shape((2, slab, quarter), WIDE), shape((slab, QUAD), WIDE), shape((slab, 2 * quarter + QUAD), LOW)],
    )
    queries_grad, head_grad, contract_bias_grad, gain_two, shift_two, expand_bias_grad = whole(
        spread_kernel,
        "spread",
        index,
        (spread.reshape(NZ * 4, -1, proj),),
        [shape((query_vecs.shape[0], proj), WIDE), shape((width, proj), WIDE)]
        + [vector] * 3
        + [shape((span // PAIR, PAIR), WIDE)],
    )
    triple_grad, triple_bias_grad, output_bias_grad, gain_one, shift_one = whole(
        triple_out_kernel,
        "triple_out",
        index,
        (after(packed, send),),
        [shape((3, slab, 2 * QUAD), WIDE), shape((3, 2 * QUAD), WIDE)] + [vector] * 3,
    )
    contract_grad, expand_grad, output_grad = whole(
        columns_kernel,
        "columns",
        index,
        (keep, keep_out, after(flip(send, "x"), queries_grad)),
        [shape((slab, n), WIDE) for n in (span, span, 2 * QUAD)],
    )

    return (
        second_low,
        after(loss, tokens_grad)[0, 0],
        tokens_grad,
        queries_grad,
        triple_grad.transpose(1, 0, 2),
        triple_bias_grad,
        output_grad.T,
        output_bias_grad.reshape(-1),
        gain_one.reshape(-1),
        shift_one.reshape(-1),
        expand_grad,
        expand_bias_grad.reshape(-1),
        contract_grad.T,
        contract_bias_grad.reshape(-1),
        gain_two.reshape(-1),
        shift_two.reshape(-1),
        head_grad,
    )


def solution(mesh):
    outer = mesh.shape["blk"] // 16
    five = Mesh(mesh.devices.reshape(outer, NZ, 2, 2, mesh.shape["tensor"]), BLK + ("y",))
    blk, tensor = BLK, "y"
    return jax.shard_map(
        shards,
        mesh=five,
        in_specs=(
            P(blk, None),
            P(),
            P(blk, None),
            P(),
            P(blk),
            P(),
            P(blk, None, tensor),
            P(None, tensor),
            P(tensor, blk),
            P(),
            P(),
            P(),
            P(blk, tensor),
            P(tensor),
            P(tensor, blk),
            P(),
            P(),
            P(),
            P(),
        ),
        out_specs=(
            P(blk, None),
            P(),
            P(blk, None),
            P(),
            P(blk, None, tensor),
            P(None, tensor),
            P(tensor, blk),
            P(),
            P(),
            P(),
            P(blk, tensor),
            P(tensor),
            P(tensor, blk),
            P(),
            P(),
            P(),
            P(),
        ),
        check_vma=False,
    )
```

```python
from functools import partial
import math

import jax
import jax.numpy as jnp
import numpy as np
from jax import lax
from jax.experimental import pallas as pl
from jax.experimental.pallas import tpu as pltpu
from jax.sharding import Mesh, PartitionSpec as P

HEAD_DIM = 64
PAIR = 2 * HEAD_DIM

SOFTMAX_TEMPER = 0.05
FLOOR_SCORE = -1e30
NORM_EPSILON = 1e-05
UNIT_EPSILON = 1e-06
PRECISE = lax.Precision.HIGHEST
LOW = jnp.bfloat16
WIDE = jnp.float32

BLK = ("o", "z", "x", "c")
NZ = 4
FOUR = [0, 1, 2, 3]

VMEM_BYTES = 56 * 1024 * 1024
LANES = (0, 64, 192)
QUAD = 4 * HEAD_DIM


def xor_z(value, mask):
    return lax.ppermute(value, "z", [(i, i ^ mask) for i in FOUR])


def xor_s(value, mask):
    return lax.ppermute(value, ("x", "c"), [(i, i ^ mask) for i in FOUR])


def flip(value, axis):
    return lax.ppermute(value, axis, [(0, 1), (1, 0)])


def pick(value, index, axis=0):
    return lax.dynamic_index_in_dim(value, index, axis, keepdims=False)


def after(value, *others):
    return lax.optimization_barrier((value,) + others)[0]


def place(pieces):
    first = pieces[0][1]
    whole = jnp.zeros((len(pieces),) + first.shape, first.dtype)
    for index, piece in pieces:
        whole = lax.dynamic_update_slice_in_dim(whole, piece[None], index, 0)
    return whole


def both(mine, other, where):
    return place([(where, mine), (1 - where, other)])


def doc_layout(doc_lengths, places):
    ends = jnp.cumsum(doc_lengths)
    starts = ends - doc_lengths
    passed = starts <= places[..., None]
    doc_index = jnp.sum(passed.astype(jnp.int32), axis=-1) - 1
    begin = jnp.max(jnp.where(passed, starts, 0), axis=-1)
    return (doc_index, places - begin)


def dot_nn(a, b, precision=None):
    return lax.dot_general(
        a, b, (((1,), (0,)), ((), ())), precision=precision, preferred_element_type=WIDE
    )


def dot_nt(a, b, precision=None):
    return lax.dot_general(
        a, b, (((1,), (1,)), ((), ())), precision=precision, preferred_element_type=WIDE
    )


def dot_tn(a, b, precision=None):
    return lax.dot_general(
        a, b, (((0,), (0,)), ((), ())), precision=precision, preferred_element_type=WIDE
    )


def shape(dims, dtype):
    return jax.ShapeDtypeStruct(dims, dtype)


PARAMS = pltpu.CompilerParams(vmem_limit_bytes=VMEM_BYTES)

TAKES = dict(
    prep=2.5, heads=2.0, project=3.8, attend=7.5, branch=3.5, forward=7.7, second=3.6, middle=12.0, first_back=3.8, attend_back=9.8, triple=2.9, triple_weight=3.8, tokens=3.9,
    tokens_sum=2.1, weights=5.2, output=2.3, core_sum=3.9, line_sum=2.7, pair=2.0, columns=2.2, pair_sum=1.8,
    triple_out=1.9, query_units=2.8, query_back=3.5, spread=3.5,
)


SCALE = 1.0


def cost(name):
    took = TAKES[name] * SCALE
    return pl.CostEstimate(
        flops=int(took * 1.15e9), bytes_accessed=int(took * 3.7e6), transcendentals=0
    )


def whole(kernel, name, index, inputs, outputs, scratch=(), slabs=()):
    return pl.pallas_call(
        kernel,
        in_specs=[pl.BlockSpec(memory_space=pltpu.SMEM)]
        + [pl.BlockSpec(memory_space=pltpu.VMEM)] * len(inputs)
        + [pl.BlockSpec(memory_space=pl.ANY)] * len(slabs),
        out_specs=[pl.BlockSpec(memory_space=pltpu.VMEM)] * len(outputs),
        out_shape=list(outputs),
        scratch_shapes=list(scratch),
        compiler_params=PARAMS,
        cost_estimate=cost(name),
        name=name,
    )(index, *inputs, *slabs)


def slab_copy(slabs, at, weight, sems):
    there = slabs.at[:, pl.ds(at, weight.shape[1])]
    return pltpu.make_async_copy(there, weight, sems.at[0])


def piece_copies(idx, pieces, weight, sems):
    if len(pieces) == 1:
        return [pltpu.make_async_copy(pieces[0], weight, sems.at[0])]
    count, rows, cols = pieces[0].shape
    slab = HEAD_DIM
    behind = slab + extra_count(slab)
    copies = []
    for c, piece in enumerate(pieces):
        for spot in range(count):
            row = (spot * 2 + (idx[3] ^ c)) * slab
            for i in range(2):
                here = piece.at[spot, pl.ds(behind + i * slab, slab), :]
                there = weight.at[pl.ds(pl.multiple_of(row, slab), slab), pl.ds(i * cols, cols)]
                copies.append(pltpu.make_async_copy(here, there, sems.at[len(copies)]))
    return copies


def piece_scratch(rows, cols):
    return [pltpu.VMEM((rows, cols), LOW), pltpu.SemaphoreType.DMA((NZ * 8,))]


def slab_scratch(rows, cols):
    return [pltpu.VMEM((rows, cols), LOW), pltpu.SemaphoreType.DMA((1,))]


def start(copies):
    for copy in copies:
        copy.start()


def finish(copies, weight):
    for copy in copies:
        copy.wait()
    return weight[...]


def extra_count(slab):
    return 0 if slab >= HEAD_DIM else 16


def put_extra(message, slab, extra):
    if extra_count(slab):
        message[slab : slab + 16, :] = extra
        return
    for i in range(4):
        message[i * 16 : (i + 1) * 16, PAIR : PAIR + HEAD_DIM] = extra[
            :, i * HEAD_DIM : (i + 1) * HEAD_DIM
        ]


def get_extra(message, slab):
    if extra_count(slab):
        return message[slab : slab + 16, :]
    lanes = slice(PAIR, PAIR + HEAD_DIM)
    return jnp.concatenate([message[i * 16 : (i + 1) * 16, lanes] for i in range(4)], axis=1)


def prep_kernel(idx, tw, ow, ew, cw, live, heads, low, tri):
    slab, span = ew.shape
    alive = jnp.broadcast_to(live[...], (16, live.shape[1])).astype(WIDE).astype(LOW)
    alive = jnp.concatenate([alive, jnp.zeros((16, QUAD - live.shape[1]), LOW)], axis=1)
    behind = slab + extra_count(slab)
    for spot in range(NZ * 2):
        at = spot * HEAD_DIM
        for part, lane in enumerate(LANES):
            heads[spot, :slab, lane : lane + HEAD_DIM] = tw[part, :, at : at + HEAD_DIM].astype(LOW)
        heads[spot, :slab, PAIR : PAIR + HEAD_DIM] = jnp.zeros((slab, HEAD_DIM), LOW)
        put_extra(heads.at[spot], slab, alive)
        heads[spot, behind : behind + slab, :] = ow[:, :QUAD].astype(LOW)
        heads[spot, behind + slab :, :] = ow[:, QUAD:].astype(LOW)
    low[:, :span] = ew[...].astype(LOW)
    low[:, span:] = cw[...].astype(LOW)
    for part in range(3):
        tri[:, part * 2 * QUAD : (part + 1) * 2 * QUAD] = tw[part].astype(LOW)


def heads_kernel(idx, own, other, weight, live0, live1):
    slab, mc = HEAD_DIM, idx[3]
    for spot in range(NZ * 2):
        for source, c, live in ((own, mc, live0), (other, 1 - mc, live1)):
            rows = pl.ds(pl.multiple_of((spot * 2 + c) * slab, slab), slab)
            weight[rows, :] = source[spot, :slab, :]
            live[spot : spot + 1, :] = get_extra(source.at[spot], slab)[:, :PAIR].astype(WIDE)[:1]


def swap_halves(value):
    lane = lax.broadcasted_iota(jnp.int32, value.shape, 1)
    half = HEAD_DIM // 2
    return jnp.where(
        (lane & half) == 0,
        pltpu.roll(value, PAIR - half, 1),
        pltpu.roll(value, half, 1),
    )


def turn(value, cosine, sine):
    return value * cosine + swap_halves(value) * sine


def sheet_rows(idx, sheets):
    rows = sheets[0].shape[0]
    half = rows // 2
    parts = []
    for x in range(2):
        spot = idx[1] * 2 + (idx[2] ^ x)
        parts.append((sheets[x][...], pl.ds(pl.multiple_of(spot * rows, rows), rows)))
    for at, sheet in enumerate(sheets[2:]):
        z, y = at // 2 + 1, at % 2
        for x in range(2):
            spot = (idx[1] ^ z) * 2 + (idx[2] ^ x)
            row = spot * rows + (idx[4] ^ y) * half
            parts.append((sheet[x], pl.ds(pl.multiple_of(row, half), half)))
    return parts


def project_kernel(idx, *refs):
    sheets, (weight, cosine, sine, bias, query, kv) = refs[:8], refs[8:]
    parts = sheet_rows(idx, sheets)
    mz, mx = idx[1], idx[2]
    mine = mz * 2 + mx
    biases = []
    for part in range(3):
        total = jnp.zeros((1, HEAD_DIM), WIDE)
        for h in range(NZ * 2):
            here = bias[part : part + 1, h * HEAD_DIM : (h + 1) * HEAD_DIM]
            total = jnp.where(mine == h, here, total)
        biases.append(total)
    empty = jnp.zeros((1, HEAD_DIM), WIDE)
    offset = jnp.concatenate([biases[0], biases[1], empty, biases[2]], axis=1)
    weights = weight[...]
    for value, at in parts:
        low_lanes = lax.broadcasted_iota(jnp.int32, (value.shape[0], PAIR), 1) < HEAD_DIM
        triple = dot_nn(value, weights) + offset
        turned = turn(triple[:, :PAIR], cosine[at, :], sine[at, :])
        query[at, :] = jnp.where(low_lanes, turned * HEAD_DIM ** (-0.5), 0.0).astype(LOW)
        kv[at, :] = jnp.where(
            low_lanes, pltpu.roll(turned, HEAD_DIM, 1), triple[:, PAIR:]
        ).astype(LOW)


def key_row(ref):
    rows = ref[...]
    return jnp.concatenate([rows[i : i + 1] for i in range(rows.shape[0])], axis=1)


def places_of(token, rows, half, blocks, idx, z, part):
    x, upper, row = token // (2 * rows), token // rows % 2, token % rows
    block = ((idx[0] * NZ + z) * 2 + x) * 2 + idx[3]
    return (upper * half + part * rows + row) * blocks + block


def docs_of(places, lens):
    doc, begin = jnp.full(places.shape, -1, jnp.int32), jnp.int32(0)
    for i in range(lens.shape[0]):
        doc = jnp.where(begin <= places, doc + 1, doc)
        begin = begin + lens[i]
    return doc


def as_row(column):
    count = column.shape[0]
    row = lax.broadcasted_iota(jnp.int32, (count, count), 0)
    same = row == lax.broadcasted_iota(jnp.int32, (count, count), 1)
    return jnp.sum(jnp.where(same, column, 0.0), axis=0, keepdims=True)


def attend_kernel(
    blocks, idx, lens, q_ref, kv0_ref, kv1_ref, kdoc0_ref, kdoc1_ref, out_ref, log_ref, pack_ref
):
    rows, half = q_ref.shape[3], kdoc0_ref.shape[1] // 2
    queries = q_ref[0].reshape(4 * rows, PAIR)
    kv = (kv0_ref[...], kv1_ref[...])
    token = lax.broadcasted_iota(jnp.int32, (4 * rows, 1), 0)
    z, part = pl.program_id(0), pl.program_id(1)
    doc = docs_of(places_of(token, rows, half, blocks, idx, z, part), lens)
    scores = [
        jnp.where(doc == key_row(ref), dot_nt(queries, keys), FLOOR_SCORE)
        for ref, keys in zip((kdoc0_ref, kdoc1_ref), kv)
    ]
    peak = jnp.maximum(*[jnp.max(s, axis=-1, keepdims=True) for s in scores])
    weights = [jnp.exp(s - peak) for s in scores]
    total = sum(jnp.sum(w, axis=-1, keepdims=True) for w in weights)
    mixed = sum(dot_nn(w.astype(LOW), keys) for w, keys in zip(weights, kv)) / total
    out_ref[0] = mixed.reshape(2, 2, rows, PAIR)
    log_ref[0, 0] = as_row(peak + jnp.log(total))
    low_lanes = lax.broadcasted_iota(jnp.int32, (rows, PAIR), 1) < HEAD_DIM
    for x in range(2):
        upper = mixed[2 * x * rows : (2 * x + 1) * rows]
        lower = mixed[(2 * x + 1) * rows : (2 * x + 2) * rows]
        pack_ref[0, x] = jnp.where(low_lanes, pltpu.roll(upper, HEAD_DIM, 1), lower).astype(LOW)


def attend_specs(rows, keys, key_rows):
    half = rows // 2
    size = max(16, min(half, half * 2048 // (2 * keys)))
    full = lambda n, m: pl.BlockSpec((n, m), lambda i, j: (0, 0))
    part = lambda m: pl.BlockSpec((1, 2, 2, size, m), lambda i, j: (i, 0, 0, j, 0))
    pack = pl.BlockSpec((1, 2, size, PAIR), lambda i, j: (i, 0, j, 0))
    logs = pl.BlockSpec((1, 1, 1, 4 * size), lambda i, j: (i, j, 0, 0))
    kv, docs = full(keys, PAIR), full(key_rows, rows)
    return (NZ, half // size), part, pack, logs, kv, docs


SCALARS = [pl.BlockSpec(memory_space=pltpu.SMEM)] * 2


def attend(blocks, index, lens, queries, kv0, kv1, kdoc0, kdoc1):
    rows = kdoc0.shape[1]
    half = rows // 2
    grid, part, pack, logs, kv, docs = attend_specs(rows, kv0.shape[0], kdoc0.shape[0])
    return pl.pallas_call(
        partial(attend_kernel, blocks),
        grid=grid,
        in_specs=SCALARS + [part(PAIR), kv, kv, docs, docs],
        out_specs=[part(PAIR), logs, pack],
        out_shape=[
            shape((NZ, 2, 2, half, PAIR), WIDE),
            shape((NZ, grid[1], 1, 4 * half // grid[1]), WIDE),
            shape((NZ, 2, half, PAIR), LOW),
        ],
        compiler_params=PARAMS,
        cost_estimate=cost("attend"),
        name="attend",
    )(index, lens, queries.reshape(NZ, 2, 2, half, PAIR), kv0, kv1, kdoc0, kdoc1)


def attend_back_kernel(
    blocks, idx, lens, q_ref, g_ref, o_ref, log_ref, kv0_ref, kv1_ref, kdoc0_ref, kdoc1_ref,
    dq_ref, dkv0_ref, dkv1_ref, column0, column1,
):
    rows, width = q_ref.shape[3], kdoc0_ref.shape[1]
    z, part = pl.program_id(0), pl.program_id(1)

    @pl.when((z == 0) & (part == 0))
    def _():
        dkv0_ref[...] = jnp.zeros_like(dkv0_ref)
        dkv1_ref[...] = jnp.zeros_like(dkv1_ref)
        for ref, column in ((kdoc0_ref, column0), (kdoc1_ref, column1)):
            turned = jnp.transpose(ref[...].astype(WIDE))
            for i in range(ref.shape[0]):
                column[i * width : (i + 1) * width, :] = turned[:, i : i + 1]

    queries = q_ref[0].reshape(4 * rows, PAIR)
    high_lanes = lax.broadcasted_iota(jnp.int32, (rows, PAIR), 1) >= HEAD_DIM
    parts = []
    for x in range(2):
        packed = g_ref[0, x].astype(WIDE)
        parts.append(jnp.where(high_lanes, pltpu.roll(packed, HEAD_DIM, 1), 0.0))
        parts.append(jnp.where(high_lanes, packed, 0.0))
    wide = jnp.concatenate(parts, axis=0)
    grads = wide.astype(LOW)
    delta = as_row(jnp.sum(wide * o_ref[0].reshape(4 * rows, PAIR), axis=-1, keepdims=True))
    token = lax.broadcasted_iota(jnp.int32, (1, 4 * rows), 1)
    doc = docs_of(places_of(token, rows, width // 2, blocks, idx, z, part), lens).astype(WIDE)
    log_total = log_ref[0, 0]
    total = jnp.zeros((4 * rows, PAIR), WIDE)
    for kv_ref, column, dkv_ref in ((kv0_ref, column0, dkv0_ref), (kv1_ref, column1, dkv1_ref)):
        keys = kv_ref[...]
        raw = dot_nt(keys, queries)
        probs = jnp.where(column[...] == doc, jnp.exp(raw - log_total), 0.0)
        dprobs = dot_nt(keys, grads)
        dscores = (probs * (dprobs - delta)).astype(LOW)
        total = total + dot_tn(dscores, keys)
        dkv_ref[...] += dot_nn(dscores, queries) + dot_nn(probs.astype(LOW), grads)
    dq_ref[0] = (total * HEAD_DIM ** (-0.5)).reshape(2, 2, rows, PAIR)


def attend_back(blocks, index, lens, queries, grads, out, log_total, kv0, kv1, kdoc0, kdoc1):
    rows, keys = kdoc0.shape[1], kv0.shape[0]
    half = rows // 2
    grid, part, pack, logs, kv, docs = attend_specs(rows, keys, kdoc0.shape[0])
    return pl.pallas_call(
        partial(attend_back_kernel, blocks),
        grid=grid,
        in_specs=SCALARS + [part(PAIR), pack, part(PAIR), logs, kv, kv, docs, docs],
        out_specs=[part(PAIR), kv, kv],
        out_shape=[
            shape((NZ, 2, 2, half, PAIR), WIDE),
            shape((keys, PAIR), WIDE),
            shape((keys, PAIR), WIDE),
        ],
        scratch_shapes=[pltpu.VMEM((keys, 1), WIDE)] * 2,
        compiler_params=PARAMS,
        cost_estimate=cost("attend_back"),
        name="attend_back",
    )(
        index, lens, queries.reshape(NZ, 2, 2, half, PAIR), grads, out, log_total, kv0, kv1,
        kdoc0, kdoc1,
    )


def branch_kernel(pieces, idx, got, *refs):
    slabs, (low, part, held, sems) = refs[:pieces], refs[pieces:]
    copy = piece_copies(idx, slabs, held, sems)
    start(copy)
    half = got.shape[1]
    for h in range(NZ * 2):
        lanes = slice(h * HEAD_DIM, (h + 1) * HEAD_DIM)
        low[:half, lanes] = got[h, :, :HEAD_DIM]
        low[half:, lanes] = got[h, :, HEAD_DIM:]
    part[...] = dot_nt(low[...], finish(copy, held)).astype(LOW)


def normalize(value):
    center = value - jnp.mean(value, axis=-1, keepdims=True)
    spread = jnp.mean(center * center, axis=-1, keepdims=True)
    inverse = lax.rsqrt(spread + NORM_EPSILON)
    return center * inverse, inverse


def pair(own, other):
    return own[...].astype(WIDE) + other[...].astype(WIDE)


def forward_kernel(
    idx, own, other, tokens, bias, gain, shift, hidden_bias, attended, slabs,
    first, unitary, inverse, hidden_in, keep, send, part,
    low, hidden, expand, sems1, contract, sems2,
):
    copy1 = [slab_copy(slabs, 0, expand, sems1)]
    copy2 = [slab_copy(slabs, expand.shape[1], contract, sems2)]
    start(copy1 + copy2)
    value = tokens[...].astype(WIDE) + (pair(own, other) + bias[...])
    unitary[...], inverse[...] = normalize(value)
    first[...] = unitary[...] * gain[...] + shift[...]
    low[...] = first[...].astype(LOW)
    value = dot_nn(low[...], finish(copy1, expand)) + hidden_bias[...]
    hidden_in[...] = value
    hidden[...] = (0.5 * value * (1.0 + lax.erf(value * (0.5**0.5)))).astype(LOW)
    part[...] = dot_nt(hidden[...], finish(copy2, contract)).astype(LOW)
    rows, width = low.shape
    few = rows * QUAD // width
    for out, x in ((keep, idx[2]), (send, 1 - idx[2])):
        out[:rows, :] = low[...]
        out[rows : 2 * rows, :] = columns_of(hidden, x, width)
        for i in range(width // QUAD):
            out[2 * rows :, i * QUAD : (i + 1) * QUAD] = attended[
                i * few : (i + 1) * few, pl.ds(pl.multiple_of(x * QUAD, QUAD), QUAD)
            ]


def columns_of(ref, x, span):
    return ref[:, pl.ds(pl.multiple_of(x * span, 128), span)]


def unit_scale(value):
    return lax.rsqrt(jnp.sum(value * value, axis=-1, keepdims=True) + UNIT_EPSILON)


def second_kernel(
    idx, own, other, first, bias, gain, shift, head, query, kdoc,
    low, unitary, inverse, embed, unit, expo, totals, message,
):
    value = first[...] + (pair(own, other) + bias[...])
    unitary[...], inverse[...] = normalize(value)
    low[...] = (unitary[...] * gain[...] + shift[...]).astype(LOW)
    embed[...] = dot_nn(low[...], head[...].astype(LOW))
    unit[...] = (embed[...] * unit_scale(embed[...])).astype(LOW)
    message[...] = unit[...].astype(WIDE)
    expo[...] = jnp.exp(dot_nt(unit[...], query[...]) / SOFTMAX_TEMPER)
    totals[...] = dot_nn(member(idx, kdoc, totals.shape[0]), expo[...], PRECISE)


def query_kernel(idx, vecs, out, own):
    block, shares = (idx[1] * 2 + idx[2]) * 2 + idx[3], own.shape[0]
    own[...] = vecs[pl.ds(pl.multiple_of(block * shares, shares), shares), :]
    value = vecs[...].astype(WIDE)
    out[...] = (value * unit_scale(value)).astype(LOW)


def member(idx, kdoc, docs):
    row = kdoc[pl.ds((idx[0] * NZ + idx[1]) * 2 + idx[2], 1), :]
    label = lax.broadcasted_iota(jnp.int32, (docs, row.shape[1]), 0)
    return jnp.where(row == label, 1.0, 0.0)


def group_sum(value, length):
    column = lax.broadcasted_iota(jnp.int32, value.shape, 1)
    span = value.shape[1]
    step = 1
    while step < length:
        ahead, behind = pltpu.roll(value, span - step, 1), pltpu.roll(value, step, 1)
        value = value + jnp.where((column & step) == 0, ahead, behind)
        step *= 2
    return value


def loss_of(count, totals, kdocs, positive):
    docs, columns = totals.shape
    length = columns // count
    label = lax.broadcasted_iota(jnp.int32, (docs, 1), 0)
    tokens = jnp.zeros((docs, 1), WIDE)
    for ref in kdocs:
        tokens = tokens + jnp.sum(jnp.where(key_row(ref) == label, 1.0, 0.0), axis=1, keepdims=True)
    doc_score = group_sum(SOFTMAX_TEMPER * (jnp.log(totals) - jnp.log(tokens)), length)
    best = jnp.max(doc_score, axis=0, keepdims=True)
    shifted = jnp.exp(doc_score - best)
    shifted_sum = jnp.sum(shifted, axis=0, keepdims=True)
    chosen = jnp.where(label == positive, 1.0, 0.0)
    each = best + jnp.log(shifted_sum) - jnp.sum(doc_score * chosen, axis=0, keepdims=True)
    loss = jnp.sum(each, axis=1, keepdims=True) / columns
    return loss, (shifted / shifted_sum - chosen) / (totals * count)


def unit_back(value, grad):
    scale = unit_scale(value)
    along = jnp.sum(grad * value, axis=-1, keepdims=True)
    return scale * grad - value * (along * scale * scale * scale)


def query_back_kernel(half, idx, kdoc0, kdoc1, coefficients, value, units, got, out):
    shares = value.shape[0]
    block = (idx[1] * 2 + idx[2]) * 2 + idx[3]
    columns_here = pl.ds(pl.multiple_of(block * shares, shares), shares)
    coefficient = coefficients[:, columns_here]
    docs = coefficient.shape[0]
    pads = jnp.zeros((-docs % 8, shares), WIDE)
    coefficient = jnp.transpose(jnp.concatenate([coefficient, pads]) if docs % 8 else coefficient)
    queries = value[...].astype(WIDE)
    query = (queries * unit_scale(queries)).astype(LOW)
    rows, group = kdoc0.shape[1], 4
    count = units.shape[0] // rows

    def add(at, total):
        labels = []
        for step in range(group):
            block = at * group + step
            spot = block // 2
            labels.append(
                jnp.where(block % 2 == idx[3], kdoc0[pl.ds(spot, 1), :], kdoc1[pl.ds(spot, 1), :])
            )
        row = jnp.concatenate(labels, axis=1)
        unit = units[pl.ds(at * group * rows, group * rows), :].astype(LOW)
        if docs <= 8:
            chosen = jnp.zeros((shares, group * rows), WIDE)
            for doc in range(docs):
                chosen = jnp.where(row == doc, coefficient[:, doc : doc + 1], chosen)
        else:
            label = lax.broadcasted_iota(jnp.int32, (coefficient.shape[1], group * rows), 0)
            chosen = dot_nn(coefficient, jnp.where(row == label, 1.0, 0.0), PRECISE)
        expo = jnp.exp(dot_nt(query, unit) / SOFTMAX_TEMPER)
        return total + dot_nn((chosen * expo).astype(LOW), unit)

    steps, total = count // group, jnp.zeros(queries.shape, WIDE)
    if steps <= 4:
        for at in range(steps):
            total = add(at, total)
    else:
        total = lax.fori_loop(0, steps, add, total)
    out[:shares, :] = unit_back(queries, total).astype(LOW)
    sums = [got[spot, half:, :].astype(WIDE) for spot in range(NZ * 2)]
    while len(sums) > 1:
        sums = [a + b for a, b in zip(sums[::2], sums[1::2])]
    out[shares:, :] = sums[0].astype(LOW)


def spread_kernel(idx, got, queries, head, *vectors):
    rows = got.shape[1]
    chunk = head.shape[0] // (NZ * 4)
    shares = rows - chunk - 16
    pieces = []
    for i in range(NZ * 4):
        queries[i * shares : (i + 1) * shares, :] = got[i, :shares, :].astype(WIDE)
        head[i * chunk : (i + 1) * chunk, :] = got[i, shares : shares + chunk, :].astype(WIDE)
        pieces.append(got[i, shares + chunk : shares + chunk + 16, :].astype(WIDE))
    row = 0
    for out in vectors:
        for i in range(0, out.shape[0], 8):
            out[i : i + 8, :] = pieces[row // 16][row % 16 : row % 16 + 8]
            row += 8


def norm_back(grad, gain, unitary, inverse):
    scaled = grad * gain
    along = jnp.mean(scaled * unitary, axis=-1, keepdims=True)
    return inverse * (scaled - jnp.mean(scaled, axis=-1, keepdims=True) - unitary * along)


def column_sum(value):
    return jnp.sum(value, axis=0, keepdims=True)


def middle_kernel(
    count, idx, t0, t1, t2, t3, kdoc0, kdoc1, positive, expo, query, unit,
    embed, low, head, cotangent, unitary, inverse, gain, hidden_in, slabs,
    grad_in, keep, send, part, loss, coefficients, sums0, sums1,
    similar, grad_low, grad_hidden_in, head_part, rows_part, expand, sems1, contract, sems2,
):
    copy1 = [slab_copy(slabs, 0, expand, sems1)]
    copy2 = [slab_copy(slabs, expand.shape[1], contract, sems2)]
    start(copy2 + copy1)
    totals = (t0[...] + t1[...]) + (t2[...] + t3[...])
    value, coefficient = loss_of(count, totals, (kdoc0, kdoc1), positive[...])
    loss[...] = jnp.broadcast_to(value, loss.shape)
    coefficients[...] = coefficient
    here = member(idx, kdoc0, totals.shape[0])
    similar[...] = (dot_tn(here, coefficient, PRECISE) * expo[...]).astype(LOW)
    grad_embed = unit_back(embed[...], dot_nn(similar[...], query[...])).astype(LOW)
    rows, width = embed.shape[0], low.shape[1]
    head_part[...] = dot_tn(low[...], grad_embed)
    grad_second = dot_nt(grad_embed, head[...].astype(LOW)) + cotangent[...].astype(WIDE)
    grad_in[...] = norm_back(grad_second, gain[...], unitary[...], inverse[...])
    grad_low[...] = grad_in[...].astype(LOW)
    sums = [
        column_sum(grad_low[...].astype(WIDE)),
        column_sum(grad_second * unitary[...]),
        column_sum(grad_second),
    ]
    value = hidden_in[...]
    grad = dot_nn(grad_low[...], finish(copy2, contract))
    bell = jnp.exp(-0.5 * value * value) * (1.0 / math.sqrt(2.0 * math.pi))
    slope = 0.5 * (1.0 + lax.erf(value * (0.5**0.5))) + value * bell
    grad_hidden_in[...] = (slope * grad).astype(LOW)
    sums.append(column_sum(grad_hidden_in[...].astype(WIDE)))
    part[...] = dot_nt(grad_hidden_in[...], finish(copy1, expand)).astype(LOW)
    for out, x in ((keep, idx[2]), (send, 1 - idx[2])):
        out[:rows, :] = grad_low[...]
        out[rows:, :] = columns_of(grad_hidden_in, x, width)
    rows_part[...] = jnp.zeros_like(rows_part)
    at = 0
    for value in sums:
        for i in range(value.shape[1] // PAIR):
            rows_part[at : at + 1, :] = value[:, i * PAIR : (i + 1) * PAIR]
            at += 1
    chunk = width // (NZ * 4)
    for spot in range(NZ * 2):
        for out, c in ((sums0, idx[3]), (sums1, 1 - idx[3])):
            at = spot * 2 + c
            out[spot, :chunk, :] = head_part[
                pl.ds(pl.multiple_of(at * chunk, chunk), chunk), :
            ].astype(out.dtype)
            out[spot, chunk:, :] = rows_part[pl.ds(pl.multiple_of(at * 16, 16), 16), :].astype(
                out.dtype
            )


def slab_products(idx, left, right, outs):
    slab = outs[0].shape[-2]
    for z, out in enumerate(outs):
        mine = []
        for x in range(2):
            spot = (idx[1] ^ z) * 2 + (idx[2] ^ x)
            lanes = left[:, pl.ds(pl.multiple_of(spot * 2 * slab, 2 * slab), 2 * slab)]
            mine.append(jnp.where(idx[3] == 0, lanes[:, :slab], lanes[:, slab:]))
        both_rows = dot_tn(jnp.concatenate(mine, axis=1), right)
        for x in range(2):
            out[x] = both_rows[x * slab : (x + 1) * slab].astype(out.dtype)


def weights_kernel(idx, f0, f1, f2, f3, g0, g1, g2, g3, *refs):
    keep0, send0, keep1, send1, left, right = refs
    rows = g0.shape[0] // 2
    firsts, grads = (f0, f1, f2, f3), (g0, g1, g2, g3)
    for keep, send, lefts, rights in ((keep0, send0, grads, firsts), (keep1, send1, firsts, grads)):
        for i in range(4):
            left[i * rows : (i + 1) * rows, :] = lefts[i][:rows, :]
            right[i * rows : (i + 1) * rows, :] = rights[i][rows : 2 * rows, :]
        slab_products(idx, left, right[...], [keep.at[0], send.at[0], keep.at[1], send.at[1]])


def pair_kernel(idx, *refs):
    count = (len(refs) - 1) // 3
    gots, owns, send, at = refs[: 2 * count], refs[2 * count : -1], refs[-1], 0
    for i, own in enumerate(owns):
        keep, got, span = gots[2 * i], gots[2 * i + 1], own.shape[-1]
        own[...] = keep[0] + got[0].astype(WIDE)
        send[:, :, at : at + span] = (keep[1] + got[1].astype(WIDE)).astype(LOW)
        at += span


def output_kernel(idx, f0, f1, f2, f3, g0, g1, g2, g3, keep, send, left, right):
    rows, width = g0.shape
    few = rows * QUAD // width
    for i, (f, g) in enumerate(zip((f0, f1, f2, f3), (g0, g1, g2, g3))):
        left[i * rows : (i + 1) * rows, :] = g[...]
        for j in range(width // QUAD):
            right[i * rows + j * few : i * rows + (j + 1) * few, :] = f[
                2 * rows :, j * QUAD : (j + 1) * QUAD
            ]
    slab_products(idx, left, right[...], [keep.at[0], send.at[0], keep.at[1], send.at[1]])


def line_sum_kernel(idx, own0, got0, own1, own2, got, keep, keep_out, send):
    at = 0
    for own, other, out in (
        (own0, got0[...], keep.at[0]),
        (own1, got[:, :, : own1.shape[-1]], keep.at[1]),
        (own2, got[:, :, own1.shape[-1] :], keep_out),
    ):
        span = own.shape[-1]
        out[...] = own[0] + other[0].astype(WIDE)
        send[:, at : at + span] = (own[1] + other[1].astype(WIDE)).astype(LOW)
        at += span


def columns_kernel(idx, keep, keep_out, got, contract, expand, output):
    span = keep.shape[-1]
    for at, mine, out in ((0, keep[0], contract), (span, keep[1], expand), (2 * span, keep_out[...], output)):
        cols = mine.shape[1]
        out[:, pl.ds(pl.multiple_of(idx[2] * cols, 128), cols)] = mine
        out[:, pl.ds(pl.multiple_of((1 - idx[2]) * cols, 128), cols)] = got[
            :, at : at + cols
        ].astype(WIDE)


def first_back_kernel(
    pieces, idx, own, other, grad_second_in, unitary, inverse, gain, sums0, sums1, *refs
):
    slabs, (grad_in, grad_low, vectors, pack, held, sems) = refs[:pieces], refs[pieces:]
    copy = piece_copies(idx, slabs, held, sems)
    start(copy)
    grad_first = grad_second_in[...] + pair(own, other)
    grad_in[...] = norm_back(grad_first, gain[...], unitary[...], inverse[...])
    grad_low[...] = grad_in[...].astype(LOW)
    vectors[...] = jnp.zeros_like(vectors)
    vectors[0:1, :] = column_sum(grad_low[...].astype(WIDE))
    vectors[1:2, :] = column_sum(grad_first * unitary[...])
    vectors[2:3, :] = column_sum(grad_first)
    grad = dot_nn(grad_low[...], finish(copy, held)).astype(LOW)
    half = grad.shape[0] // 2
    for h in range(NZ * 2):
        lanes = slice(h * HEAD_DIM, (h + 1) * HEAD_DIM)
        pack[h, :half, :HEAD_DIM] = grad[:half, lanes]
        pack[h, :half, HEAD_DIM:] = grad[half:, lanes]
        pack[h, half:, :] = (sums0[h] + sums1[h].astype(WIDE)).astype(LOW)


def triple_kernel(idx, dq, dkv, got, cosine, sine, out, dense):
    rows = dq.shape[0]
    low_lanes = lax.broadcasted_iota(jnp.int32, (rows, PAIR), 1) < HEAD_DIM
    grads = dkv[...] + got[...]
    both_parts = jnp.where(low_lanes, dq[...], pltpu.roll(grads, HEAD_DIM, 1))
    turned = turn(both_parts, cosine[...], -sine[...])
    turned, value = turned.astype(LOW), grads[:, HEAD_DIM:].astype(LOW)
    out[:, :PAIR] = turned
    out[:, PAIR:] = jnp.where(low_lanes, 0.0, grads).astype(LOW)
    rows = dense.shape[1] * 4 // 3
    half, few = rows // 2, rows // 4
    for i in range(dense.shape[0]):
        at = i * rows
        dense[i, :half, :PAIR] = turned[at : at + half]
        dense[i, :half, PAIR:] = turned[at + half : at + rows]
        for j in range(4):
            dense[i, half:, j * HEAD_DIM : (j + 1) * HEAD_DIM] = value[
                at + j * few : at + (j + 1) * few
            ]


def extra_rows(bias, vectors):
    cols = bias.shape[1]
    rows = [bias]
    for i in range(3):
        for j in range(vectors.shape[1] // cols):
            rows.append(vectors[i : i + 1, j * cols : (j + 1) * cols])
    return jnp.concatenate(rows + [jnp.zeros((16 - len(rows), cols), WIDE)], axis=0)


def triple_weight_kernel(idx, *refs):
    sheets, (grad, vectors, keep, send, total) = refs[:8], refs[8:]
    mc = idx[3]
    slab = HEAD_DIM
    for i, (value, at) in enumerate(sheet_rows(idx, sheets)):
        part = dot_tn(value, grad[at, :])
        if i == 0:
            total[...] = part
        else:
            total[...] += part
    extra = extra_rows(column_sum(grad[...].astype(WIDE)), vectors).astype(LOW)
    for spot in range(NZ * 2):
        for out, c in ((keep, mc), (send, 1 - mc)):
            at = pl.ds(pl.multiple_of((spot * 2 + c) * slab, slab), slab)
            out[spot, :slab, :] = total[at, :].astype(LOW)
            put_extra(out.at[spot], slab, extra)


def pair_sum_kernel(idx, one, two, out):
    out[...] = (one[...].astype(WIDE) + two[...].astype(WIDE)).astype(out.dtype)


def triple_out_kernel(idx, got, weight, bias, *vectors):
    slab = weight.shape[1]
    total = 0.0
    for spot in range(NZ * 2):
        at = spot * HEAD_DIM
        here, extra = got[spot].astype(WIDE), get_extra(got.at[spot], slab).astype(WIDE)
        for part, lane in enumerate(LANES):
            weight[part, :, at : at + HEAD_DIM] = here[:slab, lane : lane + HEAD_DIM]
            bias[part : part + 1, at : at + HEAD_DIM] = extra[:1, lane : lane + HEAD_DIM]
        total = total + extra
    row = 1
    for out in vectors:
        for i in range(0, out.shape[0], 2):
            out[i : i + 1, :] = total[row : row + 1, :PAIR]
            out[i + 1 : i + 2, :] = total[row : row + 1, PAIR:]
            row += 1


def tokens_kernel(idx, got, message, part, group, held, sems):
    copy = slab_copy(message, 0, held, sems)
    copy.start()
    rows = part.shape[0]
    half, few = rows // 2, rows // 4
    for h in range(NZ * 2):
        for p in range(2):
            at = (p * NZ * 2 + h) * HEAD_DIM
            for i in range(2):
                lane = i * PAIR + p * HEAD_DIM
                group[i * half : (i + 1) * half, at : at + HEAD_DIM] = got[
                    h, :half, lane : lane + HEAD_DIM
                ]
        at = (2 * NZ * 2 + h) * HEAD_DIM
        for j in range(4):
            group[j * few : (j + 1) * few, at : at + HEAD_DIM] = got[
                h, half:, j * HEAD_DIM : (j + 1) * HEAD_DIM
            ]
    copy.wait()
    part[...] = dot_nt(group[...], held[...]).astype(LOW)


def tokens_sum_kernel(idx, own, other, grad, out):
    out[...] = grad[...] + pair(own, other)


def shards(
    tokens,
    query_vecs,
    out_cotangent,
    doc_lengths,
    live_mask,
    positives,
    triple_weight,
    triple_bias,
    output_weight,
    output_bias,
    first_gain,
    first_shift,
    expand_weight,
    expand_bias,
    contract_weight,
    contract_bias,
    second_gain,
    second_shift,
    head_weight,
):
    outer = lax.axis_size("o")
    mo, mz, mx, mc, my = [lax.axis_index(a) for a in ("o", "z", "x", "c", "y")]
    index = jnp.stack([mo, mz, mx, mc, my]).astype(jnp.int32)
    rows, width = tokens.shape
    half = rows // 2
    slab = triple_weight.shape[0]
    docs = doc_lengths.shape[0]
    queries_count = positives.shape[0]
    blocks = outer * NZ * 4
    span = expand_weight.shape[1]
    quarter = span // 2
    proj = head_weight.shape[1]
    line = lambda vector: vector.reshape(1, -1)

    def widen(value):
        return lax.all_gather(value, "o") if outer > 1 else value[None]

    def narrow(value):
        return lax.psum_scatter(value, "o") if outer > 1 else value[0]

    def sum_outer(value):
        return lax.psum(value, "o") if outer > 1 else value

    def stage(work):
        like = jax.eval_shape(work)
        idle = lambda: jax.tree.map(lambda leaf: jnp.zeros(leaf.shape, leaf.dtype), like)
        return lax.cond(doc_lengths[0] >= 0, work, idle)

    def key_doc(live, c):
        block = jnp.arange(outer * NZ * 2, dtype=jnp.int32) * 2 + c
        doc = doc_layout(doc_lengths, block[:, None] + where[None, :])[0]
        return jnp.where(live > 0, doc, -1)

    def head_weights(heads, heads_other):
        if outer > 1:
            pack = widen(both(heads, heads_other, mc)).transpose(0, 2, 1, 3, 4)
            head_triple = pack[..., :slab, :].reshape(width, QUAD)
            outs = pack[..., slab + 16 :, :].reshape(-1, 2, slab, QUAD).transpose(0, 2, 1, 3)
            outs = (outs.reshape(width, 2 * QUAD),)
            live0, live1 = [
                pick(pack, c, 2)[..., slab, :rows].astype(WIDE).reshape(-1, rows)
                for c in (mc, 1 - mc)
            ]
        else:
            outs = (heads, heads_other)
            head_triple, live0, live1 = whole(
                heads_kernel,
                "heads",
                index,
                (heads, heads_other),
                [shape((width, QUAD), LOW)] + [shape((NZ * 2, rows), WIDE)] * 2,
            )
        return head_triple, key_doc(live0, mc), key_doc(live1, 1 - mc), outs

    half_tokens = lax.dynamic_slice_in_dim(tokens, my * half, half, 0)
    by_z = [half_tokens] + [xor_z(half_tokens, m) for m in (1, 2, 3)]
    own_other = flip(tokens, "x")

    heads, low_slab, triple_slab = whole(
        prep_kernel,
        "prep",
        index,
        (
            triple_weight.transpose(1, 0, 2),
            output_weight.T,
            expand_weight,
            contract_weight.T,
            line(live_mask),
        ),
        [shape((NZ * 2, 3 * slab + extra_count(slab), QUAD), LOW)]
        + [shape((slab, n), LOW) for n in (2 * span, 6 * QUAD)],
    )

    where = jnp.arange(rows, dtype=jnp.int32) * blocks
    rank = jnp.arange(NZ * 2, dtype=jnp.int32) * 2
    shares = query_vecs.shape[0] // (NZ * 4)
    by_z = list(lax.optimization_barrier((*by_z, heads, own_other))[:NZ])
    gathered = lax.all_gather(after(low_slab, *by_z[1:]), BLK, axis=0, tiled=True)

    def heads_stage():
        got = lax.all_to_all(heads, ("z", "x"), 0, 0)
        sheets = [tokens, own_other]
        for piece in by_z[1:]:
            two = jnp.stack([piece, flip(piece, "x")])
            sheets += [two, flip(two, "y")]
        own_places = (mo * NZ * 4 + rank + mc)[:, None] + where[None, :]
        own_position = doc_layout(doc_lengths, own_places.reshape(-1))[1]
        lane = jnp.arange(PAIR) % (HEAD_DIM // 2)
        exponent = (2 * lane).astype(WIDE) / HEAD_DIM
        angles = own_position.astype(WIDE)[:, None] * jnp.exp(-math.log(10000.0) * exponent)[None, :]
        sign = jnp.where(jnp.arange(PAIR) % HEAD_DIM < HEAD_DIM // 2, -1.0, 1.0).astype(WIDE)
        tables = jnp.cos(angles), jnp.sin(angles) * sign[None, :]
        units = whole(
            query_kernel,
            "query_units",
            index,
            (query_vecs,),
            [shape(query_vecs.shape, LOW), shape((shares, proj), LOW)],
        )
        positive = line(jnp.repeat(positives, query_vecs.shape[0] // queries_count))
        got = after(got, sheets[3], sheets[5], sheets[7], tables[0], units[0])
        head = head_weights(got, flip(got, "c"))
        return head, sheets[2:], tables, list(units), positive

    head, sheets, (cosine, sine), (query_unit, own_queries), positive = stage(heads_stage)
    head_triple, kdoc0, kdoc1, outs = head
    pieces = len(outs)
    sheets = [tokens, own_other] + sheets
    positive = lax.optimization_barrier(positive)
    count = NZ * 2 * rows

    def project_stage():
        queries, kv = whole(
            project_kernel,
            "project",
            index,
            (*sheets, head_triple, cosine, sine, triple_bias),
            [shape((count, PAIR), LOW)] * 2,
        )
        return queries, kv, flip(kv, "c")

    queries, kv, kv_other = stage(project_stage)
    kv0, kv1 = [widen(v).reshape(-1, PAIR) for v in (kv, kv_other)]
    meta = (kdoc0, kdoc1)
    steps = (blocks, index, doc_lengths)

    def to_blocks(value):
        return lax.all_to_all(value.reshape((NZ * 2,) + value.shape[-2:]), ("z", "x"), 0, 0)

    def attention_stage():
        out, log_total, pack = attend(*steps, queries, kv0, kv1, *meta)
        return out, log_total, to_blocks(pack)

    out, log_total, pack = stage(attention_stage)
    wide_rows, low_rows, thin_rows = [shape((rows, n), t) for n, t in ((width, WIDE), (width, LOW), (1, WIDE))]
    def branch_stage():
        low, part = whole(
            partial(branch_kernel, pieces),
            "branch",
            index,
            (pack,),
            [shape((rows, 2 * QUAD), LOW), low_rows],
            piece_scratch(width, 2 * QUAD),
            outs,
        )
        return low, part, flip(part, "y")

    attended_low, part, part_other = stage(branch_stage)
    gathered = after(gathered, part)
    both_slabs = slab_scratch(width, span) * 2
    triple_low = lax.all_gather(after(triple_slab, part), BLK, axis=0, tiled=True)
    few = rows * QUAD // width
    first, unitary1, inverse1, hidden_in, keep, send, part = whole(
        forward_kernel,
        "forward",
        index,
        (
            part, part_other, tokens, line(output_bias), line(first_gain), line(first_shift),
            line(expand_bias), attended_low,
        ),
        [wide_rows, wide_rows, thin_rows, shape((rows, span), WIDE)]
        + [shape((2 * rows + few, width), LOW)] * 2
        + [low_rows],
        [pltpu.VMEM((rows, width), LOW), pltpu.VMEM((rows, span), LOW)] + both_slabs,
        (gathered,),
    )

    def over_z(parts):
        return [parts[0]] + [xor_z(parts[m], m) for m in (1, 2, 3)]

    def four_cores(keep, send):
        two = [keep, flip(send, "x")]
        return two + [flip(value, "c") for value in two]

    first_keep, first_other, first_across = keep, flip(send, "x"), flip(keep, "c")
    my_tokens = query_unit.shape[0]

    def second_stage():
        return whole(
            second_kernel,
            "second",
            index,
            (
                part, flip(part, "y"), first, line(contract_bias), line(second_gain),
                line(second_shift), head_weight, query_unit, kdoc0,
            ),
            [low_rows, wide_rows, thin_rows] + [shape((rows, proj), t) for t in (WIDE, LOW)]
            + [shape((rows, my_tokens), WIDE), shape((docs, my_tokens), WIDE)]
            + [shape((rows, proj), WIDE)],
        )

    second_low, unitary2, inverse2, embed, unit_low, expo, totals, message = stage(second_stage)
    totals = after(totals, first_across)

    def tree(own, one, two, three):
        return (own + one) + (two + three)

    chunk = width // (NZ * 4)
    sums_dims = (NZ * 2, chunk + 16, proj)
    def middle_stage():
        sums = sum_outer(tree(totals, *[xor_s(totals, m) for m in (1, 2, 3)]))
        return whole(
            partial(middle_kernel, queries_count),
            "middle",
            index,
            (
                sums, *[xor_z(sums, m) for m in (1, 2, 3)], kdoc0, kdoc1, positive, expo, query_unit,
                unit_low, embed, second_low, head_weight, out_cotangent, unitary2, inverse2,
                line(second_gain), hidden_in,
            ),
            [wide_rows]
            + [shape((2 * rows, width), LOW)] * 2
            + [low_rows, shape((8, proj), WIDE), shape((docs, my_tokens), WIDE)]
            + [shape(sums_dims, WIDE), shape(sums_dims, LOW)],
            [
                pltpu.VMEM((rows, my_tokens), LOW),
                pltpu.VMEM((rows, width), LOW),
                pltpu.VMEM((rows, span), LOW),
                pltpu.VMEM((width, proj), WIDE),
                pltpu.VMEM((NZ * 4 * 16, proj), WIDE),
            ]
            + both_slabs,
            (gathered,),
        )

    grad_second_in, keep, send, part, loss, coefficients, sums_own, sums_send = stage(middle_stage)

    triple_low, part, first_other = lax.optimization_barrier((triple_low, part, first_other))
    units = lax.all_gather(after(message, part), BLK, axis=0, tiled=True)
    keep_other, keep_across = flip(send, "x"), flip(keep, "c")

    def first_stage():
        return whole(
            partial(first_back_kernel, pieces),
            "first_back",
            index,
            (
                part, flip(part, "y"), grad_second_in, unitary1, inverse1, line(first_gain),
                sums_own, flip(sums_send, "c"),
            ),
            [wide_rows, low_rows, shape((8, width), WIDE)]
            + [shape((NZ * 2, half + chunk + 16, PAIR), LOW)],
            piece_scratch(width, 2 * QUAD),
            outs,
        )

    grad_first_in, grad_branch, vectors1, pack = stage(first_stage)
    keep_other = after(keep_other, grad_branch)
    dims, dims_out = (2, slab, quarter), (2, slab, QUAD)
    dims_both = (2, slab, quarter + QUAD)
    left_right = [pltpu.VMEM((4 * rows, width), LOW)]

    def parts_of(left, right):
        part = dot_tn(jnp.concatenate(left), jnp.concatenate(right))
        part = pick(narrow(part.reshape(outer, NZ, 2, 2, slab, -1)), mc, 2)
        for axis, spot in ((0, mz), (1, mx)):
            part = jnp.take(part, jnp.arange(part.shape[axis]) ^ spot, axis=axis)
        return part

    def low_parts(parts):
        return [parts[0]] + [parts[m].astype(LOW) for m in (1, 2, 3)]

    def weights_stage():
        got = to_blocks(pack)
        firsts = [first_keep, first_other, first_across, flip(first_other, "c")]
        grads = [keep, keep_other, keep_across, flip(keep_other, "c")]
        other = flip(grad_branch, "x")
        got = got, [other, flip(grad_branch, "c"), flip(other, "c")], firsts[3]
        if outer == 1:
            parts = whole(
                weights_kernel,
                "weights",
                index,
                (*firsts, *grads),
                [shape((2,) + dims, WIDE), shape((2,) + dims, LOW)] * 2,
                left_right * 2,
            )
            return got, list(parts)
        top, mid = slice(0, rows), slice(rows, 2 * rows)
        contract = parts_of([g[top] for g in grads], [f[mid] for f in firsts])
        expand = parts_of([f[top] for f in firsts], [g[mid] for g in grads])
        return got, [part for p in (contract, expand) for part in (p[::2], p[1::2].astype(LOW))]

    (grad_out, branches, first_last), weight_parts = stage(weights_stage)
    branches = [grad_branch] + branches
    firsts = [first_keep, first_other, first_across, first_last]
    contract_keep, contract_send, expand_keep, expand_send = weight_parts
    contract_got, expand_got = xor_z(contract_send, 1), xor_z(expand_send, 1)

    def attend_stage():
        grad_query, dkv0, dkv1 = attend_back(
            *steps, queries, grad_out.reshape(NZ, 2, -1, PAIR), out, log_total, kv0, kv1, *meta
        )
        dkv0, dkv1 = [narrow(v.reshape(outer, -1, PAIR)) for v in (dkv0, dkv1)]
        triple = whole(
            triple_kernel,
            "triple",
            index,
            (grad_query.reshape(count, PAIR), dkv0, flip(dkv1, "c"), cosine, sine),
            [shape((count, QUAD), LOW), shape((NZ * 2, rows * 3 // 4, QUAD), LOW)],
        )
        return triple

    grad_triple, dense_triple = stage(attend_stage)
    grad_triple, contract_got = lax.optimization_barrier((grad_triple, contract_got))
    contract_own, contract_send = whole(
        pair_kernel, "pair", index, (contract_keep, contract_got), [shape(dims, t) for t in (WIDE, LOW)]
    )
    contract_got = xor_z(contract_send, 2)
    grad_triple, units = lax.optimization_barrier((grad_triple, units, contract_own))[:2]
    dims_triple = (NZ * 2, slab + extra_count(slab), QUAD)
    vector = shape((width // PAIR, PAIR), WIDE)

    def triple_parts():
        if outer == 1:
            return whole(
                triple_weight_kernel,
                "triple_weight",
                index,
                (*sheets, grad_triple, vectors1),
                [shape(dims_triple, LOW)] * 2,
                [pltpu.VMEM((width, QUAD), WIDE)],
            )
        ordered = [(mz * 2 + (mx ^ x), sheets[x]) for x in range(2)]
        for m in (1, 2, 3):
            two = both(*sheets[2 * m : 2 * m + 2], my)
            for x in range(2):
                ordered.append(((mz ^ m) * 2 + (mx ^ x), two[:, x].reshape(rows, width)))
        ordered = place(ordered).reshape(count, width)
        part = narrow(dot_tn(ordered, grad_triple).reshape(outer, NZ * 2, 2, slab, QUAD))
        bias = sum_outer(jnp.sum(grad_triple, axis=0, dtype=WIDE))
        bias = extra_rows(line(bias), sum_outer(vectors1))
        bias = jnp.broadcast_to(bias, (NZ * 2, 2, 16, QUAD))
        part = jnp.concatenate([part, bias], axis=2).astype(LOW)
        return pick(part, mc, 1), pick(part, 1 - mc, 1)

    def output_parts_of():
        if outer == 1:
            return whole(
                output_kernel,
                "output",
                index,
                (*firsts, *branches),
                [shape((2,) + dims_out, t) for t in (WIDE, LOW)],
                left_right + [pltpu.VMEM((4 * rows, QUAD), LOW)],
            )
        wide = [f[2 * rows :].reshape(few, 4, QUAD).transpose(1, 0, 2).reshape(rows, QUAD) for f in firsts]
        parts = parts_of(branches, wide)
        return parts[::2], parts[1::2].astype(LOW)

    def triple_stage():
        block_triple = to_blocks(dense_triple)
        keep, send = triple_parts()
        output_parts = output_parts_of()
        packed = whole(
            pair_sum_kernel, "pair_sum", index, (keep, flip(send, "c")), [shape(dims_triple, LOW)]
        )[0]
        mine = whole(
            partial(query_back_kernel, half),
            "query_back",
            index,
            (kdoc0, kdoc1, coefficients, own_queries, units, sum_outer(grad_out)),
            [shape((shares + chunk + 16, proj), LOW)],
        )[0]
        return block_triple, packed, output_parts[0], xor_z(output_parts[1], 1), mine

    block_triple, packed, output_keep, output_got, mine = stage(triple_stage)
    block_triple, contract_got, expand_got = lax.optimization_barrier(
        (block_triple, contract_got, expand_got)
    )
    expand_own, output_own, both_send = whole(
        pair_kernel,
        "pair",
        index,
        (expand_keep, expand_got, output_keep, output_got),
        [shape(dims, WIDE), shape(dims_out, WIDE), shape(dims_both, LOW)],
    )
    both_got = xor_z(both_send, 2)
    block_triple = after(block_triple, expand_own)
    spread = lax.all_gather(after(mine, expand_own), ("z", "x", "c"))

    def tokens_stage():
        part = whole(
            tokens_kernel,
            "tokens",
            index,
            (block_triple,),
            [low_rows],
            [pltpu.VMEM((rows, 6 * QUAD), LOW)] + slab_scratch(width, 6 * QUAD),
            (triple_low,),
        )[0]
        tokens_grad = whole(
            tokens_sum_kernel, "tokens_sum", index, (part, flip(part, "y"), grad_first_in), [wide_rows]
        )[0]
        return tokens_grad

    tokens_grad = stage(tokens_stage)
    packed = lax.all_to_all(after(packed, tokens_grad), ("z", "x"), 0, 0)
    contract_own, spread = after(contract_own, tokens_grad), after(spread, tokens_grad)
    keep, keep_out, send = whole(
        line_sum_kernel,
        "line_sum",
        index,
        (contract_own, contract_got, expand_own, output_own, both_got),
        [shape((2, slab, quarter), WIDE), shape((slab, QUAD), WIDE), shape((slab, 2 * quarter + QUAD), LOW)],
    )
    triple_grad, triple_bias_grad, output_bias_grad, gain_one, shift_one = whole(
        triple_out_kernel,
        "triple_out",
        index,
        (packed,),
        [shape((3, slab, 2 * QUAD), WIDE), shape((3, 2 * QUAD), WIDE)] + [vector] * 3,
    )
    contract_grad, expand_grad, output_grad = whole(
        columns_kernel,
        "columns",
        index,
        (keep, keep_out, flip(send, "x")),
        [shape((slab, n), WIDE) for n in (span, span, 2 * QUAD)],
    )

    queries_grad, head_grad, contract_bias_grad, gain_two, shift_two, expand_bias_grad = whole(
        spread_kernel,
        "spread",
        index,
        (after(spread, contract_grad).reshape(NZ * 4, -1, proj),),
        [shape((query_vecs.shape[0], proj), WIDE), shape((width, proj), WIDE)]
        + [vector] * 3
        + [shape((span // PAIR, PAIR), WIDE)],
    )

    return (
        second_low,
        after(loss, tokens_grad)[0, 0],
        tokens_grad,
        queries_grad,
        triple_grad.transpose(1, 0, 2),
        triple_bias_grad,
        output_grad.T,
        output_bias_grad.reshape(-1),
        gain_one.reshape(-1),
        shift_one.reshape(-1),
        expand_grad,
        expand_bias_grad.reshape(-1),
        contract_grad.T,
        contract_bias_grad.reshape(-1),
        gain_two.reshape(-1),
        shift_two.reshape(-1),
        head_grad,
    )


def solution(mesh):
    outer = mesh.shape["blk"] // 16
    five = Mesh(mesh.devices.reshape(outer, NZ, 2, 2, mesh.shape["tensor"]), BLK + ("y",))
    blk, tensor = BLK, "y"
    return jax.shard_map(
        shards,
        mesh=five,
        in_specs=(
            P(blk, None),
            P(),
            P(blk, None),
            P(),
            P(blk),
            P(),
            P(blk, None, tensor),
            P(None, tensor),
            P(tensor, blk),
            P(),
            P(),
            P(),
            P(blk, tensor),
            P(tensor),
            P(tensor, blk),
            P(),
            P(),
            P(),
            P(),
        ),
        out_specs=(
            P(blk, None),
            P(),
            P(blk, None),
            P(),
            P(blk, None, tensor),
            P(None, tensor),
            P(tensor, blk),
            P(),
            P(),
            P(),
            P(blk, tensor),
            P(tensor),
            P(tensor, blk),
            P(),
            P(),
            P(),
            P(),
        ),
        check_vma=False,
    )
```

```python
from functools import partial
import math

import jax
import jax.numpy as jnp
import numpy as np
from jax import lax
from jax.experimental import pallas as pl
from jax.experimental.pallas import tpu as pltpu
from jax.sharding import Mesh, PartitionSpec as P

HEAD_DIM = 64
PAIR = 2 * HEAD_DIM

SOFTMAX_TEMPER = 0.05
FLOOR_SCORE = -1e30
NORM_EPSILON = 1e-05
UNIT_EPSILON = 1e-06
PRECISE = lax.Precision.HIGHEST
LOW = jnp.bfloat16
WIDE = jnp.float32

BLK = ("o", "z", "x", "c")
NZ = 4
FOUR = [0, 1, 2, 3]

VMEM_BYTES = 56 * 1024 * 1024
LANES = (0, 64, 192)
QUAD = 4 * HEAD_DIM


def xor_z(value, mask):
    return lax.ppermute(value, "z", [(i, i ^ mask) for i in FOUR])


def xor_s(value, mask):
    return lax.ppermute(value, ("x", "c"), [(i, i ^ mask) for i in FOUR])


def flip(value, axis):
    return lax.ppermute(value, axis, [(0, 1), (1, 0)])


def pick(value, index, axis=0):
    return lax.dynamic_index_in_dim(value, index, axis, keepdims=False)


def after(value, *others):
    return lax.optimization_barrier((value,) + others)[0]


def place(pieces):
    first = pieces[0][1]
    whole = jnp.zeros((len(pieces),) + first.shape, first.dtype)
    for index, piece in pieces:
        whole = lax.dynamic_update_slice_in_dim(whole, piece[None], index, 0)
    return whole


def both(mine, other, where):
    return place([(where, mine), (1 - where, other)])


def doc_layout(doc_lengths, places):
    ends = jnp.cumsum(doc_lengths)
    starts = ends - doc_lengths
    passed = starts <= places[..., None]
    doc_index = jnp.sum(passed.astype(jnp.int32), axis=-1) - 1
    begin = jnp.max(jnp.where(passed, starts, 0), axis=-1)
    return (doc_index, places - begin)


def dot_nn(a, b, precision=None):
    return lax.dot_general(
        a, b, (((1,), (0,)), ((), ())), precision=precision, preferred_element_type=WIDE
    )


def dot_nt(a, b, precision=None):
    return lax.dot_general(
        a, b, (((1,), (1,)), ((), ())), precision=precision, preferred_element_type=WIDE
    )


def dot_tn(a, b, precision=None):
    return lax.dot_general(
        a, b, (((0,), (0,)), ((), ())), precision=precision, preferred_element_type=WIDE
    )


def shape(dims, dtype):
    return jax.ShapeDtypeStruct(dims, dtype)


PARAMS = pltpu.CompilerParams(vmem_limit_bytes=VMEM_BYTES)

TAKES = dict(
    prep=2.5, heads=2.0, project=3.8, attend=7.5, branch=3.5, forward=7.7, second=3.6, middle=12.0, first_back=3.8, attend_back=9.8, triple=2.9, triple_weight=2.0, tokens=3.9,
    tokens_sum=2.1, weights=5.2, output=1.5, core_sum=3.9, line_sum=2.7, pair=2.0, columns=2.2, pair_sum=0.8,
    triple_out=1.9, query_units=2.8, query_back=1.0, spread=3.5,
)


SCALE = 1.0


def cost(name):
    took = TAKES[name] * SCALE
    return pl.CostEstimate(
        flops=int(took * 1.15e9), bytes_accessed=int(took * 3.7e6), transcendentals=0
    )


def whole(kernel, name, index, inputs, outputs, scratch=(), slabs=()):
    return pl.pallas_call(
        kernel,
        in_specs=[pl.BlockSpec(memory_space=pltpu.SMEM)]
        + [pl.BlockSpec(memory_space=pltpu.VMEM)] * len(inputs)
        + [pl.BlockSpec(memory_space=pl.ANY)] * len(slabs),
        out_specs=[pl.BlockSpec(memory_space=pltpu.VMEM)] * len(outputs),
        out_shape=list(outputs),
        scratch_shapes=list(scratch),
        compiler_params=PARAMS,
        cost_estimate=cost(name),
        name=name,
    )(index, *inputs, *slabs)


def slab_copy(slabs, at, weight, sems):
    there = slabs.at[:, pl.ds(at, weight.shape[1])]
    return pltpu.make_async_copy(there, weight, sems.at[0])


def piece_copies(idx, pieces, weight, sems):
    if len(pieces) == 1:
        return [pltpu.make_async_copy(pieces[0], weight, sems.at[0])]
    count, half, _ = pieces[0].shape
    span, copies = weight.shape[1], []
    for c, piece in enumerate(pieces):
        for spot in range(count):
            there = (idx[1] ^ (spot // 2)) * 2 + (idx[2] ^ (spot % 2))
            row = (there * 2 + (idx[3] ^ c)) * 2 * half
            for i in range(2):
                rows = pl.ds(pl.multiple_of(row + i * half, half), half)
                here = piece.at[spot, :, pl.ds(i * span, span)]
                copies.append(pltpu.make_async_copy(here, weight.at[rows, :], sems.at[len(copies)]))
    return copies


def piece_scratch(rows, cols):
    return [pltpu.VMEM((rows, cols), LOW), pltpu.SemaphoreType.DMA((NZ * 8,))]


def slab_scratch(rows, cols):
    return [pltpu.VMEM((rows, cols), LOW), pltpu.SemaphoreType.DMA((1,))]


def start(copies):
    for copy in copies:
        copy.start()


def finish(copies, weight):
    for copy in copies:
        copy.wait()
    return weight[...]


def extra_count(slab):
    return 0 if slab >= HEAD_DIM else 16


def put_extra(message, slab, extra):
    if extra_count(slab):
        message[slab : slab + 16, :] = extra
        return
    for i in range(4):
        message[i * 16 : (i + 1) * 16, PAIR : PAIR + HEAD_DIM] = extra[
            :, i * HEAD_DIM : (i + 1) * HEAD_DIM
        ]


def get_extra(message, slab):
    if extra_count(slab):
        return message[slab : slab + 16, :]
    lanes = slice(PAIR, PAIR + HEAD_DIM)
    return jnp.concatenate([message[i * 16 : (i + 1) * 16, lanes] for i in range(4)], axis=1)


def prep_kernel(idx, tw, ow, ew, cw, live, tokens, heads, low, tri, mine, own):
    slab, span = ew.shape
    alive = jnp.broadcast_to(live[...], (16, live.shape[1])).astype(WIDE).astype(LOW)
    alive = jnp.concatenate([alive, jnp.zeros((16, QUAD - live.shape[1]), LOW)], axis=1)
    rows, span = tokens.shape[0], ow.shape[1]
    half = rows // 2
    mine[:half, :] = tokens[pl.ds(pl.multiple_of(idx[4] * half, half), half), :]
    own[:rows, :] = tokens[...]
    if own.shape[0] > rows:
        for i in range(2):
            part = ow[i * slab // 2 : (i + 1) * slab // 2, :].astype(LOW)
            mine[half:, i * span : (i + 1) * span] = part
            own[rows:, i * span : (i + 1) * span] = part
    span = ew.shape[1]
    for spot in range(NZ * 2):
        at = spot * HEAD_DIM
        for part, lane in enumerate(LANES):
            heads[spot, :slab, lane : lane + HEAD_DIM] = tw[part, :, at : at + HEAD_DIM].astype(LOW)
        heads[spot, :slab, PAIR : PAIR + HEAD_DIM] = jnp.zeros((slab, HEAD_DIM), LOW)
        put_extra(heads.at[spot], slab, alive)
    low[:, :span] = ew[...].astype(LOW)
    low[:, span:] = cw[...].astype(LOW)
    for part in range(3):
        tri[:, part * 2 * QUAD : (part + 1) * 2 * QUAD] = tw[part].astype(LOW)


def heads_kernel(idx, own, other, weight, live0, live1):
    slab, mc = HEAD_DIM, idx[3]
    for spot in range(NZ * 2):
        for source, c, live in ((own, mc, live0), (other, 1 - mc, live1)):
            rows = pl.ds(pl.multiple_of((spot * 2 + c) * slab, slab), slab)
            weight[rows, :] = source[spot, :slab, :]
            live[spot : spot + 1, :] = get_extra(source.at[spot], slab)[:, :PAIR].astype(WIDE)[:1]


def swap_halves(value):
    lane = lax.broadcasted_iota(jnp.int32, value.shape, 1)
    half = HEAD_DIM // 2
    return jnp.where(
        (lane & half) == 0,
        pltpu.roll(value, PAIR - half, 1),
        pltpu.roll(value, half, 1),
    )


def turn(value, cosine, sine):
    return value * cosine + swap_halves(value) * sine


def sheet_rows(idx, sheets):
    rows = sheets[0].shape[0]
    half = rows // 2
    parts = []
    for x in range(2):
        spot = idx[1] * 2 + (idx[2] ^ x)
        parts.append((sheets[x][:rows, :], pl.ds(pl.multiple_of(spot * rows, rows), rows)))
    for at, sheet in enumerate(sheets[2:]):
        z, y = at // 2 + 1, at % 2
        for x in range(2):
            spot = (idx[1] ^ z) * 2 + (idx[2] ^ x)
            row = spot * rows + (idx[4] ^ y) * half
            parts.append((sheet[x], pl.ds(pl.multiple_of(row, half), half)))
    return parts


def project_kernel(idx, *refs):
    sheets, (weight, cosine, sine, bias, query, kv, held) = refs[:8], refs[8:]
    for value, at in sheet_rows(idx, sheets):
        held[at, :] = value
    mz, mx = idx[1], idx[2]
    mine = mz * 2 + mx
    biases = []
    for part in range(3):
        total = jnp.zeros((1, HEAD_DIM), WIDE)
        for h in range(NZ * 2):
            here = bias[part : part + 1, h * HEAD_DIM : (h + 1) * HEAD_DIM]
            total = jnp.where(mine == h, here, total)
        biases.append(total)
    empty = jnp.zeros((1, HEAD_DIM), WIDE)
    offset = jnp.concatenate([biases[0], biases[1], empty, biases[2]], axis=1)
    weights = weight[...]
    rows = sheets[0].shape[0]
    low_lanes = lax.broadcasted_iota(jnp.int32, (rows, PAIR), 1) < HEAD_DIM
    for i in range(NZ * 2):
        at = slice(i * rows, (i + 1) * rows)
        triple = dot_nn(held[at, :], weights) + offset
        turned = turn(triple[:, :PAIR], cosine[at, :], sine[at, :])
        query[at, :] = jnp.where(low_lanes, turned * HEAD_DIM ** (-0.5), 0.0).astype(LOW)
        kv[at, :] = jnp.where(
            low_lanes, pltpu.roll(turned, HEAD_DIM, 1), triple[:, PAIR:]
        ).astype(LOW)


def key_row(ref):
    rows = ref[...]
    return jnp.concatenate([rows[i : i + 1] for i in range(rows.shape[0])], axis=1)


def places_of(token, rows, half, blocks, idx, z, part):
    x, upper, row = token // (2 * rows), token // rows % 2, token % rows
    block = ((idx[0] * NZ + z) * 2 + x) * 2 + idx[3]
    return (upper * half + part * rows + row) * blocks + block


def docs_of(places, lens):
    doc, begin = jnp.full(places.shape, -1, jnp.int32), jnp.int32(0)
    for i in range(lens.shape[0]):
        doc = jnp.where(begin <= places, doc + 1, doc)
        begin = begin + lens[i]
    return doc


def as_row(column):
    count = column.shape[0]
    row = lax.broadcasted_iota(jnp.int32, (count, count), 0)
    same = row == lax.broadcasted_iota(jnp.int32, (count, count), 1)
    return jnp.sum(jnp.where(same, column, 0.0), axis=0, keepdims=True)


def attend_kernel(
    blocks, idx, lens, q_ref, kv0_ref, kv1_ref, kdoc0_ref, kdoc1_ref, out_ref, log_ref, pack_ref
):
    rows, half = q_ref.shape[3], kdoc0_ref.shape[1] // 2
    queries = q_ref[0].reshape(4 * rows, PAIR)
    kv = (kv0_ref[...], kv1_ref[...])
    token = lax.broadcasted_iota(jnp.int32, (4 * rows, 1), 0)
    z, part = pl.program_id(0), pl.program_id(1)
    doc = docs_of(places_of(token, rows, half, blocks, idx, z, part), lens)
    scores = [
        jnp.where(doc == key_row(ref), dot_nt(queries, keys), FLOOR_SCORE)
        for ref, keys in zip((kdoc0_ref, kdoc1_ref), kv)
    ]
    peak = jnp.maximum(*[jnp.max(s, axis=-1, keepdims=True) for s in scores])
    weights = [jnp.exp(s - peak) for s in scores]
    total = sum(jnp.sum(w, axis=-1, keepdims=True) for w in weights)
    mixed = sum(dot_nn(w.astype(LOW), keys) for w, keys in zip(weights, kv)) / total
    out_ref[0] = mixed.reshape(2, 2, rows, PAIR)
    log_ref[0, 0] = as_row(peak + jnp.log(total))
    low_lanes = lax.broadcasted_iota(jnp.int32, (rows, PAIR), 1) < HEAD_DIM
    for x in range(2):
        upper = mixed[2 * x * rows : (2 * x + 1) * rows]
        lower = mixed[(2 * x + 1) * rows : (2 * x + 2) * rows]
        pack_ref[0, x] = jnp.where(low_lanes, pltpu.roll(upper, HEAD_DIM, 1), lower).astype(LOW)


def attend_specs(rows, keys, key_rows):
    half = rows // 2
    size = max(16, min(half, half * 2048 // (2 * keys)))
    full = lambda n, m: pl.BlockSpec((n, m), lambda i, j: (0, 0))
    part = lambda m: pl.BlockSpec((1, 2, 2, size, m), lambda i, j: (i, 0, 0, j, 0))
    pack = pl.BlockSpec((1, 2, size, PAIR), lambda i, j: (i, 0, j, 0))
    logs = pl.BlockSpec((1, 1, 1, 4 * size), lambda i, j: (i, j, 0, 0))
    kv, docs = full(keys, PAIR), full(key_rows, rows)
    return (NZ, half // size), part, pack, logs, kv, docs


SCALARS = [pl.BlockSpec(memory_space=pltpu.SMEM)] * 2


def attend(blocks, index, lens, queries, kv0, kv1, kdoc0, kdoc1):
    rows = kdoc0.shape[1]
    half = rows // 2
    grid, part, pack, logs, kv, docs = attend_specs(rows, kv0.shape[0], kdoc0.shape[0])
    return pl.pallas_call(
        partial(attend_kernel, blocks),
        grid=grid,
        in_specs=SCALARS + [part(PAIR), kv, kv, docs, docs],
        out_specs=[part(PAIR), logs, pack],
        out_shape=[
            shape((NZ, 2, 2, half, PAIR), WIDE),
            shape((NZ, grid[1], 1, 4 * half // grid[1]), WIDE),
            shape((NZ, 2, half, PAIR), LOW),
        ],
        compiler_params=PARAMS,
        cost_estimate=cost("attend"),
        name="attend",
    )(index, lens, queries.reshape(NZ, 2, 2, half, PAIR), kv0, kv1, kdoc0, kdoc1)


def attend_back_kernel(
    blocks, idx, lens, q_ref, g_ref, o_ref, log_ref, kv0_ref, kv1_ref, kdoc0_ref, kdoc1_ref,
    dq_ref, dkv0_ref, dkv1_ref, column0, column1,
):
    rows, width = q_ref.shape[3], kdoc0_ref.shape[1]
    z, part = pl.program_id(0), pl.program_id(1)

    @pl.when((z == 0) & (part == 0))
    def _():
        dkv0_ref[...] = jnp.zeros_like(dkv0_ref)
        dkv1_ref[...] = jnp.zeros_like(dkv1_ref)
        for ref, column in ((kdoc0_ref, column0), (kdoc1_ref, column1)):
            turned = jnp.transpose(ref[...].astype(WIDE))
            for i in range(ref.shape[0]):
                column[i * width : (i + 1) * width, :] = turned[:, i : i + 1]

    queries = q_ref[0].reshape(4 * rows, PAIR)
    high_lanes = lax.broadcasted_iota(jnp.int32, (rows, PAIR), 1) >= HEAD_DIM
    parts = []
    for x in range(2):
        packed = g_ref[0, x].astype(WIDE)
        parts.append(jnp.where(high_lanes, pltpu.roll(packed, HEAD_DIM, 1), 0.0))
        parts.append(jnp.where(high_lanes, packed, 0.0))
    wide = jnp.concatenate(parts, axis=0)
    grads = wide.astype(LOW)
    delta = as_row(jnp.sum(wide * o_ref[0].reshape(4 * rows, PAIR), axis=-1, keepdims=True))
    token = lax.broadcasted_iota(jnp.int32, (1, 4 * rows), 1)
    doc = docs_of(places_of(token, rows, width // 2, blocks, idx, z, part), lens).astype(WIDE)
    log_total = log_ref[0, 0]
    total = jnp.zeros((4 * rows, PAIR), WIDE)
    for kv_ref, column, dkv_ref in ((kv0_ref, column0, dkv0_ref), (kv1_ref, column1, dkv1_ref)):
        keys = kv_ref[...]
        raw = dot_nt(keys, queries)
        probs = jnp.where(column[...] == doc, jnp.exp(raw - log_total), 0.0)
        dprobs = dot_nt(keys, grads)
        dscores = (probs * (dprobs - delta)).astype(LOW)
        total = total + dot_tn(dscores, keys)
        dkv_ref[...] += dot_nn(dscores, queries) + dot_nn(probs.astype(LOW), grads)
    dq_ref[0] = (total * HEAD_DIM ** (-0.5)).reshape(2, 2, rows, PAIR)


def attend_back(blocks, index, lens, queries, grads, out, log_total, kv0, kv1, kdoc0, kdoc1):
    rows, keys = kdoc0.shape[1], kv0.shape[0]
    half = rows // 2
    grid, part, pack, logs, kv, docs = attend_specs(rows, keys, kdoc0.shape[0])
    return pl.pallas_call(
        partial(attend_back_kernel, blocks),
        grid=grid,
        in_specs=SCALARS + [part(PAIR), pack, part(PAIR), logs, kv, kv, docs, docs],
        out_specs=[part(PAIR), kv, kv],
        out_shape=[
            shape((NZ, 2, 2, half, PAIR), WIDE),
            shape((keys, PAIR), WIDE),
            shape((keys, PAIR), WIDE),
        ],
        scratch_shapes=[pltpu.VMEM((keys, 1), WIDE)] * 2,
        compiler_params=PARAMS,
        cost_estimate=cost("attend_back"),
        name="attend_back",
    )(
        index, lens, queries.reshape(NZ, 2, 2, half, PAIR), grads, out, log_total, kv0, kv1,
        kdoc0, kdoc1,
    )


def branch_kernel(pieces, idx, got, *refs):
    slabs, (low, part, held, sems) = refs[:pieces], refs[pieces:]
    copy = piece_copies(idx, slabs, held, sems)
    start(copy)
    half = got.shape[1]
    for h in range(NZ * 2):
        lanes = slice(h * HEAD_DIM, (h + 1) * HEAD_DIM)
        low[:half, lanes] = got[h, :, :HEAD_DIM]
        low[half:, lanes] = got[h, :, HEAD_DIM:]
    part[...] = dot_nt(low[...], finish(copy, held)).astype(LOW)


def normalize(value):
    center = value - jnp.mean(value, axis=-1, keepdims=True)
    spread = jnp.mean(center * center, axis=-1, keepdims=True)
    inverse = lax.rsqrt(spread + NORM_EPSILON)
    return center * inverse, inverse


def pair(own, other):
    return own[...].astype(WIDE) + other[...].astype(WIDE)


def forward_kernel(
    idx, own, other, tokens, bias, gain, shift, hidden_bias, attended, slabs,
    first, unitary, inverse, hidden_in, keep, send, part,
    low, hidden, expand, sems1, contract, sems2,
):
    copy1 = [slab_copy(slabs, 0, expand, sems1)]
    copy2 = [slab_copy(slabs, expand.shape[1], contract, sems2)]
    start(copy1 + copy2)
    value = tokens[...].astype(WIDE) + (pair(own, other) + bias[...])
    unitary[...], inverse[...] = normalize(value)
    first[...] = unitary[...] * gain[...] + shift[...]
    low[...] = first[...].astype(LOW)
    value = dot_nn(low[...], finish(copy1, expand)) + hidden_bias[...]
    hidden_in[...] = value
    hidden[...] = (0.5 * value * (1.0 + lax.erf(value * (0.5**0.5)))).astype(LOW)
    part[...] = dot_nt(hidden[...], finish(copy2, contract)).astype(LOW)
    rows, width = low.shape
    few = rows * QUAD // width
    for out, x in ((keep, idx[2]), (send, 1 - idx[2])):
        out[:rows, :] = low[...]
        out[rows : 2 * rows, :] = columns_of(hidden, x, width)
        for i in range(width // QUAD):
            out[2 * rows :, i * QUAD : (i + 1) * QUAD] = attended[
                i * few : (i + 1) * few, pl.ds(pl.multiple_of(x * QUAD, QUAD), QUAD)
            ]


def columns_of(ref, x, span):
    return ref[:, pl.ds(pl.multiple_of(x * span, 128), span)]


def unit_scale(value):
    return lax.rsqrt(jnp.sum(value * value, axis=-1, keepdims=True) + UNIT_EPSILON)


def second_kernel(
    idx, own, other, first, bias, gain, shift, head, query, kdoc,
    low, unitary, inverse, embed, unit, expo, totals, message,
):
    value = first[...] + (pair(own, other) + bias[...])
    unitary[...], inverse[...] = normalize(value)
    low[...] = (unitary[...] * gain[...] + shift[...]).astype(LOW)
    embed[...] = dot_nn(low[...], head[...].astype(LOW))
    unit[...] = (embed[...] * unit_scale(embed[...])).astype(LOW)
    message[...] = unit[...].astype(WIDE)
    expo[...] = jnp.exp(dot_nt(unit[...], query[...]) / SOFTMAX_TEMPER)
    totals[...] = dot_nn(member(idx, kdoc, totals.shape[0]), expo[...], PRECISE)


def query_kernel(idx, vecs, out, own):
    block, shares = (idx[1] * 2 + idx[2]) * 2 + idx[3], own.shape[0]
    own[...] = vecs[pl.ds(pl.multiple_of(block * shares, shares), shares), :]
    value = vecs[...].astype(WIDE)
    out[...] = (value * unit_scale(value)).astype(LOW)


def member(idx, kdoc, docs):
    row = kdoc[pl.ds((idx[0] * NZ + idx[1]) * 2 + idx[2], 1), :]
    label = lax.broadcasted_iota(jnp.int32, (docs, row.shape[1]), 0)
    return jnp.where(row == label, 1.0, 0.0)


def group_sum(value, length):
    column = lax.broadcasted_iota(jnp.int32, value.shape, 1)
    span = value.shape[1]
    step = 1
    while step < length:
        ahead, behind = pltpu.roll(value, span - step, 1), pltpu.roll(value, step, 1)
        value = value + jnp.where((column & step) == 0, ahead, behind)
        step *= 2
    return value


def loss_of(count, totals, kdocs, positive):
    docs, columns = totals.shape
    length = columns // count
    label = lax.broadcasted_iota(jnp.int32, (docs, 1), 0)
    tokens = jnp.zeros((docs, 1), WIDE)
    for ref in kdocs:
        tokens = tokens + jnp.sum(jnp.where(key_row(ref) == label, 1.0, 0.0), axis=1, keepdims=True)
    doc_score = group_sum(SOFTMAX_TEMPER * (jnp.log(totals) - jnp.log(tokens)), length)
    best = jnp.max(doc_score, axis=0, keepdims=True)
    shifted = jnp.exp(doc_score - best)
    shifted_sum = jnp.sum(shifted, axis=0, keepdims=True)
    chosen = jnp.where(label == positive, 1.0, 0.0)
    each = best + jnp.log(shifted_sum) - jnp.sum(doc_score * chosen, axis=0, keepdims=True)
    loss = jnp.sum(each, axis=1, keepdims=True) / columns
    return loss, (shifted / shifted_sum - chosen) / (totals * count)


def unit_back(value, grad):
    scale = unit_scale(value)
    along = jnp.sum(grad * value, axis=-1, keepdims=True)
    return scale * grad - value * (along * scale * scale * scale)


def query_back_kernel(half, idx, kdoc0, kdoc1, coefficients, value, units, got, out):
    shares = value.shape[0]
    block = (idx[1] * 2 + idx[2]) * 2 + idx[3]
    columns_here = pl.ds(pl.multiple_of(block * shares, shares), shares)
    coefficient = coefficients[:, columns_here]
    docs = coefficient.shape[0]
    pads = jnp.zeros((-docs % 8, shares), WIDE)
    coefficient = jnp.transpose(jnp.concatenate([coefficient, pads]) if docs % 8 else coefficient)
    queries = value[...].astype(WIDE)
    query = (queries * unit_scale(queries)).astype(LOW)
    rows, group = kdoc0.shape[1], 4
    count = units.shape[0] // rows

    def add(at, total):
        labels = []
        for step in range(group):
            block = at * group + step
            spot = block // 2
            labels.append(
                jnp.where(block % 2 == idx[3], kdoc0[pl.ds(spot, 1), :], kdoc1[pl.ds(spot, 1), :])
            )
        row = jnp.concatenate(labels, axis=1)
        unit = units[pl.ds(at * group * rows, group * rows), :].astype(LOW)
        if docs <= 8:
            chosen = jnp.zeros((shares, group * rows), WIDE)
            for doc in range(docs):
                chosen = jnp.where(row == doc, coefficient[:, doc : doc + 1], chosen)
        else:
            label = lax.broadcasted_iota(jnp.int32, (coefficient.shape[1], group * rows), 0)
            chosen = dot_nn(coefficient, jnp.where(row == label, 1.0, 0.0), PRECISE)
        expo = jnp.exp(dot_nt(query, unit) / SOFTMAX_TEMPER)
        return total + dot_nn((chosen * expo).astype(LOW), unit)

    steps, total = count // group, jnp.zeros(queries.shape, WIDE)
    if steps <= 4:
        for at in range(steps):
            total = add(at, total)
    else:
        total = lax.fori_loop(0, steps, add, total)
    out[:shares, :] = unit_back(queries, total).astype(LOW)
    sums = [got[spot, half:, :].astype(WIDE) for spot in range(NZ * 2)]
    while len(sums) > 1:
        sums = [a + b for a, b in zip(sums[::2], sums[1::2])]
    out[shares:, :] = sums[0].astype(LOW)


def spread_kernel(idx, got, queries, head, *vectors):
    rows = got.shape[1]
    chunk = head.shape[0] // (NZ * 4)
    shares = rows - chunk - 16
    pieces = []
    for i in range(NZ * 4):
        queries[i * shares : (i + 1) * shares, :] = got[i, :shares, :].astype(WIDE)
        head[i * chunk : (i + 1) * chunk, :] = got[i, shares : shares + chunk, :].astype(WIDE)
        pieces.append(got[i, shares + chunk : shares + chunk + 16, :].astype(WIDE))
    row = 0
    for out in vectors:
        for i in range(0, out.shape[0], 8):
            out[i : i + 8, :] = pieces[row // 16][row % 16 : row % 16 + 8]
            row += 8


def norm_back(grad, gain, unitary, inverse):
    scaled = grad * gain
    along = jnp.mean(scaled * unitary, axis=-1, keepdims=True)
    return inverse * (scaled - jnp.mean(scaled, axis=-1, keepdims=True) - unitary * along)


def column_sum(value):
    return jnp.sum(value, axis=0, keepdims=True)


def middle_kernel(
    count, idx, t0, t1, t2, t3, kdoc0, kdoc1, positive, expo, query, unit,
    embed, low, head, cotangent, unitary, inverse, gain, hidden_in, slabs,
    grad_in, keep, send, part, loss, coefficients, sums0, sums1,
    similar, grad_low, grad_hidden_in, head_part, rows_part, expand, sems1, contract, sems2,
):
    copy1 = [slab_copy(slabs, 0, expand, sems1)]
    copy2 = [slab_copy(slabs, expand.shape[1], contract, sems2)]
    start(copy2 + copy1)
    totals = (t0[...] + t1[...]) + (t2[...] + t3[...])
    value, coefficient = loss_of(count, totals, (kdoc0, kdoc1), positive[...])
    loss[...] = jnp.broadcast_to(value, loss.shape)
    coefficients[...] = coefficient
    here = member(idx, kdoc0, totals.shape[0])
    similar[...] = (dot_tn(here, coefficient, PRECISE) * expo[...]).astype(LOW)
    grad_embed = unit_back(embed[...], dot_nn(similar[...], query[...])).astype(LOW)
    rows, width = embed.shape[0], low.shape[1]
    head_part[...] = dot_tn(low[...], grad_embed)
    grad_second = dot_nt(grad_embed, head[...].astype(LOW)) + cotangent[...].astype(WIDE)
    grad_in[...] = norm_back(grad_second, gain[...], unitary[...], inverse[...])
    grad_low[...] = grad_in[...].astype(LOW)
    sums = [
        column_sum(grad_low[...].astype(WIDE)),
        column_sum(grad_second * unitary[...]),
        column_sum(grad_second),
    ]
    value = hidden_in[...]
    grad = dot_nn(grad_low[...], finish(copy2, contract))
    bell = jnp.exp(-0.5 * value * value) * (1.0 / math.sqrt(2.0 * math.pi))
    slope = 0.5 * (1.0 + lax.erf(value * (0.5**0.5))) + value * bell
    grad_hidden_in[...] = (slope * grad).astype(LOW)
    sums.append(column_sum(grad_hidden_in[...].astype(WIDE)))
    part[...] = dot_nt(grad_hidden_in[...], finish(copy1, expand)).astype(LOW)
    for out, x in ((keep, idx[2]), (send, 1 - idx[2])):
        out[:rows, :] = grad_low[...]
        out[rows:, :] = columns_of(grad_hidden_in, x, width)
    rows_part[...] = jnp.zeros_like(rows_part)
    at = 0
    for value in sums:
        for i in range(value.shape[1] // PAIR):
            rows_part[at : at + 1, :] = value[:, i * PAIR : (i + 1) * PAIR]
            at += 1
    chunk = width // (NZ * 4)
    for spot in range(NZ * 2):
        for out, c in ((sums0, idx[3]), (sums1, 1 - idx[3])):
            at = spot * 2 + c
            out[spot, :chunk, :] = head_part[
                pl.ds(pl.multiple_of(at * chunk, chunk), chunk), :
            ].astype(out.dtype)
            out[spot, chunk:, :] = rows_part[pl.ds(pl.multiple_of(at * 16, 16), 16), :].astype(
                out.dtype
            )


def slab_products(idx, left, right, outs):
    slab = outs[0].shape[-2]
    for z, out in enumerate(outs):
        mine = []
        for x in range(2):
            spot = (idx[1] ^ z) * 2 + (idx[2] ^ x)
            lanes = left[:, pl.ds(pl.multiple_of(spot * 2 * slab, 2 * slab), 2 * slab)]
            mine.append(jnp.where(idx[3] == 0, lanes[:, :slab], lanes[:, slab:]))
        both_rows = dot_tn(jnp.concatenate(mine, axis=1), right)
        for x in range(2):
            out[x] = both_rows[x * slab : (x + 1) * slab].astype(out.dtype)


def weights_kernel(idx, f0, f1, f2, f3, g0, g1, g2, g3, *refs):
    keep0, send0, keep1, send1, left, right = refs
    rows = g0.shape[0] // 2
    firsts, grads = (f0, f1, f2, f3), (g0, g1, g2, g3)
    for keep, send, lefts, rights in ((keep0, send0, grads, firsts), (keep1, send1, firsts, grads)):
        for i in range(4):
            left[i * rows : (i + 1) * rows, :] = lefts[i][:rows, :]
            right[i * rows : (i + 1) * rows, :] = rights[i][rows : 2 * rows, :]
        slab_products(idx, left, right[...], [keep.at[0], send.at[0], keep.at[1], send.at[1]])


def pair_kernel(idx, *refs):
    count = (len(refs) - 1) // 3
    gots, owns, send, at = refs[: 2 * count], refs[2 * count : -1], refs[-1], 0
    for i, own in enumerate(owns):
        keep, got, span = gots[2 * i], gots[2 * i + 1], own.shape[-1]
        own[...] = keep[0] + got[0].astype(WIDE)
        send[:, :, at : at + span] = (keep[1] + got[1].astype(WIDE)).astype(LOW)
        at += span


def output_kernel(idx, f0, f1, f2, f3, g0, g1, g2, g3, keep, send, left, right):
    rows, width = g0.shape
    few = rows * QUAD // width
    for i, (f, g) in enumerate(zip((f0, f1, f2, f3), (g0, g1, g2, g3))):
        left[i * rows : (i + 1) * rows, :] = g[...]
        for j in range(width // QUAD):
            right[i * rows + j * few : i * rows + (j + 1) * few, :] = f[
                2 * rows :, j * QUAD : (j + 1) * QUAD
            ]
    slab_products(idx, left, right[...], [keep.at[0], send.at[0], keep.at[1], send.at[1]])


def line_sum_kernel(idx, own0, got0, own1, own2, got, keep, keep_out, send):
    at = 0
    for own, other, out in (
        (own0, got0[...], keep.at[0]),
        (own1, got[:, :, : own1.shape[-1]], keep.at[1]),
        (own2, got[:, :, own1.shape[-1] :], keep_out),
    ):
        span = own.shape[-1]
        out[...] = own[0] + other[0].astype(WIDE)
        send[:, at : at + span] = (own[1] + other[1].astype(WIDE)).astype(LOW)
        at += span


def columns_kernel(idx, keep, keep_out, got, contract, expand, output):
    span = keep.shape[-1]
    for at, mine, out in ((0, keep[0], contract), (span, keep[1], expand), (2 * span, keep_out[...], output)):
        cols = mine.shape[1]
        out[:, pl.ds(pl.multiple_of(idx[2] * cols, 128), cols)] = mine
        out[:, pl.ds(pl.multiple_of((1 - idx[2]) * cols, 128), cols)] = got[
            :, at : at + cols
        ].astype(WIDE)


def first_back_kernel(
    pieces, idx, own, other, grad_second_in, unitary, inverse, gain, sums0, sums1, *refs
):
    slabs, (grad_in, grad_low, vectors, pack, held, sems) = refs[:pieces], refs[pieces:]
    copy = piece_copies(idx, slabs, held, sems)
    start(copy)
    grad_first = grad_second_in[...] + pair(own, other)
    grad_in[...] = norm_back(grad_first, gain[...], unitary[...], inverse[...])
    grad_low[...] = grad_in[...].astype(LOW)
    vectors[...] = jnp.zeros_like(vectors)
    vectors[0:1, :] = column_sum(grad_low[...].astype(WIDE))
    vectors[1:2, :] = column_sum(grad_first * unitary[...])
    vectors[2:3, :] = column_sum(grad_first)
    grad = dot_nn(grad_low[...], finish(copy, held)).astype(LOW)
    half = grad.shape[0] // 2
    for h in range(NZ * 2):
        lanes = slice(h * HEAD_DIM, (h + 1) * HEAD_DIM)
        pack[h, :half, :HEAD_DIM] = grad[:half, lanes]
        pack[h, :half, HEAD_DIM:] = grad[half:, lanes]
        pack[h, half:, :] = (sums0[h] + sums1[h].astype(WIDE)).astype(LOW)


def triple_kernel(idx, dq, dkv, got, cosine, sine, out, dense):
    rows = dq.shape[0]
    low_lanes = lax.broadcasted_iota(jnp.int32, (rows, PAIR), 1) < HEAD_DIM
    grads = dkv[...] + got[...]
    both_parts = jnp.where(low_lanes, dq[...], pltpu.roll(grads, HEAD_DIM, 1))
    turned = turn(both_parts, cosine[...], -sine[...])
    turned, value = turned.astype(LOW), grads[:, HEAD_DIM:].astype(LOW)
    out[:, :PAIR] = turned
    out[:, PAIR:] = jnp.where(low_lanes, 0.0, grads).astype(LOW)
    rows = dense.shape[1] * 4 // 3
    half, few = rows // 2, rows // 4
    for i in range(dense.shape[0]):
        at = i * rows
        dense[i, :half, :PAIR] = turned[at : at + half]
        dense[i, :half, PAIR:] = turned[at + half : at + rows]
        for j in range(4):
            dense[i, half:, j * HEAD_DIM : (j + 1) * HEAD_DIM] = value[
                at + j * few : at + (j + 1) * few
            ]


def extra_rows(bias, vectors):
    cols = bias.shape[1]
    rows = [bias]
    for i in range(3):
        for j in range(vectors.shape[1] // cols):
            rows.append(vectors[i : i + 1, j * cols : (j + 1) * cols])
    return jnp.concatenate(rows + [jnp.zeros((16 - len(rows), cols), WIDE)], axis=0)


def triple_weight_kernel(idx, *refs):
    sheets, (grad, vectors, keep, send, total, held) = refs[:8], refs[8:]
    mc = idx[3]
    slab = HEAD_DIM
    for value, at in sheet_rows(idx, sheets):
        held[at, :] = value
    total[...] = dot_tn(held[...], grad[...])
    extra = extra_rows(column_sum(grad[...].astype(WIDE)), vectors).astype(LOW)
    for spot in range(NZ * 2):
        for out, c in ((keep, mc), (send, 1 - mc)):
            at = pl.ds(pl.multiple_of((spot * 2 + c) * slab, slab), slab)
            out[spot, :slab, :] = total[at, :].astype(LOW)
            put_extra(out.at[spot], slab, extra)


def pair_sum_kernel(idx, one, two, out):
    out[...] = (one[...].astype(WIDE) + two[...].astype(WIDE)).astype(out.dtype)


def triple_out_kernel(idx, got, weight, bias, *vectors):
    slab = weight.shape[1]
    total = 0.0
    for spot in range(NZ * 2):
        at = spot * HEAD_DIM
        here, extra = got[spot].astype(WIDE), get_extra(got.at[spot], slab).astype(WIDE)
        for part, lane in enumerate(LANES):
            weight[part, :, at : at + HEAD_DIM] = here[:slab, lane : lane + HEAD_DIM]
            bias[part : part + 1, at : at + HEAD_DIM] = extra[:1, lane : lane + HEAD_DIM]
        total = total + extra
    row = 1
    for out in vectors:
        for i in range(0, out.shape[0], 2):
            out[i : i + 1, :] = total[row : row + 1, :PAIR]
            out[i + 1 : i + 2, :] = total[row : row + 1, PAIR:]
            row += 1


def tokens_kernel(idx, got, message, part, group, held, sems):
    copy = slab_copy(message, 0, held, sems)
    copy.start()
    rows = part.shape[0]
    half, few = rows // 2, rows // 4
    for h in range(NZ * 2):
        for p in range(2):
            at = (p * NZ * 2 + h) * HEAD_DIM
            for i in range(2):
                lane = i * PAIR + p * HEAD_DIM
                group[i * half : (i + 1) * half, at : at + HEAD_DIM] = got[
                    h, :half, lane : lane + HEAD_DIM
                ]
        at = (2 * NZ * 2 + h) * HEAD_DIM
        for j in range(4):
            group[j * few : (j + 1) * few, at : at + HEAD_DIM] = got[
                h, half:, j * HEAD_DIM : (j + 1) * HEAD_DIM
            ]
    copy.wait()
    part[...] = dot_nt(group[...], held[...]).astype(LOW)


def tokens_sum_kernel(idx, own, other, grad, out):
    out[...] = grad[...] + pair(own, other)


def shards(
    tokens,
    query_vecs,
    out_cotangent,
    doc_lengths,
    live_mask,
    positives,
    triple_weight,
    triple_bias,
    output_weight,
    output_bias,
    first_gain,
    first_shift,
    expand_weight,
    expand_bias,
    contract_weight,
    contract_bias,
    second_gain,
    second_shift,
    head_weight,
):
    outer = lax.axis_size("o")
    mo, mz, mx, mc, my = [lax.axis_index(a) for a in ("o", "z", "x", "c", "y")]
    index = jnp.stack([mo, mz, mx, mc, my]).astype(jnp.int32)
    rows, width = tokens.shape
    half = rows // 2
    slab = triple_weight.shape[0]
    docs = doc_lengths.shape[0]
    queries_count = positives.shape[0]
    blocks = outer * NZ * 4
    span = expand_weight.shape[1]
    quarter = span // 2
    proj = head_weight.shape[1]
    line = lambda vector: vector.reshape(1, -1)

    def widen(value):
        return lax.all_gather(value, "o") if outer > 1 else value[None]

    def narrow(value):
        return lax.psum_scatter(value, "o") if outer > 1 else value[0]

    def sum_outer(value):
        return lax.psum(value, "o") if outer > 1 else value

    def stage(work):
        like = jax.eval_shape(work)
        idle = lambda: jax.tree.map(lambda leaf: jnp.zeros(leaf.shape, leaf.dtype), like)
        return lax.cond(doc_lengths[0] >= 0, work, idle)

    def key_doc(live, c):
        block = jnp.arange(outer * NZ * 2, dtype=jnp.int32) * 2 + c
        doc = doc_layout(doc_lengths, block[:, None] + where[None, :])[0]
        return jnp.where(live > 0, doc, -1)

    def head_weights(heads, heads_other):
        if outer > 1:
            pack = widen(both(heads, heads_other, mc)).transpose(0, 2, 1, 3, 4)
            head_triple = pack[..., :slab, :].reshape(width, QUAD)
            live0, live1 = [
                pick(pack, c, 2)[..., slab, :rows].astype(WIDE).reshape(-1, rows)
                for c in (mc, 1 - mc)
            ]
        else:
            head_triple, live0, live1 = whole(
                heads_kernel,
                "heads",
                index,
                (heads, heads_other),
                [shape((width, QUAD), LOW)] + [shape((NZ * 2, rows), WIDE)] * 2,
            )
        return head_triple, key_doc(live0, mc), key_doc(live1, 1 - mc)

    few_out = slab // 2 if outer == 1 else 0
    heads, low_slab, triple_slab, mine, own = whole(
        prep_kernel,
        "prep",
        index,
        (
            triple_weight.transpose(1, 0, 2),
            output_weight.T,
            expand_weight,
            contract_weight.T,
            line(live_mask),
            tokens,
        ),
        [shape((NZ * 2, slab + extra_count(slab), QUAD), LOW)]
        + [shape((slab, n), LOW) for n in (2 * span, 6 * QUAD)]
        + [shape((half + few_out, width), LOW), shape((rows + few_out, width), LOW)],
    )
    by_z = [mine] + [xor_z(mine, m) for m in (1, 2, 3)]
    own_other = flip(own, "x")

    where = jnp.arange(rows, dtype=jnp.int32) * blocks
    rank = jnp.arange(NZ * 2, dtype=jnp.int32) * 2
    shares = query_vecs.shape[0] // (NZ * 4)
    by_z = list(lax.optimization_barrier((*by_z, heads, own_other))[:NZ])
    gathered = lax.all_gather(after(low_slab, *by_z[1:]), BLK, axis=0, tiled=True)

    def heads_stage():
        got = lax.all_to_all(heads, ("z", "x"), 0, 0)
        sheets, outs = [tokens, own_other], [own[rows:], own_other[rows:]]
        for piece in by_z[1:]:
            turned = flip(piece, "x")
            outs += [piece[half:], turned[half:]]
            two = jnp.stack([piece[:half], turned[:half]])
            sheets += [two, flip(two, "y")]
        if outer > 1:
            out_low = output_weight.T.astype(LOW)
            outs = [lax.all_gather(out_low, BLK, axis=0, tiled=True)]
        else:
            outs = [jnp.stack(outs)]
            outs.append(flip(outs[0], "c"))
        own_places = (mo * NZ * 4 + rank + mc)[:, None] + where[None, :]
        own_position = doc_layout(doc_lengths, own_places.reshape(-1))[1]
        lane = jnp.arange(PAIR) % (HEAD_DIM // 2)
        exponent = (2 * lane).astype(WIDE) / HEAD_DIM
        angles = own_position.astype(WIDE)[:, None] * jnp.exp(-math.log(10000.0) * exponent)[None, :]
        sign = jnp.where(jnp.arange(PAIR) % HEAD_DIM < HEAD_DIM // 2, -1.0, 1.0).astype(WIDE)
        tables = jnp.cos(angles), jnp.sin(angles) * sign[None, :]
        units = whole(
            query_kernel,
            "query_units",
            index,
            (query_vecs,),
            [shape(query_vecs.shape, LOW), shape((shares, proj), LOW)],
        )
        positive = line(jnp.repeat(positives, query_vecs.shape[0] // queries_count))
        got = after(got, sheets[3], sheets[5], sheets[7], tables[0], units[0])
        head = head_weights(got, flip(got, "c"))
        return head, outs, sheets[2:], tables, list(units), positive

    head, outs, sheets, (cosine, sine), (query_unit, own_queries), positive = stage(heads_stage)
    outs = tuple(outs)
    head_triple, kdoc0, kdoc1 = head
    pieces = len(outs)
    sheets = [tokens, own_other] + sheets
    positive = lax.optimization_barrier(positive)
    count = NZ * 2 * rows

    def project_stage():
        queries, kv = whole(
            project_kernel,
            "project",
            index,
            (*sheets, head_triple, cosine, sine, triple_bias),
            [shape((count, PAIR), LOW)] * 2,
            [pltpu.VMEM((count, width), LOW)],
        )
        return queries, kv, flip(kv, "c")

    queries, kv, kv_other = stage(project_stage)
    kv0, kv1 = [widen(v).reshape(-1, PAIR) for v in (kv, kv_other)]
    meta = (kdoc0, kdoc1)
    steps = (blocks, index, doc_lengths)

    def to_blocks(value):
        return lax.all_to_all(value.reshape((NZ * 2,) + value.shape[-2:]), ("z", "x"), 0, 0)

    def attention_stage():
        out, log_total, pack = attend(*steps, queries, kv0, kv1, *meta)
        return out, log_total, to_blocks(pack)

    out, log_total, pack = stage(attention_stage)
    wide_rows, low_rows, thin_rows = [shape((rows, n), t) for n, t in ((width, WIDE), (width, LOW), (1, WIDE))]
    def branch_stage():
        low, part = whole(
            partial(branch_kernel, pieces),
            "branch",
            index,
            (pack,),
            [shape((rows, 2 * QUAD), LOW), low_rows],
            piece_scratch(width, 2 * QUAD),
            outs,
        )
        return low, part, flip(part, "y")

    attended_low, part, part_other = stage(branch_stage)
    gathered = after(gathered, part)
    both_slabs = slab_scratch(width, span) * 2
    triple_low = lax.all_gather(after(triple_slab, part), BLK, axis=0, tiled=True)
    few = rows * QUAD // width
    first, unitary1, inverse1, hidden_in, keep, send, part = whole(
        forward_kernel,
        "forward",
        index,
        (
            part, part_other, tokens, line(output_bias), line(first_gain), line(first_shift),
            line(expand_bias), attended_low,
        ),
        [wide_rows, wide_rows, thin_rows, shape((rows, span), WIDE)]
        + [shape((2 * rows + few, width), LOW)] * 2
        + [low_rows],
        [pltpu.VMEM((rows, width), LOW), pltpu.VMEM((rows, span), LOW)] + both_slabs,
        (gathered,),
    )

    def over_z(parts):
        return [parts[0]] + [xor_z(parts[m], m) for m in (1, 2, 3)]

    def four_cores(keep, send):
        two = [keep, flip(send, "x")]
        return two + [flip(value, "c") for value in two]

    first_keep, first_other, first_across = keep, flip(send, "x"), flip(keep, "c")
    my_tokens = query_unit.shape[0]

    def second_stage():
        return whole(
            second_kernel,
            "second",
            index,
            (
                part, flip(part, "y"), first, line(contract_bias), line(second_gain),
                line(second_shift), head_weight, query_unit, kdoc0,
            ),
            [low_rows, wide_rows, thin_rows] + [shape((rows, proj), t) for t in (WIDE, LOW)]
            + [shape((rows, my_tokens), WIDE), shape((docs, my_tokens), WIDE)]
            + [shape((rows, proj), WIDE)],
        )

    second_low, unitary2, inverse2, embed, unit_low, expo, totals, message = stage(second_stage)
    totals = after(totals, first_across)

    def tree(own, one, two, three):
        return (own + one) + (two + three)

    chunk = width // (NZ * 4)
    sums_dims = (NZ * 2, chunk + 16, proj)
    def middle_stage():
        sums = sum_outer(tree(totals, *[xor_s(totals, m) for m in (1, 2, 3)]))
        return whole(
            partial(middle_kernel, queries_count),
            "middle",
            index,
            (
                sums, *[xor_z(sums, m) for m in (1, 2, 3)], kdoc0, kdoc1, positive, expo, query_unit,
                unit_low, embed, second_low, head_weight, out_cotangent, unitary2, inverse2,
                line(second_gain), hidden_in,
            ),
            [wide_rows]
            + [shape((2 * rows, width), LOW)] * 2
            + [low_rows, shape((8, proj), WIDE), shape((docs, my_tokens), WIDE)]
            + [shape(sums_dims, WIDE), shape(sums_dims, LOW)],
            [
                pltpu.VMEM((rows, my_tokens), LOW),
                pltpu.VMEM((rows, width), LOW),
                pltpu.VMEM((rows, span), LOW),
                pltpu.VMEM((width, proj), WIDE),
                pltpu.VMEM((NZ * 4 * 16, proj), WIDE),
            ]
            + both_slabs,
            (gathered,),
        )

    grad_second_in, keep, send, part, loss, coefficients, sums_own, sums_send = stage(middle_stage)

    triple_low, part, first_other = lax.optimization_barrier((triple_low, part, first_other))
    units = lax.all_gather(after(message, part), BLK, axis=0, tiled=True)
    keep_other, keep_across = flip(send, "x"), flip(keep, "c")

    def first_stage():
        return whole(
            partial(first_back_kernel, pieces),
            "first_back",
            index,
            (
                part, flip(part, "y"), grad_second_in, unitary1, inverse1, line(first_gain),
                sums_own, flip(sums_send, "c"),
            ),
            [wide_rows, low_rows, shape((8, width), WIDE)]
            + [shape((NZ * 2, half + chunk + 16, PAIR), LOW)],
            piece_scratch(width, 2 * QUAD),
            outs,
        )

    grad_first_in, grad_branch, vectors1, pack = stage(first_stage)
    keep_other = after(keep_other, grad_branch)
    dims, dims_out = (2, slab, quarter), (2, slab, QUAD)
    dims_both = (2, slab, quarter + QUAD)
    left_right = [pltpu.VMEM((4 * rows, width), LOW)]

    def parts_of(left, right):
        part = dot_tn(jnp.concatenate(left), jnp.concatenate(right))
        part = pick(narrow(part.reshape(outer, NZ, 2, 2, slab, -1)), mc, 2)
        for axis, spot in ((0, mz), (1, mx)):
            part = jnp.take(part, jnp.arange(part.shape[axis]) ^ spot, axis=axis)
        return part

    def low_parts(parts):
        return [parts[0]] + [parts[m].astype(LOW) for m in (1, 2, 3)]

    def weights_stage():
        got = to_blocks(pack)
        firsts = [first_keep, first_other, first_across, flip(first_other, "c")]
        grads = [keep, keep_other, keep_across, flip(keep_other, "c")]
        other = flip(grad_branch, "x")
        got = got, [other, flip(grad_branch, "c"), flip(other, "c")], firsts[3]
        if outer == 1:
            parts = whole(
                weights_kernel,
                "weights",
                index,
                (*firsts, *grads),
                [shape((2,) + dims, WIDE), shape((2,) + dims, LOW)] * 2,
                left_right * 2,
            )
            return got, list(parts)
        top, mid = slice(0, rows), slice(rows, 2 * rows)
        contract = parts_of([g[top] for g in grads], [f[mid] for f in firsts])
        expand = parts_of([f[top] for f in firsts], [g[mid] for g in grads])
        return got, [part for p in (contract, expand) for part in (p[::2], p[1::2].astype(LOW))]

    (grad_out, branches, first_last), weight_parts = stage(weights_stage)
    branches = [grad_branch] + branches
    firsts = [first_keep, first_other, first_across, first_last]
    contract_keep, contract_send, expand_keep, expand_send = weight_parts
    contract_got, expand_got = xor_z(contract_send, 1), xor_z(expand_send, 1)

    def attend_stage():
        grad_query, dkv0, dkv1 = attend_back(
            *steps, queries, grad_out.reshape(NZ, 2, -1, PAIR), out, log_total, kv0, kv1, *meta
        )
        dkv0, dkv1 = [narrow(v.reshape(outer, -1, PAIR)) for v in (dkv0, dkv1)]
        triple = whole(
            triple_kernel,
            "triple",
            index,
            (grad_query.reshape(count, PAIR), dkv0, flip(dkv1, "c"), cosine, sine),
            [shape((count, QUAD), LOW), shape((NZ * 2, rows * 3 // 4, QUAD), LOW)],
        )
        return triple

    grad_triple, dense_triple = stage(attend_stage)
    grad_triple, contract_got = lax.optimization_barrier((grad_triple, contract_got))
    contract_own, contract_send = whole(
        pair_kernel, "pair", index, (contract_keep, contract_got), [shape(dims, t) for t in (WIDE, LOW)]
    )
    contract_got = xor_z(contract_send, 2)
    grad_triple, units = lax.optimization_barrier((grad_triple, units, contract_own))[:2]
    dims_triple = (NZ * 2, slab + extra_count(slab), QUAD)
    vector = shape((width // PAIR, PAIR), WIDE)

    def triple_parts():
        if outer == 1:
            return whole(
                triple_weight_kernel,
                "triple_weight",
                index,
                (*sheets, grad_triple, vectors1),
                [shape(dims_triple, LOW)] * 2,
                [pltpu.VMEM((width, QUAD), WIDE), pltpu.VMEM((count, width), LOW)],
            )
        ordered = [(mz * 2 + (mx ^ x), sheets[x]) for x in range(2)]
        for m in (1, 2, 3):
            two = both(*sheets[2 * m : 2 * m + 2], my)
            for x in range(2):
                ordered.append(((mz ^ m) * 2 + (mx ^ x), two[:, x].reshape(rows, width)))
        ordered = place(ordered).reshape(count, width)
        part = narrow(dot_tn(ordered, grad_triple).reshape(outer, NZ * 2, 2, slab, QUAD))
        bias = sum_outer(jnp.sum(grad_triple, axis=0, dtype=WIDE))
        bias = extra_rows(line(bias), sum_outer(vectors1))
        bias = jnp.broadcast_to(bias, (NZ * 2, 2, 16, QUAD))
        part = jnp.concatenate([part, bias], axis=2).astype(LOW)
        return pick(part, mc, 1), pick(part, 1 - mc, 1)

    def output_parts_of():
        if outer == 1:
            return whole(
                output_kernel,
                "output",
                index,
                (*firsts, *branches),
                [shape((2,) + dims_out, t) for t in (WIDE, LOW)],
                left_right + [pltpu.VMEM((4 * rows, QUAD), LOW)],
            )
        wide = [f[2 * rows :].reshape(few, 4, QUAD).transpose(1, 0, 2).reshape(rows, QUAD) for f in firsts]
        parts = parts_of(branches, wide)
        return parts[::2], parts[1::2].astype(LOW)

    def triple_stage():
        block_triple = to_blocks(dense_triple)
        keep, send = triple_parts()
        output_parts = output_parts_of()
        mine = whole(
            partial(query_back_kernel, half),
            "query_back",
            index,
            (kdoc0, kdoc1, coefficients, own_queries, units, sum_outer(grad_out)),
            [shape((shares + chunk + 16, proj), LOW)],
        )[0]
        return block_triple, keep, send, output_parts[0], xor_z(output_parts[1], 1), mine

    block_triple, packed_keep, packed_send, output_keep, output_got, mine = stage(triple_stage)
    block_triple, contract_got, expand_got = lax.optimization_barrier(
        (block_triple, contract_got, expand_got)
    )
    expand_own, output_own, both_send = whole(
        pair_kernel,
        "pair",
        index,
        (expand_keep, expand_got, output_keep, output_got),
        [shape(dims, WIDE), shape(dims_out, WIDE), shape(dims_both, LOW)],
    )
    both_got = xor_z(both_send, 2)
    block_triple = after(block_triple, expand_own)
    spread = lax.all_gather(after(mine, expand_own), ("z", "x", "c"))

    def tokens_stage():
        part = whole(
            tokens_kernel,
            "tokens",
            index,
            (block_triple,),
            [low_rows],
            [pltpu.VMEM((rows, 6 * QUAD), LOW)] + slab_scratch(width, 6 * QUAD),
            (triple_low,),
        )[0]
        part_other = flip(part, "y")
        packed = whole(
            pair_sum_kernel,
            "pair_sum",
            index,
            (packed_keep, flip(packed_send, "c")),
            [shape(dims_triple, LOW)],
        )[0]
        tokens_grad = whole(
            tokens_sum_kernel, "tokens_sum", index, (after(part, packed), part_other, grad_first_in), [wide_rows]
        )[0]
        return tokens_grad, packed

    tokens_grad, packed = stage(tokens_stage)
    packed = lax.all_to_all(after(packed, tokens_grad), ("z", "x"), 0, 0)
    contract_own, spread = after(contract_own, tokens_grad), after(spread, tokens_grad)
    keep, keep_out, send = whole(
        line_sum_kernel,
        "line_sum",
        index,
        (contract_own, contract_got, expand_own, output_own, both_got),
        [shape((2, slab, quarter), WIDE), shape((slab, QUAD), WIDE), shape((slab, 2 * quarter + QUAD), LOW)],
    )
    triple_grad, triple_bias_grad, output_bias_grad, gain_one, shift_one = whole(
        triple_out_kernel,
        "triple_out",
        index,
        (packed,),
        [shape((3, slab, 2 * QUAD), WIDE), shape((3, 2 * QUAD), WIDE)] + [vector] * 3,
    )
    contract_grad, expand_grad, output_grad = whole(
        columns_kernel,
        "columns",
        index,
        (keep, keep_out, flip(send, "x")),
        [shape((slab, n), WIDE) for n in (span, span, 2 * QUAD)],
    )

    queries_grad, head_grad, contract_bias_grad, gain_two, shift_two, expand_bias_grad = whole(
        spread_kernel,
        "spread",
        index,
        (after(spread, contract_grad).reshape(NZ * 4, -1, proj),),
        [shape((query_vecs.shape[0], proj), WIDE), shape((width, proj), WIDE)]
        + [vector] * 3
        + [shape((span // PAIR, PAIR), WIDE)],
    )

    return (
        second_low,
        after(loss, tokens_grad)[0, 0],
        tokens_grad,
        queries_grad,
        triple_grad.transpose(1, 0, 2),
        triple_bias_grad,
        output_grad.T,
        output_bias_grad.reshape(-1),
        gain_one.reshape(-1),
        shift_one.reshape(-1),
        expand_grad,
        expand_bias_grad.reshape(-1),
        contract_grad.T,
        contract_bias_grad.reshape(-1),
        gain_two.reshape(-1),
        shift_two.reshape(-1),
        head_grad,
    )


def solution(mesh):
    outer = mesh.shape["blk"] // 16
    five = Mesh(mesh.devices.reshape(outer, NZ, 2, 2, mesh.shape["tensor"]), BLK + ("y",))
    blk, tensor = BLK, "y"
    return jax.shard_map(
        shards,
        mesh=five,
        in_specs=(
            P(blk, None),
            P(),
            P(blk, None),
            P(),
            P(blk),
            P(),
            P(blk, None, tensor),
            P(None, tensor),
            P(tensor, blk),
            P(),
            P(),
            P(),
            P(blk, tensor),
            P(tensor),
            P(tensor, blk),
            P(),
            P(),
            P(),
            P(),
        ),
        out_specs=(
            P(blk, None),
            P(),
            P(blk, None),
            P(),
            P(blk, None, tensor),
            P(None, tensor),
            P(tensor, blk),
            P(),
            P(),
            P(),
            P(blk, tensor),
            P(tensor),
            P(tensor, blk),
            P(),
            P(),
            P(),
            P(),
        ),
        check_vma=False,
    )
```

```python
from functools import partial
import math

import jax
import jax.numpy as jnp
import numpy as np
from jax import lax
from jax.experimental import pallas as pl
from jax.experimental.pallas import tpu as pltpu
from jax.sharding import Mesh, PartitionSpec as P

HEAD_DIM = 64
PAIR = 2 * HEAD_DIM

SOFTMAX_TEMPER = 0.05
FLOOR_SCORE = -1e30
NORM_EPSILON = 1e-05
UNIT_EPSILON = 1e-06
PRECISE = lax.Precision.HIGHEST
LOW = jnp.bfloat16
WIDE = jnp.float32

BLK = ("o", "z", "x", "c")
NZ = 4
FOUR = [0, 1, 2, 3]

VMEM_BYTES = 56 * 1024 * 1024
LANES = (0, 64, 192)
QUAD = 4 * HEAD_DIM


def xor_z(value, mask):
    return lax.ppermute(value, "z", [(i, i ^ mask) for i in FOUR])


def xor_s(value, mask):
    return lax.ppermute(value, ("x", "c"), [(i, i ^ mask) for i in FOUR])


def flip(value, axis):
    return lax.ppermute(value, axis, [(0, 1), (1, 0)])


def pick(value, index, axis=0):
    return lax.dynamic_index_in_dim(value, index, axis, keepdims=False)


def after(value, *others):
    return lax.optimization_barrier((value,) + others)[0]


def place(pieces):
    first = pieces[0][1]
    whole = jnp.zeros((len(pieces),) + first.shape, first.dtype)
    for index, piece in pieces:
        whole = lax.dynamic_update_slice_in_dim(whole, piece[None], index, 0)
    return whole


def both(mine, other, where):
    return place([(where, mine), (1 - where, other)])


def doc_layout(doc_lengths, places):
    ends = jnp.cumsum(doc_lengths)
    starts = ends - doc_lengths
    passed = starts <= places[..., None]
    doc_index = jnp.sum(passed.astype(jnp.int32), axis=-1) - 1
    begin = jnp.max(jnp.where(passed, starts, 0), axis=-1)
    return (doc_index, places - begin)


def dot_nn(a, b, precision=None):
    return lax.dot_general(
        a, b, (((1,), (0,)), ((), ())), precision=precision, preferred_element_type=WIDE
    )


def dot_nt(a, b, precision=None):
    return lax.dot_general(
        a, b, (((1,), (1,)), ((), ())), precision=precision, preferred_element_type=WIDE
    )


def dot_tn(a, b, precision=None):
    return lax.dot_general(
        a, b, (((0,), (0,)), ((), ())), precision=precision, preferred_element_type=WIDE
    )


def shape(dims, dtype):
    return jax.ShapeDtypeStruct(dims, dtype)


PARAMS = pltpu.CompilerParams(vmem_limit_bytes=VMEM_BYTES)

TAKES = dict(
    prep=2.5, heads=2.0, project=3.8, attend=7.5, branch=3.5, forward=7.7, second=3.6, middle=12.0, first_back=3.8, attend_back=9.8, triple=2.9, triple_weight=2.0, tokens=3.9,
    tokens_sum=2.1, weights=5.2, output=1.5, core_sum=3.9, line_sum=2.7, pair=2.0, columns=2.2, pair_sum=0.8,
    triple_out=1.9, query_units=2.8, query_back=1.0, spread=3.5,
)


SCALE = 1.0


def cost(name):
    took = TAKES[name] * SCALE
    return pl.CostEstimate(
        flops=int(took * 1.15e9), bytes_accessed=int(took * 3.7e6), transcendentals=0
    )


def whole(kernel, name, index, inputs, outputs, scratch=(), slabs=()):
    return pl.pallas_call(
        kernel,
        in_specs=[pl.BlockSpec(memory_space=pltpu.SMEM)]
        + [pl.BlockSpec(memory_space=pltpu.VMEM)] * len(inputs)
        + [pl.BlockSpec(memory_space=pl.ANY)] * len(slabs),
        out_specs=[pl.BlockSpec(memory_space=pltpu.VMEM)] * len(outputs),
        out_shape=list(outputs),
        scratch_shapes=list(scratch),
        compiler_params=PARAMS,
        cost_estimate=cost(name),
        name=name,
    )(index, *inputs, *slabs)


def slab_copy(slabs, at, weight, sems):
    there = slabs.at[:, pl.ds(at, weight.shape[1])]
    return pltpu.make_async_copy(there, weight, sems.at[0])


def piece_copies(idx, pieces, weight, sems):
    if len(pieces) == 1:
        return [pltpu.make_async_copy(pieces[0], weight, sems.at[0])]
    count, half, _ = pieces[0].shape
    span, copies = weight.shape[1], []
    for c, piece in enumerate(pieces):
        for spot in range(count):
            there = (idx[1] ^ (spot // 2)) * 2 + (idx[2] ^ (spot % 2))
            row = (there * 2 + (idx[3] ^ c)) * 2 * half
            for i in range(2):
                rows = pl.ds(pl.multiple_of(row + i * half, half), half)
                here = piece.at[spot, :, pl.ds(i * span, span)]
                copies.append(pltpu.make_async_copy(here, weight.at[rows, :], sems.at[len(copies)]))
    return copies


def piece_scratch(rows, cols):
    return [pltpu.VMEM((rows, cols), LOW), pltpu.SemaphoreType.DMA((NZ * 8,))]


def slab_scratch(rows, cols):
    return [pltpu.VMEM((rows, cols), LOW), pltpu.SemaphoreType.DMA((1,))]


def start(copies):
    for copy in copies:
        copy.start()


def finish(copies, weight):
    for copy in copies:
        copy.wait()
    return weight[...]


def extra_count(slab):
    return 0 if slab >= HEAD_DIM else 16


def put_extra(message, slab, extra):
    if extra_count(slab):
        message[slab : slab + 16, :] = extra
        return
    for i in range(4):
        message[i * 16 : (i + 1) * 16, PAIR : PAIR + HEAD_DIM] = extra[
            :, i * HEAD_DIM : (i + 1) * HEAD_DIM
        ]


def get_extra(message, slab):
    if extra_count(slab):
        return message[slab : slab + 16, :]
    lanes = slice(PAIR, PAIR + HEAD_DIM)
    return jnp.concatenate([message[i * 16 : (i + 1) * 16, lanes] for i in range(4)], axis=1)


def prep_kernel(idx, tw, ow, ew, cw, live, tokens, heads, low, tri, mine, own):
    slab, span = ew.shape
    alive = jnp.broadcast_to(live[...], (16, live.shape[1])).astype(WIDE).astype(LOW)
    alive = jnp.concatenate([alive, jnp.zeros((16, QUAD - live.shape[1]), LOW)], axis=1)
    rows, span = tokens.shape[0], ow.shape[1]
    half = rows // 2
    mine[:half, :] = tokens[pl.ds(pl.multiple_of(idx[4] * half, half), half), :]
    own[:rows, :] = tokens[...]
    if own.shape[0] > rows:
        for i in range(2):
            part = ow[i * slab // 2 : (i + 1) * slab // 2, :].astype(LOW)
            mine[half:, i * span : (i + 1) * span] = part
            own[rows:, i * span : (i + 1) * span] = part
    span = ew.shape[1]
    for spot in range(NZ * 2):
        at = spot * HEAD_DIM
        for part, lane in enumerate(LANES):
            heads[spot, :slab, lane : lane + HEAD_DIM] = tw[part, :, at : at + HEAD_DIM].astype(LOW)
        heads[spot, :slab, PAIR : PAIR + HEAD_DIM] = jnp.zeros((slab, HEAD_DIM), LOW)
        put_extra(heads.at[spot], slab, alive)
    low[:, :span] = ew[...].astype(LOW)
    low[:, span:] = cw[...].astype(LOW)
    for part in range(3):
        tri[:, part * 2 * QUAD : (part + 1) * 2 * QUAD] = tw[part].astype(LOW)


def heads_kernel(idx, own, other, weight, live0, live1):
    slab, mc = HEAD_DIM, idx[3]
    for spot in range(NZ * 2):
        for source, c, live in ((own, mc, live0), (other, 1 - mc, live1)):
            rows = pl.ds(pl.multiple_of((spot * 2 + c) * slab, slab), slab)
            weight[rows, :] = source[spot, :slab, :]
            live[spot : spot + 1, :] = get_extra(source.at[spot], slab)[:, :PAIR].astype(WIDE)[:1]


def swap_halves(value):
    lane = lax.broadcasted_iota(jnp.int32, value.shape, 1)
    half = HEAD_DIM // 2
    return jnp.where(
        (lane & half) == 0,
        pltpu.roll(value, PAIR - half, 1),
        pltpu.roll(value, half, 1),
    )


def turn(value, cosine, sine):
    return value * cosine + swap_halves(value) * sine


def sheet_rows(idx, sheets):
    rows = sheets[0].shape[0]
    half = rows // 2
    parts = []
    for x in range(2):
        spot = idx[1] * 2 + (idx[2] ^ x)
        parts.append((sheets[x][:rows, :], pl.ds(pl.multiple_of(spot * rows, rows), rows)))
    for at, sheet in enumerate(sheets[2:]):
        z, y = at // 2 + 1, at % 2
        for x in range(2):
            spot = (idx[1] ^ z) * 2 + (idx[2] ^ x)
            row = spot * rows + (idx[4] ^ y) * half
            parts.append((sheet[x], pl.ds(pl.multiple_of(row, half), half)))
    return parts


def project_kernel(idx, *refs):
    sheets, (weight, cosine, sine, bias, query, kv, held) = refs[:8], refs[8:]
    for value, at in sheet_rows(idx, sheets):
        held[at, :] = value
    mz, mx = idx[1], idx[2]
    mine = mz * 2 + mx
    biases = []
    for part in range(3):
        total = jnp.zeros((1, HEAD_DIM), WIDE)
        for h in range(NZ * 2):
            here = bias[part : part + 1, h * HEAD_DIM : (h + 1) * HEAD_DIM]
            total = jnp.where(mine == h, here, total)
        biases.append(total)
    empty = jnp.zeros((1, HEAD_DIM), WIDE)
    offset = jnp.concatenate([biases[0], biases[1], empty, biases[2]], axis=1)
    weights = weight[...]
    rows = sheets[0].shape[0]
    low_lanes = lax.broadcasted_iota(jnp.int32, (rows, PAIR), 1) < HEAD_DIM
    for i in range(NZ * 2):
        at = slice(i * rows, (i + 1) * rows)
        triple = dot_nn(held[at, :], weights) + offset
        turned = turn(triple[:, :PAIR], cosine[at, :], sine[at, :])
        query[at, :] = jnp.where(low_lanes, turned * HEAD_DIM ** (-0.5), 0.0).astype(LOW)
        kv[at, :] = jnp.where(
            low_lanes, pltpu.roll(turned, HEAD_DIM, 1), triple[:, PAIR:]
        ).astype(LOW)


def key_row(ref):
    rows = ref[...]
    return jnp.concatenate([rows[i : i + 1] for i in range(rows.shape[0])], axis=1)


def places_of(token, rows, half, blocks, idx, z, part):
    x, upper, row = token // (2 * rows), token // rows % 2, token % rows
    block = ((idx[0] * NZ + z) * 2 + x) * 2 + idx[3]
    return (upper * half + part * rows + row) * blocks + block


def docs_of(places, lens):
    doc, begin = jnp.full(places.shape, -1, jnp.int32), jnp.int32(0)
    for i in range(lens.shape[0]):
        doc = jnp.where(begin <= places, doc + 1, doc)
        begin = begin + lens[i]
    return doc


def as_row(column):
    count = column.shape[0]
    row = lax.broadcasted_iota(jnp.int32, (count, count), 0)
    same = row == lax.broadcasted_iota(jnp.int32, (count, count), 1)
    return jnp.sum(jnp.where(same, column, 0.0), axis=0, keepdims=True)


def attend_kernel(
    blocks, idx, lens, q_ref, kv0_ref, kv1_ref, kdoc0_ref, kdoc1_ref, out_ref, log_ref, pack_ref
):
    rows, half = q_ref.shape[3], kdoc0_ref.shape[1] // 2
    queries = q_ref[0].reshape(4 * rows, PAIR)
    kv = (kv0_ref[...], kv1_ref[...])
    token = lax.broadcasted_iota(jnp.int32, (4 * rows, 1), 0)
    z, part = pl.program_id(0), pl.program_id(1)
    doc = docs_of(places_of(token, rows, half, blocks, idx, z, part), lens)
    scores = [
        jnp.where(doc == key_row(ref), dot_nt(queries, keys), FLOOR_SCORE)
        for ref, keys in zip((kdoc0_ref, kdoc1_ref), kv)
    ]
    peak = jnp.maximum(*[jnp.max(s, axis=-1, keepdims=True) for s in scores])
    weights = [jnp.exp(s - peak) for s in scores]
    total = sum(jnp.sum(w, axis=-1, keepdims=True) for w in weights)
    mixed = sum(dot_nn(w.astype(LOW), keys) for w, keys in zip(weights, kv)) / total
    out_ref[0] = mixed.reshape(2, 2, rows, PAIR)
    log_ref[0, 0] = as_row(peak + jnp.log(total))
    low_lanes = lax.broadcasted_iota(jnp.int32, (rows, PAIR), 1) < HEAD_DIM
    for x in range(2):
        upper = mixed[2 * x * rows : (2 * x + 1) * rows]
        lower = mixed[(2 * x + 1) * rows : (2 * x + 2) * rows]
        pack_ref[0, x] = jnp.where(low_lanes, pltpu.roll(upper, HEAD_DIM, 1), lower).astype(LOW)


def attend_specs(rows, keys, key_rows):
    half = rows // 2
    size = max(16, min(half, half * 2048 // (2 * keys)))
    full = lambda n, m: pl.BlockSpec((n, m), lambda i, j: (0, 0))
    part = lambda m: pl.BlockSpec((1, 2, 2, size, m), lambda i, j: (i, 0, 0, j, 0))
    pack = pl.BlockSpec((1, 2, size, PAIR), lambda i, j: (i, 0, j, 0))
    logs = pl.BlockSpec((1, 1, 1, 4 * size), lambda i, j: (i, j, 0, 0))
    kv, docs = full(keys, PAIR), full(key_rows, rows)
    return (NZ, half // size), part, pack, logs, kv, docs


SCALARS = [pl.BlockSpec(memory_space=pltpu.SMEM)] * 2


def attend(blocks, index, lens, queries, kv0, kv1, kdoc0, kdoc1):
    rows = kdoc0.shape[1]
    half = rows // 2
    grid, part, pack, logs, kv, docs = attend_specs(rows, kv0.shape[0], kdoc0.shape[0])
    return pl.pallas_call(
        partial(attend_kernel, blocks),
        grid=grid,
        in_specs=SCALARS + [part(PAIR), kv, kv, docs, docs],
        out_specs=[part(PAIR), logs, pack],
        out_shape=[
            shape((NZ, 2, 2, half, PAIR), WIDE),
            shape((NZ, grid[1], 1, 4 * half // grid[1]), WIDE),
            shape((NZ, 2, half, PAIR), LOW),
        ],
        compiler_params=PARAMS,
        cost_estimate=cost("attend"),
        name="attend",
    )(index, lens, queries.reshape(NZ, 2, 2, half, PAIR), kv0, kv1, kdoc0, kdoc1)


def attend_back_kernel(
    blocks, idx, lens, q_ref, g_ref, o_ref, log_ref, kv0_ref, kv1_ref, kdoc0_ref, kdoc1_ref,
    dq_ref, dkv0_ref, dkv1_ref, column0, column1,
):
    rows, width = q_ref.shape[3], kdoc0_ref.shape[1]
    z, part = pl.program_id(0), pl.program_id(1)

    @pl.when((z == 0) & (part == 0))
    def _():
        dkv0_ref[...] = jnp.zeros_like(dkv0_ref)
        dkv1_ref[...] = jnp.zeros_like(dkv1_ref)
        for ref, column in ((kdoc0_ref, column0), (kdoc1_ref, column1)):
            turned = jnp.transpose(ref[...].astype(WIDE))
            for i in range(ref.shape[0]):
                column[i * width : (i + 1) * width, :] = turned[:, i : i + 1]

    queries = q_ref[0].reshape(4 * rows, PAIR)
    high_lanes = lax.broadcasted_iota(jnp.int32, (rows, PAIR), 1) >= HEAD_DIM
    parts = []
    for x in range(2):
        packed = g_ref[0, x].astype(WIDE)
        parts.append(jnp.where(high_lanes, pltpu.roll(packed, HEAD_DIM, 1), 0.0))
        parts.append(jnp.where(high_lanes, packed, 0.0))
    wide = jnp.concatenate(parts, axis=0)
    grads = wide.astype(LOW)
    delta = as_row(jnp.sum(wide * o_ref[0].reshape(4 * rows, PAIR), axis=-1, keepdims=True))
    token = lax.broadcasted_iota(jnp.int32, (1, 4 * rows), 1)
    doc = docs_of(places_of(token, rows, width // 2, blocks, idx, z, part), lens).astype(WIDE)
    log_total = log_ref[0, 0]
    total = jnp.zeros((4 * rows, PAIR), WIDE)
    for kv_ref, column, dkv_ref in ((kv0_ref, column0, dkv0_ref), (kv1_ref, column1, dkv1_ref)):
        keys = kv_ref[...]
        raw = dot_nt(keys, queries)
        probs = jnp.where(column[...] == doc, jnp.exp(raw - log_total), 0.0)
        dprobs = dot_nt(keys, grads)
        dscores = (probs * (dprobs - delta)).astype(LOW)
        total = total + dot_tn(dscores, keys)
        dkv_ref[...] += dot_nn(dscores, queries) + dot_nn(probs.astype(LOW), grads)
    dq_ref[0] = (total * HEAD_DIM ** (-0.5)).reshape(2, 2, rows, PAIR)


def attend_back(blocks, index, lens, queries, grads, out, log_total, kv0, kv1, kdoc0, kdoc1):
    rows, keys = kdoc0.shape[1], kv0.shape[0]
    half = rows // 2
    grid, part, pack, logs, kv, docs = attend_specs(rows, keys, kdoc0.shape[0])
    return pl.pallas_call(
        partial(attend_back_kernel, blocks),
        grid=grid,
        in_specs=SCALARS + [part(PAIR), pack, part(PAIR), logs, kv, kv, docs, docs],
        out_specs=[part(PAIR), kv, kv],
        out_shape=[
            shape((NZ, 2, 2, half, PAIR), WIDE),
            shape((keys, PAIR), WIDE),
            shape((keys, PAIR), WIDE),
        ],
        scratch_shapes=[pltpu.VMEM((keys, 1), WIDE)] * 2,
        compiler_params=PARAMS,
        cost_estimate=cost("attend_back"),
        name="attend_back",
    )(
        index, lens, queries.reshape(NZ, 2, 2, half, PAIR), grads, out, log_total, kv0, kv1,
        kdoc0, kdoc1,
    )


def branch_kernel(pieces, idx, got, *refs):
    slabs, (low, part, held, sems) = refs[:pieces], refs[pieces:]
    copy = piece_copies(idx, slabs, held, sems)
    start(copy)
    half = got.shape[1]
    for h in range(NZ * 2):
        lanes = slice(h * HEAD_DIM, (h + 1) * HEAD_DIM)
        low[:half, lanes] = got[h, :, :HEAD_DIM]
        low[half:, lanes] = got[h, :, HEAD_DIM:]
    part[...] = dot_nt(low[...], finish(copy, held)).astype(LOW)


def normalize(value):
    center = value - jnp.mean(value, axis=-1, keepdims=True)
    spread = jnp.mean(center * center, axis=-1, keepdims=True)
    inverse = lax.rsqrt(spread + NORM_EPSILON)
    return center * inverse, inverse


def pair(own, other):
    return own[...].astype(WIDE) + other[...].astype(WIDE)


def forward_kernel(
    idx, own, other, tokens, bias, gain, shift, hidden_bias, attended, slabs,
    first, unitary, inverse, hidden_in, keep, send, part,
    low, hidden, expand, sems1, contract, sems2,
):
    copy1 = [slab_copy(slabs, 0, expand, sems1)]
    copy2 = [slab_copy(slabs, expand.shape[1], contract, sems2)]
    start(copy1 + copy2)
    value = tokens[...].astype(WIDE) + (pair(own, other) + bias[...])
    unitary[...], inverse[...] = normalize(value)
    first[...] = unitary[...] * gain[...] + shift[...]
    low[...] = first[...].astype(LOW)
    value = dot_nn(low[...], finish(copy1, expand)) + hidden_bias[...]
    hidden_in[...] = value
    hidden[...] = (0.5 * value * (1.0 + lax.erf(value * (0.5**0.5)))).astype(LOW)
    part[...] = dot_nt(hidden[...], finish(copy2, contract)).astype(LOW)
    rows, width = low.shape
    few = rows * QUAD // width
    for out, x in ((keep, idx[2]), (send, 1 - idx[2])):
        out[:rows, :] = low[...]
        out[rows : 2 * rows, :] = columns_of(hidden, x, width)
        for i in range(width // QUAD):
            out[2 * rows :, i * QUAD : (i + 1) * QUAD] = attended[
                i * few : (i + 1) * few, pl.ds(pl.multiple_of(x * QUAD, QUAD), QUAD)
            ]


def columns_of(ref, x, span):
    return ref[:, pl.ds(pl.multiple_of(x * span, 128), span)]


def unit_scale(value):
    return lax.rsqrt(jnp.sum(value * value, axis=-1, keepdims=True) + UNIT_EPSILON)


def second_kernel(
    idx, own, other, first, bias, gain, shift, head, query, kdoc,
    low, unitary, inverse, embed, unit, expo, totals, message,
):
    value = first[...] + (pair(own, other) + bias[...])
    unitary[...], inverse[...] = normalize(value)
    low[...] = (unitary[...] * gain[...] + shift[...]).astype(LOW)
    embed[...] = dot_nn(low[...], head[...].astype(LOW))
    unit[...] = (embed[...] * unit_scale(embed[...])).astype(LOW)
    message[...] = unit[...].astype(WIDE)
    expo[...] = jnp.exp(dot_nt(unit[...], query[...]) / SOFTMAX_TEMPER)
    totals[...] = dot_nn(member(idx, kdoc, totals.shape[0]), expo[...], PRECISE).astype(LOW)


def query_kernel(idx, vecs, out, own):
    block, shares = (idx[1] * 2 + idx[2]) * 2 + idx[3], own.shape[0]
    own[...] = vecs[pl.ds(pl.multiple_of(block * shares, shares), shares), :]
    value = vecs[...].astype(WIDE)
    out[...] = (value * unit_scale(value)).astype(LOW)


def member(idx, kdoc, docs):
    row = kdoc[pl.ds((idx[0] * NZ + idx[1]) * 2 + idx[2], 1), :]
    label = lax.broadcasted_iota(jnp.int32, (docs, row.shape[1]), 0)
    return jnp.where(row == label, 1.0, 0.0)


def group_sum(value, length):
    column = lax.broadcasted_iota(jnp.int32, value.shape, 1)
    span = value.shape[1]
    step = 1
    while step < length:
        ahead, behind = pltpu.roll(value, span - step, 1), pltpu.roll(value, step, 1)
        value = value + jnp.where((column & step) == 0, ahead, behind)
        step *= 2
    return value


def loss_of(count, totals, kdocs, positive):
    docs, columns = totals.shape
    length = columns // count
    label = lax.broadcasted_iota(jnp.int32, (docs, 1), 0)
    tokens = jnp.zeros((docs, 1), WIDE)
    for ref in kdocs:
        tokens = tokens + jnp.sum(jnp.where(key_row(ref) == label, 1.0, 0.0), axis=1, keepdims=True)
    doc_score = group_sum(SOFTMAX_TEMPER * (jnp.log(totals) - jnp.log(tokens)), length)
    best = jnp.max(doc_score, axis=0, keepdims=True)
    shifted = jnp.exp(doc_score - best)
    shifted_sum = jnp.sum(shifted, axis=0, keepdims=True)
    chosen = jnp.where(label == positive, 1.0, 0.0)
    each = best + jnp.log(shifted_sum) - jnp.sum(doc_score * chosen, axis=0, keepdims=True)
    loss = jnp.sum(each, axis=1, keepdims=True) / columns
    return loss, (shifted / shifted_sum - chosen) / (totals * count)


def unit_back(value, grad):
    scale = unit_scale(value)
    along = jnp.sum(grad * value, axis=-1, keepdims=True)
    return scale * grad - value * (along * scale * scale * scale)


def query_back_kernel(half, idx, kdoc0, kdoc1, coefficients, value, units, got, out):
    shares = value.shape[0]
    block = (idx[1] * 2 + idx[2]) * 2 + idx[3]
    columns_here = pl.ds(pl.multiple_of(block * shares, shares), shares)
    coefficient = coefficients[:, columns_here]
    docs = coefficient.shape[0]
    pads = jnp.zeros((-docs % 8, shares), WIDE)
    coefficient = jnp.transpose(jnp.concatenate([coefficient, pads]) if docs % 8 else coefficient)
    queries = value[...].astype(WIDE)
    query = (queries * unit_scale(queries)).astype(LOW)
    rows, group = kdoc0.shape[1], 4
    count = units.shape[0] // rows

    def add(at, total):
        labels = []
        for step in range(group):
            block = at * group + step
            spot = block // 2
            labels.append(
                jnp.where(block % 2 == idx[3], kdoc0[pl.ds(spot, 1), :], kdoc1[pl.ds(spot, 1), :])
            )
        row = jnp.concatenate(labels, axis=1)
        unit = units[pl.ds(at * group * rows, group * rows), :].astype(LOW)
        if docs <= 8:
            chosen = jnp.zeros((shares, group * rows), WIDE)
            for doc in range(docs):
                chosen = jnp.where(row == doc, coefficient[:, doc : doc + 1], chosen)
        else:
            label = lax.broadcasted_iota(jnp.int32, (coefficient.shape[1], group * rows), 0)
            chosen = dot_nn(coefficient, jnp.where(row == label, 1.0, 0.0), PRECISE)
        expo = jnp.exp(dot_nt(query, unit) / SOFTMAX_TEMPER)
        return total + dot_nn((chosen * expo).astype(LOW), unit)

    steps, total = count // group, jnp.zeros(queries.shape, WIDE)
    if steps <= 4:
        for at in range(steps):
            total = add(at, total)
    else:
        total = lax.fori_loop(0, steps, add, total)
    out[:shares, :] = unit_back(queries, total).astype(LOW)
    sums = [got[spot, half:, :].astype(WIDE) for spot in range(NZ * 2)]
    while len(sums) > 1:
        sums = [a + b for a, b in zip(sums[::2], sums[1::2])]
    out[shares:, :] = sums[0].astype(LOW)


def spread_kernel(idx, got, queries, head, *vectors):
    rows = got.shape[1]
    chunk = head.shape[0] // (NZ * 4)
    shares = rows - chunk - 16
    pieces = []
    for i in range(NZ * 4):
        queries[i * shares : (i + 1) * shares, :] = got[i, :shares, :].astype(WIDE)
        head[i * chunk : (i + 1) * chunk, :] = got[i, shares : shares + chunk, :].astype(WIDE)
        pieces.append(got[i, shares + chunk : shares + chunk + 16, :].astype(WIDE))
    row = 0
    for out in vectors:
        for i in range(0, out.shape[0], 8):
            out[i : i + 8, :] = pieces[row // 16][row % 16 : row % 16 + 8]
            row += 8


def norm_back(grad, gain, unitary, inverse):
    scaled = grad * gain
    along = jnp.mean(scaled * unitary, axis=-1, keepdims=True)
    return inverse * (scaled - jnp.mean(scaled, axis=-1, keepdims=True) - unitary * along)


def column_sum(value):
    return jnp.sum(value, axis=0, keepdims=True)


def middle_kernel(
    count, idx, t0, t1, t2, t3, kdoc0, kdoc1, positive, expo, query, unit,
    embed, low, head, cotangent, unitary, inverse, gain, hidden_in, slabs,
    grad_in, keep, send, part, loss, coefficients, sums0, sums1,
    similar, grad_low, grad_hidden_in, head_part, rows_part, expand, sems1, contract, sems2,
):
    copy1 = [slab_copy(slabs, 0, expand, sems1)]
    copy2 = [slab_copy(slabs, expand.shape[1], contract, sems2)]
    start(copy2 + copy1)
    totals = pair(t0, t1) + pair(t2, t3)
    value, coefficient = loss_of(count, totals, (kdoc0, kdoc1), positive[...])
    loss[...] = jnp.broadcast_to(value, loss.shape)
    coefficients[...] = coefficient
    here = member(idx, kdoc0, totals.shape[0])
    similar[...] = (dot_tn(here, coefficient, PRECISE) * expo[...]).astype(LOW)
    grad_embed = unit_back(embed[...], dot_nn(similar[...], query[...])).astype(LOW)
    rows, width = embed.shape[0], low.shape[1]
    head_part[...] = dot_tn(low[...], grad_embed)
    grad_second = dot_nt(grad_embed, head[...].astype(LOW)) + cotangent[...].astype(WIDE)
    grad_in[...] = norm_back(grad_second, gain[...], unitary[...], inverse[...])
    grad_low[...] = grad_in[...].astype(LOW)
    sums = [
        column_sum(grad_low[...].astype(WIDE)),
        column_sum(grad_second * unitary[...]),
        column_sum(grad_second),
    ]
    value = hidden_in[...]
    grad = dot_nn(grad_low[...], finish(copy2, contract))
    bell = jnp.exp(-0.5 * value * value) * (1.0 / math.sqrt(2.0 * math.pi))
    slope = 0.5 * (1.0 + lax.erf(value * (0.5**0.5))) + value * bell
    grad_hidden_in[...] = (slope * grad).astype(LOW)
    sums.append(column_sum(grad_hidden_in[...].astype(WIDE)))
    part[...] = dot_nt(grad_hidden_in[...], finish(copy1, expand)).astype(LOW)
    for out, x in ((keep, idx[2]), (send, 1 - idx[2])):
        out[:rows, :] = grad_low[...]
        out[rows:, :] = columns_of(grad_hidden_in, x, width)
    rows_part[...] = jnp.zeros_like(rows_part)
    at = 0
    for value in sums:
        for i in range(value.shape[1] // PAIR):
            rows_part[at : at + 1, :] = value[:, i * PAIR : (i + 1) * PAIR]
            at += 1
    chunk = width // (NZ * 4)
    for spot in range(NZ * 2):
        for out, c in ((sums0, idx[3]), (sums1, 1 - idx[3])):
            at = spot * 2 + c
            out[spot, :chunk, :] = head_part[
                pl.ds(pl.multiple_of(at * chunk, chunk), chunk), :
            ].astype(out.dtype)
            out[spot, chunk:, :] = rows_part[pl.ds(pl.multiple_of(at * 16, 16), 16), :].astype(
                out.dtype
            )


def slab_products(idx, left, right, outs):
    slab = outs[0].shape[-2]
    for z, out in enumerate(outs):
        mine = []
        for x in range(2):
            spot = (idx[1] ^ z) * 2 + (idx[2] ^ x)
            lanes = left[:, pl.ds(pl.multiple_of(spot * 2 * slab, 2 * slab), 2 * slab)]
            mine.append(jnp.where(idx[3] == 0, lanes[:, :slab], lanes[:, slab:]))
        both_rows = dot_tn(jnp.concatenate(mine, axis=1), right)
        for x in range(2):
            out[x] = both_rows[x * slab : (x + 1) * slab].astype(out.dtype)


def weights_kernel(idx, f0, f1, f2, f3, g0, g1, g2, g3, *refs):
    keep0, send0, keep1, send1, left, right = refs
    rows = g0.shape[0] // 2
    firsts, grads = (f0, f1, f2, f3), (g0, g1, g2, g3)
    for keep, send, lefts, rights in ((keep0, send0, grads, firsts), (keep1, send1, firsts, grads)):
        for i in range(4):
            left[i * rows : (i + 1) * rows, :] = lefts[i][:rows, :]
            right[i * rows : (i + 1) * rows, :] = rights[i][rows : 2 * rows, :]
        slab_products(idx, left, right[...], [keep.at[0], send.at[0], keep.at[1], send.at[1]])


def pair_kernel(idx, *refs):
    count = (len(refs) - 1) // 3
    gots, owns, send, at = refs[: 2 * count], refs[2 * count : -1], refs[-1], 0
    for i, own in enumerate(owns):
        keep, got, span = gots[2 * i], gots[2 * i + 1], own.shape[-1]
        own[...] = keep[0] + got[0].astype(WIDE)
        send[:, :, at : at + span] = (keep[1] + got[1].astype(WIDE)).astype(LOW)
        at += span


def output_kernel(idx, f0, f1, f2, f3, g0, g1, g2, g3, keep, send, left, right):
    rows, width = g0.shape
    few = rows * QUAD // width
    for i, (f, g) in enumerate(zip((f0, f1, f2, f3), (g0, g1, g2, g3))):
        left[i * rows : (i + 1) * rows, :] = g[...]
        for j in range(width // QUAD):
            right[i * rows + j * few : i * rows + (j + 1) * few, :] = f[
                2 * rows :, j * QUAD : (j + 1) * QUAD
            ]
    slab_products(idx, left, right[...], [keep.at[0], send.at[0], keep.at[1], send.at[1]])


def line_sum_kernel(idx, own0, got0, own1, own2, got, keep, keep_out, send):
    at = 0
    for own, other, out in (
        (own0, got0[...], keep.at[0]),
        (own1, got[:, :, : own1.shape[-1]], keep.at[1]),
        (own2, got[:, :, own1.shape[-1] :], keep_out),
    ):
        span = own.shape[-1]
        out[...] = own[0] + other[0].astype(WIDE)
        send[:, at : at + span] = (own[1] + other[1].astype(WIDE)).astype(LOW)
        at += span


def columns_kernel(idx, keep, keep_out, got, contract, expand, output):
    span = keep.shape[-1]
    for at, mine, out in ((0, keep[0], contract), (span, keep[1], expand), (2 * span, keep_out[...], output)):
        cols = mine.shape[1]
        out[:, pl.ds(pl.multiple_of(idx[2] * cols, 128), cols)] = mine
        out[:, pl.ds(pl.multiple_of((1 - idx[2]) * cols, 128), cols)] = got[
            :, at : at + cols
        ].astype(WIDE)


def first_back_kernel(
    pieces, idx, own, other, grad_second_in, unitary, inverse, gain, sums0, sums1, *refs
):
    slabs, (grad_in, grad_low, vectors, pack, held, sems) = refs[:pieces], refs[pieces:]
    copy = piece_copies(idx, slabs, held, sems)
    start(copy)
    grad_first = grad_second_in[...] + pair(own, other)
    grad_in[...] = norm_back(grad_first, gain[...], unitary[...], inverse[...])
    grad_low[...] = grad_in[...].astype(LOW)
    vectors[...] = jnp.zeros_like(vectors)
    vectors[0:1, :] = column_sum(grad_low[...].astype(WIDE))
    vectors[1:2, :] = column_sum(grad_first * unitary[...])
    vectors[2:3, :] = column_sum(grad_first)
    grad = dot_nn(grad_low[...], finish(copy, held)).astype(LOW)
    half = grad.shape[0] // 2
    for h in range(NZ * 2):
        lanes = slice(h * HEAD_DIM, (h + 1) * HEAD_DIM)
        pack[h, :half, :HEAD_DIM] = grad[:half, lanes]
        pack[h, :half, HEAD_DIM:] = grad[half:, lanes]
        pack[h, half:, :] = (sums0[h] + sums1[h].astype(WIDE)).astype(LOW)


def triple_kernel(idx, dq, dkv, got, cosine, sine, out, dense):
    rows = dq.shape[0]
    low_lanes = lax.broadcasted_iota(jnp.int32, (rows, PAIR), 1) < HEAD_DIM
    grads = dkv[...] + got[...]
    both_parts = jnp.where(low_lanes, dq[...], pltpu.roll(grads, HEAD_DIM, 1))
    turned = turn(both_parts, cosine[...], -sine[...])
    turned, value = turned.astype(LOW), grads[:, HEAD_DIM:].astype(LOW)
    out[:, :PAIR] = turned
    out[:, PAIR:] = jnp.where(low_lanes, 0.0, grads).astype(LOW)
    rows = dense.shape[1] * 4 // 3
    half, few = rows // 2, rows // 4
    for i in range(dense.shape[0]):
        at = i * rows
        dense[i, :half, :PAIR] = turned[at : at + half]
        dense[i, :half, PAIR:] = turned[at + half : at + rows]
        for j in range(4):
            dense[i, half:, j * HEAD_DIM : (j + 1) * HEAD_DIM] = value[
                at + j * few : at + (j + 1) * few
            ]


def extra_rows(bias, vectors):
    cols = bias.shape[1]
    rows = [bias]
    for i in range(3):
        for j in range(vectors.shape[1] // cols):
            rows.append(vectors[i : i + 1, j * cols : (j + 1) * cols])
    return jnp.concatenate(rows + [jnp.zeros((16 - len(rows), cols), WIDE)], axis=0)


def triple_weight_kernel(idx, *refs):
    sheets, (grad, vectors, keep, send, total, held) = refs[:8], refs[8:]
    mc = idx[3]
    slab = HEAD_DIM
    for value, at in sheet_rows(idx, sheets):
        held[at, :] = value
    total[...] = dot_tn(held[...], grad[...])
    extra = extra_rows(column_sum(grad[...].astype(WIDE)), vectors).astype(LOW)
    for spot in range(NZ * 2):
        for out, c in ((keep, mc), (send, 1 - mc)):
            at = pl.ds(pl.multiple_of((spot * 2 + c) * slab, slab), slab)
            out[spot, :slab, :] = total[at, :].astype(LOW)
            put_extra(out.at[spot], slab, extra)


def pair_sum_kernel(idx, one, two, out):
    out[...] = (one[...].astype(WIDE) + two[...].astype(WIDE)).astype(out.dtype)


def triple_out_kernel(idx, got, weight, bias, *vectors):
    slab = weight.shape[1]
    total = 0.0
    for spot in range(NZ * 2):
        at = spot * HEAD_DIM
        here, extra = got[spot].astype(WIDE), get_extra(got.at[spot], slab).astype(WIDE)
        for part, lane in enumerate(LANES):
            weight[part, :, at : at + HEAD_DIM] = here[:slab, lane : lane + HEAD_DIM]
            bias[part : part + 1, at : at + HEAD_DIM] = extra[:1, lane : lane + HEAD_DIM]
        total = total + extra
    row = 1
    for out in vectors:
        for i in range(0, out.shape[0], 2):
            out[i : i + 1, :] = total[row : row + 1, :PAIR]
            out[i + 1 : i + 2, :] = total[row : row + 1, PAIR:]
            row += 1


def tokens_kernel(idx, got, message, part, group, held, sems):
    copy = slab_copy(message, 0, held, sems)
    copy.start()
    rows = part.shape[0]
    half, few = rows // 2, rows // 4
    for h in range(NZ * 2):
        for p in range(2):
            at = (p * NZ * 2 + h) * HEAD_DIM
            for i in range(2):
                lane = i * PAIR + p * HEAD_DIM
                group[i * half : (i + 1) * half, at : at + HEAD_DIM] = got[
                    h, :half, lane : lane + HEAD_DIM
                ]
        at = (2 * NZ * 2 + h) * HEAD_DIM
        for j in range(4):
            group[j * few : (j + 1) * few, at : at + HEAD_DIM] = got[
                h, half:, j * HEAD_DIM : (j + 1) * HEAD_DIM
            ]
    copy.wait()
    part[...] = dot_nt(group[...], held[...]).astype(LOW)


def tokens_sum_kernel(idx, own, other, grad, out):
    out[...] = grad[...] + pair(own, other)


def shards(
    tokens,
    query_vecs,
    out_cotangent,
    doc_lengths,
    live_mask,
    positives,
    triple_weight,
    triple_bias,
    output_weight,
    output_bias,
    first_gain,
    first_shift,
    expand_weight,
    expand_bias,
    contract_weight,
    contract_bias,
    second_gain,
    second_shift,
    head_weight,
):
    outer = lax.axis_size("o")
    mo, mz, mx, mc, my = [lax.axis_index(a) for a in ("o", "z", "x", "c", "y")]
    index = jnp.stack([mo, mz, mx, mc, my]).astype(jnp.int32)
    rows, width = tokens.shape
    half = rows // 2
    slab = triple_weight.shape[0]
    docs = doc_lengths.shape[0]
    queries_count = positives.shape[0]
    blocks = outer * NZ * 4
    span = expand_weight.shape[1]
    quarter = span // 2
    proj = head_weight.shape[1]
    line = lambda vector: vector.reshape(1, -1)

    def widen(value):
        return lax.all_gather(value, "o") if outer > 1 else value[None]

    def narrow(value):
        return lax.psum_scatter(value, "o") if outer > 1 else value[0]

    def sum_outer(value):
        return lax.psum(value, "o") if outer > 1 else value

    def stage(work):
        like = jax.eval_shape(work)
        idle = lambda: jax.tree.map(lambda leaf: jnp.zeros(leaf.shape, leaf.dtype), like)
        return lax.cond(doc_lengths[0] >= 0, work, idle)

    def key_doc(live, c):
        block = jnp.arange(outer * NZ * 2, dtype=jnp.int32) * 2 + c
        doc = doc_layout(doc_lengths, block[:, None] + where[None, :])[0]
        return jnp.where(live > 0, doc, -1)

    def head_weights(heads, heads_other):
        if outer > 1:
            pack = widen(both(heads, heads_other, mc)).transpose(0, 2, 1, 3, 4)
            head_triple = pack[..., :slab, :].reshape(width, QUAD)
            live0, live1 = [
                pick(pack, c, 2)[..., slab, :rows].astype(WIDE).reshape(-1, rows)
                for c in (mc, 1 - mc)
            ]
        else:
            head_triple, live0, live1 = whole(
                heads_kernel,
                "heads",
                index,
                (heads, heads_other),
                [shape((width, QUAD), LOW)] + [shape((NZ * 2, rows), WIDE)] * 2,
            )
        return head_triple, key_doc(live0, mc), key_doc(live1, 1 - mc)

    few_out = slab // 2 if outer == 1 else 0
    heads, low_slab, triple_slab, mine, own = whole(
        prep_kernel,
        "prep",
        index,
        (
            triple_weight.transpose(1, 0, 2),
            output_weight.T,
            expand_weight,
            contract_weight.T,
            line(live_mask),
            tokens,
        ),
        [shape((NZ * 2, slab + extra_count(slab), QUAD), LOW)]
        + [shape((slab, n), LOW) for n in (2 * span, 6 * QUAD)]
        + [shape((half + few_out, width), LOW), shape((rows + few_out, width), LOW)],
    )
    by_z = [mine] + [xor_z(mine, m) for m in (1, 2, 3)]
    own_other = flip(own, "x")

    where = jnp.arange(rows, dtype=jnp.int32) * blocks
    rank = jnp.arange(NZ * 2, dtype=jnp.int32) * 2
    shares = query_vecs.shape[0] // (NZ * 4)
    by_z = list(lax.optimization_barrier((*by_z, heads, own_other))[:NZ])
    gathered = lax.all_gather(after(low_slab, *by_z[1:]), BLK, axis=0, tiled=True)

    def heads_stage():
        got = lax.all_to_all(heads, ("z", "x"), 0, 0)
        sheets, outs = [tokens, own_other], [own[rows:], own_other[rows:]]
        for piece in by_z[1:]:
            turned = flip(piece, "x")
            outs += [piece[half:], turned[half:]]
            two = jnp.stack([piece[:half], turned[:half]])
            sheets += [two, flip(two, "y")]
        if outer > 1:
            out_low = output_weight.T.astype(LOW)
            outs = [lax.all_gather(out_low, BLK, axis=0, tiled=True)]
        else:
            outs = [jnp.stack(outs)]
            outs.append(flip(outs[0], "c"))
        own_places = (mo * NZ * 4 + rank + mc)[:, None] + where[None, :]
        own_position = doc_layout(doc_lengths, own_places.reshape(-1))[1]
        lane = jnp.arange(PAIR) % (HEAD_DIM // 2)
        exponent = (2 * lane).astype(WIDE) / HEAD_DIM
        angles = own_position.astype(WIDE)[:, None] * jnp.exp(-math.log(10000.0) * exponent)[None, :]
        sign = jnp.where(jnp.arange(PAIR) % HEAD_DIM < HEAD_DIM // 2, -1.0, 1.0).astype(WIDE)
        tables = jnp.cos(angles), jnp.sin(angles) * sign[None, :]
        units = whole(
            query_kernel,
            "query_units",
            index,
            (query_vecs,),
            [shape(query_vecs.shape, LOW), shape((shares, proj), LOW)],
        )
        positive = line(jnp.repeat(positives, query_vecs.shape[0] // queries_count))
        got = after(got, sheets[3], sheets[5], sheets[7], tables[0], units[0])
        head = head_weights(got, flip(got, "c"))
        return head, outs, sheets[2:], tables, list(units), positive

    head, outs, sheets, (cosine, sine), (query_unit, own_queries), positive = stage(heads_stage)
    outs = tuple(outs)
    head_triple, kdoc0, kdoc1 = head
    pieces = len(outs)
    sheets = [tokens, own_other] + sheets
    positive = lax.optimization_barrier(positive)
    count = NZ * 2 * rows

    def project_stage():
        queries, kv = whole(
            project_kernel,
            "project",
            index,
            (*sheets, head_triple, cosine, sine, triple_bias),
            [shape((count, PAIR), LOW)] * 2,
            [pltpu.VMEM((count, width), LOW)],
        )
        return queries, kv, flip(kv, "c")

    queries, kv, kv_other = stage(project_stage)
    kv0, kv1 = [widen(v).reshape(-1, PAIR) for v in (kv, kv_other)]
    meta = (kdoc0, kdoc1)
    steps = (blocks, index, doc_lengths)

    def to_blocks(value):
        return lax.all_to_all(value.reshape((NZ * 2,) + value.shape[-2:]), ("z", "x"), 0, 0)

    def attention_stage():
        out, log_total, pack = attend(*steps, queries, kv0, kv1, *meta)
        return out, log_total, to_blocks(pack)

    out, log_total, pack = stage(attention_stage)
    wide_rows, low_rows, thin_rows = [shape((rows, n), t) for n, t in ((width, WIDE), (width, LOW), (1, WIDE))]
    def branch_stage():
        low, part = whole(
            partial(branch_kernel, pieces),
            "branch",
            index,
            (pack,),
            [shape((rows, 2 * QUAD), LOW), low_rows],
            piece_scratch(width, 2 * QUAD),
            outs,
        )
        return low, part, flip(part, "y")

    attended_low, part, part_other = stage(branch_stage)
    gathered = after(gathered, part)
    both_slabs = slab_scratch(width, span) * 2
    triple_low = lax.all_gather(after(triple_slab, part), BLK, axis=0, tiled=True)
    few = rows * QUAD // width
    first, unitary1, inverse1, hidden_in, keep, send, part = whole(
        forward_kernel,
        "forward",
        index,
        (
            part, part_other, tokens, line(output_bias), line(first_gain), line(first_shift),
            line(expand_bias), attended_low,
        ),
        [wide_rows, wide_rows, thin_rows, shape((rows, span), WIDE)]
        + [shape((2 * rows + few, width), LOW)] * 2
        + [low_rows],
        [pltpu.VMEM((rows, width), LOW), pltpu.VMEM((rows, span), LOW)] + both_slabs,
        (gathered,),
    )

    def over_z(parts):
        return [parts[0]] + [xor_z(parts[m], m) for m in (1, 2, 3)]

    def four_cores(keep, send):
        two = [keep, flip(send, "x")]
        return two + [flip(value, "c") for value in two]

    first_keep, first_other, first_across = keep, flip(send, "x"), flip(keep, "c")
    my_tokens = query_unit.shape[0]

    def second_stage():
        return whole(
            second_kernel,
            "second",
            index,
            (
                part, flip(part, "y"), first, line(contract_bias), line(second_gain),
                line(second_shift), head_weight, query_unit, kdoc0,
            ),
            [low_rows, wide_rows, thin_rows] + [shape((rows, proj), t) for t in (WIDE, LOW)]
            + [shape((rows, my_tokens), WIDE), shape((docs, my_tokens), LOW)]
            + [shape((rows, proj), WIDE)],
        )

    second_low, unitary2, inverse2, embed, unit_low, expo, totals, message = stage(second_stage)
    totals = after(totals, first_across)

    def tree(own, one, two, three):
        one, two, three = [part.astype(WIDE) for part in (one, two, three)]
        return ((own.astype(WIDE) + one) + (two + three)).astype(LOW)

    chunk = width // (NZ * 4)
    sums_dims = (NZ * 2, chunk + 16, proj)
    def middle_stage():
        sums = sum_outer(tree(totals, *[xor_s(totals, m) for m in (1, 2, 3)]))
        return whole(
            partial(middle_kernel, queries_count),
            "middle",
            index,
            (
                sums, *[xor_z(sums, m) for m in (1, 2, 3)], kdoc0, kdoc1, positive, expo, query_unit,
                unit_low, embed, second_low, head_weight, out_cotangent, unitary2, inverse2,
                line(second_gain), hidden_in,
            ),
            [wide_rows]
            + [shape((2 * rows, width), LOW)] * 2
            + [low_rows, shape((8, proj), WIDE), shape((docs, my_tokens), WIDE)]
            + [shape(sums_dims, WIDE), shape(sums_dims, LOW)],
            [
                pltpu.VMEM((rows, my_tokens), LOW),
                pltpu.VMEM((rows, width), LOW),
                pltpu.VMEM((rows, span), LOW),
                pltpu.VMEM((width, proj), WIDE),
                pltpu.VMEM((NZ * 4 * 16, proj), WIDE),
            ]
            + both_slabs,
            (gathered,),
        )

    grad_second_in, keep, send, part, loss, coefficients, sums_own, sums_send = stage(middle_stage)

    part, first_other = lax.optimization_barrier((part, first_other))
    units = lax.all_gather(after(message, part), BLK, axis=0, tiled=True)
    keep_other, keep_across = flip(send, "x"), flip(keep, "c")

    def first_stage():
        return whole(
            partial(first_back_kernel, pieces),
            "first_back",
            index,
            (
                part, flip(part, "y"), grad_second_in, unitary1, inverse1, line(first_gain),
                sums_own, flip(sums_send, "c"),
            ),
            [wide_rows, low_rows, shape((8, width), WIDE)]
            + [shape((NZ * 2, half + chunk + 16, PAIR), LOW)],
            piece_scratch(width, 2 * QUAD),
            outs,
        )

    grad_first_in, grad_branch, vectors1, pack = stage(first_stage)
    keep_other, triple_low, grad_branch = lax.optimization_barrier((keep_other, triple_low, grad_branch))
    dims, dims_out = (2, slab, quarter), (2, slab, QUAD)
    dims_both = (2, slab, quarter + QUAD)
    left_right = [pltpu.VMEM((4 * rows, width), LOW)]

    def parts_of(left, right):
        part = dot_tn(jnp.concatenate(left), jnp.concatenate(right))
        part = pick(narrow(part.reshape(outer, NZ, 2, 2, slab, -1)), mc, 2)
        for axis, spot in ((0, mz), (1, mx)):
            part = jnp.take(part, jnp.arange(part.shape[axis]) ^ spot, axis=axis)
        return part

    def low_parts(parts):
        return [parts[0]] + [parts[m].astype(LOW) for m in (1, 2, 3)]

    def weights_stage():
        got = to_blocks(pack)
        firsts = [first_keep, first_other, first_across, flip(first_other, "c")]
        grads = [keep, keep_other, keep_across, flip(keep_other, "c")]
        other = flip(grad_branch, "x")
        got = got, [other, flip(grad_branch, "c"), flip(other, "c")], firsts[3]
        if outer == 1:
            parts = whole(
                weights_kernel,
                "weights",
                index,
                (*firsts, *grads),
                [shape((2,) + dims, WIDE), shape((2,) + dims, LOW)] * 2,
                left_right * 2,
            )
            return got, list(parts)
        top, mid = slice(0, rows), slice(rows, 2 * rows)
        contract = parts_of([g[top] for g in grads], [f[mid] for f in firsts])
        expand = parts_of([f[top] for f in firsts], [g[mid] for g in grads])
        return got, [part for p in (contract, expand) for part in (p[::2], p[1::2].astype(LOW))]

    (grad_out, branches, first_last), weight_parts = stage(weights_stage)
    branches = [grad_branch] + branches
    firsts = [first_keep, first_other, first_across, first_last]
    contract_keep, contract_send, expand_keep, expand_send = weight_parts
    contract_got, expand_got = xor_z(contract_send, 1), xor_z(expand_send, 1)

    def attend_stage():
        grad_query, dkv0, dkv1 = attend_back(
            *steps, queries, grad_out.reshape(NZ, 2, -1, PAIR), out, log_total, kv0, kv1, *meta
        )
        dkv0, dkv1 = [narrow(v.reshape(outer, -1, PAIR)) for v in (dkv0, dkv1)]
        triple = whole(
            triple_kernel,
            "triple",
            index,
            (grad_query.reshape(count, PAIR), dkv0, flip(dkv1, "c"), cosine, sine),
            [shape((count, QUAD), LOW), shape((NZ * 2, rows * 3 // 4, QUAD), LOW)],
        )
        return triple

    grad_triple, dense_triple = stage(attend_stage)
    grad_triple, contract_got = lax.optimization_barrier((grad_triple, contract_got))
    contract_own, contract_send = whole(
        pair_kernel, "pair", index, (contract_keep, contract_got), [shape(dims, t) for t in (WIDE, LOW)]
    )
    contract_got = xor_z(contract_send, 2)
    grad_triple, units = lax.optimization_barrier((grad_triple, units, contract_own))[:2]
    dims_triple = (NZ * 2, slab + extra_count(slab), QUAD)
    vector = shape((width // PAIR, PAIR), WIDE)

    def triple_parts():
        if outer == 1:
            return whole(
                triple_weight_kernel,
                "triple_weight",
                index,
                (*sheets, grad_triple, vectors1),
                [shape(dims_triple, LOW)] * 2,
                [pltpu.VMEM((width, QUAD), WIDE), pltpu.VMEM((count, width), LOW)],
            )
        ordered = [(mz * 2 + (mx ^ x), sheets[x]) for x in range(2)]
        for m in (1, 2, 3):
            two = both(*sheets[2 * m : 2 * m + 2], my)
            for x in range(2):
                ordered.append(((mz ^ m) * 2 + (mx ^ x), two[:, x].reshape(rows, width)))
        ordered = place(ordered).reshape(count, width)
        part = narrow(dot_tn(ordered, grad_triple).reshape(outer, NZ * 2, 2, slab, QUAD))
        bias = sum_outer(jnp.sum(grad_triple, axis=0, dtype=WIDE))
        bias = extra_rows(line(bias), sum_outer(vectors1))
        bias = jnp.broadcast_to(bias, (NZ * 2, 2, 16, QUAD))
        part = jnp.concatenate([part, bias], axis=2).astype(LOW)
        return pick(part, mc, 1), pick(part, 1 - mc, 1)

    def output_parts_of():
        if outer == 1:
            return whole(
                output_kernel,
                "output",
                index,
                (*firsts, *branches),
                [shape((2,) + dims_out, t) for t in (WIDE, LOW)],
                left_right + [pltpu.VMEM((4 * rows, QUAD), LOW)],
            )
        wide = [f[2 * rows :].reshape(few, 4, QUAD).transpose(1, 0, 2).reshape(rows, QUAD) for f in firsts]
        parts = parts_of(branches, wide)
        return parts[::2], parts[1::2].astype(LOW)

    def triple_stage():
        block_triple = to_blocks(dense_triple)
        keep, send = triple_parts()
        output_parts = output_parts_of()
        mine = whole(
            partial(query_back_kernel, half),
            "query_back",
            index,
            (kdoc0, kdoc1, coefficients, own_queries, units, sum_outer(grad_out)),
            [shape((shares + chunk + 16, proj), LOW)],
        )[0]
        return block_triple, keep, send, output_parts[0], xor_z(output_parts[1], 1), mine

    block_triple, packed_keep, packed_send, output_keep, output_got, mine = stage(triple_stage)
    block_triple, contract_got, expand_got = lax.optimization_barrier(
        (block_triple, contract_got, expand_got)
    )
    expand_own, output_own, both_send = whole(
        pair_kernel,
        "pair",
        index,
        (expand_keep, expand_got, output_keep, output_got),
        [shape(dims, WIDE), shape(dims_out, WIDE), shape(dims_both, LOW)],
    )
    both_got = xor_z(both_send, 2)
    block_triple = after(block_triple, expand_own)
    spread = lax.all_gather(after(mine, expand_own), ("z", "x", "c"))

    def tokens_stage():
        part = whole(
            tokens_kernel,
            "tokens",
            index,
            (block_triple,),
            [low_rows],
            [pltpu.VMEM((rows, 6 * QUAD), LOW)] + slab_scratch(width, 6 * QUAD),
            (triple_low,),
        )[0]
        part_other = flip(part, "y")
        packed = whole(
            pair_sum_kernel,
            "pair_sum",
            index,
            (packed_keep, flip(packed_send, "c")),
            [shape(dims_triple, LOW)],
        )[0]
        tokens_grad = whole(
            tokens_sum_kernel, "tokens_sum", index, (after(part, packed), part_other, grad_first_in), [wide_rows]
        )[0]
        return tokens_grad, packed

    tokens_grad, packed = stage(tokens_stage)
    packed = lax.all_to_all(after(packed, tokens_grad), ("z", "x"), 0, 0)
    contract_own, spread = after(contract_own, tokens_grad), after(spread, tokens_grad)
    keep, keep_out, send = whole(
        line_sum_kernel,
        "line_sum",
        index,
        (contract_own, contract_got, expand_own, output_own, both_got),
        [shape((2, slab, quarter), WIDE), shape((slab, QUAD), WIDE), shape((slab, 2 * quarter + QUAD), LOW)],
    )
    triple_grad, triple_bias_grad, output_bias_grad, gain_one, shift_one = whole(
        triple_out_kernel,
        "triple_out",
        index,
        (packed,),
        [shape((3, slab, 2 * QUAD), WIDE), shape((3, 2 * QUAD), WIDE)] + [vector] * 3,
    )
    contract_grad, expand_grad, output_grad = whole(
        columns_kernel,
        "columns",
        index,
        (keep, keep_out, flip(send, "x")),
        [shape((slab, n), WIDE) for n in (span, span, 2 * QUAD)],
    )

    queries_grad, head_grad, contract_bias_grad, gain_two, shift_two, expand_bias_grad = whole(
        spread_kernel,
        "spread",
        index,
        (after(spread, contract_grad).reshape(NZ * 4, -1, proj),),
        [shape((query_vecs.shape[0], proj), WIDE), shape((width, proj), WIDE)]
        + [vector] * 3
        + [shape((span // PAIR, PAIR), WIDE)],
    )

    return (
        second_low,
        after(loss, tokens_grad)[0, 0],
        tokens_grad,
        queries_grad,
        triple_grad.transpose(1, 0, 2),
        triple_bias_grad,
        output_grad.T,
        output_bias_grad.reshape(-1),
        gain_one.reshape(-1),
        shift_one.reshape(-1),
        expand_grad,
        expand_bias_grad.reshape(-1),
        contract_grad.T,
        contract_bias_grad.reshape(-1),
        gain_two.reshape(-1),
        shift_two.reshape(-1),
        head_grad,
    )


def solution(mesh):
    outer = mesh.shape["blk"] // 16
    five = Mesh(mesh.devices.reshape(outer, NZ, 2, 2, mesh.shape["tensor"]), BLK + ("y",))
    blk, tensor = BLK, "y"
    return jax.shard_map(
        shards,
        mesh=five,
        in_specs=(
            P(blk, None),
            P(),
            P(blk, None),
            P(),
            P(blk),
            P(),
            P(blk, None, tensor),
            P(None, tensor),
            P(tensor, blk),
            P(),
            P(),
            P(),
            P(blk, tensor),
            P(tensor),
            P(tensor, blk),
            P(),
            P(),
            P(),
            P(),
        ),
        out_specs=(
            P(blk, None),
            P(),
            P(blk, None),
            P(),
            P(blk, None, tensor),
            P(None, tensor),
            P(tensor, blk),
            P(),
            P(),
            P(),
            P(blk, tensor),
            P(tensor),
            P(tensor, blk),
            P(),
            P(),
            P(),
            P(),
        ),
        check_vma=False,
    )
```

```python
from functools import partial
import math

import jax
import jax.numpy as jnp
import numpy as np
from jax import lax
from jax.experimental import pallas as pl
from jax.experimental.pallas import tpu as pltpu
from jax.sharding import Mesh, PartitionSpec as P

HEAD_DIM = 64
PAIR = 2 * HEAD_DIM

SOFTMAX_TEMPER = 0.05
FLOOR_SCORE = -1e30
NORM_EPSILON = 1e-05
UNIT_EPSILON = 1e-06
PRECISE = lax.Precision.HIGHEST
LOW = jnp.bfloat16
WIDE = jnp.float32

BLK = ("o", "z", "x", "c")
NZ = 4
FOUR = [0, 1, 2, 3]

VMEM_BYTES = 56 * 1024 * 1024
LANES = (0, 64, 192)
QUAD = 4 * HEAD_DIM


def xor_z(value, mask):
    return lax.ppermute(value, "z", [(i, i ^ mask) for i in FOUR])


def xor_s(value, mask):
    return lax.ppermute(value, ("x", "c"), [(i, i ^ mask) for i in FOUR])


def flip(value, axis):
    return lax.ppermute(value, axis, [(0, 1), (1, 0)])


def pick(value, index, axis=0):
    return lax.dynamic_index_in_dim(value, index, axis, keepdims=False)


def after(value, *others):
    return lax.optimization_barrier((value,) + others)[0]


def place(pieces):
    first = pieces[0][1]
    whole = jnp.zeros((len(pieces),) + first.shape, first.dtype)
    for index, piece in pieces:
        whole = lax.dynamic_update_slice_in_dim(whole, piece[None], index, 0)
    return whole


def both(mine, other, where):
    return place([(where, mine), (1 - where, other)])


def doc_layout(doc_lengths, places):
    ends = jnp.cumsum(doc_lengths)
    starts = ends - doc_lengths
    passed = starts <= places[..., None]
    doc_index = jnp.sum(passed.astype(jnp.int32), axis=-1) - 1
    begin = jnp.max(jnp.where(passed, starts, 0), axis=-1)
    return (doc_index, places - begin)


def dot_nn(a, b, precision=None):
    return lax.dot_general(
        a, b, (((1,), (0,)), ((), ())), precision=precision, preferred_element_type=WIDE
    )


def dot_nt(a, b, precision=None):
    return lax.dot_general(
        a, b, (((1,), (1,)), ((), ())), precision=precision, preferred_element_type=WIDE
    )


def dot_tn(a, b, precision=None):
    return lax.dot_general(
        a, b, (((0,), (0,)), ((), ())), precision=precision, preferred_element_type=WIDE
    )


def shape(dims, dtype):
    return jax.ShapeDtypeStruct(dims, dtype)


PARAMS = pltpu.CompilerParams(vmem_limit_bytes=VMEM_BYTES)

TAKES = dict(
    prep=2.5, heads=2.0, project=3.8, attend=7.5, branch=3.5, forward=7.7, second=3.6, middle=12.0, first_back=3.8, attend_back=9.8, triple=2.9, triple_weight=2.0, tokens=3.9,
    tokens_sum=2.1, weights=5.2, output=1.5, core_sum=3.9, line_sum=2.7, pair=2.0, columns=2.2, pair_sum=0.8,
    triple_out=1.9, query_units=2.8, query_back=1.0, spread=3.5,
)


SCALE = 1.0


def cost(name):
    took = TAKES[name] * SCALE
    return pl.CostEstimate(
        flops=int(took * 1.15e9), bytes_accessed=int(took * 3.7e6), transcendentals=0
    )


def whole(kernel, name, index, inputs, outputs, scratch=(), slabs=()):
    return pl.pallas_call(
        kernel,
        in_specs=[pl.BlockSpec(memory_space=pltpu.SMEM)]
        + [pl.BlockSpec(memory_space=pltpu.VMEM)] * len(inputs)
        + [pl.BlockSpec(memory_space=pl.ANY)] * len(slabs),
        out_specs=[pl.BlockSpec(memory_space=pltpu.VMEM)] * len(outputs),
        out_shape=list(outputs),
        scratch_shapes=list(scratch),
        compiler_params=PARAMS,
        cost_estimate=cost(name),
        name=name,
    )(index, *inputs, *slabs)


def slab_copy(slabs, at, weight, sems):
    there = slabs.at[:, pl.ds(at, weight.shape[1])]
    return pltpu.make_async_copy(there, weight, sems.at[0])


def piece_copies(idx, pieces, weight, sems):
    if len(pieces) == 1:
        return [pltpu.make_async_copy(pieces[0], weight, sems.at[0])]
    count, half, _ = pieces[0].shape
    span, copies = weight.shape[1], []
    for c, piece in enumerate(pieces):
        for spot in range(count):
            there = (idx[1] ^ (spot // 2)) * 2 + (idx[2] ^ (spot % 2))
            row = (there * 2 + (idx[3] ^ c)) * 2 * half
            for i in range(2):
                rows = pl.ds(pl.multiple_of(row + i * half, half), half)
                here = piece.at[spot, :, pl.ds(i * span, span)]
                copies.append(pltpu.make_async_copy(here, weight.at[rows, :], sems.at[len(copies)]))
    return copies


def piece_scratch(rows, cols):
    return [pltpu.VMEM((rows, cols), LOW), pltpu.SemaphoreType.DMA((NZ * 8,))]


def slab_scratch(rows, cols):
    return [pltpu.VMEM((rows, cols), LOW), pltpu.SemaphoreType.DMA((1,))]


def start(copies):
    for copy in copies:
        copy.start()


def finish(copies, weight):
    for copy in copies:
        copy.wait()
    return weight[...]


def extra_count(slab):
    return 0 if slab >= HEAD_DIM else 16


def put_extra(message, slab, extra):
    if extra_count(slab):
        message[slab : slab + 16, :] = extra
        return
    for i in range(4):
        message[i * 16 : (i + 1) * 16, PAIR : PAIR + HEAD_DIM] = extra[
            :, i * HEAD_DIM : (i + 1) * HEAD_DIM
        ]


def get_extra(message, slab):
    if extra_count(slab):
        return message[slab : slab + 16, :]
    lanes = slice(PAIR, PAIR + HEAD_DIM)
    return jnp.concatenate([message[i * 16 : (i + 1) * 16, lanes] for i in range(4)], axis=1)


def prep_kernel(idx, tw, ow, ew, cw, live, tokens, heads, low, tri, mine, own):
    slab, span = ew.shape
    alive = jnp.broadcast_to(live[...], (16, live.shape[1])).astype(WIDE).astype(LOW)
    alive = jnp.concatenate([alive, jnp.zeros((16, QUAD - live.shape[1]), LOW)], axis=1)
    rows, span = tokens.shape[0], ow.shape[1]
    half = rows // 2
    mine[:half, :] = tokens[pl.ds(pl.multiple_of(idx[4] * half, half), half), :]
    own[:rows, :] = tokens[...]
    if own.shape[0] > rows:
        for i in range(2):
            part = ow[i * slab // 2 : (i + 1) * slab // 2, :].astype(LOW)
            mine[half:, i * span : (i + 1) * span] = part
            own[rows:, i * span : (i + 1) * span] = part
    span = ew.shape[1]
    for spot in range(NZ * 2):
        at = spot * HEAD_DIM
        for part, lane in enumerate(LANES):
            heads[spot, :slab, lane : lane + HEAD_DIM] = tw[part, :, at : at + HEAD_DIM].astype(LOW)
        heads[spot, :slab, PAIR : PAIR + HEAD_DIM] = jnp.zeros((slab, HEAD_DIM), LOW)
        put_extra(heads.at[spot], slab, alive)
    low[:, :span] = ew[...].astype(LOW)
    low[:, span:] = cw[...].astype(LOW)
    for part in range(3):
        tri[:, part * 2 * QUAD : (part + 1) * 2 * QUAD] = tw[part].astype(LOW)


def heads_kernel(idx, own, other, weight, live0, live1):
    slab, mc = HEAD_DIM, idx[3]
    for spot in range(NZ * 2):
        for source, c, live in ((own, mc, live0), (other, 1 - mc, live1)):
            rows = pl.ds(pl.multiple_of((spot * 2 + c) * slab, slab), slab)
            weight[rows, :] = source[spot, :slab, :]
            live[spot : spot + 1, :] = get_extra(source.at[spot], slab)[:, :PAIR].astype(WIDE)[:1]


def swap_halves(value):
    lane = lax.broadcasted_iota(jnp.int32, value.shape, 1)
    half = HEAD_DIM // 2
    return jnp.where(
        (lane & half) == 0,
        pltpu.roll(value, PAIR - half, 1),
        pltpu.roll(value, half, 1),
    )


def turn(value, cosine, sine):
    return value * cosine + swap_halves(value) * sine


def sheet_rows(idx, sheets):
    rows = sheets[0].shape[0]
    half = rows // 2
    parts = []
    for x in range(2):
        spot = idx[1] * 2 + (idx[2] ^ x)
        parts.append((sheets[x][:rows, :], pl.ds(pl.multiple_of(spot * rows, rows), rows)))
    for at, sheet in enumerate(sheets[2:]):
        z, y = at // 2 + 1, at % 2
        for x in range(2):
            spot = (idx[1] ^ z) * 2 + (idx[2] ^ x)
            row = spot * rows + (idx[4] ^ y) * half
            parts.append((sheet[x], pl.ds(pl.multiple_of(row, half), half)))
    return parts


def project_kernel(idx, *refs):
    sheets, (weight, cosine, sine, bias, query, kv, held) = refs[:8], refs[8:]
    for value, at in sheet_rows(idx, sheets):
        held[at, :] = value
    mz, mx = idx[1], idx[2]
    mine = mz * 2 + mx
    biases = []
    for part in range(3):
        total = jnp.zeros((1, HEAD_DIM), WIDE)
        for h in range(NZ * 2):
            here = bias[part : part + 1, h * HEAD_DIM : (h + 1) * HEAD_DIM]
            total = jnp.where(mine == h, here, total)
        biases.append(total)
    empty = jnp.zeros((1, HEAD_DIM), WIDE)
    offset = jnp.concatenate([biases[0], biases[1], empty, biases[2]], axis=1)
    weights = weight[...]
    rows = sheets[0].shape[0]
    low_lanes = lax.broadcasted_iota(jnp.int32, (rows, PAIR), 1) < HEAD_DIM
    for i in range(NZ * 2):
        at = slice(i * rows, (i + 1) * rows)
        triple = dot_nn(held[at, :], weights) + offset
        turned = turn(triple[:, :PAIR], cosine[at, :], sine[at, :])
        query[at, :] = jnp.where(low_lanes, turned * HEAD_DIM ** (-0.5), 0.0).astype(LOW)
        kv[at, :] = jnp.where(
            low_lanes, pltpu.roll(turned, HEAD_DIM, 1), triple[:, PAIR:]
        ).astype(LOW)


def key_row(ref):
    rows = ref[...]
    return jnp.concatenate([rows[i : i + 1] for i in range(rows.shape[0])], axis=1)


def places_of(token, rows, half, blocks, idx, z, part):
    x, upper, row = token // (2 * rows), token // rows % 2, token % rows
    block = ((idx[0] * NZ + z) * 2 + x) * 2 + idx[3]
    return (upper * half + part * rows + row) * blocks + block


def docs_of(places, lens):
    doc, begin = jnp.full(places.shape, -1, jnp.int32), jnp.int32(0)
    for i in range(lens.shape[0]):
        doc = jnp.where(begin <= places, doc + 1, doc)
        begin = begin + lens[i]
    return doc


def as_row(column):
    count = column.shape[0]
    row = lax.broadcasted_iota(jnp.int32, (count, count), 0)
    same = row == lax.broadcasted_iota(jnp.int32, (count, count), 1)
    return jnp.sum(jnp.where(same, column, 0.0), axis=0, keepdims=True)


def attend_kernel(
    blocks, idx, lens, q_ref, kv0_ref, kv1_ref, kdoc0_ref, kdoc1_ref, out_ref, log_ref, pack_ref
):
    rows, half = q_ref.shape[3], kdoc0_ref.shape[1] // 2
    queries = q_ref[0].reshape(4 * rows, PAIR)
    kv = (kv0_ref[...], kv1_ref[...])
    token = lax.broadcasted_iota(jnp.int32, (4 * rows, 1), 0)
    z, part = pl.program_id(0), pl.program_id(1)
    doc = docs_of(places_of(token, rows, half, blocks, idx, z, part), lens)
    scores = [
        jnp.where(doc == key_row(ref), dot_nt(queries, keys), FLOOR_SCORE)
        for ref, keys in zip((kdoc0_ref, kdoc1_ref), kv)
    ]
    peak = jnp.maximum(*[jnp.max(s, axis=-1, keepdims=True) for s in scores])
    weights = [jnp.exp(s - peak) for s in scores]
    total = sum(jnp.sum(w, axis=-1, keepdims=True) for w in weights)
    mixed = sum(dot_nn(w.astype(LOW), keys) for w, keys in zip(weights, kv)) / total
    out_ref[0] = mixed.reshape(2, 2, rows, PAIR)
    log_ref[0, 0] = as_row(peak + jnp.log(total))
    low_lanes = lax.broadcasted_iota(jnp.int32, (rows, PAIR), 1) < HEAD_DIM
    for x in range(2):
        upper = mixed[2 * x * rows : (2 * x + 1) * rows]
        lower = mixed[(2 * x + 1) * rows : (2 * x + 2) * rows]
        pack_ref[0, x] = jnp.where(low_lanes, pltpu.roll(upper, HEAD_DIM, 1), lower).astype(LOW)


def attend_specs(rows, keys, key_rows):
    half = rows // 2
    size = max(16, min(half, half * 2048 // (2 * keys)))
    full = lambda n, m: pl.BlockSpec((n, m), lambda i, j: (0, 0))
    part = lambda m: pl.BlockSpec((1, 2, 2, size, m), lambda i, j: (i, 0, 0, j, 0))
    pack = pl.BlockSpec((1, 2, size, PAIR), lambda i, j: (i, 0, j, 0))
    logs = pl.BlockSpec((1, 1, 1, 4 * size), lambda i, j: (i, j, 0, 0))
    kv, docs = full(keys, PAIR), full(key_rows, rows)
    return (NZ, half // size), part, pack, logs, kv, docs


SCALARS = [pl.BlockSpec(memory_space=pltpu.SMEM)] * 2


def attend(blocks, index, lens, queries, kv0, kv1, kdoc0, kdoc1):
    rows = kdoc0.shape[1]
    half = rows // 2
    grid, part, pack, logs, kv, docs = attend_specs(rows, kv0.shape[0], kdoc0.shape[0])
    return pl.pallas_call(
        partial(attend_kernel, blocks),
        grid=grid,
        in_specs=SCALARS + [part(PAIR), kv, kv, docs, docs],
        out_specs=[part(PAIR), logs, pack],
        out_shape=[
            shape((NZ, 2, 2, half, PAIR), WIDE),
            shape((NZ, grid[1], 1, 4 * half // grid[1]), WIDE),
            shape((NZ, 2, half, PAIR), LOW),
        ],
        compiler_params=PARAMS,
        cost_estimate=cost("attend"),
        name="attend",
    )(index, lens, queries.reshape(NZ, 2, 2, half, PAIR), kv0, kv1, kdoc0, kdoc1)


def attend_back_kernel(
    blocks, idx, lens, q_ref, g_ref, o_ref, log_ref, kv0_ref, kv1_ref, kdoc0_ref, kdoc1_ref,
    dq_ref, dkv0_ref, dkv1_ref, column0, column1, held,
):
    rows, width = q_ref.shape[3], kdoc0_ref.shape[1]
    z, part = pl.program_id(0), pl.program_id(1)

    @pl.when((z == 0) & (part == 0))
    def _():
        dkv0_ref[...] = jnp.zeros_like(dkv0_ref)
        held[...] = jnp.zeros_like(held)
        for ref, column in ((kdoc0_ref, column0), (kdoc1_ref, column1)):
            turned = jnp.transpose(ref[...].astype(WIDE))
            for i in range(ref.shape[0]):
                column[i * width : (i + 1) * width, :] = turned[:, i : i + 1]

    queries = q_ref[0].reshape(4 * rows, PAIR)
    high_lanes = lax.broadcasted_iota(jnp.int32, (rows, PAIR), 1) >= HEAD_DIM
    parts = []
    for x in range(2):
        packed = g_ref[0, x].astype(WIDE)
        parts.append(jnp.where(high_lanes, pltpu.roll(packed, HEAD_DIM, 1), 0.0))
        parts.append(jnp.where(high_lanes, packed, 0.0))
    wide = jnp.concatenate(parts, axis=0)
    grads = wide.astype(LOW)
    delta = as_row(jnp.sum(wide * o_ref[0].reshape(4 * rows, PAIR), axis=-1, keepdims=True))
    token = lax.broadcasted_iota(jnp.int32, (1, 4 * rows), 1)
    doc = docs_of(places_of(token, rows, width // 2, blocks, idx, z, part), lens).astype(WIDE)
    log_total = log_ref[0, 0]
    total = jnp.zeros((4 * rows, PAIR), WIDE)
    for kv_ref, column, dkv_ref in ((kv0_ref, column0, dkv0_ref), (kv1_ref, column1, held)):
        keys = kv_ref[...]
        raw = dot_nt(keys, queries)
        probs = jnp.where(column[...] == doc, jnp.exp(raw - log_total), 0.0)
        dprobs = dot_nt(keys, grads)
        dscores = (probs * (dprobs - delta)).astype(LOW)
        total = total + dot_tn(dscores, keys)
        dkv_ref[...] += dot_nn(dscores, queries) + dot_nn(probs.astype(LOW), grads)
    dq_ref[0] = (total * HEAD_DIM ** (-0.5)).reshape(2, 2, rows, PAIR)

    @pl.when((z == pl.num_programs(0) - 1) & (part == pl.num_programs(1) - 1))
    def _():
        dkv1_ref[...] = held[...].astype(LOW)


def attend_back(blocks, index, lens, queries, grads, out, log_total, kv0, kv1, kdoc0, kdoc1):
    rows, keys = kdoc0.shape[1], kv0.shape[0]
    half = rows // 2
    grid, part, pack, logs, kv, docs = attend_specs(rows, keys, kdoc0.shape[0])
    return pl.pallas_call(
        partial(attend_back_kernel, blocks),
        grid=grid,
        in_specs=SCALARS + [part(PAIR), pack, part(PAIR), logs, kv, kv, docs, docs],
        out_specs=[part(PAIR), kv, kv],
        out_shape=[
            shape((NZ, 2, 2, half, PAIR), WIDE),
            shape((keys, PAIR), WIDE),
            shape((keys, PAIR), LOW),
        ],
        scratch_shapes=[pltpu.VMEM((keys, 1), WIDE)] * 2 + [pltpu.VMEM((keys, PAIR), WIDE)],
        compiler_params=PARAMS,
        cost_estimate=cost("attend_back"),
        name="attend_back",
    )(
        index, lens, queries.reshape(NZ, 2, 2, half, PAIR), grads, out, log_total, kv0, kv1,
        kdoc0, kdoc1,
    )


def branch_kernel(pieces, idx, got, *refs):
    slabs, (low, part, held, sems) = refs[:pieces], refs[pieces:]
    copy = piece_copies(idx, slabs, held, sems)
    start(copy)
    half = got.shape[1]
    for h in range(NZ * 2):
        lanes = slice(h * HEAD_DIM, (h + 1) * HEAD_DIM)
        low[:half, lanes] = got[h, :, :HEAD_DIM]
        low[half:, lanes] = got[h, :, HEAD_DIM:]
    part[...] = dot_nt(low[...], finish(copy, held)).astype(LOW)


def normalize(value):
    center = value - jnp.mean(value, axis=-1, keepdims=True)
    spread = jnp.mean(center * center, axis=-1, keepdims=True)
    inverse = lax.rsqrt(spread + NORM_EPSILON)
    return center * inverse, inverse


def pair(own, other):
    return own[...].astype(WIDE) + other[...].astype(WIDE)


def forward_kernel(
    idx, own, other, tokens, bias, gain, shift, hidden_bias, attended, slabs,
    first, unitary, inverse, hidden_in, keep, send, part,
    low, hidden, expand, sems1, contract, sems2,
):
    copy1 = [slab_copy(slabs, 0, expand, sems1)]
    copy2 = [slab_copy(slabs, expand.shape[1], contract, sems2)]
    start(copy1 + copy2)
    value = tokens[...].astype(WIDE) + (pair(own, other) + bias[...])
    unitary[...], inverse[...] = normalize(value)
    first[...] = unitary[...] * gain[...] + shift[...]
    low[...] = first[...].astype(LOW)
    value = dot_nn(low[...], finish(copy1, expand)) + hidden_bias[...]
    hidden_in[...] = value
    hidden[...] = (0.5 * value * (1.0 + lax.erf(value * (0.5**0.5)))).astype(LOW)
    part[...] = dot_nt(hidden[...], finish(copy2, contract)).astype(LOW)
    rows, width = low.shape
    few = rows * QUAD // width
    for out, x in ((keep, idx[2]), (send, 1 - idx[2])):
        out[:rows, :] = low[...]
        out[rows : 2 * rows, :] = columns_of(hidden, x, width)
        for i in range(width // QUAD):
            out[2 * rows :, i * QUAD : (i + 1) * QUAD] = attended[
                i * few : (i + 1) * few, pl.ds(pl.multiple_of(x * QUAD, QUAD), QUAD)
            ]


def columns_of(ref, x, span):
    return ref[:, pl.ds(pl.multiple_of(x * span, 128), span)]


def unit_scale(value):
    return lax.rsqrt(jnp.sum(value * value, axis=-1, keepdims=True) + UNIT_EPSILON)


def second_kernel(
    idx, own, other, first, bias, gain, shift, head, query, kdoc,
    low, unitary, inverse, embed, unit, expo, totals, message,
):
    value = first[...] + (pair(own, other) + bias[...])
    unitary[...], inverse[...] = normalize(value)
    low[...] = (unitary[...] * gain[...] + shift[...]).astype(LOW)
    embed[...] = dot_nn(low[...], head[...].astype(LOW))
    unit[...] = (embed[...] * unit_scale(embed[...])).astype(LOW)
    message[...] = unit[...].astype(WIDE)
    expo[...] = jnp.exp(dot_nt(unit[...], query[...]) / SOFTMAX_TEMPER)
    totals[...] = dot_nn(member(idx, kdoc, totals.shape[0]), expo[...], PRECISE).astype(LOW)


def query_kernel(idx, vecs, out, own):
    block, shares = (idx[1] * 2 + idx[2]) * 2 + idx[3], own.shape[0]
    own[...] = vecs[pl.ds(pl.multiple_of(block * shares, shares), shares), :]
    value = vecs[...].astype(WIDE)
    out[...] = (value * unit_scale(value)).astype(LOW)


def member(idx, kdoc, docs):
    row = kdoc[pl.ds((idx[0] * NZ + idx[1]) * 2 + idx[2], 1), :]
    label = lax.broadcasted_iota(jnp.int32, (docs, row.shape[1]), 0)
    return jnp.where(row == label, 1.0, 0.0)


def group_sum(value, length):
    column = lax.broadcasted_iota(jnp.int32, value.shape, 1)
    span = value.shape[1]
    step = 1
    while step < length:
        ahead, behind = pltpu.roll(value, span - step, 1), pltpu.roll(value, step, 1)
        value = value + jnp.where((column & step) == 0, ahead, behind)
        step *= 2
    return value


def loss_of(count, totals, kdocs, positive):
    docs, columns = totals.shape
    length = columns // count
    label = lax.broadcasted_iota(jnp.int32, (docs, 1), 0)
    tokens = jnp.zeros((docs, 1), WIDE)
    for ref in kdocs:
        tokens = tokens + jnp.sum(jnp.where(key_row(ref) == label, 1.0, 0.0), axis=1, keepdims=True)
    doc_score = group_sum(SOFTMAX_TEMPER * (jnp.log(totals) - jnp.log(tokens)), length)
    best = jnp.max(doc_score, axis=0, keepdims=True)
    shifted = jnp.exp(doc_score - best)
    shifted_sum = jnp.sum(shifted, axis=0, keepdims=True)
    chosen = jnp.where(label == positive, 1.0, 0.0)
    each = best + jnp.log(shifted_sum) - jnp.sum(doc_score * chosen, axis=0, keepdims=True)
    loss = jnp.sum(each, axis=1, keepdims=True) / columns
    return loss, (shifted / shifted_sum - chosen) / (totals * count)


def unit_back(value, grad):
    scale = unit_scale(value)
    along = jnp.sum(grad * value, axis=-1, keepdims=True)
    return scale * grad - value * (along * scale * scale * scale)


def query_back_kernel(half, idx, kdoc0, kdoc1, coefficients, value, units, got, out):
    shares = value.shape[0]
    block = (idx[1] * 2 + idx[2]) * 2 + idx[3]
    columns_here = pl.ds(pl.multiple_of(block * shares, shares), shares)
    coefficient = coefficients[:, columns_here]
    docs = coefficient.shape[0]
    pads = jnp.zeros((-docs % 8, shares), WIDE)
    coefficient = jnp.transpose(jnp.concatenate([coefficient, pads]) if docs % 8 else coefficient)
    queries = value[...].astype(WIDE)
    query = (queries * unit_scale(queries)).astype(LOW)
    rows, group = kdoc0.shape[1], 4
    count = units.shape[0] // rows

    def add(at, total):
        labels = []
        for step in range(group):
            block = at * group + step
            spot = block // 2
            labels.append(
                jnp.where(block % 2 == idx[3], kdoc0[pl.ds(spot, 1), :], kdoc1[pl.ds(spot, 1), :])
            )
        row = jnp.concatenate(labels, axis=1)
        unit = units[pl.ds(at * group * rows, group * rows), :].astype(LOW)
        if docs <= 8:
            chosen = jnp.zeros((shares, group * rows), WIDE)
            for doc in range(docs):
                chosen = jnp.where(row == doc, coefficient[:, doc : doc + 1], chosen)
        else:
            label = lax.broadcasted_iota(jnp.int32, (coefficient.shape[1], group * rows), 0)
            chosen = dot_nn(coefficient, jnp.where(row == label, 1.0, 0.0), PRECISE)
        expo = jnp.exp(dot_nt(query, unit) / SOFTMAX_TEMPER)
        return total + dot_nn((chosen * expo).astype(LOW), unit)

    steps, total = count // group, jnp.zeros(queries.shape, WIDE)
    if steps <= 4:
        for at in range(steps):
            total = add(at, total)
    else:
        total = lax.fori_loop(0, steps, add, total)
    out[:shares, :] = unit_back(queries, total).astype(LOW)
    sums = [got[spot, half:, :].astype(WIDE) for spot in range(NZ * 2)]
    while len(sums) > 1:
        sums = [a + b for a, b in zip(sums[::2], sums[1::2])]
    out[shares:, :] = sums[0].astype(LOW)


def spread_kernel(idx, got, queries, head, *vectors):
    rows = got.shape[1]
    chunk = head.shape[0] // (NZ * 4)
    shares = rows - chunk - 16
    pieces = []
    for i in range(NZ * 4):
        queries[i * shares : (i + 1) * shares, :] = got[i, :shares, :].astype(WIDE)
        head[i * chunk : (i + 1) * chunk, :] = got[i, shares : shares + chunk, :].astype(WIDE)
        pieces.append(got[i, shares + chunk : shares + chunk + 16, :].astype(WIDE))
    row = 0
    for out in vectors:
        for i in range(0, out.shape[0], 8):
            out[i : i + 8, :] = pieces[row // 16][row % 16 : row % 16 + 8]
            row += 8


def norm_back(grad, gain, unitary, inverse):
    scaled = grad * gain
    along = jnp.mean(scaled * unitary, axis=-1, keepdims=True)
    return inverse * (scaled - jnp.mean(scaled, axis=-1, keepdims=True) - unitary * along)


def column_sum(value):
    return jnp.sum(value, axis=0, keepdims=True)


def middle_kernel(
    count, idx, t0, t1, t2, t3, kdoc0, kdoc1, positive, expo, query, unit,
    embed, low, head, cotangent, unitary, inverse, gain, hidden_in, slabs,
    grad_in, keep, send, part, loss, coefficients, sums0, sums1,
    similar, grad_low, grad_hidden_in, head_part, rows_part, expand, sems1, contract, sems2,
):
    copy1 = [slab_copy(slabs, 0, expand, sems1)]
    copy2 = [slab_copy(slabs, expand.shape[1], contract, sems2)]
    start(copy2 + copy1)
    totals = pair(t0, t1) + pair(t2, t3)
    value, coefficient = loss_of(count, totals, (kdoc0, kdoc1), positive[...])
    loss[...] = jnp.broadcast_to(value, loss.shape)
    coefficients[...] = coefficient
    here = member(idx, kdoc0, totals.shape[0])
    similar[...] = (dot_tn(here, coefficient, PRECISE) * expo[...]).astype(LOW)
    grad_embed = unit_back(embed[...], dot_nn(similar[...], query[...])).astype(LOW)
    rows, width = embed.shape[0], low.shape[1]
    head_part[...] = dot_tn(low[...], grad_embed)
    grad_second = dot_nt(grad_embed, head[...].astype(LOW)) + cotangent[...].astype(WIDE)
    grad_in[...] = norm_back(grad_second, gain[...], unitary[...], inverse[...])
    grad_low[...] = grad_in[...].astype(LOW)
    sums = [
        column_sum(grad_low[...].astype(WIDE)),
        column_sum(grad_second * unitary[...]),
        column_sum(grad_second),
    ]
    value = hidden_in[...]
    grad = dot_nn(grad_low[...], finish(copy2, contract))
    bell = jnp.exp(-0.5 * value * value) * (1.0 / math.sqrt(2.0 * math.pi))
    slope = 0.5 * (1.0 + lax.erf(value * (0.5**0.5))) + value * bell
    grad_hidden_in[...] = (slope * grad).astype(LOW)
    sums.append(column_sum(grad_hidden_in[...].astype(WIDE)))
    part[...] = dot_nt(grad_hidden_in[...], finish(copy1, expand)).astype(LOW)
    for out, x in ((keep, idx[2]), (send, 1 - idx[2])):
        out[:rows, :] = grad_low[...]
        out[rows:, :] = columns_of(grad_hidden_in, x, width)
    rows_part[...] = jnp.zeros_like(rows_part)
    at = 0
    for value in sums:
        for i in range(value.shape[1] // PAIR):
            rows_part[at : at + 1, :] = value[:, i * PAIR : (i + 1) * PAIR]
            at += 1
    chunk = width // (NZ * 4)
    for spot in range(NZ * 2):
        for out, c in ((sums0, idx[3]), (sums1, 1 - idx[3])):
            at = spot * 2 + c
            out[spot, :chunk, :] = head_part[
                pl.ds(pl.multiple_of(at * chunk, chunk), chunk), :
            ].astype(out.dtype)
            out[spot, chunk:, :] = rows_part[pl.ds(pl.multiple_of(at * 16, 16), 16), :].astype(
                out.dtype
            )


def slab_products(idx, left, right, outs):
    slab = outs[0].shape[-2]
    for z, out in enumerate(outs):
        mine = []
        for x in range(2):
            spot = (idx[1] ^ z) * 2 + (idx[2] ^ x)
            lanes = left[:, pl.ds(pl.multiple_of(spot * 2 * slab, 2 * slab), 2 * slab)]
            mine.append(jnp.where(idx[3] == 0, lanes[:, :slab], lanes[:, slab:]))
        both_rows = dot_tn(jnp.concatenate(mine, axis=1), right)
        for x in range(2):
            out[x] = both_rows[x * slab : (x + 1) * slab].astype(out.dtype)


def weights_kernel(idx, f0, f1, f2, f3, g0, g1, g2, g3, *refs):
    keep0, send0, keep1, send1, left, right = refs
    rows = g0.shape[0] // 2
    firsts, grads = (f0, f1, f2, f3), (g0, g1, g2, g3)
    for keep, send, lefts, rights in ((keep0, send0, grads, firsts), (keep1, send1, firsts, grads)):
        for i in range(4):
            left[i * rows : (i + 1) * rows, :] = lefts[i][:rows, :]
            right[i * rows : (i + 1) * rows, :] = rights[i][rows : 2 * rows, :]
        slab_products(idx, left, right[...], [keep.at[0], send.at[0], keep.at[1], send.at[1]])


def pair_kernel(idx, *refs):
    count = (len(refs) - 1) // 3
    gots, owns, send, at = refs[: 2 * count], refs[2 * count : -1], refs[-1], 0
    for i, own in enumerate(owns):
        keep, got, span = gots[2 * i], gots[2 * i + 1], own.shape[-1]
        own[...] = keep[0] + got[0].astype(WIDE)
        send[:, :, at : at + span] = (keep[1] + got[1].astype(WIDE)).astype(LOW)
        at += span


def output_kernel(idx, f0, f1, f2, f3, g0, g1, g2, g3, keep, send, left, right):
    rows, width = g0.shape
    few = rows * QUAD // width
    for i, (f, g) in enumerate(zip((f0, f1, f2, f3), (g0, g1, g2, g3))):
        left[i * rows : (i + 1) * rows, :] = g[...]
        for j in range(width // QUAD):
            right[i * rows + j * few : i * rows + (j + 1) * few, :] = f[
                2 * rows :, j * QUAD : (j + 1) * QUAD
            ]
    slab_products(idx, left, right[...], [keep.at[0], send.at[0], keep.at[1], send.at[1]])


def line_sum_kernel(idx, own0, got0, own1, own2, got, keep, keep_out, send):
    at = 0
    for own, other, out in (
        (own0, got0[...], keep.at[0]),
        (own1, got[:, :, : own1.shape[-1]], keep.at[1]),
        (own2, got[:, :, own1.shape[-1] :], keep_out),
    ):
        span = own.shape[-1]
        out[...] = own[0] + other[0].astype(WIDE)
        send[:, at : at + span] = (own[1] + other[1].astype(WIDE)).astype(LOW)
        at += span


def columns_kernel(idx, keep, keep_out, got, contract, expand, output):
    span = keep.shape[-1]
    for at, mine, out in ((0, keep[0], contract), (span, keep[1], expand), (2 * span, keep_out[...], output)):
        cols = mine.shape[1]
        out[:, pl.ds(pl.multiple_of(idx[2] * cols, 128), cols)] = mine
        out[:, pl.ds(pl.multiple_of((1 - idx[2]) * cols, 128), cols)] = got[
            :, at : at + cols
        ].astype(WIDE)


def first_back_kernel(
    pieces, idx, own, other, grad_second_in, unitary, inverse, gain, sums0, sums1, *refs
):
    slabs, (grad_in, grad_low, vectors, pack, held, sems) = refs[:pieces], refs[pieces:]
    copy = piece_copies(idx, slabs, held, sems)
    start(copy)
    grad_first = grad_second_in[...] + pair(own, other)
    grad_in[...] = norm_back(grad_first, gain[...], unitary[...], inverse[...])
    grad_low[...] = grad_in[...].astype(LOW)
    vectors[...] = jnp.zeros_like(vectors)
    vectors[0:1, :] = column_sum(grad_low[...].astype(WIDE))
    vectors[1:2, :] = column_sum(grad_first * unitary[...])
    vectors[2:3, :] = column_sum(grad_first)
    grad = dot_nn(grad_low[...], finish(copy, held)).astype(LOW)
    half = grad.shape[0] // 2
    for h in range(NZ * 2):
        lanes = slice(h * HEAD_DIM, (h + 1) * HEAD_DIM)
        pack[h, :half, :HEAD_DIM] = grad[:half, lanes]
        pack[h, :half, HEAD_DIM:] = grad[half:, lanes]
        pack[h, half:, :] = (sums0[h] + sums1[h].astype(WIDE)).astype(LOW)


def triple_kernel(idx, dq, dkv, got, cosine, sine, out, dense):
    rows = dq.shape[0]
    low_lanes = lax.broadcasted_iota(jnp.int32, (rows, PAIR), 1) < HEAD_DIM
    grads = dkv[...] + got[...].astype(WIDE)
    both_parts = jnp.where(low_lanes, dq[...], pltpu.roll(grads, HEAD_DIM, 1))
    turned = turn(both_parts, cosine[...], -sine[...])
    turned, value = turned.astype(LOW), grads[:, HEAD_DIM:].astype(LOW)
    out[:, :PAIR] = turned
    out[:, PAIR:] = jnp.where(low_lanes, 0.0, grads).astype(LOW)
    rows = dense.shape[1] * 4 // 3
    half, few = rows // 2, rows // 4
    for i in range(dense.shape[0]):
        at = i * rows
        dense[i, :half, :PAIR] = turned[at : at + half]
        dense[i, :half, PAIR:] = turned[at + half : at + rows]
        for j in range(4):
            dense[i, half:, j * HEAD_DIM : (j + 1) * HEAD_DIM] = value[
                at + j * few : at + (j + 1) * few
            ]


def extra_rows(bias, vectors):
    cols = bias.shape[1]
    rows = [bias]
    for i in range(3):
        for j in range(vectors.shape[1] // cols):
            rows.append(vectors[i : i + 1, j * cols : (j + 1) * cols])
    return jnp.concatenate(rows + [jnp.zeros((16 - len(rows), cols), WIDE)], axis=0)


def triple_weight_kernel(idx, *refs):
    sheets, (grad, vectors, keep, send, total, held) = refs[:8], refs[8:]
    mc = idx[3]
    slab = HEAD_DIM
    for value, at in sheet_rows(idx, sheets):
        held[at, :] = value
    total[...] = dot_tn(held[...], grad[...])
    extra = extra_rows(column_sum(grad[...].astype(WIDE)), vectors).astype(LOW)
    for spot in range(NZ * 2):
        for out, c in ((keep, mc), (send, 1 - mc)):
            at = pl.ds(pl.multiple_of((spot * 2 + c) * slab, slab), slab)
            out[spot, :slab, :] = total[at, :].astype(LOW)
            put_extra(out.at[spot], slab, extra)


def pair_sum_kernel(idx, one, two, out):
    out[...] = (one[...].astype(WIDE) + two[...].astype(WIDE)).astype(out.dtype)


def triple_out_kernel(idx, got, weight, bias, *vectors):
    slab = weight.shape[1]
    total = 0.0
    for spot in range(NZ * 2):
        at = spot * HEAD_DIM
        here, extra = got[spot].astype(WIDE), get_extra(got.at[spot], slab).astype(WIDE)
        for part, lane in enumerate(LANES):
            weight[part, :, at : at + HEAD_DIM] = here[:slab, lane : lane + HEAD_DIM]
            bias[part : part + 1, at : at + HEAD_DIM] = extra[:1, lane : lane + HEAD_DIM]
        total = total + extra
    row = 1
    for out in vectors:
        for i in range(0, out.shape[0], 2):
            out[i : i + 1, :] = total[row : row + 1, :PAIR]
            out[i + 1 : i + 2, :] = total[row : row + 1, PAIR:]
            row += 1


def tokens_kernel(idx, got, message, part, group, held, sems):
    copy = slab_copy(message, 0, held, sems)
    copy.start()
    rows = part.shape[0]
    half, few = rows // 2, rows // 4
    for h in range(NZ * 2):
        for p in range(2):
            at = (p * NZ * 2 + h) * HEAD_DIM
            for i in range(2):
                lane = i * PAIR + p * HEAD_DIM
                group[i * half : (i + 1) * half, at : at + HEAD_DIM] = got[
                    h, :half, lane : lane + HEAD_DIM
                ]
        at = (2 * NZ * 2 + h) * HEAD_DIM
        for j in range(4):
            group[j * few : (j + 1) * few, at : at + HEAD_DIM] = got[
                h, half:, j * HEAD_DIM : (j + 1) * HEAD_DIM
            ]
    copy.wait()
    part[...] = dot_nt(group[...], held[...]).astype(LOW)


def tokens_sum_kernel(idx, own, other, grad, out):
    out[...] = grad[...] + pair(own, other)


def shards(
    tokens,
    query_vecs,
    out_cotangent,
    doc_lengths,
    live_mask,
    positives,
    triple_weight,
    triple_bias,
    output_weight,
    output_bias,
    first_gain,
    first_shift,
    expand_weight,
    expand_bias,
    contract_weight,
    contract_bias,
    second_gain,
    second_shift,
    head_weight,
):
    outer = lax.axis_size("o")
    mo, mz, mx, mc, my = [lax.axis_index(a) for a in ("o", "z", "x", "c", "y")]
    index = jnp.stack([mo, mz, mx, mc, my]).astype(jnp.int32)
    rows, width = tokens.shape
    half = rows // 2
    slab = triple_weight.shape[0]
    docs = doc_lengths.shape[0]
    queries_count = positives.shape[0]
    blocks = outer * NZ * 4
    span = expand_weight.shape[1]
    quarter = span // 2
    proj = head_weight.shape[1]
    line = lambda vector: vector.reshape(1, -1)

    def widen(value):
        return lax.all_gather(value, "o") if outer > 1 else value[None]

    def narrow(value):
        return lax.psum_scatter(value, "o") if outer > 1 else value[0]

    def sum_outer(value):
        return lax.psum(value, "o") if outer > 1 else value

    def stage(work):
        like = jax.eval_shape(work)
        idle = lambda: jax.tree.map(lambda leaf: jnp.zeros(leaf.shape, leaf.dtype), like)
        return lax.cond(doc_lengths[0] >= 0, work, idle)

    def key_doc(live, c):
        block = jnp.arange(outer * NZ * 2, dtype=jnp.int32) * 2 + c
        doc = doc_layout(doc_lengths, block[:, None] + where[None, :])[0]
        return jnp.where(live > 0, doc, -1)

    def head_weights(heads, heads_other):
        if outer > 1:
            pack = widen(both(heads, heads_other, mc)).transpose(0, 2, 1, 3, 4)
            head_triple = pack[..., :slab, :].reshape(width, QUAD)
            live0, live1 = [
                pick(pack, c, 2)[..., slab, :rows].astype(WIDE).reshape(-1, rows)
                for c in (mc, 1 - mc)
            ]
        else:
            head_triple, live0, live1 = whole(
                heads_kernel,
                "heads",
                index,
                (heads, heads_other),
                [shape((width, QUAD), LOW)] + [shape((NZ * 2, rows), WIDE)] * 2,
            )
        return head_triple, key_doc(live0, mc), key_doc(live1, 1 - mc)

    few_out = slab // 2 if outer == 1 else 0
    heads, low_slab, triple_slab, mine, own = whole(
        prep_kernel,
        "prep",
        index,
        (
            triple_weight.transpose(1, 0, 2),
            output_weight.T,
            expand_weight,
            contract_weight.T,
            line(live_mask),
            tokens,
        ),
        [shape((NZ * 2, slab + extra_count(slab), QUAD), LOW)]
        + [shape((slab, n), LOW) for n in (2 * span, 6 * QUAD)]
        + [shape((half + few_out, width), LOW), shape((rows + few_out, width), LOW)],
    )
    by_z = [mine] + [xor_z(mine, m) for m in (1, 2, 3)]
    own_other = flip(own, "x")

    where = jnp.arange(rows, dtype=jnp.int32) * blocks
    rank = jnp.arange(NZ * 2, dtype=jnp.int32) * 2
    shares = query_vecs.shape[0] // (NZ * 4)
    by_z = list(lax.optimization_barrier((*by_z, heads, own_other))[:NZ])
    gathered = lax.all_gather(after(low_slab, *by_z[1:]), BLK, axis=0, tiled=True)

    def heads_stage():
        got = lax.all_to_all(heads, ("z", "x"), 0, 0)
        sheets, outs = [tokens, own_other], [own[rows:], own_other[rows:]]
        for piece in by_z[1:]:
            turned = flip(piece, "x")
            outs += [piece[half:], turned[half:]]
            two = jnp.stack([piece[:half], turned[:half]])
            sheets += [two, flip(two, "y")]
        if outer > 1:
            out_low = output_weight.T.astype(LOW)
            outs = [lax.all_gather(out_low, BLK, axis=0, tiled=True)]
        else:
            outs = [jnp.stack(outs)]
            outs.append(flip(outs[0], "c"))
        own_places = (mo * NZ * 4 + rank + mc)[:, None] + where[None, :]
        own_position = doc_layout(doc_lengths, own_places.reshape(-1))[1]
        lane = jnp.arange(PAIR) % (HEAD_DIM // 2)
        exponent = (2 * lane).astype(WIDE) / HEAD_DIM
        angles = own_position.astype(WIDE)[:, None] * jnp.exp(-math.log(10000.0) * exponent)[None, :]
        sign = jnp.where(jnp.arange(PAIR) % HEAD_DIM < HEAD_DIM // 2, -1.0, 1.0).astype(WIDE)
        tables = jnp.cos(angles), jnp.sin(angles) * sign[None, :]
        units = whole(
            query_kernel,
            "query_units",
            index,
            (query_vecs,),
            [shape(query_vecs.shape, LOW), shape((shares, proj), LOW)],
        )
        positive = line(jnp.repeat(positives, query_vecs.shape[0] // queries_count))
        got = after(got, sheets[3], sheets[5], sheets[7], tables[0], units[0])
        head = head_weights(got, flip(got, "c"))
        return head, outs, sheets[2:], tables, list(units), positive

    head, outs, sheets, (cosine, sine), (query_unit, own_queries), positive = stage(heads_stage)
    outs = tuple(outs)
    head_triple, kdoc0, kdoc1 = head
    pieces = len(outs)
    sheets = [tokens, own_other] + sheets
    positive = lax.optimization_barrier(positive)
    count = NZ * 2 * rows

    def project_stage():
        queries, kv = whole(
            project_kernel,
            "project",
            index,
            (*sheets, head_triple, cosine, sine, triple_bias),
            [shape((count, PAIR), LOW)] * 2,
            [pltpu.VMEM((count, width), LOW)],
        )
        return queries, kv, flip(kv, "c")

    queries, kv, kv_other = stage(project_stage)
    kv0, kv1 = [widen(v).reshape(-1, PAIR) for v in (kv, kv_other)]
    meta = (kdoc0, kdoc1)
    steps = (blocks, index, doc_lengths)

    def to_blocks(value):
        return lax.all_to_all(value.reshape((NZ * 2,) + value.shape[-2:]), ("z", "x"), 0, 0)

    def attention_stage():
        out, log_total, pack = attend(*steps, queries, kv0, kv1, *meta)
        return out, log_total, to_blocks(pack)

    out, log_total, pack = stage(attention_stage)
    wide_rows, low_rows, thin_rows = [shape((rows, n), t) for n, t in ((width, WIDE), (width, LOW), (1, WIDE))]
    def branch_stage():
        low, part = whole(
            partial(branch_kernel, pieces),
            "branch",
            index,
            (pack,),
            [shape((rows, 2 * QUAD), LOW), low_rows],
            piece_scratch(width, 2 * QUAD),
            outs,
        )
        return low, part, flip(part, "y")

    attended_low, part, part_other = stage(branch_stage)
    gathered = after(gathered, part)
    both_slabs = slab_scratch(width, span) * 2
    triple_low = lax.all_gather(after(triple_slab, part), BLK, axis=0, tiled=True)
    few = rows * QUAD // width
    first, unitary1, inverse1, hidden_in, keep, send, part = whole(
        forward_kernel,
        "forward",
        index,
        (
            part, part_other, tokens, line(output_bias), line(first_gain), line(first_shift),
            line(expand_bias), attended_low,
        ),
        [wide_rows, wide_rows, thin_rows, shape((rows, span), WIDE)]
        + [shape((2 * rows + few, width), LOW)] * 2
        + [low_rows],
        [pltpu.VMEM((rows, width), LOW), pltpu.VMEM((rows, span), LOW)] + both_slabs,
        (gathered,),
    )

    def over_z(parts):
        return [parts[0]] + [xor_z(parts[m], m) for m in (1, 2, 3)]

    def four_cores(keep, send):
        two = [keep, flip(send, "x")]
        return two + [flip(value, "c") for value in two]

    first_keep, first_other, first_across = keep, flip(send, "x"), flip(keep, "c")
    my_tokens = query_unit.shape[0]

    def second_stage():
        return whole(
            second_kernel,
            "second",
            index,
            (
                part, flip(part, "y"), first, line(contract_bias), line(second_gain),
                line(second_shift), head_weight, query_unit, kdoc0,
            ),
            [low_rows, wide_rows, thin_rows] + [shape((rows, proj), t) for t in (WIDE, LOW)]
            + [shape((rows, my_tokens), WIDE), shape((docs, my_tokens), LOW)]
            + [shape((rows, proj), WIDE)],
        )

    second_low, unitary2, inverse2, embed, unit_low, expo, totals, message = stage(second_stage)
    totals = after(totals, first_across)

    def tree(own, one, two, three):
        one, two, three = [part.astype(WIDE) for part in (one, two, three)]
        return ((own.astype(WIDE) + one) + (two + three)).astype(LOW)

    chunk = width // (NZ * 4)
    sums_dims = (NZ * 2, chunk + 16, proj)
    def middle_stage():
        sums = sum_outer(tree(totals, *[xor_s(totals, m) for m in (1, 2, 3)]))
        return whole(
            partial(middle_kernel, queries_count),
            "middle",
            index,
            (
                sums, *[xor_z(sums, m) for m in (1, 2, 3)], kdoc0, kdoc1, positive, expo, query_unit,
                unit_low, embed, second_low, head_weight, out_cotangent, unitary2, inverse2,
                line(second_gain), hidden_in,
            ),
            [wide_rows]
            + [shape((2 * rows, width), LOW)] * 2
            + [low_rows, shape((8, proj), WIDE), shape((docs, my_tokens), WIDE)]
            + [shape(sums_dims, WIDE), shape(sums_dims, LOW)],
            [
                pltpu.VMEM((rows, my_tokens), LOW),
                pltpu.VMEM((rows, width), LOW),
                pltpu.VMEM((rows, span), LOW),
                pltpu.VMEM((width, proj), WIDE),
                pltpu.VMEM((NZ * 4 * 16, proj), WIDE),
            ]
            + both_slabs,
            (gathered,),
        )

    grad_second_in, keep, send, part, loss, coefficients, sums_own, sums_send = stage(middle_stage)

    part, first_other = lax.optimization_barrier((part, first_other))
    units = lax.all_gather(after(message, part), BLK, axis=0, tiled=True)
    keep_other, keep_across = flip(send, "x"), flip(keep, "c")

    def first_stage():
        return whole(
            partial(first_back_kernel, pieces),
            "first_back",
            index,
            (
                part, flip(part, "y"), grad_second_in, unitary1, inverse1, line(first_gain),
                sums_own, flip(sums_send, "c"),
            ),
            [wide_rows, low_rows, shape((8, width), WIDE)]
            + [shape((NZ * 2, half + chunk + 16, PAIR), LOW)],
            piece_scratch(width, 2 * QUAD),
            outs,
        )

    grad_first_in, grad_branch, vectors1, pack = stage(first_stage)
    keep_other, triple_low, grad_branch = lax.optimization_barrier((keep_other, triple_low, grad_branch))
    dims, dims_out = (2, slab, quarter), (2, slab, QUAD)
    dims_both = (2, slab, quarter + QUAD)
    left_right = [pltpu.VMEM((4 * rows, width), LOW)]

    def parts_of(left, right):
        part = dot_tn(jnp.concatenate(left), jnp.concatenate(right))
        part = pick(narrow(part.reshape(outer, NZ, 2, 2, slab, -1)), mc, 2)
        for axis, spot in ((0, mz), (1, mx)):
            part = jnp.take(part, jnp.arange(part.shape[axis]) ^ spot, axis=axis)
        return part

    def low_parts(parts):
        return [parts[0]] + [parts[m].astype(LOW) for m in (1, 2, 3)]

    def weights_stage():
        got = to_blocks(pack)
        firsts = [first_keep, first_other, first_across, flip(first_other, "c")]
        grads = [keep, keep_other, keep_across, flip(keep_other, "c")]
        other = flip(grad_branch, "x")
        got = got, [other, flip(grad_branch, "c"), flip(other, "c")], firsts[3]
        if outer == 1:
            parts = whole(
                weights_kernel,
                "weights",
                index,
                (*firsts, *grads),
                [shape((2,) + dims, WIDE), shape((2,) + dims, LOW)] * 2,
                left_right * 2,
            )
            return got, list(parts)
        top, mid = slice(0, rows), slice(rows, 2 * rows)
        contract = parts_of([g[top] for g in grads], [f[mid] for f in firsts])
        expand = parts_of([f[top] for f in firsts], [g[mid] for g in grads])
        return got, [part for p in (contract, expand) for part in (p[::2], p[1::2].astype(LOW))]

    (grad_out, branches, first_last), weight_parts = stage(weights_stage)
    branches = [grad_branch] + branches
    firsts = [first_keep, first_other, first_across, first_last]
    contract_keep, contract_send, expand_keep, expand_send = weight_parts
    contract_got, expand_got = xor_z(contract_send, 1), xor_z(expand_send, 1)

    def attend_stage():
        grad_query, dkv0, dkv1 = attend_back(
            *steps, queries, grad_out.reshape(NZ, 2, -1, PAIR), out, log_total, kv0, kv1, *meta
        )
        dkv0, dkv1 = [narrow(v.reshape(outer, -1, PAIR)) for v in (dkv0, dkv1)]
        triple = whole(
            triple_kernel,
            "triple",
            index,
            (grad_query.reshape(count, PAIR), dkv0, flip(dkv1, "c"), cosine, sine),
            [shape((count, QUAD), LOW), shape((NZ * 2, rows * 3 // 4, QUAD), LOW)],
        )
        return triple

    grad_triple, dense_triple = stage(attend_stage)
    grad_triple, contract_got = lax.optimization_barrier((grad_triple, contract_got))
    contract_own, contract_send = whole(
        pair_kernel, "pair", index, (contract_keep, contract_got), [shape(dims, t) for t in (WIDE, LOW)]
    )
    contract_got = xor_z(contract_send, 2)
    grad_triple, units = lax.optimization_barrier((grad_triple, units, contract_own))[:2]
    dims_triple = (NZ * 2, slab + extra_count(slab), QUAD)
    vector = shape((width // PAIR, PAIR), WIDE)

    def triple_parts():
        if outer == 1:
            return whole(
                triple_weight_kernel,
                "triple_weight",
                index,
                (*sheets, grad_triple, vectors1),
                [shape(dims_triple, LOW)] * 2,
                [pltpu.VMEM((width, QUAD), WIDE), pltpu.VMEM((count, width), LOW)],
            )
        ordered = [(mz * 2 + (mx ^ x), sheets[x]) for x in range(2)]
        for m in (1, 2, 3):
            two = both(*sheets[2 * m : 2 * m + 2], my)
            for x in range(2):
                ordered.append(((mz ^ m) * 2 + (mx ^ x), two[:, x].reshape(rows, width)))
        ordered = place(ordered).reshape(count, width)
        part = narrow(dot_tn(ordered, grad_triple).reshape(outer, NZ * 2, 2, slab, QUAD))
        bias = sum_outer(jnp.sum(grad_triple, axis=0, dtype=WIDE))
        bias = extra_rows(line(bias), sum_outer(vectors1))
        bias = jnp.broadcast_to(bias, (NZ * 2, 2, 16, QUAD))
        part = jnp.concatenate([part, bias], axis=2).astype(LOW)
        return pick(part, mc, 1), pick(part, 1 - mc, 1)

    def output_parts_of():
        if outer == 1:
            return whole(
                output_kernel,
                "output",
                index,
                (*firsts, *branches),
                [shape((2,) + dims_out, t) for t in (WIDE, LOW)],
                left_right + [pltpu.VMEM((4 * rows, QUAD), LOW)],
            )
        wide = [f[2 * rows :].reshape(few, 4, QUAD).transpose(1, 0, 2).reshape(rows, QUAD) for f in firsts]
        parts = parts_of(branches, wide)
        return parts[::2], parts[1::2].astype(LOW)

    def triple_stage():
        block_triple = to_blocks(dense_triple)
        keep, send = triple_parts()
        output_parts = output_parts_of()
        mine = whole(
            partial(query_back_kernel, half),
            "query_back",
            index,
            (kdoc0, kdoc1, coefficients, own_queries, units, sum_outer(grad_out)),
            [shape((shares + chunk + 16, proj), LOW)],
        )[0]
        return block_triple, keep, send, output_parts[0], xor_z(output_parts[1], 1), mine

    block_triple, packed_keep, packed_send, output_keep, output_got, mine = stage(triple_stage)
    block_triple, contract_got, expand_got = lax.optimization_barrier(
        (block_triple, contract_got, expand_got)
    )
    expand_own, output_own, both_send = whole(
        pair_kernel,
        "pair",
        index,
        (expand_keep, expand_got, output_keep, output_got),
        [shape(dims, WIDE), shape(dims_out, WIDE), shape(dims_both, LOW)],
    )
    both_got = xor_z(both_send, 2)
    block_triple = after(block_triple, expand_own)
    spread = lax.all_gather(after(mine, expand_own), ("z", "x", "c"))

    def tokens_stage():
        part = whole(
            tokens_kernel,
            "tokens",
            index,
            (block_triple,),
            [low_rows],
            [pltpu.VMEM((rows, 6 * QUAD), LOW)] + slab_scratch(width, 6 * QUAD),
            (triple_low,),
        )[0]
        part_other = flip(part, "y")
        packed = whole(
            pair_sum_kernel,
            "pair_sum",
            index,
            (packed_keep, flip(packed_send, "c")),
            [shape(dims_triple, LOW)],
        )[0]
        tokens_grad = whole(
            tokens_sum_kernel, "tokens_sum", index, (after(part, packed), part_other, grad_first_in), [wide_rows]
        )[0]
        return tokens_grad, packed

    tokens_grad, packed = stage(tokens_stage)
    packed = lax.all_to_all(after(packed, tokens_grad), ("z", "x"), 0, 0)
    contract_own, spread = after(contract_own, tokens_grad), after(spread, tokens_grad)
    keep, keep_out, send = whole(
        line_sum_kernel,
        "line_sum",
        index,
        (contract_own, contract_got, expand_own, output_own, both_got),
        [shape((2, slab, quarter), WIDE), shape((slab, QUAD), WIDE), shape((slab, 2 * quarter + QUAD), LOW)],
    )
    triple_grad, triple_bias_grad, output_bias_grad, gain_one, shift_one = whole(
        triple_out_kernel,
        "triple_out",
        index,
        (packed,),
        [shape((3, slab, 2 * QUAD), WIDE), shape((3, 2 * QUAD), WIDE)] + [vector] * 3,
    )
    contract_grad, expand_grad, output_grad = whole(
        columns_kernel,
        "columns",
        index,
        (keep, keep_out, flip(send, "x")),
        [shape((slab, n), WIDE) for n in (span, span, 2 * QUAD)],
    )

    queries_grad, head_grad, contract_bias_grad, gain_two, shift_two, expand_bias_grad = whole(
        spread_kernel,
        "spread",
        index,
        (after(spread, contract_grad).reshape(NZ * 4, -1, proj),),
        [shape((query_vecs.shape[0], proj), WIDE), shape((width, proj), WIDE)]
        + [vector] * 3
        + [shape((span // PAIR, PAIR), WIDE)],
    )

    return (
        second_low,
        after(loss, tokens_grad)[0, 0],
        tokens_grad,
        queries_grad,
        triple_grad.transpose(1, 0, 2),
        triple_bias_grad,
        output_grad.T,
        output_bias_grad.reshape(-1),
        gain_one.reshape(-1),
        shift_one.reshape(-1),
        expand_grad,
        expand_bias_grad.reshape(-1),
        contract_grad.T,
        contract_bias_grad.reshape(-1),
        gain_two.reshape(-1),
        shift_two.reshape(-1),
        head_grad,
    )


def solution(mesh):
    outer = mesh.shape["blk"] // 16
    five = Mesh(mesh.devices.reshape(outer, NZ, 2, 2, mesh.shape["tensor"]), BLK + ("y",))
    blk, tensor = BLK, "y"
    return jax.shard_map(
        shards,
        mesh=five,
        in_specs=(
            P(blk, None),
            P(),
            P(blk, None),
            P(),
            P(blk),
            P(),
            P(blk, None, tensor),
            P(None, tensor),
            P(tensor, blk),
            P(),
            P(),
            P(),
            P(blk, tensor),
            P(tensor),
            P(tensor, blk),
            P(),
            P(),
            P(),
            P(),
        ),
        out_specs=(
            P(blk, None),
            P(),
            P(blk, None),
            P(),
            P(blk, None, tensor),
            P(None, tensor),
            P(tensor, blk),
            P(),
            P(),
            P(),
            P(blk, tensor),
            P(tensor),
            P(tensor, blk),
            P(),
            P(),
            P(),
            P(),
        ),
        check_vma=False,
    )
```
